32 devices in a mesh: dp: 4 (over x, core), tile: 8 (over z, y).
Axes of the slice: x: 2, y: 2, z: 4, core: 2. Of those that a mesh axis runs over, the one named last changes fastest.
Arguments:
- embeddings: bfloat16 [4, 1024, 512], P('dp', 'tile'), may hold values from -6 to 6
- page_images: bfloat16 [4, 3, 128, 512], P('dp', None, 'tile'), may hold values from -6 to 6
- token_boxes: int32 [4, 4, 1024], P(None, 'dp', 'tile'), may hold values from 0 to 512, as said below
- segment_ids: int32 [4, 1024], P('dp', 'tile'), may hold values from 0 to 1, as said below
- down_first: bfloat16 [3, 3, 32, 3], replicated, may hold values from -1.25 to 1.25
- down_second: bfloat16 [3, 3, 64, 32], replicated, may hold values from -0.375 to 0.375
- down_third: bfloat16 [3, 3, 128, 64], replicated, may hold values from -0.25 to 0.25
- down_fourth: bfloat16 [3, 3, 256, 128], replicated, may hold values from -0.1875 to 0.1875
- down_fifth: bfloat16 [3, 3, 512, 256], replicated, may hold values from -0.125 to 0.125
- up_fourth: bfloat16 [3, 3, 256, 512], replicated, may hold values from -0.09375 to 0.09375
- up_third: bfloat16 [3, 3, 128, 256], replicated, may hold values from -0.125 to 0.125
- up_second: bfloat16 [3, 3, 64, 128], replicated, may hold values from -0.1875 to 0.1875
- up_first: bfloat16 [3, 3, 32, 64], replicated, may hold values from -0.25 to 0.25
- roi_proj: bfloat16 [128, 512], replicated, may hold values from -1 to 1
- gain_attn: bfloat16 [512], replicated, may hold values from 0.5 to 1.5
- w_query: bfloat16 [512, 512], replicated, may hold values from -0.25 to 0.25
- w_key: bfloat16 [512, 512], replicated, may hold values from -0.25 to 0.25
- w_value: bfloat16 [512, 512], replicated, may hold values from -0.25 to 0.25
- w_output: bfloat16 [512, 512], replicated, may hold values from -6 to 6
- bias_table: bfloat16 [8, 96], replicated, may hold values from -3 to 3
- gain_ffn: bfloat16 [512], replicated, may hold values from 0.5 to 1.5
- ffn_in: bfloat16 [512, 2048], replicated, may hold values from -0.25 to 0.25
- ffn_out: bfloat16 [2048, 512], replicated, may hold values from -0.125 to 0.125
- cotangent: bfloat16 [4, 1024, 512], P('dp', 'tile'), may hold values from -6 to 6
Outputs:
- output: bfloat16 [4, 1024, 512], P('dp', 'tile')
- input_grad: float32 [4, 1024, 512], P('dp', 'tile')
- grad_down_first: float32 [3, 3, 32, 3], replicated
- grad_down_second: float32 [3, 3, 64, 32], replicated
- grad_down_third: float32 [3, 3, 128, 64], replicated
- grad_down_fourth: float32 [3, 3, 256, 128], replicated
- grad_down_fifth: float32 [3, 3, 512, 256], replicated
- grad_up_fourth: float32 [3, 3, 256, 512], replicated
- grad_up_third: float32 [3, 3, 128, 256], replicated
- grad_up_second: float32 [3, 3, 64, 128], replicated
- grad_up_first: float32 [3, 3, 32, 64], replicated
- grad_roi_proj: float32 [128, 512], replicated
- grad_gain_attn: float32 [512], replicated
- grad_query: float32 [512, 512], replicated
- grad_key: float32 [512, 512], replicated
- grad_value: float32 [512, 512], replicated
- grad_output: float32 [512, 512], replicated
- grad_bias_table: float32 [8, 96], replicated
- grad_gain_ffn: float32 [512], replicated
- grad_ffn_in: float32 [512, 2048], replicated
- grad_ffn_out: float32 [2048, 512], replicated
The draws below stay inside these ranges and needn't reach their ends.
Inputs may be any that keep to these rules, and one draw needn't show every extreme that they name: `token_boxes`: each box has x1 - x0 and y1 - y0 at least 2, x1 <= 512, and its rows y0 to y1 - 1 inside one block of 16 pixel rows. In each row, of the boxes of the 128 tokens of one device at most 64 fall in any one block, and every device's tokens have exactly 64 in one common block, which so holds 512 boxes; no block holds more. `segment_ids`: never falling along a row; each row has two documents, one of fewer than 64 tokens at its start or its end.
All inputs are finite; a program needn't handle non-finite values.
Results may differ from the reference program's by a relative error of at most 0.018.
Values may be sent and summed in bfloat16 or wider, within the bound.
No kernel may reach another device: no remote copies, remote signals or barrier semaphores. Data moves between devices by JAX's collectives and lax.ppermute only.
A program may use at most 192 MiB of HBM per device.

```python
import math
import jax
import jax.numpy as jnp
from jax import lax

D = 512
HEADS = 8
HD = 64
FF = 2048
C0 = 32
NB = 32
TILE_ROWS = 16
WIDTH = 512
TOK_DEV = 128
SEQ = 1024
ROWS = 4
HEIGHT = 128
POOL = 128
PAIR_MAX = 64
N_TILE = 8


def draw_token_boxes(key, part):
    key = jax.random.fold_in(key, 11)
    subkeys = jax.random.split(key, 8)
    dense_tile = jax.random.randint(subkeys[0], (ROWS, 1), 0, N_TILE)
    rotation = jax.random.randint(subkeys[7], (ROWS, 1), 0, N_TILE - 1)
    perm_keys = jax.random.split(subkeys[1], ROWS * N_TILE)
    local_rank = jax.vmap(lambda subkey: jax.random.permutation(subkey, TOK_DEV))(perm_keys).reshape(ROWS, SEQ)
    device_of = (jnp.arange(SEQ) // TOK_DEV)[None, :]
    spread = (local_rank - PAIR_MAX + device_of + rotation) % (N_TILE - 1)
    owners = jnp.where(local_rank < PAIR_MAX, dense_tile, (dense_tile + 1 + spread) % N_TILE)
    row_off = jax.random.randint(subkeys[3], (ROWS, SEQ), 0, TILE_ROWS - 1)
    height = jax.random.randint(subkeys[4], (ROWS, SEQ), 2, TILE_ROWS - row_off + 1)
    top_row = owners * TILE_ROWS + row_off
    left_col = jax.random.randint(subkeys[5], (ROWS, SEQ), 0, WIDTH - 1)
    width_box = jax.random.randint(subkeys[6], (ROWS, SEQ), 2, jnp.minimum(WIDTH - left_col, 64) + 1)
    return jnp.stack([left_col, top_row, left_col + width_box, top_row + height]).astype(jnp.int32)


def draw_segment_ids(key, part):
    key = jax.random.fold_in(key, 12)
    subkeys = jax.random.split(key, 2)
    at_start = jax.random.randint(subkeys[0], (ROWS, 1), 0, 2)
    offset = jax.random.randint(subkeys[1], (ROWS, 1), 1, TOK_DEV // 2)
    cut_at = jnp.where(at_start == 1, offset, SEQ - offset)
    return (jnp.arange(SEQ)[None, :] >= cut_at).astype(jnp.int32)


def level_of(stream_key, extent, cuts, smallest, largest):
    def one(dim, shards_of):
        draws = jax.random.uniform(jax.random.fold_in(jax.random.fold_in(stream_key, 6), dim), (shards_of,), jnp.float32, smallest / len(cuts), largest / len(cuts))
        return jnp.repeat(jnp.exp(draws), extent[dim] // shards_of).reshape((-1,) + (1,) * (len(extent) - dim - 1))

    level = one(*cuts[0])
    for cut in cuts[1:]:
        level = level * one(*cut)
    return level


def gaussian(key, extent, width, reach, cuts=(), kind=jnp.bfloat16):
    values = jax.random.normal(key, extent, jnp.float32) * width
    if len(cuts) > 0:
        values = level_of(key, extent, cuts, -0.22, 0.18) * values
    return jnp.clip(values, min=-reach, max=reach).astype(kind)


def setup_inputs(seed: int = 0) -> dict:
    streams_of = jax.random.split(jax.random.key(seed), 25)
    embeddings = gaussian(streams_of[0], (ROWS, SEQ, D), 1.0, 6.0, ((0, 4), (1, 8)))
    page_images = gaussian(streams_of[1], (ROWS, 3, HEIGHT, WIDTH), 1.0, 6.0, ((0, 4), (2, 8)))
    token_boxes = draw_token_boxes(jax.random.fold_in(streams_of[24], 71), 0)
    segment_ids = draw_segment_ids(jax.random.fold_in(streams_of[24], 71), 0)
    down_first = gaussian(streams_of[4], (3, 3, C0, 3), 27 ** -0.5, 1.25)
    down_second = gaussian(streams_of[5], (3, 3, 2 * C0, C0), (9 * C0) ** -0.5, 0.375)
    down_third = gaussian(streams_of[6], (3, 3, 4 * C0, 2 * C0), (18 * C0) ** -0.5, 0.25)
    down_fourth = gaussian(streams_of[7], (3, 3, 8 * C0, 4 * C0), (36 * C0) ** -0.5, 0.1875)
    down_fifth = gaussian(streams_of[8], (3, 3, 16 * C0, 8 * C0), (72 * C0) ** -0.5, 0.125)
    up_fourth = gaussian(streams_of[9], (3, 3, 8 * C0, 16 * C0), (144 * C0) ** -0.5, 0.09375)
    up_third = gaussian(streams_of[10], (3, 3, 4 * C0, 8 * C0), (72 * C0) ** -0.5, 0.125)
    up_second = gaussian(streams_of[11], (3, 3, 2 * C0, 4 * C0), (36 * C0) ** -0.5, 0.1875)
    up_first = gaussian(streams_of[12], (3, 3, C0, 2 * C0), (18 * C0) ** -0.5, 0.25)
    roi_proj = gaussian(streams_of[13], (POOL, D), C0 ** -0.5, 1.0)
    gain_attn = jnp.clip(1.0 + 0.1 * jax.random.normal(streams_of[14], (D,), jnp.float32), 0.5, 1.5).astype(jnp.bfloat16)
    w_query = gaussian(streams_of[15], (D, D), D ** -0.5, 0.25)
    w_key = gaussian(streams_of[16], (D, D), D ** -0.5, 0.25)
    w_value = gaussian(streams_of[17], (D, D), D ** -0.5, 0.25)
    w_output = gaussian(streams_of[18], (D, D), 1.0, 6.0)
    bias_table = gaussian(streams_of[19], (HEADS, 3 * NB), 0.5, 3.0)
    gain_ffn = jnp.clip(1.0 + 0.1 * jax.random.normal(streams_of[20], (D,), jnp.float32), 0.5, 1.5).astype(jnp.bfloat16)
    ffn_in = gaussian(streams_of[21], (D, FF), D ** -0.5, 0.25)
    ffn_out = gaussian(streams_of[22], (FF, D), FF ** -0.5, 0.125)
    cotangent = gaussian(streams_of[23], (ROWS, SEQ, D), 1.0, 6.0, ((0, 4), (1, 8)))
    return {"embeddings": embeddings, "page_images": page_images, "token_boxes": token_boxes, "segment_ids": segment_ids, "down_first": down_first, "down_second": down_second, "down_third": down_third, "down_fourth": down_fourth, "down_fifth": down_fifth, "up_fourth": up_fourth, "up_third": up_third, "up_second": up_second, "up_first": up_first, "roi_proj": roi_proj, "gain_attn": gain_attn, "w_query": w_query, "w_key": w_key, "w_value": w_value, "w_output": w_output, "bias_table": bias_table, "gain_ffn": gain_ffn, "ffn_in": ffn_in, "ffn_out": ffn_out, "cotangent": cotangent}


@jax.custom_vjp
def low(v):
    return lax.optimization_barrier(v.astype(jnp.bfloat16)).astype(jnp.float32)

@jax.custom_vjp
def low_back(v):
    return v

def low_keep(v):
    return (low(v), None)

def low_pass(kept, grad):
    return (grad,)

def back_keep(v):
    return (v, None)

def back_low(kept, grad):
    return (low(grad),)
low.defvjp(low_keep, low_pass)
low_back.defvjp(back_keep, back_low)
eps = 1e-06
bounds = (12, 16, 23, 32, 46, 64, 91)
highest = lax.Precision.HIGHEST
neg_large = -1000000000.0

def bucket_of(signed_gap):
    distance = jnp.abs(signed_gap)
    far_steps = jnp.zeros_like(distance)
    for threshold in bounds:
        far_steps = far_steps + (distance >= threshold).astype(distance.dtype)
    nearness = jnp.where(distance < 8, distance, 8 + far_steps)
    return nearness + jnp.where(signed_gap > 0, 16, 0).astype(distance.dtype)

def rms_scale(value, gain):
    return value * lax.rsqrt(lax.optimization_barrier(jnp.mean(value * value, axis=-1, keepdims=True)) + eps) * gain

def conv_same(value, weight):
    padded = jnp.pad(value, ((0, 0), (1, 1), (1, 1)))
    rows_out = value.shape[1]
    cols_out = value.shape[2]
    total = jnp.zeros((weight.shape[2], rows_out, cols_out), value.dtype)
    for row_off in range(3):
        for col_off in range(3):
            window = padded[:, row_off:row_off + rows_out, col_off:col_off + cols_out]
            total = total + jnp.einsum('oc,chw->ohw', weight[row_off, col_off], window, precision=highest)
    return total

def conv_layer(value, weight):
    return jax.nn.gelu(low_back(conv_same(low(value), weight)))

def pool_half(value):
    chans, rows_in, cols_in = value.shape
    return lax.optimization_barrier(jnp.mean(value.reshape(chans, rows_in // 2, 2, cols_in // 2, 2), axis=(2, 4)))

def double_up(value):
    return jnp.repeat(jnp.repeat(value, 2, axis=1), 2, axis=2)

def unet_features(page_float, weights):
    down_first, down_second, down_third, down_fourth, down_fifth, up_fourth, up_third, up_second, up_first = weights
    enc_zero = conv_layer(page_float, down_first)
    enc_one = conv_layer(pool_half(enc_zero), down_second)
    enc_two = conv_layer(pool_half(enc_one), down_third)
    enc_three = conv_layer(pool_half(enc_two), down_fourth)
    enc_four = conv_layer(pool_half(enc_three), down_fifth)
    dec_three = conv_layer(double_up(enc_four), up_fourth) + enc_three
    dec_two = conv_layer(double_up(dec_three), up_third) + enc_two
    dec_one = conv_layer(double_up(dec_two), up_second) + enc_one
    dec_zero = conv_layer(double_up(dec_one), up_first) + enc_zero
    return low(dec_zero)

def roi_pool(features, boxes_row):
    left_col, top_row, right_col, bottom_row = (boxes_row[0], boxes_row[1], boxes_row[2], boxes_row[3])
    mid_row = (top_row + bottom_row) // 2
    mid_col = (left_col + right_col) // 2
    row_ids = jnp.arange(features.shape[1])[None, :]
    col_ids = jnp.arange(features.shape[2])[None, :]
    row_mask = jnp.stack([(row_ids >= top_row[:, None]) & (row_ids < mid_row[:, None]), (row_ids >= mid_row[:, None]) & (row_ids < bottom_row[:, None])], axis=1).astype(jnp.float32)
    col_mask = jnp.stack([(col_ids >= left_col[:, None]) & (col_ids < mid_col[:, None]), (col_ids >= mid_col[:, None]) & (col_ids < right_col[:, None])], axis=1).astype(jnp.float32)
    heights = jnp.stack([mid_row - top_row, bottom_row - mid_row], axis=1).astype(jnp.float32)
    widths_box = jnp.stack([mid_col - left_col, right_col - mid_col], axis=1).astype(jnp.float32)
    partial_cols = jnp.einsum('tbx,cyx->tbcy', col_mask, features, precision=highest)
    totals = jnp.einsum('tay,tbcy->tabc', row_mask, partial_cols, precision=highest)
    band_area = heights[:, :, None] * widths_box[:, None, :]
    pooled = totals / band_area[..., None]
    return pooled.reshape(pooled.shape[0], -1)

def attend_row(normed, w_query, w_key, w_value, bias_table, seg_row, centers):
    seq_len = normed.shape[0]

    def project(weight):
        flat_proj = low(low_back(jnp.dot(normed, weight, precision=highest)))
        return flat_proj.reshape(seq_len, HEADS, HD).transpose(1, 0, 2)
    query_heads = project(w_query)
    key_heads = project(w_key)
    value_heads = project(w_value)
    positions = jnp.arange(seq_len)
    center_x, center_y = centers
    block_len = math.gcd(seq_len, 512)
    block_count = seq_len // block_len

    def one_block(query_blk, pos_blk, seg_blk, cx_blk, cy_blk, key_all, value_all, table_all):
        scores = jnp.einsum('hqd,hkd->hqk', query_blk, key_all, precision=highest) * HD ** (-0.5)
        rel_bucket = bucket_of(positions[None, :] - pos_blk[:, None])
        hor_bucket = bucket_of(center_x[None, :] - cx_blk[:, None]) + NB
        ver_bucket = bucket_of(center_y[None, :] - cy_blk[:, None]) + 2 * NB
        bias_sum = table_all[:, rel_bucket] + table_all[:, hor_bucket] + table_all[:, ver_bucket]
        scores = low_back(scores + bias_sum)
        allowed = seg_blk[:, None] == seg_row[None, :]
        attn_prob = low(jax.nn.softmax(jnp.where(allowed[None], scores, neg_large), axis=-1))
        return jnp.einsum('hqk,hkd->hqd', attn_prob, value_all, precision=highest)
    checked = jax.checkpoint(one_block)

    def run_block(members):
        return checked(members[0], members[1], members[2], members[3], members[4], key_heads, value_heads, bias_table)
    blocks = (query_heads.reshape(HEADS, block_count, block_len, HD).transpose(1, 0, 2, 3), positions.reshape(block_count, block_len), seg_row.reshape(block_count, block_len), center_x.reshape(block_count, block_len), center_y.reshape(block_count, block_len))
    outputs = lax.map(run_block, blocks)
    attn_flat = outputs.transpose(0, 2, 1, 3).reshape(seq_len, HEADS * HD)
    return low(low_back(attn_flat))

def layer_forward(emb_float, page_float, params, token_boxes, segment_ids):
    down_first, down_second, down_third, down_fourth, down_fifth, up_fourth, up_third, up_second, up_first, roi_proj, gain_attn, w_query, w_key, w_value, w_output, bias_table, gain_ffn, ffn_in, ffn_out = params
    results = []
    for row_index in range(ROWS):
        features = unet_features(page_float[row_index], (down_first, down_second, down_third, down_fourth, down_fifth, up_fourth, up_third, up_second, up_first))
        boxes_row = token_boxes[:, row_index]
        pooled = low(roi_pool(features, boxes_row))
        residual = emb_float[row_index] + low_back(jnp.dot(pooled, roi_proj, precision=highest))
        normed = low(rms_scale(residual, gain_attn))
        centers = ((boxes_row[0] + boxes_row[2]) // 2, (boxes_row[1] + boxes_row[3]) // 2)
        attn_flat = attend_row(normed, w_query, w_key, w_value, bias_table, segment_ids[row_index], centers)
        mixed_rows = residual + low_back(jnp.dot(attn_flat, w_output, precision=highest))
        ffn_normed = low(rms_scale(mixed_rows, gain_ffn))
        pre_ffn = low_back(jnp.dot(ffn_normed, ffn_in, precision=highest))
        ffn_part = low_back(jnp.dot(low(jax.nn.gelu(pre_ffn)), ffn_out, precision=highest))
        results.append(mixed_rows + ffn_part)
    return jnp.stack(results)

def reference(embeddings, page_images, token_boxes, segment_ids, down_first, down_second, down_third, down_fourth, down_fifth, up_fourth, up_third, up_second, up_first, roi_proj, gain_attn, w_query, w_key, w_value, w_output, bias_table, gain_ffn, ffn_in, ffn_out, cotangent):
    params = tuple((member.astype(jnp.float32) for member in (down_first, down_second, down_third, down_fourth, down_fifth, up_fourth, up_third, up_second, up_first, roi_proj, gain_attn, w_query, w_key, w_value, w_output, bias_table, gain_ffn, ffn_in, ffn_out)))
    page_float = page_images.astype(jnp.float32)

    def forward(emb_float, *weights):
        return layer_forward(emb_float, page_float, weights, token_boxes, segment_ids)
    result, pullback = jax.vjp(forward, embeddings.astype(jnp.float32), *params)
    grads = pullback(cotangent.astype(jnp.float32))
    return (result.astype(jnp.bfloat16), grads[0], grads[1], grads[2], grads[3], grads[4], grads[5], grads[6], grads[7], grads[8], grads[9], grads[10], grads[11], grads[12], grads[13], grads[14], grads[15], grads[16], grads[17], grads[18], grads[19])
```

```python
import functools
import math

import jax
import jax.numpy as jnp
from jax import lax
from jax.experimental import pallas as pl
from jax.experimental.pallas import tpu as pltpu
from jax.sharding import Mesh
from jax.sharding import PartitionSpec as P

HEADS = 8
HD = 64
NB = 32

eps = 1e-06
bounds = (12, 16, 23, 32, 46, 64, 91)
neg_large = -1000000000.0
HOPS = (("core", 1), ("x", 1), ("tile", 1), ("tile", 4), ("tile", 2))
PAGES = ("x", "core")
f32 = jnp.float32
bf16 = jnp.bfloat16
gelu_scale = math.sqrt(2.0 / math.pi)
VMEM_CAP = 28 * 1024 * 1024


def gelu_of(x):
    x = x.astype(f32)
    half = 0.5 * x
    inner = x * (gelu_scale + (gelu_scale * 0.044715) * (x * x))
    return half + half * jnp.tanh(inner)


def gelu_slope(x):
    x = x.astype(f32)
    sq = x * x
    bent = jnp.tanh(x * (gelu_scale + (gelu_scale * 0.044715) * sq))
    rise = gelu_scale + (3.0 * gelu_scale * 0.044715) * sq
    return 0.5 + 0.5 * bent + (0.5 * x) * (1.0 - bent * bent) * rise


def mm(a, b):
    return jnp.dot(a, b, preferred_element_type=f32)


def mm_tn(a, b):
    return lax.dot_general(a, b, (((0,), (0,)), ((), ())), preferred_element_type=f32)


def mm_nt(a, b):
    return lax.dot_general(a, b, (((1,), (1,)), ((), ())), preferred_element_type=f32)


def mm_fine(a, b):
    high = a.astype(bf16)
    low = (a - high.astype(f32)).astype(bf16)
    return mm(high, b) + mm(low, b)


def lane_ids(shape):
    return lax.broadcasted_iota(jnp.int32, shape, len(shape) - 1)


def row_ids_of(shape):
    return lax.broadcasted_iota(jnp.int32, shape, len(shape) - 2)


def halving(wide, value):
    hit = row_ids_of((wide, wide // 2)) >> 1 == lane_ids((wide, wide // 2))
    return jnp.where(hit, value, 0.0).astype(bf16)


def doubling(narrow):
    hit = row_ids_of((narrow, 2 * narrow)) == lane_ids((narrow, 2 * narrow)) >> 1
    return jnp.where(hit, 1.0, 0.0).astype(bf16)


def pair_halving(value):
    shape = (256, 128)
    source = row_ids_of(shape)
    target = lane_ids(shape)
    hit = source >> 1 == target
    return jnp.where(hit, value, 0.0).astype(bf16)


def side_doubling(side):
    shape = (128, 128)
    hit = row_ids_of(shape) == (lane_ids(shape) >> 1) + 64 * side
    return jnp.where(hit, 1.0, 0.0).astype(bf16)


def quad_map(coarse_lanes, coarse_width):
    shape = (coarse_lanes, 4 * coarse_lanes)
    fine = lane_ids((1, shape[1]))
    shift = coarse_width.bit_length() - 1
    home = (fine >> (shift + 2) << shift) + ((fine & (2 * coarse_width - 1)) >> 1)
    return jnp.where(row_ids_of(shape) == home, 1.0, 0.0).astype(bf16)


def masked(x, keep):
    return x * jnp.where(keep, 1.0, 0.0).astype(x.dtype)


def col_shift(x, step, width):
    if step == 0:
        return x
    lanes = x.shape[1]
    col = lane_ids((1, lanes)) & (width - 1)
    keep = col < width - 1 if step > 0 else col > 0
    return masked(pltpu.roll(x, -step % lanes, 1), keep)


def row_shift(x, step, width):
    if step == 0:
        return x
    lanes = x.shape[1]
    lane = lane_ids((1, lanes))
    keep = lane < lanes - width if step > 0 else lane >= width
    return masked(pltpu.roll(x, (-step * width) % lanes, 1), keep)


def stack_cols(x, width):
    return jnp.concatenate([col_shift(x, step, width) for step in (-1, 0, 1)], axis=0)


def row_ok(first_row, rows, width, low, high):
    row = (lane_ids((1, rows * width)) >> (width.bit_length() - 1)) + first_row
    return (row >= low) & (row < high)


def keep_rows(x, first_row, width, high):
    ok = row_ok(first_row, x.shape[1] // width, width, 0, high)
    return jnp.where(ok, x, 0.0)


def price(micros):
    return pl.CostEstimate(
        flops=int(micros * 5e8), transcendentals=0, bytes_accessed=int(micros * 2e6)
    )


class Fetched:
    def __init__(self, ref, copy):
        self.ref, self.copy, self.waited = ref, copy, False
        self.shape = ref.shape
        copy.start()

    def ready(self):
        if not self.waited:
            self.copy.wait()
            self.waited = True
        return self.ref

    def __getitem__(self, spot):
        return self.ready()[spot]


class Sent:
    def __init__(self, ref, copy):
        self.ref, self.copy, self.started = ref, copy, False
        self.shape = ref.shape

    def send(self):
        if not self.started:
            self.copy.start()
            self.started = True

    def __getitem__(self, spot):
        return self.ref[spot]

    def __setitem__(self, spot, value):
        self.ref[spot] = value


def in_hbm(array):
    return pltpu.with_memory_space_constraint(array, pltpu.HBM)


TOKEN = ((8, 128), f32)


def call(micros, body, outs, scratch, ids, arrays, after=(), late=(), sent=(), table=None):
    count = len(arrays)
    moved = [(arrays[n].shape, arrays[n].dtype) for n in late] + [outs[n] for n in sent]
    arrays = [in_hbm(array) if n in late else array for n, array in enumerate(arrays)]
    after = [in_hbm(token) for token in after]

    scalars = (ids,) if table is None else (ids, table)

    def ordered(*refs):
        refs, heads = refs[len(scalars) :], refs[: len(scalars)]
        ins = list(refs[:count])
        refs = refs[count + len(after) :]
        results = list(refs[: len(outs)])
        own = refs[len(outs) : len(outs) + len(scratch)]
        if moved:
            *stages, marks = refs[len(outs) + len(scratch) :]
        for k, n in enumerate(late):
            ins[n] = Fetched(stages[k], pltpu.make_async_copy(ins[n], stages[k], marks.at[k]))
        for k, n in enumerate(sent, len(late)):
            copy = pltpu.make_async_copy(stages[k], results[n], marks.at[k])
            results[n] = Sent(stages[k], copy)
        body(*heads, *ins, *results, *own)
        for n in late:
            ins[n].ready()
        for n in sent:
            results[n].send()
        for n in sent:
            results[n].copy.wait()

    def place(chosen, total):
        return [
            pl.BlockSpec(memory_space=pltpu.HBM if n in chosen else pltpu.VMEM) for n in range(total)
        ]

    return pl.pallas_call(
        ordered,
        cost_estimate=price(micros),
        out_shape=[
            pltpu.HBM(*out) if n in sent or out == TOKEN else jax.ShapeDtypeStruct(*out)
            for n, out in enumerate(outs)
        ],
        in_specs=[pl.BlockSpec(memory_space=pltpu.SMEM)] * len(scalars)
        + place(late, count)
        + [pl.BlockSpec(memory_space=pltpu.HBM) for _ in after],
        out_specs=place([n for n, out in enumerate(outs) if n in sent or out == TOKEN], len(outs)),
        scratch_shapes=[pltpu.VMEM(shape, kind) for shape, kind in scratch]
        + [pltpu.VMEM(shape, kind) for shape, kind in moved]
        + ([pltpu.SemaphoreType.DMA((len(moved),))] if moved else []),
        compiler_params=pltpu.CompilerParams(vmem_limit_bytes=VMEM_CAP),
    )(*scalars, *arrays, *after)


def lanes_at(start, size):
    return pl.ds(pl.multiple_of(start, 128), size)


def down_body(ids, pages, w_zero, w_one, w_two, pre_zero, pre_one, p_one, pre_two, p_two, p_three, page_own, page, cols, pool_one, stack_one, pool_two):
    tile, high, at = ids[0], ids[1], ids[4]
    page[...] = jnp.zeros_like(page)
    for side in range(-2, 3):
        block = at + side

        @pl.when((block >= 0) & (block < pages.shape[0]))
        def _(block=block, side=side):
            lines = pages[block, :, 0:1024].astype(f32)
            for g in range(8):
                first = (2 + side) * 8192 + 1024 * g
                for c in range(3):
                    page[c : c + 1, first : first + 1024] = lines[8 * c + g : 8 * c + g + 1, :]

    page_full = page[:, 11 * 512 : 69 * 512]
    page_own[...] = page_full[:, 20 * 512 : 38 * 512].astype(bf16)
    for j in range(3):
        cols[j] = col_shift(page_full, j - 1, 512)
    halve = halving(512, 0.25)

    def top(k, keep_pre):
        pieces = [
            cols[j, :, lanes_at((4 * k + i) * 512, 2048)] for i in range(3) for j in range(3)
        ]
        pre = mm(w_zero[...], jnp.concatenate(pieces, axis=0).astype(bf16))
        if keep_pre:
            pre_zero[:, lanes_at((k - 5) * 2048, 2048)] = pre.astype(bf16)
        enc = gelu_of(pre)
        pairs = jnp.concatenate(
            [enc[:, :512] + enc[:, 512:1024], enc[:, 1024:1536] + enc[:, 1536:]], axis=0
        )
        pooled = mm_fine(pairs, halve)
        first = tile * 8 - 10 + 2 * k
        for n in range(2):
            ok = (first + n >= 0) & (first + n < high // 2)
            part = jnp.where(ok, pooled[32 * n : 32 * n + 32], 0.0)
            pool_one[:, lanes_at((2 * k + n) * 256, 256)] = part.astype(bf16)

    for low, end, keep_pre in ((0, 5, False), (5, 9, True), (9, 14, False)):

        @pl.loop(low, end)
        def _(k, keep_pre=keep_pre):
            top(k, keep_pre)

    pre_zero.send()
    page_own.send()
    p_one[...] = pool_one[:, 9 * 256 : 19 * 256]
    p_one.send()
    stack_one[...] = stack_cols(pool_one[...], 256)
    halve_one = halving(256, 0.25)

    @pl.loop(0, 6)
    def _(k):
        pre = sum(
            mm(w_one[i], stack_one[:, lanes_at((4 * k + 1 + i) * 256, 1024)]) for i in range(3)
        )

        @pl.when((k >= 1) & (k < 5))
        def _():
            pre_one[:, lanes_at((k - 1) * 1024, 1024)] = pre.astype(bf16)

        enc = gelu_of(pre)
        pairs = jnp.concatenate(
            [enc[:, :256] + enc[:, 256:512], enc[:, 512:768] + enc[:, 768:]], axis=0
        )
        pooled = mm_fine(pairs, halve_one)
        first = tile * 4 - 4 + 2 * k
        for n in range(2):
            ok = (first + n >= 0) & (first + n < high // 4)
            part = jnp.where(ok, pooled[64 * n : 64 * n + 64], 0.0)
            pool_two[:, lanes_at((2 * k + n) * 128, 128)] = part.astype(bf16)

    pre_one.send()
    p_two[...] = pool_two[:, 3 * 128 : 9 * 128]
    p_two.send()
    stacked = stack_cols(pool_two[...], 128)
    pre = sum(mm(w_two[i], stacked[:, i * 128 : i * 128 + 1280]) for i in range(3))
    pre_two[...] = pre.astype(bf16)
    pre_two.send()
    enc = gelu_of(pre[:, 384:896])
    pairs = jnp.concatenate([enc[:, :128] + enc[:, 128:256], enc[:, 256:384] + enc[:, 384:]], axis=1)
    p_three[...] = mm_fine(pairs, pair_halving(0.25)).astype(bf16)


def run_down(ids, pages, w_zero, w_one, w_two):
    return call(
        10,
        down_body,
        [
            ((32, 16 * 512), bf16),
            ((64, 16 * 256), bf16),
            ((32, 10 * 256), bf16),
            ((128, 10 * 128), bf16),
            ((64, 6 * 128), bf16),
            ((128, 128), bf16),
            ((8, 18 * 512), bf16),
        ],
        [
            ((8, 80 * 512), f32),
            ((3, 8, 58 * 512), f32),
            ((32, 28 * 256), bf16),
            ((96, 28 * 256), bf16),
            ((64, 12 * 128), bf16),
        ],
        ids,
        (pages, w_zero, w_one, w_two),
        sent=(0, 1, 2, 3, 4, 6),
    )


def conv_taps(x, weight, width):
    total = None
    for i in range(3):
        lined = row_shift(x, i - 1, width)
        for j in range(3):
            term = mm(weight[i, j], col_shift(lined, j - 1, width))
            total = term if total is None else total + term
    return total


def conv_taps_back(x, weight, width):
    total = None
    for i in range(3):
        lined = row_shift(x, i - 1, width)
        for j in range(3):
            term = mm_tn(weight[2 - i, 2 - j], col_shift(lined, j - 1, width))
            total = term if total is None else total + term
    return total


def laid_out(blocks):
    return jnp.concatenate([blocks[n] for n in range(blocks.shape[0])], axis=1)


def bottom_body(cut, ids, p_three, w_three, w_four, w_up, pre_three, pre_four, p_four, e_four, pre_up, dec_three):
    lanes = 128 * p_three.shape[0]
    first, high = ids[3], ids[1]

    def kept(x, width, shrink):
        return keep_rows(x, first * (16 // shrink), width, high // shrink) if cut else x

    pre = conv_taps(laid_out(p_three), w_three, 64)
    pre_three[...] = pre.astype(bf16)
    pre_three.send()
    enc_three = kept(gelu_of(pre), 64, 8)
    spread = quad_map(lanes // 4, 32)
    high_part = enc_three.astype(bf16)
    low_part = (enc_three - high_part.astype(f32)).astype(bf16)
    pooled = ((mm_nt(high_part, spread) + mm_nt(low_part, spread)) * 0.25).astype(bf16)
    p_four[...] = pooled
    p_four.send()
    pre = conv_taps(pooled, w_four, 32)
    pre_four[...] = pre.astype(bf16)
    pre_four.send()
    low = kept(gelu_of(pre), 32, 16).astype(bf16)
    e_four[...] = low
    e_four.send()
    pre = conv_taps(mm(low, spread).astype(bf16), w_up, 64)
    pre_up[...] = pre.astype(bf16)
    pre_up.send()
    dec = kept(gelu_of(pre) + enc_three, 64, 8).astype(bf16)
    zero = jnp.zeros((256, 128), bf16)
    dec_three[:, 0:128] = zero
    dec_three[:, 128 : 128 + lanes] = dec
    dec_three[:, 128 + lanes :] = zero


def run_bottom(cut, ids, p_three, w_three, w_four, w_up):
    lanes = 128 * p_three.shape[0]
    return call(
        11,
        functools.partial(bottom_body, cut),
        [
            ((256, lanes), bf16),
            ((512, lanes // 4), bf16),
            ((256, lanes // 4), bf16),
            ((512, lanes // 4), bf16),
            ((256, lanes), bf16),
            ((256, lanes + 256), bf16),
        ],
        [],
        ids,
        (p_three, w_three, w_four, w_up),
        late=(2, 3),
        sent=(0, 1, 2, 3, 4),
    )


def widened(block):
    parts = []
    for n in range(block.shape[1] // 128):
        piece = block[:, 128 * n : 128 * n + 128]
        for side in range(2):
            line = mm(piece, side_doubling(side)).astype(bf16)
            parts += [line, line]
    return jnp.concatenate(parts, axis=1)


def spread_rows(source, target, width):
    spread = doubling(width)
    for n in range(source.shape[1] // width):
        line = mm(source[:, n * width : n * width + width], spread).astype(bf16)
        for m in range(2):
            target[:, (2 * n + m) * 2 * width : (2 * n + m + 1) * 2 * width] = line


def up_body(ids, dec_three, pre_two, pre_one, pre_zero, w_third, w_second, w_first, pre_up_two, pre_up_one, pre_up_zero, u_three, dec_two, dec_one, features, wide_two, stack_two, wide_one, stack_one):
    tile, high, place = ids[0], ids[1], ids[2]
    block = dec_three[:, lanes_at(place * 128, 384)]
    wide = widened(block)
    u_three[...] = wide[:, 384 : 384 + 768]
    u_three.send()
    total = None
    for j in range(3):
        moved = col_shift(wide, j - 1, 128)
        for i in range(3):
            term = mm(w_third[i, j], moved[:, i * 128 : i * 128 + 1280])
            total = term if total is None else total + term
    pre_up_two[...] = total.astype(bf16)
    pre_up_two.send()
    dec = gelu_of(total) + gelu_of(pre_two[...])
    dec = keep_rows(dec, tile * 4 - 3, 128, high // 4).astype(bf16)
    dec_two[...] = dec[:, 128 : 128 + 1024]
    dec_two.send()
    spread_rows(dec, wide_two, 128)
    stack_two[...] = stack_cols(wide_two[...], 256)
    for k in range(3):
        pre = sum(
            mm(w_second[i], stack_two[:, (6 * k + i) * 256 : (6 * k + i) * 256 + 1536])
            for i in range(3)
        )
        pre_up_one[:, 1536 * k : 1536 * k + 1536] = pre.astype(bf16)
    pre_up_one.send()
    dec = gelu_of(pre_up_one[:, 4 * 256 : 14 * 256]) + gelu_of(pre_one[:, 3 * 256 : 13 * 256])
    dec = keep_rows(dec, tile * 8 - 1, 256, high // 2).astype(bf16)
    dec_one[...] = dec
    dec_one.send()
    spread_rows(dec, wide_one, 256)
    stack_one[...] = stack_cols(wide_one[...], 512)
    pre_zero.ready()

    @pl.loop(0, 4)
    def _(k):
        pre = sum(
            mm(w_first[i], stack_one[:, lanes_at((4 * k + 1 + i) * 512, 2048)]) for i in range(3)
        )
        own = lanes_at(k * 2048, 2048)
        pre_up_zero[:, own] = pre.astype(bf16)
        found = (gelu_of(pre) + gelu_of(pre_zero[:, own])).astype(bf16)
        for n in range(4):
            features[pl.ds(pl.multiple_of((4 * k + n) * 32, 32), 32), :] = found[
                :, 512 * n : 512 * n + 512
            ]


def run_up(ids, dec_three, pre_two, pre_one, pre_zero, w_third, w_second, w_first):
    return call(
        9,
        up_body,
        [
            ((128, 10 * 128), bf16),
            ((64, 18 * 256), bf16),
            ((32, 16 * 512), bf16),
            ((256, 6 * 128), bf16),
            ((128, 8 * 128), bf16),
            ((64, 10 * 256), bf16),
            ((16 * 32, 512), bf16),
        ],
        [
            ((128, 20 * 256), bf16),
            ((384, 20 * 256), bf16),
            ((64, 20 * 512), bf16),
            ((192, 20 * 512), bf16),
        ],
        ids,
        (dec_three, pre_two, pre_one, pre_zero, w_third, w_second, w_first),
        late=(1, 2, 3),
        sent=(0, 1, 2, 3, 4, 5),
    )


def band_edges(boxes):
    left, top, right, bottom = (boxes[:, n : n + 1] for n in range(4))
    mid_col = (left + right) >> 1
    mid_row = (top + bottom) >> 1
    return ((left, mid_col, right), (top, mid_row, bottom))


def band_hits(edges, ids_wide, band):
    return (ids_wide >= edges[band]) & (ids_wide < edges[band + 1])


def area_inverse(cols, rows, a, b):
    return 1.0 / ((rows[a + 1] - rows[a]) * (cols[b + 1] - cols[b])).astype(f32)


def pool_body(step, ids, boxes, features, pooled):
    tile = ids[0]
    x_ids = lane_ids((1, 512))
    y_ids = (x_ids >> 5) + tile * 16
    group = lane_ids((1, 128)) >> 5

    @pl.loop(0, boxes.shape[0] // step)
    def _(k):
        own = pl.ds(pl.multiple_of(k * step, step), step)
        cols, rows = band_edges(boxes[own, :])
        result = jnp.zeros((step, 128), f32)
        inside = [jnp.where(band_hits(rows, y_ids, a), 1.0, 0.0) for a in range(2)]
        for b in range(2):
            hits = jnp.where(band_hits(cols, x_ids, b), 1.0, 0.0).astype(bf16)
            lines = mm_nt(hits, features[...])
            for a in range(2):
                part = lines * inside[a]
                part = part[:, :128] + part[:, 128:256] + (part[:, 256:384] + part[:, 384:])
                part = part + pltpu.roll(part, 64, 1)
                part = part + pltpu.roll(part, 32, 1)
                scaled = part * area_inverse(cols, rows, a, b)
                result = jnp.where(group == 2 * a + b, scaled, result)
        pooled[own, :] = result.astype(bf16)


def run_pool(ids, boxes, features, step):
    count = boxes.shape[0]
    return call(
        8, functools.partial(pool_body, step), [((count, 128), bf16)], [], ids, (boxes, features)
    )[0]


def unpool_body(step, ids, boxes, d_pooled, pre_up, d_features, d_low, low_end, low_start, token, total):
    tile = ids[0]
    x_ids = lane_ids((1, 512))
    y_ids = (x_ids >> 5) + tile * 16
    group = lane_ids((1, 128)) >> 5
    source = row_ids_of((128, 512))
    target = lane_ids((1, 512)) & 31
    copies = [
        jnp.where(source == target + 32 * n, 1.0, 0.0).astype(bf16) for n in range(4)
    ]
    total[...] = jnp.zeros_like(total)

    @pl.loop(0, boxes.shape[0] // step)
    def _(k):
        own = pl.ds(pl.multiple_of(k * step, step), step)
        cols, rows = band_edges(boxes[own, :])
        scale = jnp.zeros((step, 128), f32)
        for a in range(2):
            for b in range(2):
                scale = jnp.where(group == 2 * a + b, area_inverse(cols, rows, a, b), scale)
        share = (d_pooled[own, :].astype(f32) * scale).astype(bf16)
        found = None
        inside = [jnp.where(band_hits(rows, y_ids, a), 1.0, 0.0) for a in range(2)]
        for b in range(2):
            placed = mm(share, copies[b]) * inside[0] + mm(share, copies[2 + b]) * inside[1]
            hits = jnp.where(band_hits(cols, x_ids, b), 1.0, 0.0).astype(bf16)
            term = mm_tn(placed.astype(bf16), hits)
            found = term if found is None else found + term
        total[...] += found

    for y in range(16):
        own = slice(512 * y, 512 * y + 512)
        line = total[32 * y : 32 * y + 32, :]
        d_features[:, own] = line
        low = (line * gelu_slope(pre_up[:, own])).astype(bf16)
        d_low[:, own] = low
        if y >= 5:
            low_end[:, 512 * (y - 5) : 512 * (y - 4)] = low
        if y < 11:
            low_start[:, own] = low


def run_unpool(ids, after, boxes, d_pooled, pre_up, step):
    return call(
        8,
        functools.partial(unpool_body, step),
        [
            ((32, 8192), f32),
            ((32, 8192), bf16),
            ((32, 11 * 512), bf16),
            ((32, 11 * 512), bf16),
            TOKEN,
        ],
        [((512, 512), f32)],
        ids,
        (boxes, d_pooled, pre_up),
        after,
        late=(2,),
        sent=(0,),
    )


def up_back_body(ids, before, d_low, behind, pre_up_one, pre_up_two, wd_first, wd_second, w_third, d_dec_one, d_dec_two, d_dec_three, low_one, low_two, token, stack_zero, wide_low):
    tile, high = ids[0], ids[1]
    reach = 11 * 512
    for first, piece in ((0, before), (reach, d_low), (reach + 8192, behind)):
        stack_zero[:, first : first + piece.shape[1]] = stack_cols(piece[...], 512)
    halve = halving(512, 1.0)
    pre_up_one.ready()

    @pl.loop(0, 9)
    def _(k):
        back = sum(
            mm(wd_first[i], stack_zero[:, lanes_at((4 * k + i) * 512, 2048)]) for i in range(3)
        )
        pairs = jnp.concatenate(
            [back[:, :512] + back[:, 512:1024], back[:, 1024:1536] + back[:, 1536:]], axis=0
        )
        summed = mm_fine(pairs, halve)
        first = tile * 8 - 5 + 2 * k
        for n in range(2):
            ok = (first + n >= 0) & (first + n < high // 2)
            own = lanes_at((2 * k + n) * 256, 256)
            part = jnp.where(ok, summed[64 * n : 64 * n + 64], 0.0)
            d_dec_one[:, own] = part
            wide_low[:, own] = (part * gelu_slope(pre_up_one[:, own])).astype(bf16)

    d_dec_one.send()
    low_one[...] = wide_low[:, 5 * 256 : 13 * 256]
    low_one.send()
    stacked = stack_cols(wide_low[...], 256)
    halve_one = halving(256, 1.0)
    for k in range(4):
        back = sum(
            mm(wd_second[i], stacked[:, (4 * k + i) * 256 : (4 * k + i) * 256 + 1024])
            for i in range(3)
        )
        pairs = jnp.concatenate(
            [back[:, :256] + back[:, 256:512], back[:, 512:768] + back[:, 768:]], axis=0
        )
        summed = mm_fine(pairs, halve_one)
        for n in range(2):
            line = 2 * k + n
            row = tile * 4 - 2 + line
            ok = (row >= 0) & (row < high // 4)
            part = jnp.where(ok, summed[128 * n : 128 * n + 128], 0.0)
            d_dec_two[:, 128 * line : 128 * line + 128] = part
    low = d_dec_two[:, 128 : 7 * 128] * gelu_slope(pre_up_two[:, 2 * 128 : 8 * 128])
    low = low.astype(bf16)
    d_dec_two.send()
    low_two[...] = low[:, 128 : 5 * 128]
    low_two.send()
    total = None
    for j in range(3):
        moved = col_shift(low, j - 1, 128)
        for i in range(3):
            term = mm_tn(w_third[2 - i, 2 - j], moved[:, i * 128 : i * 128 + 512])
            total = term if total is None else total + term
    pairs = jnp.concatenate(
        [total[:, :128] + total[:, 128:256], total[:, 256:384] + total[:, 384:]], axis=1
    )
    d_dec_three[...] = mm_fine(pairs, pair_halving(1.0)).astype(bf16)


def run_up_back(ids, after, before, d_low, behind, pre_up_one, pre_up_two, wd_first, wd_second, w_third):
    return call(
        9,
        up_back_body,
        [
            ((64, 18 * 256), f32),
            ((128, 8 * 128), f32),
            ((256, 128), bf16),
            ((64, 8 * 256), bf16),
            ((128, 4 * 128), bf16),
            TOKEN,
        ],
        [((96, 38 * 512), bf16), ((64, 18 * 256), bf16)],
        ids,
        (before, d_low, behind, pre_up_one, pre_up_two, wd_first, wd_second, w_third),
        after,
        late=(3, 4),
        sent=(0, 1, 3, 4),
    )


def bottom_back_body(cut, ids, d_dec_three, pre_up, pre_four, pre_three, w_up, w_four, w_three, low_up, low_four, low_three, d_pool, token, padded):
    lanes = 128 * d_dec_three.shape[0]
    first, high, place = ids[3], ids[1], ids[2]

    def kept(x, width, shrink):
        return keep_rows(x, first * (16 // shrink), width, high // shrink) if cut else x

    d_dec = laid_out(d_dec_three).astype(f32)
    low = (d_dec * gelu_slope(pre_up[...])).astype(bf16)
    low_up[...] = low
    spread = quad_map(lanes // 4, 32)
    back = conv_taps_back(low, w_up, 64)
    high_part = back.astype(bf16)
    low_part = (back - high_part.astype(f32)).astype(bf16)
    d_enc = kept(mm_nt(high_part, spread) + mm_nt(low_part, spread), 32, 16)
    low = (d_enc * gelu_slope(pre_four[...])).astype(bf16)
    low_four[...] = low
    back = conv_taps_back(low, w_four, 32) * 0.25
    d_enc = kept(d_dec + mm_fine(back, spread), 64, 8)
    low = (d_enc * gelu_slope(pre_three[...])).astype(bf16)
    low_three[...] = low
    zero = jnp.zeros((256, 128), bf16)
    padded[:, 0:128] = zero
    padded[:, 128 : 128 + lanes] = low
    padded[:, 128 + lanes :] = zero
    window = padded[:, lanes_at(place * 128, 384)]
    d_pool[...] = conv_taps_back(window, w_three, 64)[:, 0:384]


def run_bottom_back(cut, ids, after, d_dec_three, pre_up, pre_four, pre_three, w_up, w_four, w_three):
    lanes = 128 * d_dec_three.shape[0]
    return call(
        10,
        functools.partial(bottom_back_body, cut),
        [
            ((256, lanes), bf16),
            ((512, lanes // 4), bf16),
            ((256, lanes), bf16),
            ((128, 384), f32),
            TOKEN,
        ],
        [((256, lanes + 256), bf16)],
        ids,
        (d_dec_three, pre_up, pre_four, pre_three, w_up, w_four, w_three),
        after,
        late=(1, 4, 2, 5, 3, 6),
        sent=(3,),
    )


def down_back_body(ids, d_pool_three, d_dec_two, pre_two, d_dec_one, pre_one, d_features, pre_zero, w_two, wd_one, low_two, low_one, low_zero, wide_one):
    tile, high = ids[0], ids[1]
    d_dec_one.ready()
    pre_one.ready()
    d_features.ready()
    pre_zero.ready()
    quarter = d_pool_three[...] * 0.25
    parts = []
    for n in range(3):
        piece = quarter[:, 128 * n : 128 * n + 128]
        for side in range(2):
            line = mm_fine(piece, side_doubling(side))
            parts += [line, line]
    spread = jnp.concatenate(parts[2:10], axis=1)
    d_enc = keep_rows(d_dec_two[...] + spread, tile * 4 - 2, 128, high // 4)
    low = (d_enc * gelu_slope(pre_two[:, 128 : 9 * 128])).astype(bf16)
    low_two[...] = low[:, 2 * 128 : 6 * 128]
    total = None
    for j in range(3):
        moved = col_shift(low, j - 1, 128)
        for i in range(3):
            term = mm_tn(w_two[2 - i, 2 - j], moved[:, i * 128 : i * 128 + 768])
            total = term if total is None else total + term
    total = total * 0.25
    wide = doubling(128)
    for n in range(6):
        line = mm_fine(total[:, 128 * n : 128 * n + 128], wide)
        for m in range(2):
            row = 2 * n + m
            value = d_dec_one[:, (3 + row) * 256 : (4 + row) * 256] + line
            ok = (tile * 8 - 2 + row >= 0) & (tile * 8 - 2 + row < high // 2)
            value = jnp.where(ok, value, 0.0)
            slope = gelu_slope(pre_one[:, (2 + row) * 256 : (3 + row) * 256])
            wide_one[:, row * 256 : row * 256 + 256] = (value * slope).astype(bf16)
    low_one[...] = wide_one[:, 2 * 256 : 10 * 256]
    stacked = stack_cols(wide_one[...], 256)
    back = sum(mm(wd_one[i], stacked[:, (1 + i) * 256 : (9 + i) * 256]) for i in range(3)) * 0.25
    wider = doubling(256)
    for n in range(8):
        line = mm_fine(back[:, 256 * n : 256 * n + 256], wider)
        for m in range(2):
            own = slice((2 * n + m) * 512, (2 * n + m + 1) * 512)
            value = (d_features[:, own] + line) * gelu_slope(pre_zero[:, own])
            low_zero[:, own] = value.astype(bf16)


def run_down_back(ids, after, *arrays):
    return call(
        4,
        down_back_body,
        [
            ((128, 4 * 128), bf16),
            ((64, 8 * 256), bf16),
            ((32, 16 * 512), bf16),
        ],
        [((64, 12 * 256), bf16)],
        ids,
        arrays,
        after,
        late=(0, 1, 2, 3, 4, 5, 6),
    )


def grad_up_first_body(ids, dec_one, d_low, grad, wide_one, stack_one):
    spread_rows(dec_one[...], wide_one, 256)
    stack_one[...] = stack_cols(wide_one[...], 512)
    for i in range(3):
        grad[i] = mm_nt(d_low[...], stack_one[:, (1 + i) * 512 : (17 + i) * 512])


def run_grad_up_first(ids, after, dec_one, d_low):
    return call(
        4,
        grad_up_first_body,
        [((3, 32, 192), f32)],
        [((64, 20 * 512), bf16), ((192, 20 * 512), bf16)],
        ids,
        (dec_one, d_low),
        after,
        late=(0,),
    )[0]


def grad_up_body(ids, grad_first, dec_two, low_one, u_three, low_two, table, token, wide_two, stack_two):
    spread_rows(dec_two[...], wide_two, 128)
    stack_two[...] = stack_cols(wide_two[...], 256)
    for j in range(3):
        moved = col_shift(u_three[...], j - 1, 128)
        for i in range(3):
            first = (3 * i + j) * 128
            grad = mm_nt(low_two[...], moved[:, i * 128 : i * 128 + 512])
            table[first : first + 128, :] = grad.astype(bf16)
    rest = []
    for i in range(3):
        grad = mm_nt(low_one[...], stack_two[:, (3 + i) * 256 : (11 + i) * 256]).astype(bf16)
        table[1152 + 64 * i : 1216 + 64 * i, :] = grad[:, :256]
        rest.append(grad[:, 256:])
    rest = jnp.concatenate(rest, axis=0)
    table[1344:1440, :] = jnp.concatenate([rest[:96], rest[96:]], axis=1)
    table[1440:1536, :] = jnp.zeros((96, 256), bf16)
    for i in range(3):
        table[1440 + 32 * i : 1472 + 32 * i, 0:192] = grad_first[i].astype(bf16)


def run_grad_up(ids, after, *arrays):
    return call(
        4,
        grad_up_body,
        [((1536, 256), bf16), TOKEN],
        [((128, 16 * 256), bf16), ((384, 16 * 256), bf16)],
        ids,
        arrays,
        after,
        late=(1, 2, 3, 4),
    )


def halve_body(ids, kept, got, mine, other, token):
    half = mine.shape[0]
    for bit in range(2):

        @pl.when(ids[5] == bit)
        def _(bit=bit):
            for out, side in ((mine, bit), (other, 1 - bit)):
                own = slice(half * side, half * side + half)
                out[...] = (kept[own, :].astype(f32) + got[own, :].astype(f32)).astype(bf16)


def run_halve(ids, bit, kept, got, after):
    rows, width = kept.shape
    return call(
        max(1, rows // 1500),
        halve_body,
        [((rows // 2, width), bf16)] * 2 + [TOKEN],
        [],
        ids.at[5].set(bit),
        (kept, got),
        after,
    )


def finish_body(ids, kept, got, share):
    share[...] = (kept[...].astype(f32) + got[...].astype(f32)).astype(bf16)


def total_body(ids, parts, share, token):
    total = parts[0].astype(f32)
    for n in range(1, parts.shape[0]):
        total = total + parts[n].astype(f32)
    half = total.shape[0] // 2
    share[...] = jnp.concatenate([total[:half], total[half:]], axis=1).astype(bf16)


def run_total(ids, parts):
    rows, width = parts.shape[1:]
    outs = [((rows // 2, 2 * width), bf16), TOKEN]
    return call(1, total_body, outs, [], ids, (parts,))


def gather_body(ids, heavy, embed, early, share):
    rows, width = heavy.shape[1:]
    total = heavy[0].astype(f32)
    for n in range(1, heavy.shape[0]):
        total = total + heavy[n].astype(f32)
    share[0:rows, :] = total.astype(bf16)
    share[rows : rows + 64, :] = embed[...]
    pad = jnp.zeros((8, width), f32)
    share[rows + 64 :, :] = jnp.concatenate([early[...].astype(f32), pad], axis=0).astype(bf16)


def run_gather(ids, heavy, embed, early):
    rows, width = heavy.shape[1:]
    outs = [((rows + 96, width), bf16)]
    return call(1, gather_body, outs, [], ids, (heavy, embed, early))[0]


def run_finish(ids, kept, got, after):
    return call(1, finish_body, [(kept.shape, bf16)], [], ids, (kept, got), after)[0]


def taps_of(x, width):
    for i in range(3):
        lined = row_shift(x, i - 1, width)
        for j in range(3):
            yield 3 * i + j, col_shift(lined, j - 1, width)


def grad_bottom_body(split, ids, low_up, e_four, low_four, p_four, low_three, p_three, table, token, up_part, four_part, three_part):
    place = ids[2]
    lanes = low_up.shape[1]
    spread = quad_map(lanes // 4, 32)
    shares = table.shape[0]

    def own_part(low):
        rows = low.shape[0] // split
        return low[pl.ds(pl.multiple_of(place * rows, rows), rows), :]

    low = own_part(low_up)
    for tap, x in taps_of(mm(e_four[...], spread).astype(bf16), 64):
        up_part[tap] = mm_nt(low, x)
    low = own_part(low_four)
    for tap, x in taps_of(p_four[...], 32):
        four_part[tap] = mm_nt(low, x)
    low = own_part(low_three)
    for tap, x in taps_of(laid_out(p_three), 64):
        three_part[tap] = mm_nt(low, x)
    for n in range(shares):
        for tap in range(9):
            fifth = jnp.concatenate(
                [
                    four_part[tap, 16 * n : 16 * n + 8, :],
                    four_part[tap, 16 * n + 8 : 16 * n + 16, :],
                ],
                axis=1,
            )
            main = jnp.concatenate([up_part[tap, 8 * n : 8 * n + 8, :], fifth], axis=0)
            table[n, 16 * tap : 16 * tap + 16, :] = main.astype(bf16)
        zero = jnp.zeros((8, 128), f32)
        sides = [three_part[tap, 8 * n : 8 * n + 8, :] for tap in range(9)] + [zero] * 7
        sides = [jnp.concatenate(sides[4 * k : 4 * k + 4], axis=1) for k in range(4)]
        table[n, 144:176, :] = jnp.concatenate(sides, axis=0).astype(bf16)


def run_grad_bottom(split, shares, ids, after, *arrays):
    return call(
        6,
        functools.partial(grad_bottom_body, split),
        [((shares, 176, 512), bf16), TOKEN],
        [
            ((9, 256 // split, 512), f32),
            ((9, 512 // split, 256), f32),
            ((9, 256 // split, 128), f32),
        ],
        ids,
        arrays,
        after,
        late=(1, 3),
    )


def unpack_body(split, whole, *refs):
    stage, marks = refs[-2:]
    plain = list(refs[:-2])
    step = pl.program_id(0)
    last = pl.num_programs(0) - 1

    def fetch(n):
        return pltpu.make_async_copy(whole.at[n], stage.at[n % 4], marks.at[n % 4])

    @pl.when(step == 0)
    def _():
        for n in range(3):
            fetch(n).start()

    @pl.when(step + 3 <= last)
    def _():
        fetch(step + 3).start()

    fetch(step).wait()
    held = stage.at[step % 4]
    first = 0
    if split:
        up, fifth, fourth, *plain, early = plain
        for tap in range(9):
            block = held[16 * tap : 16 * tap + 16, :].astype(f32)
            up[tap] = block[0:8, :]
            fifth[tap, 0:8, :] = block[8:16, 0:256]
            fifth[tap, 8:16, :] = block[8:16, 256:512]
        sides = held[144:176, :].astype(f32)
        for tap in range(9):
            rows = slice(8 * (tap // 4), 8 * (tap // 4) + 8)
            fourth[tap] = sides[rows, 128 * (tap % 4) : 128 * (tap % 4) + 128]
        first = 176
    for out in plain:
        rows = out.shape[0]
        out[...] = held[first : first + rows, :].astype(f32)
        first = first + rows
    if split:
        block = held[first : first + 32, :].astype(f32)
        early[0:24, :] = block[0:24, 0:256]
        early[24:48, :] = block[0:24, 256:512]


def run_unpack(whole, split, rows):
    tiles = whole.shape[0] // 4

    def by_page(n):
        return (0, n % tiles * 4 + n // tiles, 0)

    def chunk_of(n):
        tile, page = n % tiles, n // tiles
        return page % 2 * 16 + page // 2 * 8 + tile % 2 * 4 + tile // 4 * 2 + tile // 2 % 2

    def by_chunk(n):
        return (chunk_of(n), 0)

    def by_column(n):
        return (chunk_of(n) % 8, chunk_of(n) // 8)

    outs = [
        (
            jax.ShapeDtypeStruct((total, width), f32),
            pl.BlockSpec((size, 512), by_column if width > 512 else by_chunk),
        )
        for total, width, size in rows
    ]
    if split:
        outs = (
            [
                (jax.ShapeDtypeStruct((9, 256, 512), f32), pl.BlockSpec((9, 8, 512), by_page)),
                (jax.ShapeDtypeStruct((9, 512, 256), f32), pl.BlockSpec((9, 16, 256), by_page)),
                (jax.ShapeDtypeStruct((9, 256, 128), f32), pl.BlockSpec((9, 8, 128), by_page)),
            ]
            + outs
            + [(jax.ShapeDtypeStruct((1536, 256), f32), pl.BlockSpec((48, 256), lambda n: (n, 0)))]
        )
    return pl.pallas_call(
        functools.partial(unpack_body, split),
        cost_estimate=price(8),
        grid=(whole.shape[0],),
        out_shape=[out for out, _ in outs],
        in_specs=[pl.BlockSpec(memory_space=pltpu.HBM)],
        out_specs=[spec for _, spec in outs],
        scratch_shapes=[
            pltpu.VMEM((4, *whole.shape[1:]), bf16),
            pltpu.SemaphoreType.DMA((4,)),
        ],
        compiler_params=pltpu.CompilerParams(vmem_limit_bytes=VMEM_CAP),
    )(in_hbm(whole))


def grad_bottom_all_body(ids, low_up, e_four, low_four, p_four, low_three, p_three, grad_up, grad_four, grad_three):
    lanes = low_up.shape[1]
    spread = quad_map(lanes // 4, 32)

    def own_part(low):
        size = low.shape[1] // (lanes // 128)
        own = lane_ids(low.shape) // size == ids[2]
        return jnp.where(own, low[...], jnp.zeros((), bf16))

    low = own_part(low_up)
    for tap, x in taps_of(mm(e_four[...], spread).astype(bf16), 64):
        grad_up[tap] = mm_nt(low, x).astype(bf16)
    low = own_part(low_four)
    for tap, x in taps_of(p_four[...], 32):
        grad_four[tap] = mm_nt(low, x).astype(bf16)
    low = own_part(low_three)
    for tap, x in taps_of(laid_out(p_three), 64):
        grad_three[tap] = mm_nt(low, x).astype(bf16)


def run_grad_bottom_all(ids, *arrays):
    return call(
        6,
        grad_bottom_all_body,
        [((9, 256, 512), bf16), ((9, 512, 256), bf16), ((9, 256, 128), bf16)],
        [],
        ids,
        arrays,
    )


def grad_down_body(ids, p_two, low_two, p_one, low_one, page, low_zero, table, cols):
    stacked = stack_cols(p_two[...], 128)
    for i in range(3):
        grad = mm_nt(low_two[...], stacked[:, i * 128 : i * 128 + 512]).astype(bf16)
        table[128 * i : 128 * i + 128, 0:192] = grad
    table[0:384, 192:256] = jnp.zeros((384, 64), bf16)
    table[384:512, :] = jnp.zeros((128, 256), bf16)
    stacked = stack_cols(p_one[...], 256)
    parts = [
        mm_nt(low_one[...], stacked[:, i * 256 : i * 256 + 2048]).astype(bf16) for i in range(3)
    ]
    grad = jnp.concatenate(parts, axis=0)
    table[384:480, 0:96] = grad[:96]
    table[384:480, 128:224] = grad[96:]
    rows = page[...].astype(f32)
    for j in range(3):
        cols[j] = col_shift(rows, j - 1, 512)
    pieces = [cols[j, :, i * 512 : i * 512 + 8192] for i in range(3) for j in range(3)]
    grad = mm_nt(low_zero[...], jnp.concatenate(pieces, axis=0).astype(bf16))
    table[480:512, 0:72] = grad.astype(bf16)


def run_grad_down(ids, *arrays):
    return call(
        3,
        grad_down_body,
        [((512, 256), bf16)],
        [((3, 8, 18 * 512), f32)],
        ids,
        arrays,
        late=(0, 2, 4),
    )[0]


def bucket_of(signed_gap):
    distance = jnp.abs(signed_gap)
    far_steps = jnp.zeros_like(distance)
    for threshold in bounds:
        far_steps = far_steps + (distance >= threshold).astype(jnp.int32)
    nearness = jnp.where(distance < 8, distance, 8 + far_steps)
    return nearness + jnp.where(signed_gap > 0, 16, 0).astype(jnp.int32)


def rms_scale(value, gain):
    return value * lax.rsqrt(jnp.mean(value * value, axis=-1, keepdims=True) + eps) * gain


def gelu_back(pre_act, upstream):
    return jax.vjp(jax.nn.gelu, pre_act)[1](upstream)[0]


def block_scores(query_heads, key_heads, query_meta, key_meta, bias_table, score_scale):
    query_pos, query_cx, query_cy, query_seg = query_meta
    key_pos, key_cx, key_cy, key_seg = key_meta
    rel_bucket = bucket_of(key_pos[None, :] - query_pos[:, None])
    hor_bucket = bucket_of(key_cx[None, :] - query_cx[:, None]) + NB
    ver_bucket = bucket_of(key_cy[None, :] - query_cy[:, None]) + 2 * NB
    slot_ids = jnp.arange(3 * NB)
    one_hot = (
        (rel_bucket[..., None] == slot_ids)
        | (hor_bucket[..., None] == slot_ids)
        | (ver_bucket[..., None] == slot_ids)
    ).astype(jnp.bfloat16)
    scores = (
        jnp.einsum("hqd,hkd->hqk", query_heads, key_heads, preferred_element_type=jnp.float32)
        * score_scale
    )
    scores = scores + jnp.einsum(
        "qkn,hn->hqk", one_hot, bias_table, preferred_element_type=jnp.float32
    )
    allowed = query_seg[:, None] == key_seg[None, :]
    return (scores, allowed, one_hot)


def norm_parts(value):
    scale = lax.rsqrt(jnp.mean(value * value, axis=-1, keepdims=True) + eps)
    return scale


def norm_back(value, gain, upstream):
    scale = norm_parts(value)
    weighted = upstream * gain
    inner = jnp.mean(weighted * value, axis=-1, keepdims=True)
    d_value = weighted * scale - value * (inner * scale * scale * scale)
    d_gain = jnp.sum(upstream * value * scale, axis=0, keepdims=True)
    return d_value, d_gain


def embed_body(ids, pieces, emb, roi, gain, wq, wk, wv, residual, normed, pooled, shared):
    total = pieces[0].astype(f32)
    for n in range(1, pieces.shape[0]):
        total = total + pieces[n].astype(f32)
    low = total.astype(bf16)
    pooled[...] = low
    resid = emb[...].astype(f32) + mm(low, roi[...])
    residual[...] = resid
    normal = (resid * norm_parts(resid) * gain[...].astype(f32)).astype(bf16)
    normed[...] = normal
    for n, weight in enumerate((wq, wk, wv)):
        turned = mm(normal, weight[...]).T.astype(bf16)
        for h in range(HEADS):
            shared[h, HD * n : HD * n + HD, :] = turned[HD * h : HD * h + HD, :]


def run_embed(ids, pieces, emb, *arrays):
    rows, width = emb.shape
    return call(
        2,
        embed_body,
        [
            ((rows, width), f32),
            ((rows, width), bf16),
            ((rows, pieces.shape[2]), bf16),
            ((HEADS, 3 * HD, rows), bf16),
        ],
        [],
        ids,
        (pieces, emb, *arrays),
    )


def looked_up(bucket, table, head, first):
    value = jnp.zeros(bucket.shape, f32)
    for n in range(NB):
        value = jnp.where(bucket == n, table[head, first + n], value)
    return value


def toeplitz(span, table, head, first):
    lane = lane_ids((1, 2 * span))
    gap = jnp.where(lane < span, -lane, 2 * span - lane)
    line = looked_up(bucket_of(gap), table, head, first)
    square = jnp.broadcast_to(line, (span, 2 * span))
    return pltpu.roll(square, 0, 1, stride=1, stride_axis=0)[:, :span].astype(bf16)


def centers(meta):
    return ((meta[0:1, :] + meta[2:3, :]) >> 1, (meta[1:2, :] + meta[3:4, :]) >> 1)


def one_hot_rows(value, span, turned):
    row = row_ids_of((span, value.shape[1]))
    if turned:
        row = span - 1 - row
    return jnp.where(row == value, 1.0, 0.0).astype(bf16)


def attend_body(tall, ids, table, meta, meta_cols, shared, prob, out_low, out_full, hits, spread, near):
    head = ids[0]
    seq = meta.shape[1]
    count = shared.shape[0]
    spans = (512, tall)
    for n, (value, span) in enumerate(zip(centers(meta), spans)):
        chart = toeplitz(span, table, head, NB * (n + 1))
        low = sum(spans[:n])
        spread[low : low + span, :] = mm(chart, one_hot_rows(value, span, False)).astype(bf16)
    cols = meta_cols[...]
    for n, span in enumerate(spans):
        value = (cols[:, n : n + 1] + cols[:, n + 2 : n + 3]) >> 1
        low = sum(spans[:n])
        same = lane_ids((1, span)) == value
        hits[:, low : low + span] = jnp.where(same, 1.0, 0.0).astype(bf16)
    edge = seq - 128
    near[0 : edge - 128, :] = jnp.full((edge - 128, 128), table[head, NB // 2 - 1], f32)
    near[edge + 256 :, :] = jnp.full((seq - 256, 128), table[head, NB - 1], f32)
    gap = row_ids_of((384, 128)) - 128 - lane_ids((384, 128))
    near[edge - 128 : edge + 256, :] = looked_up(bucket_of(gap), table, head, 0)
    query = jnp.concatenate([shared[n, 0:HD, :] for n in range(count)], axis=1)
    key = jnp.concatenate([shared[n, HD : 2 * HD, :] for n in range(count)], axis=1)
    value = jnp.concatenate([shared[n, 2 * HD :, :] for n in range(count)], axis=1)
    key = (key.astype(f32) * (HD**-0.5)).astype(bf16)
    seg_key = cols[:, 4:5]
    for block in range(seq // 256):
        own = slice(256 * block, 256 * block + 256)
        first = edge - 256 * block
        scores = mm_tn(key, query[:, own]) + mm(hits[...], spread[:, own])
        scores = scores + jnp.concatenate(
            [near[first : first + seq, :], near[first - 128 : first - 128 + seq, :]], axis=1
        )
        scores = jnp.where(seg_key == meta[4:5, own], scores, neg_large)
        weight = jnp.exp(scores - jnp.max(scores, axis=0, keepdims=True))
        weight = weight * (1.0 / jnp.sum(weight, axis=0, keepdims=True))
        low = weight.astype(bf16)
        prob[block] = low
        found = mm(value, low)
        out_full[:, own] = found
        for n in range(2):
            out_low[2 * block + n] = found[:, 128 * n : 128 * n + 128].astype(bf16)


def run_attend(tall, ids, table, meta, meta_cols, shared):
    seq = meta.shape[1]
    count = shared.shape[0]
    return call(
        9,
        functools.partial(attend_body, tall),
        [
            ((seq // 256, seq, 256), bf16),
            ((count, HD, seq // count), bf16),
            ((HD, seq), f32),
        ],
        [
            ((seq, 512 + tall), bf16),
            ((512 + tall, seq), bf16),
            ((2 * seq - 128, 128), f32),
        ],
        ids,
        (meta, meta_cols, shared),
        sent=(0, 2),
        table=table,
    )


def bucket_sums(value, bucket):
    lines = [
        jnp.sum(jnp.where(bucket == n, value, 0.0), axis=0, keepdims=True) for n in range(NB)
    ]
    return jnp.sum(jnp.concatenate(lines, axis=0), axis=1, keepdims=True)


def attend_back_body(tall, ids, meta, shared, prob, out_full, d_out, d_shared, d_table, near, drift, key_sum, value_sum):
    seq = meta.shape[1]
    count = shared.shape[0]
    spans = (512, tall)
    query = jnp.concatenate([shared[n, 0:HD, :] for n in range(count)], axis=1)
    key = jnp.concatenate([shared[n, HD : 2 * HD, :] for n in range(count)], axis=1)
    value = jnp.concatenate([shared[n, 2 * HD :, :] for n in range(count)], axis=1)
    d_found = jnp.concatenate([d_out[n] for n in range(count)], axis=1)
    delta = jnp.sum(d_found.astype(f32) * out_full[...], axis=0, keepdims=True)
    near[...] = jnp.zeros_like(near)
    key_sum[...] = jnp.zeros_like(key_sum)
    value_sum[...] = jnp.zeros_like(value_sum)
    places = centers(meta)
    turned = jnp.concatenate(
        [one_hot_rows(place, span, True) for place, span in zip(places, spans)], axis=0
    )
    edge = seq - 128
    scale = HD**-0.5
    for block in range(seq // 256):
        own = slice(256 * block, 256 * block + 256)
        first = edge - 256 * block
        low = prob[block]
        d_prob = mm_tn(value, d_found[:, own])
        d_score = low.astype(f32) * (d_prob - delta[:, own])
        near[first : first + seq, :] += d_score[:, :128]
        near[first - 128 : first - 128 + seq, :] += d_score[:, 128:]
        d_low = d_score.astype(bf16)
        d_query = (mm(key, d_low) * scale).astype(bf16)
        for n in range(2):
            d_shared[2 * block + n, 0:HD, :] = d_query[:, 128 * n : 128 * n + 128]
        key_sum[...] += mm_nt(query[:, own], d_low)
        value_sum[...] += mm_nt(d_found[:, own], low)
        drift[:, own] = mm(turned, d_low).astype(bf16)
    d_key = (key_sum[...] * scale).astype(bf16)
    d_value = value_sum[...].astype(bf16)
    for n in range(count):
        d_shared[n, HD : 2 * HD, :] = d_key[:, 128 * n : 128 * n + 128]
        d_shared[n, 2 * HD :, :] = d_value[:, 128 * n : 128 * n + 128]
    sums = []
    slot = 3 * ids[0]
    gap = row_ids_of((384, 128)) - 128 - lane_ids((384, 128))
    sums.append(bucket_sums(near[edge - 128 : edge + 256, :], bucket_of(gap)))
    row = row_ids_of((NB, 128))
    lane = lane_ids((NB, 128))
    behind = jnp.sum(near[0 : edge - 128, :], axis=0, keepdims=True)
    ahead = jnp.sum(near[edge + 256 :, :], axis=0, keepdims=True)
    far = jnp.where(row == NB // 2 - 1, behind, jnp.where(row == NB - 1, ahead, 0.0))
    sums[0] = sums[0] + jnp.sum(far, axis=1, keepdims=True)
    for n, (place, span) in enumerate(zip(places, spans)):
        low = sum(spans[:n])
        square = mm_nt(drift[low : low + span, :], one_hot_rows(place, span, False))
        square = jnp.concatenate([square, jnp.zeros_like(square)], axis=1)
        lined = pltpu.roll(square, 0, 1, stride=1, stride_axis=0)
        line = jnp.sum(lined, axis=0, keepdims=True)
        bucket = bucket_of(span - 1 - lane_ids((1, 2 * span)))
        sums.append(bucket_sums(line, bucket))
    d_table[...] = jnp.where(
        lane == slot,
        sums[0],
        jnp.where(lane == slot + 1, sums[1], jnp.where(lane == slot + 2, sums[2], 0.0)),
    )


def run_attend_back(tall, ids, after, meta, *arrays):
    seq = meta.shape[1]
    shared = arrays[0]
    return call(
        6,
        functools.partial(attend_back_body, tall),
        [(shared.shape, bf16), ((NB, 128), f32)],
        [
            ((2 * seq - 128, 128), f32),
            ((512 + tall, seq), bf16),
            ((HD, seq), f32),
            ((HD, seq), f32),
        ],
        ids,
        (meta, *arrays),
        after,
        late=(3, 2),
    )


def mixer_body(ids, found, residual, upstream, w_out, gain, w_in, w_down, result, act, d_pre, ffn_low, d_mixed, d_low, d_found, d_gain):
    attn = jnp.concatenate([found[h] for h in range(HEADS)], axis=0)
    mixed = residual[...] + mm_tn(attn, w_out[...])
    wide_gain = gain[...].astype(f32)
    low = (mixed * norm_parts(mixed) * wide_gain).astype(bf16)
    ffn_low[...] = low
    pre = mm(low, w_in[...])
    hidden = gelu_of(pre).astype(bf16)
    act[...] = hidden
    result[...] = (mixed + mm(hidden, w_down[...])).astype(bf16)
    d_hidden = (mm_nt(upstream[...], w_down[...]) * gelu_slope(pre)).astype(bf16)
    d_pre[...] = d_hidden
    d_norm, gain_sum = norm_back(mixed, wide_gain, mm_nt(d_hidden, w_in[...]))
    d_gain[...] = gain_sum
    d_sum = upstream[...].astype(f32) + d_norm
    d_mixed[...] = d_sum
    narrow = d_sum.astype(bf16)
    d_low[...] = narrow
    back = mm_nt(w_out[...], narrow).astype(bf16)
    for h in range(HEADS):
        d_found[h] = back[HD * h : HD * h + HD, :]


def run_mixer(ids, found, residual, upstream, w_out, gain, w_in, w_down):
    rows, width = residual.shape
    wide = w_in.shape[1]
    return call(
        5,
        mixer_body,
        [
            ((rows, width), bf16),
            ((rows, wide), bf16),
            ((rows, wide), bf16),
            ((rows, width), bf16),
            ((rows, width), f32),
            ((rows, width), bf16),
            ((HEADS, HD, rows), bf16),
            ((1, width), f32),
        ],
        [],
        ids,
        (found, residual, upstream, w_out, gain, w_in, w_down),
        late=(5, 6),
    )


def put_halves(ids, first, second, mine, other):
    for bit in range(2):

        @pl.when(ids[5] == bit)
        def _(bit=bit):
            mine[...] = first[...] if bit == 0 else second[...]
            other[...] = second[...] if bit == 0 else first[...]


def mixer_grads_body(ids, found, act, d_pre, ffn_low, d_low, upstream, mine, other, token, table):
    width = ffn_low.shape[1]
    grad_out = mm_tn(act[...], upstream[...]).astype(bf16)
    grad_in = mm_tn(ffn_low[...], d_pre[...]).astype(bf16)
    attn = jnp.concatenate([found[h] for h in range(HEADS)], axis=0)
    grad_attn = mm(attn, d_low[...]).astype(bf16)
    for c in range(32):
        spot, row = 144 * (c % 16), 64 * (c % 8)
        table[c // 16, spot : spot + 64, :] = grad_out[64 * c : 64 * c + 64, :]
        column = width * (c // 8)
        table[c // 16, spot + 64 : spot + 128, :] = grad_in[row : row + 64, column : column + width]
        table[c // 16, spot + 128 : spot + 144, :] = grad_attn[16 * c : 16 * c + 16, :]
    put_halves(ids, table.at[0], table.at[1], mine, other)


def run_mixer_grads(ids, bit, *arrays):
    return call(
        4,
        mixer_grads_body,
        [((2304, 512), bf16)] * 2 + [TOKEN],
        [((2, 2304, 512), bf16)],
        ids.at[5].set(bit),
        arrays,
    )


def embed_back_body(ids, d_shared, residual, d_mixed, gain, wq, wk, wv, roi, d_resid, d_low, d_pooled, d_gain, d_rows, token):
    turned = None
    for n, weight in enumerate((wq, wk, wv)):
        lines = jnp.concatenate([d_shared[h, HD * n : HD * n + HD, :] for h in range(HEADS)], axis=0)
        d_rows[n] = lines
        term = mm(weight[...], lines)
        turned = term if turned is None else turned + term
    d_norm, gain_sum = norm_back(residual[...], gain[...].astype(f32), turned.T)
    d_gain[...] = gain_sum
    total = d_mixed[...] + d_norm
    d_resid[...] = total
    low = total.astype(bf16)
    d_low[...] = low
    d_pooled[...] = mm_nt(low, roi[...]).astype(bf16)


def run_embed_back(ids, d_shared, residual, *arrays):
    rows, width = residual.shape
    roi = arrays[-1]
    return call(
        2,
        embed_back_body,
        [
            ((rows, width), f32),
            ((rows, width), bf16),
            ((rows, roi.shape[0]), bf16),
            ((1, width), f32),
            ((3, HEADS * HD, rows), bf16),
            TOKEN,
        ],
        [],
        ids,
        (d_shared, residual, *arrays),
    )


def embed_grads_body(ids, normed, d_rows, pooled, d_low, gains_one, gains_two, d_table, mine, other, token, table):
    width = normed.shape[1]
    turned = normed[...].astype(f32).T.astype(bf16)
    grads = [mm_nt(turned, d_rows[n]).astype(bf16) for n in range(3)]
    roi = mm_tn(pooled[...], d_low[...])
    lane = lane_ids((1, width))
    buckets = jnp.concatenate([d_table[...]] * (width // 128), axis=1)
    buckets = jnp.where(lane < 128, buckets, 0.0)
    blank = jnp.zeros((1, width), f32)
    for c in range(32):
        spot = 64 * (c % 16)
        for n in range(3):
            table[c // 16, spot + 16 * n : spot + 16 * n + 16, :] = grads[n][16 * c : 16 * c + 16, :]
        gains = [gains_one[...], gains_two[...]] if c == 0 else [blank, blank]
        lines = [roi[4 * c : 4 * c + 4, :], buckets[c : c + 1, :], *gains, blank]
        lines = jnp.concatenate(lines + [jnp.zeros((8, width), f32)], axis=0)
        table[c // 16, spot + 48 : spot + 64, :] = lines.astype(bf16)
    put_halves(ids, table.at[0], table.at[1], mine, other)


def run_embed_grads(ids, bit, after, *arrays):
    return call(
        3,
        embed_grads_body,
        [((1024, 512), bf16)] * 2 + [TOKEN],
        [((2, 1024, 512), bf16)],
        ids.at[5].set(bit),
        arrays,
        after,
    )


def on_device(
    embeddings,
    page_images,
    token_boxes,
    segment_ids,
    down_first,
    down_second,
    down_third,
    down_fourth,
    down_fifth,
    up_fourth,
    up_third,
    up_second,
    up_first,
    roi_proj,
    gain_attn,
    w_query,
    w_key,
    w_value,
    w_output,
    bias_table,
    gain_ffn,
    ffn_in,
    ffn_out,
    cotangent,
):
    tok_rows = embeddings.shape[1]
    model_width = embeddings.shape[2]
    tile_rows = page_images.shape[2]
    my_tile = lax.axis_index("tile")
    tile_count = lax.axis_size("tile")
    score_scale = HD ** (-0.5)
    cut = tile_count > 12
    window = 12 if cut else tile_count
    place = 6 if cut else my_tile
    ids = jnp.stack(
        [
            my_tile,
            jnp.asarray(tile_rows * tile_count, my_tile.dtype),
            jnp.asarray(place, my_tile.dtype),
            my_tile - place,
            jnp.asarray(2 if cut else my_tile, my_tile.dtype),
            jnp.asarray(0, my_tile.dtype),
        ]
    ).astype(jnp.int32)

    def gathered(block):
        copies = jnp.broadcast_to(block[None], (tile_count, *block.shape))
        return lax.all_to_all(copies, "tile", 0, 0, tiled=True)

    def windowed(block):
        if not cut:
            return gathered(block)
        blocks = lax.all_gather(block, "tile", axis=0)
        blocks = jnp.pad(blocks, ((6, 6), (0, 0), (0, 0)))
        return lax.dynamic_slice_in_dim(blocks, my_tile, window, 0)

    def from_side(block, step):
        hops = [
            (source, source + step) for source in range(tile_count) if 0 <= source + step < tile_count
        ]
        return lax.ppermute(block, "tile", hops)

    def lined(weight):
        return weight.transpose(0, 2, 1, 3).reshape(3, weight.shape[2], -1)

    def lined_back(weight):
        flipped = weight[::-1, ::-1]
        return flipped.transpose(0, 3, 1, 2).reshape(3, weight.shape[3], -1)

    def beside(table, count):
        return jnp.concatenate(jnp.split(table, count, axis=0), axis=1)

    def below(table, count):
        return jnp.concatenate(jnp.split(table, count, axis=1), axis=0)

    def as_rows(member):
        return member.reshape(-1, member.shape[-1])

    def bit_of(axis, mask):
        return (lax.axis_index(axis) & mask) // mask

    def swapped(block, axis, mask):
        hops = [(source, source ^ mask) for source in range(lax.axis_size(axis))]
        return lax.ppermute(block, axis, hops)

    def halved(halves, step, *after):
        mine, other, _ = halves
        got = swapped(other, *HOPS[step])
        if step + 1 == len(HOPS):
            return run_finish(ids, mine, got, after)
        return run_halve(ids, bit_of(*HOPS[step + 1]), mine, got, after)

    line = page_images.shape[3]
    meta = jnp.concatenate([token_boxes[:, 0], segment_ids])
    digits = jnp.concatenate([meta // 256, meta % 256, jnp.zeros((2, tok_rows), jnp.int32)])
    digits = digits.astype(jnp.bfloat16).reshape(24, -1)
    sheet = jnp.concatenate([page_images[0].reshape(24, -1), digits], axis=1)
    sheets = gathered(sheet)
    digits_all = sheets[:, :, 2 * line :].reshape(tile_count, 12, tok_rows)
    digits_all = digits_all.transpose(1, 0, 2).reshape(12, -1).astype(jnp.int32)
    meta_all = jnp.pad(digits_all[:5] * 256 + digits_all[5:10], ((0, 3), (0, 0)))
    if cut:
        sheets = jnp.pad(sheets, ((2, 2), (0, 0), (0, 0)))
        sheets = lax.dynamic_slice_in_dim(sheets, my_tile, 5, 0)
    left_all, top_all, right_all, bottom_all, seg_all = (meta_all[n] for n in range(5))
    box_rows = meta_all.T
    seq_all = seg_all.shape[0]
    w_zero = jnp.pad(down_first.transpose(2, 0, 1, 3), ((0, 0), (0, 0), (0, 0), (0, 5)))
    w_zero = w_zero.reshape(w_zero.shape[0], -1)
    pre_zero, pre_one, p_one, pre_two, p_two, p_three, page_own = run_down(
        ids, sheets, w_zero, lined(down_second), lined(down_third)
    )
    p_three_all = windowed(p_three)
    pre_three, pre_four, p_four, e_four, pre_up_three, dec_three = run_bottom(
        cut, ids, p_three_all, down_fourth, down_fifth, up_fourth
    )
    pre_up_two, pre_up_one, pre_up_zero, u_three, dec_two, dec_one, features = run_up(
        ids, dec_three, pre_two, pre_one, pre_zero, up_third, lined(up_second), lined(up_first)
    )
    pooled_own = run_pool(ids, box_rows, features, 256)
    pieces = lax.all_to_all(
        pooled_own.reshape(tile_count, tok_rows, -1), "tile", 0, 0, tiled=True
    )
    gain_row_one = gain_attn.reshape(1, -1)
    gain_row_two = gain_ffn.reshape(1, -1)
    heads_first = tile_count == HEADS
    if heads_first:
        tall = tile_rows * tile_count
        residual, normed_low, pooled_low, shared = run_embed(
            ids, pieces, embeddings[0], roi_proj, gain_row_one, w_query, w_key, w_value
        )
        shared = lax.all_to_all(shared, "tile", 0, 0, tiled=True)
        prob, found_low, found_full = run_attend(
            tall, ids, bias_table.astype(jnp.float32), meta_all, box_rows, shared
        )
        found = lax.all_to_all(found_low, "tile", 0, 0, tiled=True)
        result_low, act_low, d_pre, ffn_low, d_mixed, d_mixed_low, d_found, grad_gain_ffn = run_mixer(
            ids, found, residual, cotangent[0], w_output, gain_row_two, ffn_in, ffn_out
        )
        d_found = lax.all_to_all(d_found, "tile", 0, 0, tiled=True)
        mixer_halves = run_mixer_grads(
            ids, bit_of(*HOPS[0]), found, act_low, d_pre, ffn_low, d_mixed_low, cotangent[0]
        )
        mixer_halves = halved(mixer_halves, 0)
        d_shared, d_table = run_attend_back(
            tall, ids, mixer_halves[2:], meta_all, shared, prob, found_full, d_found
        )
        d_shared = lax.all_to_all(d_shared, "tile", 0, 0, tiled=True)
        d_residual, d_resid_low, d_pooled, grad_gain_attn, d_rows, embed_token = run_embed_back(
            ids, d_shared, residual, d_mixed, gain_row_one, w_query, w_key, w_value, roi_proj
        )
        embed_halves = run_embed_grads(
            ids,
            bit_of(*HOPS[0]),
            (),
            normed_low,
            d_rows,
            pooled_low,
            d_resid_low,
            grad_gain_attn,
            grad_gain_ffn,
            d_table,
        )
        mixer_halves = halved(mixer_halves, 1, embed_token)
        mixer_halves = halved(mixer_halves, 2)
        embed_halves = halved(embed_halves, 0)
        ordering = (embed_halves[2], mixer_halves[2])
    else:
        ordering = ()
        pooled_low = jnp.sum(pieces.astype(jnp.float32), axis=0).astype(jnp.bfloat16)
        residual = embeddings[0].astype(jnp.float32) + jnp.dot(
            pooled_low, roi_proj, preferred_element_type=jnp.float32
        )
        gain_one = gain_attn.astype(jnp.float32)
        normed_low = rms_scale(residual, gain_one).astype(jnp.bfloat16)
        query_low = jnp.dot(normed_low, w_query, preferred_element_type=jnp.float32).astype(
            jnp.bfloat16
        )
        key_low = jnp.dot(normed_low, w_key, preferred_element_type=jnp.float32).astype(jnp.bfloat16)
        value_low = jnp.dot(normed_low, w_value, preferred_element_type=jnp.float32).astype(
            jnp.bfloat16
        )

        def to_heads(flat_rows):
            return flat_rows.reshape(tok_rows, HEADS, HD).transpose(1, 0, 2)

        def from_heads(head_rows):
            return head_rows.transpose(1, 0, 2).reshape(tok_rows, model_width)

        query_heads = to_heads(query_low)
        own_keys = to_heads(key_low)
        own_values = to_heads(value_low)
        key_all, value_all = (
            lax.all_gather(own_keys, "tile", axis=1, tiled=True),
            lax.all_gather(own_values, "tile", axis=1, tiled=True),
        )
        center_x = (left_all + right_all) // 2
        center_y = (top_all + bottom_all) // 2
        key_meta = (jnp.arange(seq_all), center_x, center_y, seg_all)
        first_tok = my_tile * tok_rows
        query_meta = tuple(
            (lax.dynamic_slice_in_dim(member, first_tok, tok_rows, 0) for member in key_meta)
        )
        key_block = math.gcd(seq_all, 1024)
        block_count = seq_all // key_block

        def key_slice(block_id):
            first_key = block_id * key_block
            keys_blk = lax.dynamic_slice_in_dim(key_all, first_key, key_block, 1)
            values_blk = lax.dynamic_slice_in_dim(value_all, first_key, key_block, 1)
            meta_blk = tuple(
                (lax.dynamic_slice_in_dim(member, first_key, key_block, 0) for member in key_meta)
            )
            return (keys_blk, values_blk, meta_blk)

        def stats_step(running, block_id):
            run_max, run_sum = running
            keys_blk, values_blk, meta_blk = key_slice(block_id)
            scores, allowed, one_hot = block_scores(
                query_heads, keys_blk, query_meta, meta_blk, bias_table, score_scale
            )
            scores = jnp.where(allowed[None], scores, neg_large)
            new_max = jnp.maximum(run_max, jnp.max(scores, axis=-1))
            run_sum = run_sum * jnp.exp(run_max - new_max) + jnp.sum(
                jnp.exp(scores - new_max[..., None]), axis=-1
            )
            return ((new_max, run_sum), None)

        start_stats = (
            jnp.full((HEADS, tok_rows), neg_large, jnp.float32),
            jnp.zeros((HEADS, tok_rows), jnp.float32),
        )
        (run_max, run_sum), _ = lax.scan(stats_step, start_stats, jnp.arange(block_count))
        log_total = run_max + jnp.log(run_sum)

        def out_step(attn_acc, block_id):
            keys_blk, values_blk, meta_blk = key_slice(block_id)
            scores, allowed, one_hot = block_scores(
                query_heads, keys_blk, query_meta, meta_blk, bias_table, score_scale
            )
            attn_prob = jnp.where(allowed[None], jnp.exp(scores - log_total[..., None]), 0.0)
            attn_acc = attn_acc + jnp.einsum(
                "hqk,hkd->hqd",
                attn_prob.astype(jnp.bfloat16),
                values_blk,
                preferred_element_type=jnp.float32,
            )
            return (attn_acc, None)

        attn_heads, _ = lax.scan(
            out_step, jnp.zeros((HEADS, tok_rows, HD), jnp.float32), jnp.arange(block_count)
        )
        attn_low = from_heads(attn_heads).astype(jnp.bfloat16)
        mixed_rows = residual + jnp.dot(attn_low, w_output, preferred_element_type=jnp.float32)
        gain_two = gain_ffn.astype(jnp.float32)
        ffn_low = rms_scale(mixed_rows, gain_two).astype(jnp.bfloat16)
        pre_ffn = jnp.dot(ffn_low, ffn_in, preferred_element_type=jnp.float32)
        act_low = jax.nn.gelu(pre_ffn).astype(jnp.bfloat16)
        result_rows = mixed_rows + jnp.dot(act_low, ffn_out, preferred_element_type=jnp.float32)
        upstream = cotangent[0]
        grad_ffn_out = jnp.einsum("tf,td->fd", act_low, upstream, preferred_element_type=jnp.float32)
        d_act = jnp.einsum("td,fd->tf", upstream, ffn_out, preferred_element_type=jnp.float32)
        d_pre = gelu_back(pre_ffn, d_act).astype(jnp.bfloat16)
        grad_ffn_in = jnp.einsum("td,tf->df", ffn_low, d_pre, preferred_element_type=jnp.float32)
        d_ffn_norm = jnp.einsum("tf,df->td", d_pre, ffn_in, preferred_element_type=jnp.float32)
        d_mixed_norm, grad_gain_ffn = jax.vjp(rms_scale, mixed_rows, gain_two)[1](d_ffn_norm)
        d_mixed = upstream.astype(jnp.float32) + d_mixed_norm
        d_mixed_low = d_mixed.astype(jnp.bfloat16)
        grad_output = jnp.einsum("tc,td->cd", attn_low, d_mixed_low, preferred_element_type=jnp.float32)
        d_attn = jnp.einsum(
            "td,cd->tc", d_mixed_low, w_output, preferred_element_type=jnp.float32
        ).astype(jnp.bfloat16)
        dout_heads = to_heads(d_attn)
        row_delta = jnp.sum(dout_heads.astype(jnp.float32) * attn_heads, axis=-1)

        def back_step(running, block_id):
            keys_blk, values_blk, meta_blk = key_slice(block_id)
            scores, allowed, one_hot = block_scores(
                query_heads, keys_blk, query_meta, meta_blk, bias_table, score_scale
            )
            attn_prob = jnp.where(allowed[None], jnp.exp(scores - log_total[..., None]), 0.0)
            d_prob = jnp.einsum(
                "hqd,hkd->hqk", dout_heads, values_blk, preferred_element_type=jnp.float32
            )
            d_score = (attn_prob * (d_prob - row_delta[..., None])).astype(jnp.bfloat16)
            query_acc = running[0] + jnp.einsum(
                "hqk,hkd->hqd", d_score, keys_blk, preferred_element_type=jnp.float32
            )
            table_acc = running[1] + jnp.einsum(
                "hqk,qkn->hn", d_score, one_hot, preferred_element_type=jnp.float32
            )
            first_key = block_id * key_block
            key_part = (
                jnp.einsum("hqk,hqd->hkd", d_score, query_heads, preferred_element_type=jnp.float32)
                * score_scale
            )
            value_part = jnp.einsum(
                "hqk,hqd->hkd",
                attn_prob.astype(jnp.bfloat16),
                dout_heads,
                preferred_element_type=jnp.float32,
            )
            key_acc = lax.dynamic_update_slice_in_dim(running[2], key_part, first_key, 1)
            value_acc = lax.dynamic_update_slice_in_dim(running[3], value_part, first_key, 1)
            return ((query_acc, table_acc, key_acc, value_acc), None)

        start_back = (
            jnp.zeros((HEADS, tok_rows, HD), jnp.float32),
            jnp.zeros((HEADS, 3 * NB), jnp.float32),
        )
        start_back = start_back + (
            jnp.zeros((HEADS, seq_all, HD), jnp.float32),
            jnp.zeros((HEADS, seq_all, HD), jnp.float32),
        )
        back_out, _ = lax.scan(back_step, start_back, jnp.arange(block_count))
        query_acc = back_out[0]
        grad_bias_table = back_out[1]
        key_grad, value_grad = (
            lax.psum_scatter(back_out[2], "tile", scatter_dimension=1, tiled=True),
            lax.psum_scatter(back_out[3], "tile", scatter_dimension=1, tiled=True),
        )
        dq_low = from_heads(query_acc * score_scale).astype(jnp.bfloat16)
        dk_low = from_heads(key_grad).astype(jnp.bfloat16)
        dv_low = from_heads(value_grad).astype(jnp.bfloat16)
        grad_query = jnp.einsum("td,te->de", normed_low, dq_low, preferred_element_type=jnp.float32)
        grad_key = jnp.einsum("td,te->de", normed_low, dk_low, preferred_element_type=jnp.float32)
        grad_value = jnp.einsum("td,te->de", normed_low, dv_low, preferred_element_type=jnp.float32)
        d_normed = (
            jnp.einsum("te,de->td", dq_low, w_query, preferred_element_type=jnp.float32)
            + jnp.einsum("te,de->td", dk_low, w_key, preferred_element_type=jnp.float32)
            + jnp.einsum("te,de->td", dv_low, w_value, preferred_element_type=jnp.float32)
        )
        d_resid_norm, grad_gain_attn = jax.vjp(rms_scale, residual, gain_one)[1](d_normed)
        d_residual = d_mixed + d_resid_norm
        d_resid_low = d_residual.astype(jnp.bfloat16)
        grad_roi_proj = jnp.einsum(
            "tp,td->pd", pooled_low, d_resid_low, preferred_element_type=jnp.float32
        )
        d_pooled = jnp.einsum("td,pd->tp", d_resid_low, roi_proj, preferred_element_type=jnp.float32)
        d_pooled = d_pooled.astype(jnp.bfloat16)
        result_low = result_rows.astype(jnp.bfloat16)
        mixer_table = jnp.concatenate([grad_ffn_out, below(grad_ffn_in, 4), grad_output], axis=0)
        mixer_table = mixer_table.astype(jnp.bfloat16)
        chart = grad_bias_table.reshape(HEADS, 3, NB).transpose(2, 0, 1).reshape(NB, 3 * HEADS)
        embed_table = jnp.concatenate(
            [
                grad_query,
                grad_key,
                grad_value,
                grad_roi_proj,
                jnp.pad(jnp.stack([grad_gain_attn, grad_gain_ffn]), ((0, 14), (0, 0))),
                jnp.pad(chart, ((0, 80), (0, model_width - 3 * HEADS))),
            ],
            axis=0,
        ).astype(jnp.bfloat16)
    d_pooled_all = gathered(d_pooled).reshape(seq_all, -1)
    d_features, low_zero_up, low_end, low_start, box_token = run_unpool(
        ids, ordering, box_rows, d_pooled_all, pre_up_zero, 256
    )
    if heads_first:
        mixer_halves = halved(mixer_halves, 3, box_token)
        embed_halves = halved(embed_halves, 1, box_token)
        ordering = (embed_halves[2], mixer_halves[2])
    d_dec_one, d_dec_two, d_dec_three, low_one_up, low_two_up, up_token = run_up_back(
        ids,
        ordering,
        from_side(low_end, 1),
        low_zero_up,
        from_side(low_start, -1),
        pre_up_one,
        pre_up_two,
        lined_back(up_first),
        lined_back(up_second),
        up_third,
    )
    d_dec_three_all = windowed(d_dec_three)
    grad_up_first = run_grad_up_first(ids, (up_token,), dec_one, low_zero_up)
    light_early, early_token = run_grad_up(ids, (), grad_up_first, dec_two, low_one_up, u_three, low_two_up)
    if heads_first:
        mixer_share = halved(mixer_halves, 4, up_token)
        embed_halves = halved(embed_halves, 2, up_token)
        ordering = embed_halves[2:]
    low_three_up, low_four, low_three, d_pool_three, bottom_token = run_bottom_back(
        cut,
        ids,
        (*ordering, early_token),
        d_dec_three_all,
        pre_up_three,
        pre_four,
        pre_three,
        up_fourth,
        down_fifth,
        down_fourth,
    )
    dp_count = lax.axis_size(PAGES)
    if heads_first:
        embed_halves = halved(embed_halves, 3, bottom_token)
        early_parts = lax.all_to_all(
            light_early.reshape(32, -1, 256), (*PAGES, "tile"), 0, 0, tiled=True
        )
        early_share, early_done = run_total(ids, early_parts)
        ordering = (embed_halves[2], early_done)
    bottom_parts = (low_three_up, e_four, low_four, p_four, low_three, p_three_all)
    if cut:
        heavy = run_grad_bottom_all(ids, *bottom_parts)
        heavy_token = ()
    else:
        heavy, *heavy_token = run_grad_bottom(tile_count, dp_count, ids, ordering, *bottom_parts)
    low_two, low_one, low_zero = run_down_back(
        ids,
        heavy_token,
        d_pool_three,
        d_dec_two,
        pre_two,
        d_dec_one,
        pre_one,
        d_features,
        pre_zero,
        down_third,
        lined_back(down_second),
    )
    light_late = run_grad_down(ids, p_two, low_two, p_one, low_one, page_own, low_zero)
    both_axes = (*PAGES, "tile")
    device_total = dp_count * tile_count

    def summed_share(table):
        parts = table.reshape(device_total, -1, table.shape[1])
        parts = lax.all_to_all(parts, both_axes, 0, 0, tiled=True)
        return jnp.sum(parts.astype(jnp.float32), axis=0).astype(jnp.bfloat16)

    def spread_out(share):
        copies = jnp.broadcast_to(share[None], (device_total, *share.shape))
        return lax.all_to_all(copies, both_axes, 0, 0, tiled=True)

    late = spread_out(summed_share(light_late)).reshape(light_late.shape).astype(jnp.float32)
    wide = ffn_in.shape[1]
    if heads_first:
        embed_share = halved(embed_halves, 4)
        parts = lax.all_to_all(heavy, PAGES, 0, 0, tiled=True)
        share = run_gather(ids, parts, embed_share, early_share)
        mixer_all = lax.all_gather(mixer_share, both_axes, axis=0)
        whole = lax.all_gather(share, both_axes, axis=0)
        sum_ffn_out, sum_ffn_in, sum_output = run_unpack(
            mixer_all, False, [(2048, 512, 64), (512, 2048, 64), (512, 512, 16)]
        )
        *heavy_sums, sum_query, sum_key, sum_value, rest, early = run_unpack(
            whole, True, [(512, 512, 16)] * 4
        )
        rest = rest.reshape(NB, 16, model_width)
        sum_roi = rest[:, :4].reshape(-1, model_width)
        sum_bias = rest[:, 4, : 3 * HEADS].reshape(NB, HEADS, 3)
        sum_gain_attn, sum_gain_ffn = rest[0, 5], rest[0, 6]
    else:
        early = spread_out(summed_share(light_early)).reshape(light_early.shape)
        early = early.astype(jnp.float32)
        heavy_sums = [lax.psum(member, both_axes).astype(jnp.float32) for member in heavy]
        mixer_all = lax.psum(mixer_table, both_axes).astype(jnp.float32)
        embed_all = lax.psum(embed_table, both_axes).astype(jnp.float32)
        sum_ffn_out = mixer_all[:wide]
        sum_ffn_in = beside(mixer_all[wide : 2 * wide], wide // model_width)
        sum_output = mixer_all[2 * wide :]
        sum_query, sum_key, sum_value = (
            embed_all[n * model_width : (n + 1) * model_width] for n in range(3)
        )
        last = 3 * model_width + roi_proj.shape[0]
        sum_roi = embed_all[3 * model_width : last]
        sum_bias = embed_all[last + 16 : last + 16 + NB, : 3 * HEADS].reshape(NB, HEADS, 3)
        sum_gain_attn, sum_gain_ffn = embed_all[last], embed_all[last + 1]
    sum_bias = sum_bias.transpose(1, 2, 0).reshape(bias_table.shape)

    def unlined(table, kind):
        return table.reshape(3, kind.shape[2], 3, kind.shape[3]).transpose(0, 2, 1, 3)

    second_rest = below(early[1344:1440], 2)
    sum_up_second = jnp.concatenate([early[1152:1344], second_rest], axis=1)
    sum_down_second = jnp.concatenate([late[384:480, :96], late[384:480, 128:224]], axis=0)
    sum_first = late[480:512, :72].reshape(32, 3, 3, 8)[..., :3].transpose(1, 2, 0, 3)
    summed = [
        sum_first,
        unlined(sum_down_second, down_second),
        unlined(late[:384, :192], down_third),
        heavy_sums[2].reshape(down_fourth.shape),
        heavy_sums[1].reshape(down_fifth.shape),
        heavy_sums[0].reshape(up_fourth.shape),
        early[:1152].reshape(up_third.shape),
        unlined(sum_up_second, up_second),
        unlined(early[1440:1536, :192], up_first),
        sum_roi,
        sum_gain_attn,
        sum_query,
        sum_key,
        sum_value,
        sum_output,
        sum_bias,
        sum_gain_ffn,
        sum_ffn_in,
        sum_ffn_out,
    ]
    return (
        result_low[None],
        d_residual[None],
        summed[0],
        summed[1],
        summed[2],
        summed[3],
        summed[4],
        summed[5],
        summed[6],
        summed[7],
        summed[8],
        summed[9],
        summed[10],
        summed[11],
        summed[12],
        summed[13],
        summed[14],
        summed[15],
        summed[16],
        summed[17],
        summed[18],
    )


def solution(mesh):
    tiles = mesh.shape["tile"]
    split = Mesh(mesh.devices.reshape(mesh.shape["dp"] // 2, 2, tiles), (*PAGES, "tile"))
    return jax.shard_map(
        on_device,
        mesh=split,
        in_specs=(
            P(PAGES, "tile", None),
            P(PAGES, None, "tile", None),
            P(None, PAGES, "tile"),
            P(PAGES, "tile"),
            P(),
            P(),
            P(),
            P(),
            P(),
            P(),
            P(),
            P(),
            P(),
            P(),
            P(),
            P(),
            P(),
            P(),
            P(),
            P(),
            P(),
            P(),
            P(),
            P(PAGES, "tile", None),
        ),
        out_specs=(
            P(PAGES, "tile", None),
            P(PAGES, "tile", None),
            P(),
            P(),
            P(),
            P(),
            P(),
            P(),
            P(),
            P(),
            P(),
            P(),
            P(),
            P(),
            P(),
            P(),
            P(),
            P(),
            P(),
            P(),
            P(),
        ),
        check_vma=False,
    )
```

```python
import functools
import math

import jax
import jax.numpy as jnp
from jax import lax
from jax.experimental import pallas as pl
from jax.experimental.pallas import tpu as pltpu
from jax.sharding import Mesh
from jax.sharding import PartitionSpec as P

HEADS = 8
HD = 64
NB = 32

eps = 1e-06
bounds = (12, 16, 23, 32, 46, 64, 91)
neg_large = -1000000000.0
HOPS = (("core", 1), ("x", 1), ("tile", 1), ("tile", 4), ("tile", 2))
PAGES = ("x", "core")
f32 = jnp.float32
bf16 = jnp.bfloat16
gelu_scale = math.sqrt(2.0 / math.pi)
VMEM_CAP = 28 * 1024 * 1024


def gelu_of(x):
    x = x.astype(f32)
    half = 0.5 * x
    inner = x * (gelu_scale + (gelu_scale * 0.044715) * (x * x))
    return half + half * jnp.tanh(inner)


def gelu_slope(x):
    x = x.astype(f32)
    sq = x * x
    bent = jnp.tanh(x * (gelu_scale + (gelu_scale * 0.044715) * sq))
    rise = gelu_scale + (3.0 * gelu_scale * 0.044715) * sq
    return 0.5 + 0.5 * bent + (0.5 * x) * (1.0 - bent * bent) * rise


def mm(a, b):
    return jnp.dot(a, b, preferred_element_type=f32)


def mm_tn(a, b):
    return lax.dot_general(a, b, (((0,), (0,)), ((), ())), preferred_element_type=f32)


def mm_nt(a, b):
    return lax.dot_general(a, b, (((1,), (1,)), ((), ())), preferred_element_type=f32)


def mm_fine(a, b):
    high = a.astype(bf16)
    low = (a - high.astype(f32)).astype(bf16)
    return mm(high, b) + mm(low, b)


def lane_ids(shape):
    return lax.broadcasted_iota(jnp.int32, shape, len(shape) - 1)


def row_ids_of(shape):
    return lax.broadcasted_iota(jnp.int32, shape, len(shape) - 2)


def halving(wide, value):
    hit = row_ids_of((wide, wide // 2)) >> 1 == lane_ids((wide, wide // 2))
    return jnp.where(hit, value, 0.0).astype(bf16)


def doubling(narrow):
    hit = row_ids_of((narrow, 2 * narrow)) == lane_ids((narrow, 2 * narrow)) >> 1
    return jnp.where(hit, 1.0, 0.0).astype(bf16)


def pair_halving(value):
    shape = (256, 128)
    source = row_ids_of(shape)
    target = lane_ids(shape)
    hit = source >> 1 == target
    return jnp.where(hit, value, 0.0).astype(bf16)


def side_doubling(side):
    shape = (128, 128)
    hit = row_ids_of(shape) == (lane_ids(shape) >> 1) + 64 * side
    return jnp.where(hit, 1.0, 0.0).astype(bf16)


def quad_map(coarse_lanes, coarse_width):
    shape = (coarse_lanes, 4 * coarse_lanes)
    fine = lane_ids((1, shape[1]))
    shift = coarse_width.bit_length() - 1
    home = (fine >> (shift + 2) << shift) + ((fine & (2 * coarse_width - 1)) >> 1)
    return jnp.where(row_ids_of(shape) == home, 1.0, 0.0).astype(bf16)


def masked(x, keep):
    return x * jnp.where(keep, 1.0, 0.0).astype(x.dtype)


def col_shift(x, step, width):
    if step == 0:
        return x
    lanes = x.shape[1]
    col = lane_ids((1, lanes)) & (width - 1)
    keep = col < width - 1 if step > 0 else col > 0
    return masked(pltpu.roll(x, -step % lanes, 1), keep)


def row_shift(x, step, width):
    if step == 0:
        return x
    lanes = x.shape[1]
    lane = lane_ids((1, lanes))
    keep = lane < lanes - width if step > 0 else lane >= width
    return masked(pltpu.roll(x, (-step * width) % lanes, 1), keep)


def stack_cols(x, width):
    return jnp.concatenate([col_shift(x, step, width) for step in (-1, 0, 1)], axis=0)


def row_ok(first_row, rows, width, low, high):
    row = (lane_ids((1, rows * width)) >> (width.bit_length() - 1)) + first_row
    return (row >= low) & (row < high)


def keep_rows(x, first_row, width, high):
    ok = row_ok(first_row, x.shape[1] // width, width, 0, high)
    return jnp.where(ok, x, 0.0)


def price(micros):
    return pl.CostEstimate(
        flops=int(micros * 5e8), transcendentals=0, bytes_accessed=int(micros * 2e6)
    )


class Fetched:
    def __init__(self, ref, copy):
        self.ref, self.copy, self.waited = ref, copy, False
        self.shape = ref.shape
        copy.start()

    def ready(self):
        if not self.waited:
            self.copy.wait()
            self.waited = True
        return self.ref

    def __getitem__(self, spot):
        return self.ready()[spot]


class Sent:
    def __init__(self, ref, copy):
        self.ref, self.copy, self.started = ref, copy, False
        self.shape = ref.shape

    def send(self):
        if not self.started:
            self.copy.start()
            self.started = True

    def __getitem__(self, spot):
        return self.ref[spot]

    def __setitem__(self, spot, value):
        self.ref[spot] = value


def in_hbm(array):
    return pltpu.with_memory_space_constraint(array, pltpu.HBM)


TOKEN = ((8, 128), f32)


def call(micros, body, outs, scratch, ids, arrays, after=(), late=(), sent=(), table=None):
    count = len(arrays)
    moved = [(arrays[n].shape, arrays[n].dtype) for n in late] + [outs[n] for n in sent]
    arrays = [in_hbm(array) if n in late else array for n, array in enumerate(arrays)]
    after = [in_hbm(token) for token in after]

    scalars = (ids,) if table is None else (ids, table)

    def ordered(*refs):
        refs, heads = refs[len(scalars) :], refs[: len(scalars)]
        ins = list(refs[:count])
        refs = refs[count + len(after) :]
        results = list(refs[: len(outs)])
        own = refs[len(outs) : len(outs) + len(scratch)]
        if moved:
            *stages, marks = refs[len(outs) + len(scratch) :]
        for k, n in enumerate(late):
            ins[n] = Fetched(stages[k], pltpu.make_async_copy(ins[n], stages[k], marks.at[k]))
        for k, n in enumerate(sent, len(late)):
            copy = pltpu.make_async_copy(stages[k], results[n], marks.at[k])
            results[n] = Sent(stages[k], copy)
        body(*heads, *ins, *results, *own)
        for n in late:
            ins[n].ready()
        for n in sent:
            results[n].send()
        for n in sent:
            results[n].copy.wait()

    def place(chosen, total):
        return [
            pl.BlockSpec(memory_space=pltpu.HBM if n in chosen else pltpu.VMEM) for n in range(total)
        ]

    return pl.pallas_call(
        ordered,
        cost_estimate=price(micros),
        out_shape=[
            pltpu.HBM(*out) if n in sent or out == TOKEN else jax.ShapeDtypeStruct(*out)
            for n, out in enumerate(outs)
        ],
        in_specs=[pl.BlockSpec(memory_space=pltpu.SMEM)] * len(scalars)
        + place(late, count)
        + [pl.BlockSpec(memory_space=pltpu.HBM) for _ in after],
        out_specs=place([n for n, out in enumerate(outs) if n in sent or out == TOKEN], len(outs)),
        scratch_shapes=[pltpu.VMEM(shape, kind) for shape, kind in scratch]
        + [pltpu.VMEM(shape, kind) for shape, kind in moved]
        + ([pltpu.SemaphoreType.DMA((len(moved),))] if moved else []),
        compiler_params=pltpu.CompilerParams(vmem_limit_bytes=VMEM_CAP),
    )(*scalars, *arrays, *after)


def lanes_at(start, size):
    return pl.ds(pl.multiple_of(start, 128), size)


def down_body(ids, pages, w_zero, w_one, w_two, pre_zero, pre_one, p_one, pre_two, p_two, p_three, page_own, page, cols, pool_one, stack_one, pool_two):
    tile, high, at = ids[0], ids[1], ids[4]
    page[...] = jnp.zeros_like(page)
    for side in range(-2, 3):
        block = at + side

        @pl.when((block >= 0) & (block < pages.shape[0]))
        def _(block=block, side=side):
            lines = pages[block, :, 0:1024].astype(f32)
            for g in range(8):
                first = (2 + side) * 8192 + 1024 * g
                for c in range(3):
                    page[c : c + 1, first : first + 1024] = lines[8 * c + g : 8 * c + g + 1, :]

    page_full = page[:, 11 * 512 : 69 * 512]
    page_own[...] = page_full[:, 20 * 512 : 38 * 512].astype(bf16)
    for j in range(3):
        cols[j] = col_shift(page_full, j - 1, 512)
    halve = halving(512, 0.25)

    def top(k, keep_pre):
        pieces = [
            cols[j, :, lanes_at((4 * k + i) * 512, 2048)] for i in range(3) for j in range(3)
        ]
        pre = mm(w_zero[...], jnp.concatenate(pieces, axis=0).astype(bf16))
        if keep_pre:
            pre_zero[:, lanes_at((k - 5) * 2048, 2048)] = pre.astype(bf16)
        enc = gelu_of(pre)
        pairs = jnp.concatenate(
            [enc[:, :512] + enc[:, 512:1024], enc[:, 1024:1536] + enc[:, 1536:]], axis=0
        )
        pooled = mm_fine(pairs, halve)
        first = tile * 8 - 10 + 2 * k
        for n in range(2):
            ok = (first + n >= 0) & (first + n < high // 2)
            part = jnp.where(ok, pooled[32 * n : 32 * n + 32], 0.0)
            pool_one[:, lanes_at((2 * k + n) * 256, 256)] = part.astype(bf16)

    for low, end, keep_pre in ((0, 5, False), (5, 9, True), (9, 14, False)):

        @pl.loop(low, end)
        def _(k, keep_pre=keep_pre):
            top(k, keep_pre)

    pre_zero.send()
    page_own.send()
    p_one[...] = pool_one[:, 9 * 256 : 19 * 256]
    p_one.send()
    stack_one[...] = stack_cols(pool_one[...], 256)
    halve_one = halving(256, 0.25)

    @pl.loop(0, 6)
    def _(k):
        pre = sum(
            mm(w_one[i], stack_one[:, lanes_at((4 * k + 1 + i) * 256, 1024)]) for i in range(3)
        )

        @pl.when((k >= 1) & (k < 5))
        def _():
            pre_one[:, lanes_at((k - 1) * 1024, 1024)] = pre.astype(bf16)

        enc = gelu_of(pre)
        pairs = jnp.concatenate(
            [enc[:, :256] + enc[:, 256:512], enc[:, 512:768] + enc[:, 768:]], axis=0
        )
        pooled = mm_fine(pairs, halve_one)
        first = tile * 4 - 4 + 2 * k
        for n in range(2):
            ok = (first + n >= 0) & (first + n < high // 4)
            part = jnp.where(ok, pooled[64 * n : 64 * n + 64], 0.0)
            pool_two[:, lanes_at((2 * k + n) * 128, 128)] = part.astype(bf16)

    pre_one.send()
    p_two[...] = pool_two[:, 3 * 128 : 9 * 128]
    p_two.send()
    stacked = stack_cols(pool_two[...], 128)
    pre = sum(mm(w_two[i], stacked[:, i * 128 : i * 128 + 1280]) for i in range(3))
    pre_two[...] = pre.astype(bf16)
    pre_two.send()
    enc = gelu_of(pre[:, 384:896])
    pairs = jnp.concatenate([enc[:, :128] + enc[:, 128:256], enc[:, 256:384] + enc[:, 384:]], axis=1)
    p_three[...] = mm_fine(pairs, pair_halving(0.25)).astype(bf16)


def run_down(ids, pages, w_zero, w_one, w_two):
    return call(
        10,
        down_body,
        [
            ((32, 16 * 512), bf16),
            ((64, 16 * 256), bf16),
            ((32, 10 * 256), bf16),
            ((128, 10 * 128), bf16),
            ((64, 6 * 128), bf16),
            ((128, 128), bf16),
            ((8, 18 * 512), bf16),
        ],
        [
            ((8, 80 * 512), f32),
            ((3, 8, 58 * 512), f32),
            ((32, 28 * 256), bf16),
            ((96, 28 * 256), bf16),
            ((64, 12 * 128), bf16),
        ],
        ids,
        (pages, w_zero, w_one, w_two),
        sent=(0, 1, 2, 3, 4, 6),
    )


def conv_taps(x, weight, width):
    total = None
    for i in range(3):
        lined = row_shift(x, i - 1, width)
        for j in range(3):
            term = mm(weight[i, j], col_shift(lined, j - 1, width))
            total = term if total is None else total + term
    return total


def conv_taps_back(x, weight, width):
    total = None
    for i in range(3):
        lined = row_shift(x, i - 1, width)
        for j in range(3):
            term = mm_tn(weight[2 - i, 2 - j], col_shift(lined, j - 1, width))
            total = term if total is None else total + term
    return total


def laid_out(blocks):
    return jnp.concatenate([blocks[n] for n in range(blocks.shape[0])], axis=1)


def bottom_body(cut, ids, p_three, w_three, w_four, w_up, pre_three, pre_four, p_four, e_four, pre_up, dec_three):
    lanes = 128 * p_three.shape[0]
    first, high = ids[3], ids[1]

    def kept(x, width, shrink):
        return keep_rows(x, first * (16 // shrink), width, high // shrink) if cut else x

    pre = conv_taps(laid_out(p_three), w_three, 64)
    pre_three[...] = pre.astype(bf16)
    pre_three.send()
    enc_three = kept(gelu_of(pre), 64, 8)
    spread = quad_map(lanes // 4, 32)
    high_part = enc_three.astype(bf16)
    low_part = (enc_three - high_part.astype(f32)).astype(bf16)
    pooled = ((mm_nt(high_part, spread) + mm_nt(low_part, spread)) * 0.25).astype(bf16)
    p_four[...] = pooled
    p_four.send()
    pre = conv_taps(pooled, w_four, 32)
    pre_four[...] = pre.astype(bf16)
    pre_four.send()
    low = kept(gelu_of(pre), 32, 16).astype(bf16)
    e_four[...] = low
    e_four.send()
    pre = conv_taps(mm(low, spread).astype(bf16), w_up, 64)
    pre_up[...] = pre.astype(bf16)
    pre_up.send()
    dec = kept(gelu_of(pre) + enc_three, 64, 8).astype(bf16)
    zero = jnp.zeros((256, 128), bf16)
    dec_three[:, 0:128] = zero
    dec_three[:, 128 : 128 + lanes] = dec
    dec_three[:, 128 + lanes :] = zero


def run_bottom(cut, ids, p_three, w_three, w_four, w_up):
    lanes = 128 * p_three.shape[0]
    return call(
        11,
        functools.partial(bottom_body, cut),
        [
            ((256, lanes), bf16),
            ((512, lanes // 4), bf16),
            ((256, lanes // 4), bf16),
            ((512, lanes // 4), bf16),
            ((256, lanes), bf16),
            ((256, lanes + 256), bf16),
        ],
        [],
        ids,
        (p_three, w_three, w_four, w_up),
        late=(2, 3),
        sent=(0, 1, 2, 3, 4),
    )


def widened(block):
    parts = []
    for n in range(block.shape[1] // 128):
        piece = block[:, 128 * n : 128 * n + 128]
        for side in range(2):
            line = mm(piece, side_doubling(side)).astype(bf16)
            parts += [line, line]
    return jnp.concatenate(parts, axis=1)


def spread_rows(source, target, width):
    spread = doubling(width)
    for n in range(source.shape[1] // width):
        line = mm(source[:, n * width : n * width + width], spread).astype(bf16)
        for m in range(2):
            target[:, (2 * n + m) * 2 * width : (2 * n + m + 1) * 2 * width] = line


def up_body(ids, dec_three, pre_two, pre_one, pre_zero, w_third, w_second, w_first, pre_up_two, pre_up_one, pre_up_zero, u_three, dec_two, dec_one, features, wide_two, stack_two, wide_one, stack_one):
    tile, high, place = ids[0], ids[1], ids[2]
    block = dec_three[:, lanes_at(place * 128, 384)]
    wide = widened(block)
    u_three[...] = wide[:, 384 : 384 + 768]
    u_three.send()
    total = None
    for j in range(3):
        moved = col_shift(wide, j - 1, 128)
        for i in range(3):
            term = mm(w_third[i, j], moved[:, i * 128 : i * 128 + 1280])
            total = term if total is None else total + term
    pre_up_two[...] = total.astype(bf16)
    pre_up_two.send()
    dec = gelu_of(total) + gelu_of(pre_two[...])
    dec = keep_rows(dec, tile * 4 - 3, 128, high // 4).astype(bf16)
    dec_two[...] = dec[:, 128 : 128 + 1024]
    dec_two.send()
    spread_rows(dec, wide_two, 128)
    stack_two[...] = stack_cols(wide_two[...], 256)
    for k in range(3):
        pre = sum(
            mm(w_second[i], stack_two[:, (6 * k + i) * 256 : (6 * k + i) * 256 + 1536])
            for i in range(3)
        )
        pre_up_one[:, 1536 * k : 1536 * k + 1536] = pre.astype(bf16)
    pre_up_one.send()
    dec = gelu_of(pre_up_one[:, 4 * 256 : 14 * 256]) + gelu_of(pre_one[:, 3 * 256 : 13 * 256])
    dec = keep_rows(dec, tile * 8 - 1, 256, high // 2).astype(bf16)
    dec_one[...] = dec
    dec_one.send()
    spread_rows(dec, wide_one, 256)
    stack_one[...] = stack_cols(wide_one[...], 512)
    pre_zero.ready()

    @pl.loop(0, 4)
    def _(k):
        pre = sum(
            mm(w_first[i], stack_one[:, lanes_at((4 * k + 1 + i) * 512, 2048)]) for i in range(3)
        )
        own = lanes_at(k * 2048, 2048)
        pre_up_zero[:, own] = pre.astype(bf16)
        found = (gelu_of(pre) + gelu_of(pre_zero[:, own])).astype(bf16)
        for n in range(4):
            features[pl.ds(pl.multiple_of((4 * k + n) * 32, 32), 32), :] = found[
                :, 512 * n : 512 * n + 512
            ]


def run_up(ids, dec_three, pre_two, pre_one, pre_zero, w_third, w_second, w_first):
    return call(
        9,
        up_body,
        [
            ((128, 10 * 128), bf16),
            ((64, 18 * 256), bf16),
            ((32, 16 * 512), bf16),
            ((256, 6 * 128), bf16),
            ((128, 8 * 128), bf16),
            ((64, 10 * 256), bf16),
            ((16 * 32, 512), bf16),
        ],
        [
            ((128, 20 * 256), bf16),
            ((384, 20 * 256), bf16),
            ((64, 20 * 512), bf16),
            ((192, 20 * 512), bf16),
        ],
        ids,
        (dec_three, pre_two, pre_one, pre_zero, w_third, w_second, w_first),
        late=(1, 2, 3),
        sent=(0, 1, 2, 3, 4, 5),
    )


def band_edges(boxes):
    left, top, right, bottom = (boxes[:, n : n + 1] for n in range(4))
    mid_col = (left + right) >> 1
    mid_row = (top + bottom) >> 1
    return ((left, mid_col, right), (top, mid_row, bottom))


def band_hits(edges, ids_wide, band):
    return (ids_wide >= edges[band]) & (ids_wide < edges[band + 1])


def area_inverse(cols, rows, a, b):
    return 1.0 / ((rows[a + 1] - rows[a]) * (cols[b + 1] - cols[b])).astype(f32)


def pool_body(step, ids, boxes, features, pooled):
    tile = ids[0]
    x_ids = lane_ids((1, 512))
    y_ids = (x_ids >> 5) + tile * 16
    group = lane_ids((1, 128)) >> 5

    @pl.loop(0, boxes.shape[0] // step)
    def _(k):
        own = pl.ds(pl.multiple_of(k * step, step), step)
        cols, rows = band_edges(boxes[own, :])
        result = jnp.zeros((step, 128), f32)
        inside = [jnp.where(band_hits(rows, y_ids, a), 1.0, 0.0) for a in range(2)]
        for b in range(2):
            hits = jnp.where(band_hits(cols, x_ids, b), 1.0, 0.0).astype(bf16)
            lines = mm_nt(hits, features[...])
            for a in range(2):
                part = lines * inside[a]
                part = part[:, :128] + part[:, 128:256] + (part[:, 256:384] + part[:, 384:])
                part = part + pltpu.roll(part, 64, 1)
                part = part + pltpu.roll(part, 32, 1)
                scaled = part * area_inverse(cols, rows, a, b)
                result = jnp.where(group == 2 * a + b, scaled, result)
        pooled[own, :] = result.astype(bf16)


def run_pool(ids, boxes, features, step):
    count = boxes.shape[0]
    return call(
        8, functools.partial(pool_body, step), [((count, 128), bf16)], [], ids, (boxes, features)
    )[0]


def unpool_body(step, ids, boxes, d_pooled, pre_up, d_features, d_low, low_end, low_start, token, total):
    tile = ids[0]
    x_ids = lane_ids((1, 512))
    y_ids = (x_ids >> 5) + tile * 16
    group = lane_ids((1, 128)) >> 5
    source = row_ids_of((128, 512))
    target = lane_ids((1, 512)) & 31
    copies = [
        jnp.where(source == target + 32 * n, 1.0, 0.0).astype(bf16) for n in range(4)
    ]
    total[...] = jnp.zeros_like(total)

    @pl.loop(0, boxes.shape[0] // step)
    def _(k):
        own = pl.ds(pl.multiple_of(k * step, step), step)
        cols, rows = band_edges(boxes[own, :])
        scale = jnp.zeros((step, 128), f32)
        for a in range(2):
            for b in range(2):
                scale = jnp.where(group == 2 * a + b, area_inverse(cols, rows, a, b), scale)
        share = (d_pooled[own, :].astype(f32) * scale).astype(bf16)
        found = None
        inside = [jnp.where(band_hits(rows, y_ids, a), 1.0, 0.0) for a in range(2)]
        for b in range(2):
            placed = mm(share, copies[b]) * inside[0] + mm(share, copies[2 + b]) * inside[1]
            hits = jnp.where(band_hits(cols, x_ids, b), 1.0, 0.0).astype(bf16)
            term = mm_tn(placed.astype(bf16), hits)
            found = term if found is None else found + term
        total[...] += found

    for y in range(16):
        own = slice(512 * y, 512 * y + 512)
        line = total[32 * y : 32 * y + 32, :]
        d_features[:, own] = line
        low = (line * gelu_slope(pre_up[:, own])).astype(bf16)
        d_low[:, own] = low
        if y >= 5:
            low_end[:, 512 * (y - 5) : 512 * (y - 4)] = low
        if y < 11:
            low_start[:, own] = low


def run_unpool(ids, after, boxes, d_pooled, pre_up, step):
    return call(
        8,
        functools.partial(unpool_body, step),
        [
            ((32, 8192), f32),
            ((32, 8192), bf16),
            ((32, 11 * 512), bf16),
            ((32, 11 * 512), bf16),
            TOKEN,
        ],
        [((512, 512), f32)],
        ids,
        (boxes, d_pooled, pre_up),
        after,
        late=(2,),
        sent=(0,),
    )


def up_back_body(ids, before, d_low, behind, pre_up_one, pre_up_two, wd_first, wd_second, w_third, d_dec_one, d_dec_two, d_dec_three, low_one, low_two, token, stack_zero, wide_low):
    tile, high = ids[0], ids[1]
    reach = 11 * 512
    for first, piece in ((0, before), (reach, d_low), (reach + 8192, behind)):
        stack_zero[:, first : first + piece.shape[1]] = stack_cols(piece[...], 512)
    halve = halving(512, 1.0)
    pre_up_one.ready()

    @pl.loop(0, 9)
    def _(k):
        back = sum(
            mm(wd_first[i], stack_zero[:, lanes_at((4 * k + i) * 512, 2048)]) for i in range(3)
        )
        pairs = jnp.concatenate(
            [back[:, :512] + back[:, 512:1024], back[:, 1024:1536] + back[:, 1536:]], axis=0
        )
        summed = mm_fine(pairs, halve)
        first = tile * 8 - 5 + 2 * k
        for n in range(2):
            ok = (first + n >= 0) & (first + n < high // 2)
            own = lanes_at((2 * k + n) * 256, 256)
            part = jnp.where(ok, summed[64 * n : 64 * n + 64], 0.0)
            d_dec_one[:, own] = part
            wide_low[:, own] = (part * gelu_slope(pre_up_one[:, own])).astype(bf16)

    d_dec_one.send()
    low_one[...] = wide_low[:, 5 * 256 : 13 * 256]
    low_one.send()
    stacked = stack_cols(wide_low[...], 256)
    halve_one = halving(256, 1.0)
    for k in range(4):
        back = sum(
            mm(wd_second[i], stacked[:, (4 * k + i) * 256 : (4 * k + i) * 256 + 1024])
            for i in range(3)
        )
        pairs = jnp.concatenate(
            [back[:, :256] + back[:, 256:512], back[:, 512:768] + back[:, 768:]], axis=0
        )
        summed = mm_fine(pairs, halve_one)
        for n in range(2):
            line = 2 * k + n
            row = tile * 4 - 2 + line
            ok = (row >= 0) & (row < high // 4)
            part = jnp.where(ok, summed[128 * n : 128 * n + 128], 0.0)
            d_dec_two[:, 128 * line : 128 * line + 128] = part
    low = d_dec_two[:, 128 : 7 * 128] * gelu_slope(pre_up_two[:, 2 * 128 : 8 * 128])
    low = low.astype(bf16)
    d_dec_two.send()
    low_two[...] = low[:, 128 : 5 * 128]
    low_two.send()
    total = None
    for j in range(3):
        moved = col_shift(low, j - 1, 128)
        for i in range(3):
            term = mm_tn(w_third[2 - i, 2 - j], moved[:, i * 128 : i * 128 + 512])
            total = term if total is None else total + term
    pairs = jnp.concatenate(
        [total[:, :128] + total[:, 128:256], total[:, 256:384] + total[:, 384:]], axis=1
    )
    d_dec_three[...] = mm_fine(pairs, pair_halving(1.0)).astype(bf16)


def run_up_back(ids, after, before, d_low, behind, pre_up_one, pre_up_two, wd_first, wd_second, w_third):
    return call(
        9,
        up_back_body,
        [
            ((64, 18 * 256), f32),
            ((128, 8 * 128), f32),
            ((256, 128), bf16),
            ((64, 8 * 256), bf16),
            ((128, 4 * 128), bf16),
            TOKEN,
        ],
        [((96, 38 * 512), bf16), ((64, 18 * 256), bf16)],
        ids,
        (before, d_low, behind, pre_up_one, pre_up_two, wd_first, wd_second, w_third),
        after,
        late=(3, 4),
        sent=(0, 1, 3, 4),
    )


def bottom_back_body(cut, ids, d_dec_three, pre_up, pre_four, pre_three, w_up, w_four, w_three, low_up, low_four, low_three, d_pool, token, padded):
    lanes = 128 * d_dec_three.shape[0]
    first, high, place = ids[3], ids[1], ids[2]

    def kept(x, width, shrink):
        return keep_rows(x, first * (16 // shrink), width, high // shrink) if cut else x

    d_dec = laid_out(d_dec_three).astype(f32)
    low = (d_dec * gelu_slope(pre_up[...])).astype(bf16)
    low_up[...] = low
    spread = quad_map(lanes // 4, 32)
    back = conv_taps_back(low, w_up, 64)
    high_part = back.astype(bf16)
    low_part = (back - high_part.astype(f32)).astype(bf16)
    d_enc = kept(mm_nt(high_part, spread) + mm_nt(low_part, spread), 32, 16)
    low = (d_enc * gelu_slope(pre_four[...])).astype(bf16)
    low_four[...] = low
    back = conv_taps_back(low, w_four, 32) * 0.25
    d_enc = kept(d_dec + mm_fine(back, spread), 64, 8)
    low = (d_enc * gelu_slope(pre_three[...])).astype(bf16)
    low_three[...] = low
    zero = jnp.zeros((256, 128), bf16)
    padded[:, 0:128] = zero
    padded[:, 128 : 128 + lanes] = low
    padded[:, 128 + lanes :] = zero
    window = padded[:, lanes_at(place * 128, 384)]
    d_pool[...] = conv_taps_back(window, w_three, 64)[:, 0:384]


def run_bottom_back(cut, ids, after, d_dec_three, pre_up, pre_four, pre_three, w_up, w_four, w_three):
    lanes = 128 * d_dec_three.shape[0]
    return call(
        10,
        functools.partial(bottom_back_body, cut),
        [
            ((256, lanes), bf16),
            ((512, lanes // 4), bf16),
            ((256, lanes), bf16),
            ((128, 384), f32),
            TOKEN,
        ],
        [((256, lanes + 256), bf16)],
        ids,
        (d_dec_three, pre_up, pre_four, pre_three, w_up, w_four, w_three),
        after,
        late=(1, 4, 2, 5, 3, 6),
        sent=(3,),
    )


def down_back_body(ids, d_pool_three, d_dec_two, pre_two, d_dec_one, pre_one, d_features, pre_zero, w_two, wd_one, low_two, low_one, low_zero, wide_one):
    tile, high = ids[0], ids[1]
    d_dec_one.ready()
    pre_one.ready()
    d_features.ready()
    pre_zero.ready()
    quarter = d_pool_three[...] * 0.25
    parts = []
    for n in range(3):
        piece = quarter[:, 128 * n : 128 * n + 128]
        for side in range(2):
            line = mm_fine(piece, side_doubling(side))
            parts += [line, line]
    spread = jnp.concatenate(parts[2:10], axis=1)
    d_enc = keep_rows(d_dec_two[...] + spread, tile * 4 - 2, 128, high // 4)
    low = (d_enc * gelu_slope(pre_two[:, 128 : 9 * 128])).astype(bf16)
    low_two[...] = low[:, 2 * 128 : 6 * 128]
    total = None
    for j in range(3):
        moved = col_shift(low, j - 1, 128)
        for i in range(3):
            term = mm_tn(w_two[2 - i, 2 - j], moved[:, i * 128 : i * 128 + 768])
            total = term if total is None else total + term
    total = total * 0.25
    wide = doubling(128)
    for n in range(6):
        line = mm_fine(total[:, 128 * n : 128 * n + 128], wide)
        for m in range(2):
            row = 2 * n + m
            value = d_dec_one[:, (3 + row) * 256 : (4 + row) * 256] + line
            ok = (tile * 8 - 2 + row >= 0) & (tile * 8 - 2 + row < high // 2)
            value = jnp.where(ok, value, 0.0)
            slope = gelu_slope(pre_one[:, (2 + row) * 256 : (3 + row) * 256])
            wide_one[:, row * 256 : row * 256 + 256] = (value * slope).astype(bf16)
    low_one[...] = wide_one[:, 2 * 256 : 10 * 256]
    stacked = stack_cols(wide_one[...], 256)
    back = sum(mm(wd_one[i], stacked[:, (1 + i) * 256 : (9 + i) * 256]) for i in range(3)) * 0.25
    wider = doubling(256)
    for n in range(8):
        line = mm_fine(back[:, 256 * n : 256 * n + 256], wider)
        for m in range(2):
            own = slice((2 * n + m) * 512, (2 * n + m + 1) * 512)
            value = (d_features[:, own] + line) * gelu_slope(pre_zero[:, own])
            low_zero[:, own] = value.astype(bf16)


def run_down_back(ids, after, *arrays):
    return call(
        4,
        down_back_body,
        [
            ((128, 4 * 128), bf16),
            ((64, 8 * 256), bf16),
            ((32, 16 * 512), bf16),
        ],
        [((64, 12 * 256), bf16)],
        ids,
        arrays,
        after,
        late=(0, 1, 2, 3, 4, 5, 6),
    )


def grad_up_first_body(ids, dec_one, d_low, grad, wide_one, stack_one):
    spread_rows(dec_one[...], wide_one, 256)
    stack_one[...] = stack_cols(wide_one[...], 512)
    for i in range(3):
        grad[i] = mm_nt(d_low[...], stack_one[:, (1 + i) * 512 : (17 + i) * 512])


def run_grad_up_first(ids, after, dec_one, d_low):
    return call(
        4,
        grad_up_first_body,
        [((3, 32, 192), f32)],
        [((64, 20 * 512), bf16), ((192, 20 * 512), bf16)],
        ids,
        (dec_one, d_low),
        after,
        late=(0,),
    )[0]


def grad_up_body(ids, grad_first, dec_two, low_one, u_three, low_two, table, token, wide_two, stack_two):
    spread_rows(dec_two[...], wide_two, 128)
    stack_two[...] = stack_cols(wide_two[...], 256)
    for j in range(3):
        moved = col_shift(u_three[...], j - 1, 128)
        for i in range(3):
            first = (3 * i + j) * 128
            grad = mm_nt(low_two[...], moved[:, i * 128 : i * 128 + 512])
            table[first : first + 128, :] = grad.astype(bf16)
    rest = []
    for i in range(3):
        grad = mm_nt(low_one[...], stack_two[:, (3 + i) * 256 : (11 + i) * 256]).astype(bf16)
        table[1152 + 64 * i : 1216 + 64 * i, :] = grad[:, :256]
        rest.append(grad[:, 256:])
    rest = jnp.concatenate(rest, axis=0)
    table[1344:1440, :] = jnp.concatenate([rest[:96], rest[96:]], axis=1)
    table[1440:1536, :] = jnp.zeros((96, 256), bf16)
    for i in range(3):
        table[1440 + 32 * i : 1472 + 32 * i, 0:192] = grad_first[i].astype(bf16)


def run_grad_up(ids, after, *arrays):
    return call(
        4,
        grad_up_body,
        [((1536, 256), bf16), TOKEN],
        [((128, 16 * 256), bf16), ((384, 16 * 256), bf16)],
        ids,
        arrays,
        after,
        late=(1, 2, 3, 4),
    )


def halve_body(ids, kept, got, mine, other, token):
    half = mine.shape[0]
    for bit in range(2):

        @pl.when(ids[5] == bit)
        def _(bit=bit):
            for out, side in ((mine, bit), (other, 1 - bit)):
                own = slice(half * side, half * side + half)
                out[...] = (kept[own, :].astype(f32) + got[own, :].astype(f32)).astype(bf16)


def run_halve(ids, bit, kept, got, after):
    rows, width = kept.shape
    return call(
        max(1, rows // 1500),
        halve_body,
        [((rows // 2, width), bf16)] * 2 + [TOKEN],
        [],
        ids.at[5].set(bit),
        (kept, got),
        after,
    )


def finish_body(ids, kept, got, share):
    share[...] = (kept[...].astype(f32) + got[...].astype(f32)).astype(bf16)


def total_body(ids, parts, share, token):
    total = parts[0].astype(f32)
    for n in range(1, parts.shape[0]):
        total = total + parts[n].astype(f32)
    half = total.shape[0] // 2
    share[...] = jnp.concatenate([total[:half], total[half:]], axis=1).astype(bf16)


def run_total(ids, parts):
    rows, width = parts.shape[1:]
    outs = [((rows // 2, 2 * width), bf16), TOKEN]
    return call(1, total_body, outs, [], ids, (parts,))


def gather_body(ids, heavy, mixer, embed, early, share):
    rows, width = heavy.shape[1:]
    total = heavy[0].astype(f32)
    for n in range(1, heavy.shape[0]):
        total = total + heavy[n].astype(f32)
    share[0:rows, :] = total.astype(bf16)
    share[rows : rows + 144, :] = mixer[...]
    share[rows + 144 : rows + 208, :] = embed[...]
    pad = jnp.zeros((8, width), f32)
    share[rows + 208 :, :] = jnp.concatenate([early[...].astype(f32), pad], axis=0).astype(bf16)


def run_gather(ids, *arrays):
    rows, width = arrays[0].shape[1:]
    return call(1, gather_body, [((rows + 240, width), bf16)], [], ids, arrays)[0]


def run_finish(ids, kept, got, after):
    return call(1, finish_body, [(kept.shape, bf16)], [], ids, (kept, got), after)[0]


def taps_of(x, width):
    for i in range(3):
        lined = row_shift(x, i - 1, width)
        for j in range(3):
            yield 3 * i + j, col_shift(lined, j - 1, width)


def grad_bottom_body(split, ids, low_up, e_four, low_four, p_four, low_three, p_three, table, token, up_part, four_part, three_part):
    place = ids[2]
    lanes = low_up.shape[1]
    spread = quad_map(lanes // 4, 32)
    shares = table.shape[0]

    def own_part(low):
        rows = low.shape[0] // split
        return low[pl.ds(pl.multiple_of(place * rows, rows), rows), :]

    low = own_part(low_up)
    for tap, x in taps_of(mm(e_four[...], spread).astype(bf16), 64):
        up_part[tap] = mm_nt(low, x)
    low = own_part(low_four)
    for tap, x in taps_of(p_four[...], 32):
        four_part[tap] = mm_nt(low, x)
    low = own_part(low_three)
    for tap, x in taps_of(laid_out(p_three), 64):
        three_part[tap] = mm_nt(low, x)
    for n in range(shares):
        for tap in range(9):
            fifth = jnp.concatenate(
                [
                    four_part[tap, 16 * n : 16 * n + 8, :],
                    four_part[tap, 16 * n + 8 : 16 * n + 16, :],
                ],
                axis=1,
            )
            main = jnp.concatenate([up_part[tap, 8 * n : 8 * n + 8, :], fifth], axis=0)
            table[n, 16 * tap : 16 * tap + 16, :] = main.astype(bf16)
        zero = jnp.zeros((8, 128), f32)
        sides = [three_part[tap, 8 * n : 8 * n + 8, :] for tap in range(9)] + [zero] * 7
        sides = [jnp.concatenate(sides[4 * k : 4 * k + 4], axis=1) for k in range(4)]
        table[n, 144:176, :] = jnp.concatenate(sides, axis=0).astype(bf16)


def run_grad_bottom(split, shares, ids, after, *arrays):
    return call(
        6,
        functools.partial(grad_bottom_body, split),
        [((shares, 176, 512), bf16), TOKEN],
        [
            ((9, 256 // split, 512), f32),
            ((9, 512 // split, 256), f32),
            ((9, 256 // split, 128), f32),
        ],
        ids,
        arrays,
        after,
        late=(1, 3),
    )


def unpack_body(whole, *refs):
    stage, marks = refs[-2:]
    plain = list(refs[:-2])
    step = pl.program_id(0)
    last = pl.num_programs(0) - 1

    def fetch(n):
        return pltpu.make_async_copy(whole.at[n], stage.at[n % 4], marks.at[n % 4])

    @pl.when(step == 0)
    def _():
        for n in range(3):
            fetch(n).start()

    @pl.when(step + 3 <= last)
    def _():
        fetch(step + 3).start()

    fetch(step).wait()
    held = stage.at[step % 4]
    up, fifth, fourth, *plain, early = plain
    for tap in range(9):
        block = held[16 * tap : 16 * tap + 16, :].astype(f32)
        up[tap] = block[0:8, :]
        fifth[tap, 0:8, :] = block[8:16, 0:256]
        fifth[tap, 8:16, :] = block[8:16, 256:512]
    sides = held[144:176, :].astype(f32)
    for tap in range(9):
        rows = slice(8 * (tap // 4), 8 * (tap // 4) + 8)
        fourth[tap] = sides[rows, 128 * (tap % 4) : 128 * (tap % 4) + 128]
    first = 176
    for out in plain:
        rows = out.shape[0]
        out[...] = held[first : first + rows, :].astype(f32)
        first = first + rows
    block = held[first : first + 32, :].astype(f32)
    early[0:24, :] = block[0:24, 0:256]
    early[24:48, :] = block[0:24, 256:512]


def run_unpack(whole):
    tiles = whole.shape[0] // 4

    def by_page(n):
        return (0, n % tiles * 4 + n // tiles, 0)

    def by_chunk(n):
        tile, page = n % tiles, n // tiles
        return (page % 2 * 16 + page // 2 * 8 + tile % 2 * 4 + tile // 4 * 2 + tile // 2 % 2, 0)

    def plain(n):
        return (n, 0)

    def by_column(n):
        return (n % 8, n // 8)

    def out(shape, block, spot):
        return jax.ShapeDtypeStruct(shape, f32), pl.BlockSpec(block, spot)

    outs = [
        out((9, 256, 512), (9, 8, 512), by_page),
        out((9, 512, 256), (9, 16, 256), by_page),
        out((9, 256, 128), (9, 8, 128), by_page),
        out((2048, 512), (64, 512), plain),
        out((512, 2048), (64, 512), by_column),
        out((512, 512), (16, 512), plain),
        out((512, 512), (16, 512), by_chunk),
        out((512, 512), (16, 512), by_chunk),
        out((512, 512), (16, 512), by_chunk),
        out((512, 512), (16, 512), by_chunk),
        out((1536, 256), (48, 256), plain),
    ]
    return pl.pallas_call(
        unpack_body,
        cost_estimate=price(14),
        grid=(whole.shape[0],),
        out_shape=[shape for shape, _ in outs],
        in_specs=[pl.BlockSpec(memory_space=pltpu.HBM)],
        out_specs=[spec for _, spec in outs],
        scratch_shapes=[
            pltpu.VMEM((4, *whole.shape[1:]), bf16),
            pltpu.SemaphoreType.DMA((4,)),
        ],
        compiler_params=pltpu.CompilerParams(vmem_limit_bytes=VMEM_CAP),
    )(in_hbm(whole))


def grad_bottom_all_body(ids, low_up, e_four, low_four, p_four, low_three, p_three, grad_up, grad_four, grad_three):
    lanes = low_up.shape[1]
    spread = quad_map(lanes // 4, 32)

    def own_part(low):
        size = low.shape[1] // (lanes // 128)
        own = lane_ids(low.shape) // size == ids[2]
        return jnp.where(own, low[...], jnp.zeros((), bf16))

    low = own_part(low_up)
    for tap, x in taps_of(mm(e_four[...], spread).astype(bf16), 64):
        grad_up[tap] = mm_nt(low, x).astype(bf16)
    low = own_part(low_four)
    for tap, x in taps_of(p_four[...], 32):
        grad_four[tap] = mm_nt(low, x).astype(bf16)
    low = own_part(low_three)
    for tap, x in taps_of(laid_out(p_three), 64):
        grad_three[tap] = mm_nt(low, x).astype(bf16)


def run_grad_bottom_all(ids, *arrays):
    return call(
        6,
        grad_bottom_all_body,
        [((9, 256, 512), bf16), ((9, 512, 256), bf16), ((9, 256, 128), bf16)],
        [],
        ids,
        arrays,
    )


def grad_down_body(ids, p_two, low_two, p_one, low_one, page, low_zero, table, cols):
    stacked = stack_cols(p_two[...], 128)
    for i in range(3):
        grad = mm_nt(low_two[...], stacked[:, i * 128 : i * 128 + 512]).astype(bf16)
        table[128 * i : 128 * i + 128, 0:192] = grad
    table[0:384, 192:256] = jnp.zeros((384, 64), bf16)
    table[384:512, :] = jnp.zeros((128, 256), bf16)
    stacked = stack_cols(p_one[...], 256)
    parts = [
        mm_nt(low_one[...], stacked[:, i * 256 : i * 256 + 2048]).astype(bf16) for i in range(3)
    ]
    grad = jnp.concatenate(parts, axis=0)
    table[384:480, 0:96] = grad[:96]
    table[384:480, 128:224] = grad[96:]
    rows = page[...].astype(f32)
    for j in range(3):
        cols[j] = col_shift(rows, j - 1, 512)
    pieces = [cols[j, :, i * 512 : i * 512 + 8192] for i in range(3) for j in range(3)]
    grad = mm_nt(low_zero[...], jnp.concatenate(pieces, axis=0).astype(bf16))
    table[480:512, 0:72] = grad.astype(bf16)


def run_grad_down(ids, *arrays):
    return call(
        3,
        grad_down_body,
        [((512, 256), bf16)],
        [((3, 8, 18 * 512), f32)],
        ids,
        arrays,
        late=(0, 2, 4),
    )[0]


def bucket_of(signed_gap):
    distance = jnp.abs(signed_gap)
    far_steps = jnp.zeros_like(distance)
    for threshold in bounds:
        far_steps = far_steps + (distance >= threshold).astype(jnp.int32)
    nearness = jnp.where(distance < 8, distance, 8 + far_steps)
    return nearness + jnp.where(signed_gap > 0, 16, 0).astype(jnp.int32)


def rms_scale(value, gain):
    return value * lax.rsqrt(jnp.mean(value * value, axis=-1, keepdims=True) + eps) * gain


def gelu_back(pre_act, upstream):
    return jax.vjp(jax.nn.gelu, pre_act)[1](upstream)[0]


def block_scores(query_heads, key_heads, query_meta, key_meta, bias_table, score_scale):
    query_pos, query_cx, query_cy, query_seg = query_meta
    key_pos, key_cx, key_cy, key_seg = key_meta
    rel_bucket = bucket_of(key_pos[None, :] - query_pos[:, None])
    hor_bucket = bucket_of(key_cx[None, :] - query_cx[:, None]) + NB
    ver_bucket = bucket_of(key_cy[None, :] - query_cy[:, None]) + 2 * NB
    slot_ids = jnp.arange(3 * NB)
    one_hot = (
        (rel_bucket[..., None] == slot_ids)
        | (hor_bucket[..., None] == slot_ids)
        | (ver_bucket[..., None] == slot_ids)
    ).astype(jnp.bfloat16)
    scores = (
        jnp.einsum("hqd,hkd->hqk", query_heads, key_heads, preferred_element_type=jnp.float32)
        * score_scale
    )
    scores = scores + jnp.einsum(
        "qkn,hn->hqk", one_hot, bias_table, preferred_element_type=jnp.float32
    )
    allowed = query_seg[:, None] == key_seg[None, :]
    return (scores, allowed, one_hot)


def norm_parts(value):
    scale = lax.rsqrt(jnp.mean(value * value, axis=-1, keepdims=True) + eps)
    return scale


def norm_back(value, gain, upstream):
    scale = norm_parts(value)
    weighted = upstream * gain
    inner = jnp.mean(weighted * value, axis=-1, keepdims=True)
    d_value = weighted * scale - value * (inner * scale * scale * scale)
    d_gain = jnp.sum(upstream * value * scale, axis=0, keepdims=True)
    return d_value, d_gain


def embed_body(ids, pieces, emb, roi, gain, wq, wk, wv, residual, normed, pooled, shared):
    total = pieces[0].astype(f32)
    for n in range(1, pieces.shape[0]):
        total = total + pieces[n].astype(f32)
    low = total.astype(bf16)
    pooled[...] = low
    resid = emb[...].astype(f32) + mm(low, roi[...])
    residual[...] = resid
    normal = (resid * norm_parts(resid) * gain[...].astype(f32)).astype(bf16)
    normed[...] = normal
    for n, weight in enumerate((wq, wk, wv)):
        turned = mm(normal, weight[...]).T.astype(bf16)
        for h in range(HEADS):
            shared[h, HD * n : HD * n + HD, :] = turned[HD * h : HD * h + HD, :]


def run_embed(ids, pieces, emb, *arrays):
    rows, width = emb.shape
    return call(
        2,
        embed_body,
        [
            ((rows, width), f32),
            ((rows, width), bf16),
            ((rows, pieces.shape[2]), bf16),
            ((HEADS, 3 * HD, rows), bf16),
        ],
        [],
        ids,
        (pieces, emb, *arrays),
    )


def looked_up(bucket, table, head, first):
    value = jnp.zeros(bucket.shape, f32)
    for n in range(NB):
        value = jnp.where(bucket == n, table[head, first + n], value)
    return value


def toeplitz(span, table, head, first):
    lane = lane_ids((1, 2 * span))
    gap = jnp.where(lane < span, -lane, 2 * span - lane)
    line = looked_up(bucket_of(gap), table, head, first)
    square = jnp.broadcast_to(line, (span, 2 * span))
    return pltpu.roll(square, 0, 1, stride=1, stride_axis=0)[:, :span].astype(bf16)


def centers(meta):
    return ((meta[0:1, :] + meta[2:3, :]) >> 1, (meta[1:2, :] + meta[3:4, :]) >> 1)


def one_hot_rows(value, span, turned):
    row = row_ids_of((span, value.shape[1]))
    if turned:
        row = span - 1 - row
    return jnp.where(row == value, 1.0, 0.0).astype(bf16)


def attend_body(tall, ids, table, meta, meta_cols, shared, prob, out_low, out_full, hits, spread, near):
    head = ids[0]
    seq = meta.shape[1]
    count = shared.shape[0]
    spans = (512, tall)
    for n, (value, span) in enumerate(zip(centers(meta), spans)):
        chart = toeplitz(span, table, head, NB * (n + 1))
        low = sum(spans[:n])
        spread[low : low + span, :] = mm(chart, one_hot_rows(value, span, False)).astype(bf16)
    cols = meta_cols[...]
    for n, span in enumerate(spans):
        value = (cols[:, n : n + 1] + cols[:, n + 2 : n + 3]) >> 1
        low = sum(spans[:n])
        same = lane_ids((1, span)) == value
        hits[:, low : low + span] = jnp.where(same, 1.0, 0.0).astype(bf16)
    edge = seq - 128
    near[0 : edge - 128, :] = jnp.full((edge - 128, 128), table[head, NB // 2 - 1], f32)
    near[edge + 256 :, :] = jnp.full((seq - 256, 128), table[head, NB - 1], f32)
    gap = row_ids_of((384, 128)) - 128 - lane_ids((384, 128))
    near[edge - 128 : edge + 256, :] = looked_up(bucket_of(gap), table, head, 0)
    query = jnp.concatenate([shared[n, 0:HD, :] for n in range(count)], axis=1)
    key = jnp.concatenate([shared[n, HD : 2 * HD, :] for n in range(count)], axis=1)
    value = jnp.concatenate([shared[n, 2 * HD :, :] for n in range(count)], axis=1)
    key = (key.astype(f32) * (HD**-0.5)).astype(bf16)
    seg_key = cols[:, 4:5]
    for block in range(seq // 256):
        own = slice(256 * block, 256 * block + 256)
        first = edge - 256 * block
        scores = mm_tn(key, query[:, own]) + mm(hits[...], spread[:, own])
        scores = scores + jnp.concatenate(
            [near[first : first + seq, :], near[first - 128 : first - 128 + seq, :]], axis=1
        )
        scores = jnp.where(seg_key == meta[4:5, own], scores, neg_large)
        weight = jnp.exp(scores - jnp.max(scores, axis=0, keepdims=True))
        weight = weight * (1.0 / jnp.sum(weight, axis=0, keepdims=True))
        low = weight.astype(bf16)
        prob[block] = low
        found = mm(value, low)
        out_full[:, own] = found
        for n in range(2):
            out_low[2 * block + n] = found[:, 128 * n : 128 * n + 128].astype(bf16)


def run_attend(tall, ids, table, meta, meta_cols, shared):
    seq = meta.shape[1]
    count = shared.shape[0]
    return call(
        9,
        functools.partial(attend_body, tall),
        [
            ((seq // 256, seq, 256), bf16),
            ((count, HD, seq // count), bf16),
            ((HD, seq), f32),
        ],
        [
            ((seq, 512 + tall), bf16),
            ((512 + tall, seq), bf16),
            ((2 * seq - 128, 128), f32),
        ],
        ids,
        (meta, meta_cols, shared),
        sent=(0, 2),
        table=table,
    )


def bucket_sums(value, bucket):
    lines = [
        jnp.sum(jnp.where(bucket == n, value, 0.0), axis=0, keepdims=True) for n in range(NB)
    ]
    return jnp.sum(jnp.concatenate(lines, axis=0), axis=1, keepdims=True)


def attend_back_body(tall, ids, meta, shared, prob, out_full, d_out, d_shared, d_table, near, drift, key_sum, value_sum):
    seq = meta.shape[1]
    count = shared.shape[0]
    spans = (512, tall)
    query = jnp.concatenate([shared[n, 0:HD, :] for n in range(count)], axis=1)
    key = jnp.concatenate([shared[n, HD : 2 * HD, :] for n in range(count)], axis=1)
    value = jnp.concatenate([shared[n, 2 * HD :, :] for n in range(count)], axis=1)
    d_found = jnp.concatenate([d_out[n] for n in range(count)], axis=1)
    delta = jnp.sum(d_found.astype(f32) * out_full[...], axis=0, keepdims=True)
    near[...] = jnp.zeros_like(near)
    key_sum[...] = jnp.zeros_like(key_sum)
    value_sum[...] = jnp.zeros_like(value_sum)
    places = centers(meta)
    turned = jnp.concatenate(
        [one_hot_rows(place, span, True) for place, span in zip(places, spans)], axis=0
    )
    edge = seq - 128
    scale = HD**-0.5
    for block in range(seq // 256):
        own = slice(256 * block, 256 * block + 256)
        first = edge - 256 * block
        low = prob[block]
        d_prob = mm_tn(value, d_found[:, own])
        d_score = low.astype(f32) * (d_prob - delta[:, own])
        near[first : first + seq, :] += d_score[:, :128]
        near[first - 128 : first - 128 + seq, :] += d_score[:, 128:]
        d_low = d_score.astype(bf16)
        d_query = (mm(key, d_low) * scale).astype(bf16)
        for n in range(2):
            d_shared[2 * block + n, 0:HD, :] = d_query[:, 128 * n : 128 * n + 128]
        key_sum[...] += mm_nt(query[:, own], d_low)
        value_sum[...] += mm_nt(d_found[:, own], low)
        drift[:, own] = mm(turned, d_low).astype(bf16)
    d_key = (key_sum[...] * scale).astype(bf16)
    d_value = value_sum[...].astype(bf16)
    for n in range(count):
        d_shared[n, HD : 2 * HD, :] = d_key[:, 128 * n : 128 * n + 128]
        d_shared[n, 2 * HD :, :] = d_value[:, 128 * n : 128 * n + 128]
    sums = []
    slot = 3 * ids[0]
    gap = row_ids_of((384, 128)) - 128 - lane_ids((384, 128))
    sums.append(bucket_sums(near[edge - 128 : edge + 256, :], bucket_of(gap)))
    row = row_ids_of((NB, 128))
    lane = lane_ids((NB, 128))
    behind = jnp.sum(near[0 : edge - 128, :], axis=0, keepdims=True)
    ahead = jnp.sum(near[edge + 256 :, :], axis=0, keepdims=True)
    far = jnp.where(row == NB // 2 - 1, behind, jnp.where(row == NB - 1, ahead, 0.0))
    sums[0] = sums[0] + jnp.sum(far, axis=1, keepdims=True)
    for n, (place, span) in enumerate(zip(places, spans)):
        low = sum(spans[:n])
        square = mm_nt(drift[low : low + span, :], one_hot_rows(place, span, False))
        square = jnp.concatenate([square, jnp.zeros_like(square)], axis=1)
        lined = pltpu.roll(square, 0, 1, stride=1, stride_axis=0)
        line = jnp.sum(lined, axis=0, keepdims=True)
        bucket = bucket_of(span - 1 - lane_ids((1, 2 * span)))
        sums.append(bucket_sums(line, bucket))
    d_table[...] = jnp.where(
        lane == slot,
        sums[0],
        jnp.where(lane == slot + 1, sums[1], jnp.where(lane == slot + 2, sums[2], 0.0)),
    )


def run_attend_back(tall, ids, after, meta, *arrays):
    seq = meta.shape[1]
    shared = arrays[0]
    return call(
        6,
        functools.partial(attend_back_body, tall),
        [(shared.shape, bf16), ((NB, 128), f32)],
        [
            ((2 * seq - 128, 128), f32),
            ((512 + tall, seq), bf16),
            ((HD, seq), f32),
            ((HD, seq), f32),
        ],
        ids,
        (meta, *arrays),
        after,
        late=(3, 2),
    )


def mixer_body(ids, found, residual, upstream, w_out, gain, w_in, w_down, result, act, d_pre, ffn_low, d_mixed, d_low, d_found, d_gain):
    attn = jnp.concatenate([found[h] for h in range(HEADS)], axis=0)
    mixed = residual[...] + mm_tn(attn, w_out[...])
    wide_gain = gain[...].astype(f32)
    low = (mixed * norm_parts(mixed) * wide_gain).astype(bf16)
    ffn_low[...] = low
    pre = mm(low, w_in[...])
    hidden = gelu_of(pre).astype(bf16)
    act[...] = hidden
    result[...] = (mixed + mm(hidden, w_down[...])).astype(bf16)
    d_hidden = (mm_nt(upstream[...], w_down[...]) * gelu_slope(pre)).astype(bf16)
    d_pre[...] = d_hidden
    d_norm, gain_sum = norm_back(mixed, wide_gain, mm_nt(d_hidden, w_in[...]))
    d_gain[...] = gain_sum
    d_sum = upstream[...].astype(f32) + d_norm
    d_mixed[...] = d_sum
    narrow = d_sum.astype(bf16)
    d_low[...] = narrow
    back = mm_nt(w_out[...], narrow).astype(bf16)
    for h in range(HEADS):
        d_found[h] = back[HD * h : HD * h + HD, :]


def run_mixer(ids, found, residual, upstream, w_out, gain, w_in, w_down):
    rows, width = residual.shape
    wide = w_in.shape[1]
    return call(
        5,
        mixer_body,
        [
            ((rows, width), bf16),
            ((rows, wide), bf16),
            ((rows, wide), bf16),
            ((rows, width), bf16),
            ((rows, width), f32),
            ((rows, width), bf16),
            ((HEADS, HD, rows), bf16),
            ((1, width), f32),
        ],
        [],
        ids,
        (found, residual, upstream, w_out, gain, w_in, w_down),
        late=(5, 6),
    )


def put_halves(ids, first, second, mine, other):
    for bit in range(2):

        @pl.when(ids[5] == bit)
        def _(bit=bit):
            mine[...] = first[...] if bit == 0 else second[...]
            other[...] = second[...] if bit == 0 else first[...]


def mixer_grads_body(ids, found, act, d_pre, ffn_low, d_low, upstream, table, token):
    width = ffn_low.shape[1]
    grad_out = mm_tn(act[...], upstream[...]).astype(bf16)
    grad_in = mm_tn(ffn_low[...], d_pre[...]).astype(bf16)
    attn = jnp.concatenate([found[h] for h in range(HEADS)], axis=0)
    grad_attn = mm(attn, d_low[...]).astype(bf16)
    for c in range(32):
        spot, row = 144 * c, 64 * (c % 8)
        table[spot : spot + 64, :] = grad_out[64 * c : 64 * c + 64, :]
        column = width * (c // 8)
        table[spot + 64 : spot + 128, :] = grad_in[row : row + 64, column : column + width]
        table[spot + 128 : spot + 144, :] = grad_attn[16 * c : 16 * c + 16, :]


def run_mixer_grads(ids, *arrays):
    return call(4, mixer_grads_body, [((4608, 512), bf16), TOKEN], [], ids, arrays)


def embed_back_body(ids, d_shared, residual, d_mixed, gain, wq, wk, wv, roi, d_resid, d_low, d_pooled, d_gain, d_rows, token):
    turned = None
    for n, weight in enumerate((wq, wk, wv)):
        lines = jnp.concatenate([d_shared[h, HD * n : HD * n + HD, :] for h in range(HEADS)], axis=0)
        d_rows[n] = lines
        term = mm(weight[...], lines)
        turned = term if turned is None else turned + term
    d_norm, gain_sum = norm_back(residual[...], gain[...].astype(f32), turned.T)
    d_gain[...] = gain_sum
    total = d_mixed[...] + d_norm
    d_resid[...] = total
    low = total.astype(bf16)
    d_low[...] = low
    d_pooled[...] = mm_nt(low, roi[...]).astype(bf16)


def run_embed_back(ids, d_shared, residual, *arrays):
    rows, width = residual.shape
    roi = arrays[-1]
    return call(
        2,
        embed_back_body,
        [
            ((rows, width), f32),
            ((rows, width), bf16),
            ((rows, roi.shape[0]), bf16),
            ((1, width), f32),
            ((3, HEADS * HD, rows), bf16),
            TOKEN,
        ],
        [],
        ids,
        (d_shared, residual, *arrays),
    )


def embed_grads_body(ids, normed, d_rows, pooled, d_low, gains_one, gains_two, d_table, mine, other, token, table):
    width = normed.shape[1]
    turned = normed[...].astype(f32).T.astype(bf16)
    grads = [mm_nt(turned, d_rows[n]).astype(bf16) for n in range(3)]
    roi = mm_tn(pooled[...], d_low[...])
    lane = lane_ids((1, width))
    buckets = jnp.concatenate([d_table[...]] * (width // 128), axis=1)
    buckets = jnp.where(lane < 128, buckets, 0.0)
    blank = jnp.zeros((1, width), f32)
    for c in range(32):
        spot = 64 * (c % 16)
        for n in range(3):
            table[c // 16, spot + 16 * n : spot + 16 * n + 16, :] = grads[n][16 * c : 16 * c + 16, :]
        gains = [gains_one[...], gains_two[...]] if c == 0 else [blank, blank]
        lines = [roi[4 * c : 4 * c + 4, :], buckets[c : c + 1, :], *gains, blank]
        lines = jnp.concatenate(lines + [jnp.zeros((8, width), f32)], axis=0)
        table[c // 16, spot + 48 : spot + 64, :] = lines.astype(bf16)
    put_halves(ids, table.at[0], table.at[1], mine, other)


def run_embed_grads(ids, bit, after, *arrays):
    return call(
        3,
        embed_grads_body,
        [((1024, 512), bf16)] * 2 + [TOKEN],
        [((2, 1024, 512), bf16)],
        ids.at[5].set(bit),
        arrays,
        after,
    )


def on_device(
    embeddings,
    page_images,
    token_boxes,
    segment_ids,
    down_first,
    down_second,
    down_third,
    down_fourth,
    down_fifth,
    up_fourth,
    up_third,
    up_second,
    up_first,
    roi_proj,
    gain_attn,
    w_query,
    w_key,
    w_value,
    w_output,
    bias_table,
    gain_ffn,
    ffn_in,
    ffn_out,
    cotangent,
):
    tok_rows = embeddings.shape[1]
    model_width = embeddings.shape[2]
    tile_rows = page_images.shape[2]
    my_tile = lax.axis_index("tile")
    tile_count = lax.axis_size("tile")
    score_scale = HD ** (-0.5)
    cut = tile_count > 12
    window = 12 if cut else tile_count
    place = 6 if cut else my_tile
    ids = jnp.stack(
        [
            my_tile,
            jnp.asarray(tile_rows * tile_count, my_tile.dtype),
            jnp.asarray(place, my_tile.dtype),
            my_tile - place,
            jnp.asarray(2 if cut else my_tile, my_tile.dtype),
            jnp.asarray(0, my_tile.dtype),
        ]
    ).astype(jnp.int32)

    def gathered(block):
        copies = jnp.broadcast_to(block[None], (tile_count, *block.shape))
        return lax.all_to_all(copies, "tile", 0, 0, tiled=True)

    def windowed(block):
        if not cut:
            return gathered(block)
        blocks = lax.all_gather(block, "tile", axis=0)
        blocks = jnp.pad(blocks, ((6, 6), (0, 0), (0, 0)))
        return lax.dynamic_slice_in_dim(blocks, my_tile, window, 0)

    def from_side(block, step):
        hops = [
            (source, source + step) for source in range(tile_count) if 0 <= source + step < tile_count
        ]
        return lax.ppermute(block, "tile", hops)

    def lined(weight):
        return weight.transpose(0, 2, 1, 3).reshape(3, weight.shape[2], -1)

    def lined_back(weight):
        flipped = weight[::-1, ::-1]
        return flipped.transpose(0, 3, 1, 2).reshape(3, weight.shape[3], -1)

    def beside(table, count):
        return jnp.concatenate(jnp.split(table, count, axis=0), axis=1)

    def below(table, count):
        return jnp.concatenate(jnp.split(table, count, axis=1), axis=0)

    def as_rows(member):
        return member.reshape(-1, member.shape[-1])

    def bit_of(axis, mask):
        return (lax.axis_index(axis) & mask) // mask

    def swapped(block, axis, mask):
        hops = [(source, source ^ mask) for source in range(lax.axis_size(axis))]
        return lax.ppermute(block, axis, hops)

    def halved(halves, step, *after):
        mine, other, _ = halves
        got = swapped(other, *HOPS[step])
        if step + 1 == len(HOPS):
            return run_finish(ids, mine, got, after)
        return run_halve(ids, bit_of(*HOPS[step + 1]), mine, got, after)

    line = page_images.shape[3]
    meta = jnp.concatenate([token_boxes[:, 0], segment_ids])
    digits = jnp.concatenate([meta // 256, meta % 256, jnp.zeros((2, tok_rows), jnp.int32)])
    digits = digits.astype(jnp.bfloat16).reshape(24, -1)
    sheet = jnp.concatenate([page_images[0].reshape(24, -1), digits], axis=1)
    sheets = gathered(sheet)
    digits_all = sheets[:, :, 2 * line :].reshape(tile_count, 12, tok_rows)
    digits_all = digits_all.transpose(1, 0, 2).reshape(12, -1).astype(jnp.int32)
    meta_all = jnp.pad(digits_all[:5] * 256 + digits_all[5:10], ((0, 3), (0, 0)))
    if cut:
        sheets = jnp.pad(sheets, ((2, 2), (0, 0), (0, 0)))
        sheets = lax.dynamic_slice_in_dim(sheets, my_tile, 5, 0)
    left_all, top_all, right_all, bottom_all, seg_all = (meta_all[n] for n in range(5))
    box_rows = meta_all.T
    seq_all = seg_all.shape[0]
    w_zero = jnp.pad(down_first.transpose(2, 0, 1, 3), ((0, 0), (0, 0), (0, 0), (0, 5)))
    w_zero = w_zero.reshape(w_zero.shape[0], -1)
    pre_zero, pre_one, p_one, pre_two, p_two, p_three, page_own = run_down(
        ids, sheets, w_zero, lined(down_second), lined(down_third)
    )
    p_three_all = windowed(p_three)
    pre_three, pre_four, p_four, e_four, pre_up_three, dec_three = run_bottom(
        cut, ids, p_three_all, down_fourth, down_fifth, up_fourth
    )
    pre_up_two, pre_up_one, pre_up_zero, u_three, dec_two, dec_one, features = run_up(
        ids, dec_three, pre_two, pre_one, pre_zero, up_third, lined(up_second), lined(up_first)
    )
    pooled_own = run_pool(ids, box_rows, features, 256)
    pieces = lax.all_to_all(
        pooled_own.reshape(tile_count, tok_rows, -1), "tile", 0, 0, tiled=True
    )
    gain_row_one = gain_attn.reshape(1, -1)
    gain_row_two = gain_ffn.reshape(1, -1)
    heads_first = tile_count == HEADS
    if heads_first:
        tall = tile_rows * tile_count
        residual, normed_low, pooled_low, shared = run_embed(
            ids, pieces, embeddings[0], roi_proj, gain_row_one, w_query, w_key, w_value
        )
        shared = lax.all_to_all(shared, "tile", 0, 0, tiled=True)
        prob, found_low, found_full = run_attend(
            tall, ids, bias_table.astype(jnp.float32), meta_all, box_rows, shared
        )
        found = lax.all_to_all(found_low, "tile", 0, 0, tiled=True)
        result_low, act_low, d_pre, ffn_low, d_mixed, d_mixed_low, d_found, grad_gain_ffn = run_mixer(
            ids, found, residual, cotangent[0], w_output, gain_row_two, ffn_in, ffn_out
        )
        d_found = lax.all_to_all(d_found, "tile", 0, 0, tiled=True)
        mixer_table, mixer_token = run_mixer_grads(
            ids, found, act_low, d_pre, ffn_low, d_mixed_low, cotangent[0]
        )
        mixer_share = lax.psum_scatter(
            mixer_table, (*PAGES, "tile"), scatter_dimension=0, tiled=True
        )
        d_shared, d_table = run_attend_back(
            tall, ids, (mixer_token,), meta_all, shared, prob, found_full, d_found
        )
        d_shared = lax.all_to_all(d_shared, "tile", 0, 0, tiled=True)
        d_residual, d_resid_low, d_pooled, grad_gain_attn, d_rows, embed_token = run_embed_back(
            ids, d_shared, residual, d_mixed, gain_row_one, w_query, w_key, w_value, roi_proj
        )
        embed_halves = run_embed_grads(
            ids,
            bit_of(*HOPS[0]),
            (),
            normed_low,
            d_rows,
            pooled_low,
            d_resid_low,
            grad_gain_attn,
            grad_gain_ffn,
            d_table,
        )
        embed_halves = halved(embed_halves, 0)
        ordering = embed_halves[2:]
    else:
        ordering = ()
        pooled_low = jnp.sum(pieces.astype(jnp.float32), axis=0).astype(jnp.bfloat16)
        residual = embeddings[0].astype(jnp.float32) + jnp.dot(
            pooled_low, roi_proj, preferred_element_type=jnp.float32
        )
        gain_one = gain_attn.astype(jnp.float32)
        normed_low = rms_scale(residual, gain_one).astype(jnp.bfloat16)
        query_low = jnp.dot(normed_low, w_query, preferred_element_type=jnp.float32).astype(
            jnp.bfloat16
        )
        key_low = jnp.dot(normed_low, w_key, preferred_element_type=jnp.float32).astype(jnp.bfloat16)
        value_low = jnp.dot(normed_low, w_value, preferred_element_type=jnp.float32).astype(
            jnp.bfloat16
        )

        def to_heads(flat_rows):
            return flat_rows.reshape(tok_rows, HEADS, HD).transpose(1, 0, 2)

        def from_heads(head_rows):
            return head_rows.transpose(1, 0, 2).reshape(tok_rows, model_width)

        query_heads = to_heads(query_low)
        own_keys = to_heads(key_low)
        own_values = to_heads(value_low)
        key_all, value_all = (
            lax.all_gather(own_keys, "tile", axis=1, tiled=True),
            lax.all_gather(own_values, "tile", axis=1, tiled=True),
        )
        center_x = (left_all + right_all) // 2
        center_y = (top_all + bottom_all) // 2
        key_meta = (jnp.arange(seq_all), center_x, center_y, seg_all)
        first_tok = my_tile * tok_rows
        query_meta = tuple(
            (lax.dynamic_slice_in_dim(member, first_tok, tok_rows, 0) for member in key_meta)
        )
        key_block = math.gcd(seq_all, 1024)
        block_count = seq_all // key_block

        def key_slice(block_id):
            first_key = block_id * key_block
            keys_blk = lax.dynamic_slice_in_dim(key_all, first_key, key_block, 1)
            values_blk = lax.dynamic_slice_in_dim(value_all, first_key, key_block, 1)
            meta_blk = tuple(
                (lax.dynamic_slice_in_dim(member, first_key, key_block, 0) for member in key_meta)
            )
            return (keys_blk, values_blk, meta_blk)

        def stats_step(running, block_id):
            run_max, run_sum = running
            keys_blk, values_blk, meta_blk = key_slice(block_id)
            scores, allowed, one_hot = block_scores(
                query_heads, keys_blk, query_meta, meta_blk, bias_table, score_scale
            )
            scores = jnp.where(allowed[None], scores, neg_large)
            new_max = jnp.maximum(run_max, jnp.max(scores, axis=-1))
            run_sum = run_sum * jnp.exp(run_max - new_max) + jnp.sum(
                jnp.exp(scores - new_max[..., None]), axis=-1
            )
            return ((new_max, run_sum), None)

        start_stats = (
            jnp.full((HEADS, tok_rows), neg_large, jnp.float32),
            jnp.zeros((HEADS, tok_rows), jnp.float32),
        )
        (run_max, run_sum), _ = lax.scan(stats_step, start_stats, jnp.arange(block_count))
        log_total = run_max + jnp.log(run_sum)

        def out_step(attn_acc, block_id):
            keys_blk, values_blk, meta_blk = key_slice(block_id)
            scores, allowed, one_hot = block_scores(
                query_heads, keys_blk, query_meta, meta_blk, bias_table, score_scale
            )
            attn_prob = jnp.where(allowed[None], jnp.exp(scores - log_total[..., None]), 0.0)
            attn_acc = attn_acc + jnp.einsum(
                "hqk,hkd->hqd",
                attn_prob.astype(jnp.bfloat16),
                values_blk,
                preferred_element_type=jnp.float32,
            )
            return (attn_acc, None)

        attn_heads, _ = lax.scan(
            out_step, jnp.zeros((HEADS, tok_rows, HD), jnp.float32), jnp.arange(block_count)
        )
        attn_low = from_heads(attn_heads).astype(jnp.bfloat16)
        mixed_rows = residual + jnp.dot(attn_low, w_output, preferred_element_type=jnp.float32)
        gain_two = gain_ffn.astype(jnp.float32)
        ffn_low = rms_scale(mixed_rows, gain_two).astype(jnp.bfloat16)
        pre_ffn = jnp.dot(ffn_low, ffn_in, preferred_element_type=jnp.float32)
        act_low = jax.nn.gelu(pre_ffn).astype(jnp.bfloat16)
        result_rows = mixed_rows + jnp.dot(act_low, ffn_out, preferred_element_type=jnp.float32)
        upstream = cotangent[0]
        grad_ffn_out = jnp.einsum("tf,td->fd", act_low, upstream, preferred_element_type=jnp.float32)
        d_act = jnp.einsum("td,fd->tf", upstream, ffn_out, preferred_element_type=jnp.float32)
        d_pre = gelu_back(pre_ffn, d_act).astype(jnp.bfloat16)
        grad_ffn_in = jnp.einsum("td,tf->df", ffn_low, d_pre, preferred_element_type=jnp.float32)
        d_ffn_norm = jnp.einsum("tf,df->td", d_pre, ffn_in, preferred_element_type=jnp.float32)
        d_mixed_norm, grad_gain_ffn = jax.vjp(rms_scale, mixed_rows, gain_two)[1](d_ffn_norm)
        d_mixed = upstream.astype(jnp.float32) + d_mixed_norm
        d_mixed_low = d_mixed.astype(jnp.bfloat16)
        grad_output = jnp.einsum("tc,td->cd", attn_low, d_mixed_low, preferred_element_type=jnp.float32)
        d_attn = jnp.einsum(
            "td,cd->tc", d_mixed_low, w_output, preferred_element_type=jnp.float32
        ).astype(jnp.bfloat16)
        dout_heads = to_heads(d_attn)
        row_delta = jnp.sum(dout_heads.astype(jnp.float32) * attn_heads, axis=-1)

        def back_step(running, block_id):
            keys_blk, values_blk, meta_blk = key_slice(block_id)
            scores, allowed, one_hot = block_scores(
                query_heads, keys_blk, query_meta, meta_blk, bias_table, score_scale
            )
            attn_prob = jnp.where(allowed[None], jnp.exp(scores - log_total[..., None]), 0.0)
            d_prob = jnp.einsum(
                "hqd,hkd->hqk", dout_heads, values_blk, preferred_element_type=jnp.float32
            )
            d_score = (attn_prob * (d_prob - row_delta[..., None])).astype(jnp.bfloat16)
            query_acc = running[0] + jnp.einsum(
                "hqk,hkd->hqd", d_score, keys_blk, preferred_element_type=jnp.float32
            )
            table_acc = running[1] + jnp.einsum(
                "hqk,qkn->hn", d_score, one_hot, preferred_element_type=jnp.float32
            )
            first_key = block_id * key_block
            key_part = (
                jnp.einsum("hqk,hqd->hkd", d_score, query_heads, preferred_element_type=jnp.float32)
                * score_scale
            )
            value_part = jnp.einsum(
                "hqk,hqd->hkd",
                attn_prob.astype(jnp.bfloat16),
                dout_heads,
                preferred_element_type=jnp.float32,
            )
            key_acc = lax.dynamic_update_slice_in_dim(running[2], key_part, first_key, 1)
            value_acc = lax.dynamic_update_slice_in_dim(running[3], value_part, first_key, 1)
            return ((query_acc, table_acc, key_acc, value_acc), None)

        start_back = (
            jnp.zeros((HEADS, tok_rows, HD), jnp.float32),
            jnp.zeros((HEADS, 3 * NB), jnp.float32),
        )
        start_back = start_back + (
            jnp.zeros((HEADS, seq_all, HD), jnp.float32),
            jnp.zeros((HEADS, seq_all, HD), jnp.float32),
        )
        back_out, _ = lax.scan(back_step, start_back, jnp.arange(block_count))
        query_acc = back_out[0]
        grad_bias_table = back_out[1]
        key_grad, value_grad = (
            lax.psum_scatter(back_out[2], "tile", scatter_dimension=1, tiled=True),
            lax.psum_scatter(back_out[3], "tile", scatter_dimension=1, tiled=True),
        )
        dq_low = from_heads(query_acc * score_scale).astype(jnp.bfloat16)
        dk_low = from_heads(key_grad).astype(jnp.bfloat16)
        dv_low = from_heads(value_grad).astype(jnp.bfloat16)
        grad_query = jnp.einsum("td,te->de", normed_low, dq_low, preferred_element_type=jnp.float32)
        grad_key = jnp.einsum("td,te->de", normed_low, dk_low, preferred_element_type=jnp.float32)
        grad_value = jnp.einsum("td,te->de", normed_low, dv_low, preferred_element_type=jnp.float32)
        d_normed = (
            jnp.einsum("te,de->td", dq_low, w_query, preferred_element_type=jnp.float32)
            + jnp.einsum("te,de->td", dk_low, w_key, preferred_element_type=jnp.float32)
            + jnp.einsum("te,de->td", dv_low, w_value, preferred_element_type=jnp.float32)
        )
        d_resid_norm, grad_gain_attn = jax.vjp(rms_scale, residual, gain_one)[1](d_normed)
        d_residual = d_mixed + d_resid_norm
        d_resid_low = d_residual.astype(jnp.bfloat16)
        grad_roi_proj = jnp.einsum(
            "tp,td->pd", pooled_low, d_resid_low, preferred_element_type=jnp.float32
        )
        d_pooled = jnp.einsum("td,pd->tp", d_resid_low, roi_proj, preferred_element_type=jnp.float32)
        d_pooled = d_pooled.astype(jnp.bfloat16)
        result_low = result_rows.astype(jnp.bfloat16)
        mixer_table = jnp.concatenate([grad_ffn_out, below(grad_ffn_in, 4), grad_output], axis=0)
        mixer_table = mixer_table.astype(jnp.bfloat16)
        chart = grad_bias_table.reshape(HEADS, 3, NB).transpose(2, 0, 1).reshape(NB, 3 * HEADS)
        embed_table = jnp.concatenate(
            [
                grad_query,
                grad_key,
                grad_value,
                grad_roi_proj,
                jnp.pad(jnp.stack([grad_gain_attn, grad_gain_ffn]), ((0, 14), (0, 0))),
                jnp.pad(chart, ((0, 80), (0, model_width - 3 * HEADS))),
            ],
            axis=0,
        ).astype(jnp.bfloat16)
    d_pooled_all = gathered(d_pooled).reshape(seq_all, -1)
    d_features, low_zero_up, low_end, low_start, box_token = run_unpool(
        ids, ordering, box_rows, d_pooled_all, pre_up_zero, 256
    )
    if heads_first:
        embed_halves = halved(embed_halves, 1, box_token)
        ordering = embed_halves[2:]
    d_dec_one, d_dec_two, d_dec_three, low_one_up, low_two_up, up_token = run_up_back(
        ids,
        ordering,
        from_side(low_end, 1),
        low_zero_up,
        from_side(low_start, -1),
        pre_up_one,
        pre_up_two,
        lined_back(up_first),
        lined_back(up_second),
        up_third,
    )
    d_dec_three_all = windowed(d_dec_three)
    grad_up_first = run_grad_up_first(ids, (up_token,), dec_one, low_zero_up)
    if heads_first:
        embed_halves = halved(embed_halves, 2, up_token)
        ordering = embed_halves[2:]
    light_early, early_token = run_grad_up(
        ids, ordering, grad_up_first, dec_two, low_one_up, u_three, low_two_up
    )
    if heads_first:
        embed_halves = halved(embed_halves, 3, up_token)
        ordering = embed_halves[2:]
    low_three_up, low_four, low_three, d_pool_three, bottom_token = run_bottom_back(
        cut,
        ids,
        (*ordering, early_token),
        d_dec_three_all,
        pre_up_three,
        pre_four,
        pre_three,
        up_fourth,
        down_fifth,
        down_fourth,
    )
    dp_count = lax.axis_size(PAGES)
    if heads_first:
        embed_share = halved(embed_halves, 4, bottom_token)
        early_parts = lax.all_to_all(
            light_early.reshape(32, -1, 256), (*PAGES, "tile"), 0, 0, tiled=True
        )
        early_share, _ = run_total(ids, early_parts)
        ordering = ()
    bottom_parts = (low_three_up, e_four, low_four, p_four, low_three, p_three_all)
    if cut:
        heavy = run_grad_bottom_all(ids, *bottom_parts)
        heavy_token = ()
    else:
        heavy, *heavy_token = run_grad_bottom(tile_count, dp_count, ids, ordering, *bottom_parts)
    low_two, low_one, low_zero = run_down_back(
        ids,
        heavy_token,
        d_pool_three,
        d_dec_two,
        pre_two,
        d_dec_one,
        pre_one,
        d_features,
        pre_zero,
        down_third,
        lined_back(down_second),
    )
    light_late = run_grad_down(ids, p_two, low_two, p_one, low_one, page_own, low_zero)
    both_axes = (*PAGES, "tile")
    device_total = dp_count * tile_count

    def summed_share(table):
        parts = table.reshape(device_total, -1, table.shape[1])
        parts = lax.all_to_all(parts, both_axes, 0, 0, tiled=True)
        return jnp.sum(parts.astype(jnp.float32), axis=0).astype(jnp.bfloat16)

    def spread_out(share):
        copies = jnp.broadcast_to(share[None], (device_total, *share.shape))
        return lax.all_to_all(copies, both_axes, 0, 0, tiled=True)

    late = spread_out(summed_share(light_late)).reshape(light_late.shape).astype(jnp.float32)
    wide = ffn_in.shape[1]
    if heads_first:
        parts = lax.all_to_all(heavy, PAGES, 0, 0, tiled=True)
        share = run_gather(ids, parts, mixer_share, embed_share, early_share)
        whole = lax.all_gather(share, both_axes, axis=0)
        *heavy_sums, sum_ffn_out, sum_ffn_in, sum_output, sum_query, sum_key, sum_value, rest, early = (
            run_unpack(whole)
        )
        rest = rest.reshape(NB, 16, model_width)
        sum_roi = rest[:, :4].reshape(-1, model_width)
        sum_bias = rest[:, 4, : 3 * HEADS].reshape(NB, HEADS, 3)
        sum_gain_attn, sum_gain_ffn = rest[0, 5], rest[0, 6]
    else:
        early = spread_out(summed_share(light_early)).reshape(light_early.shape)
        early = early.astype(jnp.float32)
        heavy_sums = [lax.psum(member, both_axes).astype(jnp.float32) for member in heavy]
        mixer_all = lax.psum(mixer_table, both_axes).astype(jnp.float32)
        embed_all = lax.psum(embed_table, both_axes).astype(jnp.float32)
        sum_ffn_out = mixer_all[:wide]
        sum_ffn_in = beside(mixer_all[wide : 2 * wide], wide // model_width)
        sum_output = mixer_all[2 * wide :]
        sum_query, sum_key, sum_value = (
            embed_all[n * model_width : (n + 1) * model_width] for n in range(3)
        )
        last = 3 * model_width + roi_proj.shape[0]
        sum_roi = embed_all[3 * model_width : last]
        sum_bias = embed_all[last + 16 : last + 16 + NB, : 3 * HEADS].reshape(NB, HEADS, 3)
        sum_gain_attn, sum_gain_ffn = embed_all[last], embed_all[last + 1]
    sum_bias = sum_bias.transpose(1, 2, 0).reshape(bias_table.shape)

    def unlined(table, kind):
        return table.reshape(3, kind.shape[2], 3, kind.shape[3]).transpose(0, 2, 1, 3)

    second_rest = below(early[1344:1440], 2)
    sum_up_second = jnp.concatenate([early[1152:1344], second_rest], axis=1)
    sum_down_second = jnp.concatenate([late[384:480, :96], late[384:480, 128:224]], axis=0)
    sum_first = late[480:512, :72].reshape(32, 3, 3, 8)[..., :3].transpose(1, 2, 0, 3)
    summed = [
        sum_first,
        unlined(sum_down_second, down_second),
        unlined(late[:384, :192], down_third),
        heavy_sums[2].reshape(down_fourth.shape),
        heavy_sums[1].reshape(down_fifth.shape),
        heavy_sums[0].reshape(up_fourth.shape),
        early[:1152].reshape(up_third.shape),
        unlined(sum_up_second, up_second),
        unlined(early[1440:1536, :192], up_first),
        sum_roi,
        sum_gain_attn,
        sum_query,
        sum_key,
        sum_value,
        sum_output,
        sum_bias,
        sum_gain_ffn,
        sum_ffn_in,
        sum_ffn_out,
    ]
    return (
        result_low[None],
        d_residual[None],
        summed[0],
        summed[1],
        summed[2],
        summed[3],
        summed[4],
        summed[5],
        summed[6],
        summed[7],
        summed[8],
        summed[9],
        summed[10],
        summed[11],
        summed[12],
        summed[13],
        summed[14],
        summed[15],
        summed[16],
        summed[17],
        summed[18],
    )


def solution(mesh):
    tiles = mesh.shape["tile"]
    split = Mesh(mesh.devices.reshape(mesh.shape["dp"] // 2, 2, tiles), (*PAGES, "tile"))
    return jax.shard_map(
        on_device,
        mesh=split,
        in_specs=(
            P(PAGES, "tile", None),
            P(PAGES, None, "tile", None),
            P(None, PAGES, "tile"),
            P(PAGES, "tile"),
            P(),
            P(),
            P(),
            P(),
            P(),
            P(),
            P(),
            P(),
            P(),
            P(),
            P(),
            P(),
            P(),
            P(),
            P(),
            P(),
            P(),
            P(),
            P(),
            P(PAGES, "tile", None),
        ),
        out_specs=(
            P(PAGES, "tile", None),
            P(PAGES, "tile", None),
            P(),
            P(),
            P(),
            P(),
            P(),
            P(),
            P(),
            P(),
            P(),
            P(),
            P(),
            P(),
            P(),
            P(),
            P(),
            P(),
            P(),
            P(),
            P(),
        ),
        check_vma=False,
    )
```

```python
import functools
import math

import jax
import jax.numpy as jnp
from jax import lax
from jax.experimental import pallas as pl
from jax.experimental.pallas import tpu as pltpu
from jax.sharding import Mesh
from jax.sharding import PartitionSpec as P

HEADS = 8
HD = 64
NB = 32

eps = 1e-06
bounds = (12, 16, 23, 32, 46, 64, 91)
neg_large = -1000000000.0
HOPS = (("core", 1), ("x", 1), ("tile", 1), ("tile", 4), ("tile", 2))
PAGES = ("x", "core")
f32 = jnp.float32
bf16 = jnp.bfloat16
gelu_scale = math.sqrt(2.0 / math.pi)
VMEM_CAP = 28 * 1024 * 1024


def gelu_of(x):
    x = x.astype(f32)
    half = 0.5 * x
    inner = x * (gelu_scale + (gelu_scale * 0.044715) * (x * x))
    return half + half * jnp.tanh(inner)


def gelu_slope(x):
    x = x.astype(f32)
    sq = x * x
    bent = jnp.tanh(x * (gelu_scale + (gelu_scale * 0.044715) * sq))
    rise = gelu_scale + (3.0 * gelu_scale * 0.044715) * sq
    return 0.5 + 0.5 * bent + (0.5 * x) * (1.0 - bent * bent) * rise


def mm(a, b):
    return jnp.dot(a, b, preferred_element_type=f32)


def mm_tn(a, b):
    return lax.dot_general(a, b, (((0,), (0,)), ((), ())), preferred_element_type=f32)


def mm_nt(a, b):
    return lax.dot_general(a, b, (((1,), (1,)), ((), ())), preferred_element_type=f32)


def mm_fine(a, b):
    high = a.astype(bf16)
    low = (a - high.astype(f32)).astype(bf16)
    return mm(high, b) + mm(low, b)


def lane_ids(shape):
    return lax.broadcasted_iota(jnp.int32, shape, len(shape) - 1)


def row_ids_of(shape):
    return lax.broadcasted_iota(jnp.int32, shape, len(shape) - 2)


def halving(wide, value):
    hit = row_ids_of((wide, wide // 2)) >> 1 == lane_ids((wide, wide // 2))
    return jnp.where(hit, value, 0.0).astype(bf16)


def doubling(narrow):
    hit = row_ids_of((narrow, 2 * narrow)) == lane_ids((narrow, 2 * narrow)) >> 1
    return jnp.where(hit, 1.0, 0.0).astype(bf16)


def pair_halving(value):
    shape = (256, 128)
    source = row_ids_of(shape)
    target = lane_ids(shape)
    hit = source >> 1 == target
    return jnp.where(hit, value, 0.0).astype(bf16)


def side_doubling(side):
    shape = (128, 128)
    hit = row_ids_of(shape) == (lane_ids(shape) >> 1) + 64 * side
    return jnp.where(hit, 1.0, 0.0).astype(bf16)


def quad_map(coarse_lanes, coarse_width):
    shape = (coarse_lanes, 4 * coarse_lanes)
    fine = lane_ids((1, shape[1]))
    shift = coarse_width.bit_length() - 1
    home = (fine >> (shift + 2) << shift) + ((fine & (2 * coarse_width - 1)) >> 1)
    return jnp.where(row_ids_of(shape) == home, 1.0, 0.0).astype(bf16)


def masked(x, keep):
    return x * jnp.where(keep, 1.0, 0.0).astype(x.dtype)


def col_shift(x, step, width):
    if step == 0:
        return x
    lanes = x.shape[1]
    col = lane_ids((1, lanes)) & (width - 1)
    keep = col < width - 1 if step > 0 else col > 0
    return masked(pltpu.roll(x, -step % lanes, 1), keep)


def row_shift(x, step, width):
    if step == 0:
        return x
    lanes = x.shape[1]
    lane = lane_ids((1, lanes))
    keep = lane < lanes - width if step > 0 else lane >= width
    return masked(pltpu.roll(x, (-step * width) % lanes, 1), keep)


def stack_cols(x, width):
    return jnp.concatenate([col_shift(x, step, width) for step in (-1, 0, 1)], axis=0)


def row_ok(first_row, rows, width, low, high):
    row = (lane_ids((1, rows * width)) >> (width.bit_length() - 1)) + first_row
    return (row >= low) & (row < high)


def keep_rows(x, first_row, width, high):
    ok = row_ok(first_row, x.shape[1] // width, width, 0, high)
    return jnp.where(ok, x, 0.0)


def price(micros):
    return pl.CostEstimate(
        flops=int(micros * 5e8), transcendentals=0, bytes_accessed=int(micros * 2e6)
    )


class Fetched:
    def __init__(self, ref, copy):
        self.ref, self.copy, self.waited = ref, copy, False
        self.shape = ref.shape
        copy.start()

    def ready(self):
        if not self.waited:
            self.copy.wait()
            self.waited = True
        return self.ref

    def __getitem__(self, spot):
        return self.ready()[spot]


class Sent:
    def __init__(self, ref, copy):
        self.ref, self.copy, self.started = ref, copy, False
        self.shape = ref.shape

    def send(self):
        if not self.started:
            self.copy.start()
            self.started = True

    def __getitem__(self, spot):
        return self.ref[spot]

    def __setitem__(self, spot, value):
        self.ref[spot] = value


def in_hbm(array):
    return pltpu.with_memory_space_constraint(array, pltpu.HBM)


TOKEN = ((8, 128), f32)


def call(micros, body, outs, scratch, ids, arrays, after=(), late=(), sent=(), table=None):
    count = len(arrays)
    moved = [(arrays[n].shape, arrays[n].dtype) for n in late] + [outs[n] for n in sent]
    arrays = [in_hbm(array) if n in late else array for n, array in enumerate(arrays)]
    after = [in_hbm(token) for token in after]

    scalars = (ids,) if table is None else (ids, table)

    def ordered(*refs):
        refs, heads = refs[len(scalars) :], refs[: len(scalars)]
        ins = list(refs[:count])
        refs = refs[count + len(after) :]
        results = list(refs[: len(outs)])
        own = refs[len(outs) : len(outs) + len(scratch)]
        if moved:
            *stages, marks = refs[len(outs) + len(scratch) :]
        for k, n in enumerate(late):
            ins[n] = Fetched(stages[k], pltpu.make_async_copy(ins[n], stages[k], marks.at[k]))
        for k, n in enumerate(sent, len(late)):
            copy = pltpu.make_async_copy(stages[k], results[n], marks.at[k])
            results[n] = Sent(stages[k], copy)
        body(*heads, *ins, *results, *own)
        for n in late:
            ins[n].ready()
        for n in sent:
            results[n].send()
        for n in sent:
            results[n].copy.wait()

    def place(chosen, total):
        return [
            pl.BlockSpec(memory_space=pltpu.HBM if n in chosen else pltpu.VMEM) for n in range(total)
        ]

    return pl.pallas_call(
        ordered,
        cost_estimate=price(micros),
        out_shape=[
            pltpu.HBM(*out) if n in sent or out == TOKEN else jax.ShapeDtypeStruct(*out)
            for n, out in enumerate(outs)
        ],
        in_specs=[pl.BlockSpec(memory_space=pltpu.SMEM)] * len(scalars)
        + place(late, count)
        + [pl.BlockSpec(memory_space=pltpu.HBM) for _ in after],
        out_specs=place([n for n, out in enumerate(outs) if n in sent or out == TOKEN], len(outs)),
        scratch_shapes=[pltpu.VMEM(shape, kind) for shape, kind in scratch]
        + [pltpu.VMEM(shape, kind) for shape, kind in moved]
        + ([pltpu.SemaphoreType.DMA((len(moved),))] if moved else []),
        compiler_params=pltpu.CompilerParams(vmem_limit_bytes=VMEM_CAP),
    )(*scalars, *arrays, *after)


def lanes_at(start, size):
    return pl.ds(pl.multiple_of(start, 128), size)


def down_body(ids, pages, w_zero, w_one, w_two, pre_zero, pre_one, p_one, pre_two, p_two, p_three, page_own, page, cols, pool_one, stack_one, pool_two):
    tile, high, at = ids[0], ids[1], ids[4]
    page[...] = jnp.zeros_like(page)
    for side in range(-2, 3):
        block = at + side

        @pl.when((block >= 0) & (block < pages.shape[0]))
        def _(block=block, side=side):
            lines = pages[block, :, 0:1024].astype(f32)
            for g in range(8):
                first = (2 + side) * 8192 + 1024 * g
                for c in range(3):
                    page[c : c + 1, first : first + 1024] = lines[8 * c + g : 8 * c + g + 1, :]

    page_full = page[:, 11 * 512 : 69 * 512]
    page_own[...] = page_full[:, 20 * 512 : 38 * 512].astype(bf16)
    for j in range(3):
        cols[j] = col_shift(page_full, j - 1, 512)
    halve = halving(512, 0.25)

    def top(k, keep_pre):
        pieces = [
            cols[j, :, lanes_at((4 * k + i) * 512, 2048)] for i in range(3) for j in range(3)
        ]
        pre = mm(w_zero[...], jnp.concatenate(pieces, axis=0).astype(bf16))
        if keep_pre:
            pre_zero[:, lanes_at((k - 5) * 2048, 2048)] = pre.astype(bf16)
        enc = gelu_of(pre)
        pairs = jnp.concatenate(
            [enc[:, :512] + enc[:, 512:1024], enc[:, 1024:1536] + enc[:, 1536:]], axis=0
        )
        pooled = mm_fine(pairs, halve)
        first = tile * 8 - 10 + 2 * k
        for n in range(2):
            ok = (first + n >= 0) & (first + n < high // 2)
            part = jnp.where(ok, pooled[32 * n : 32 * n + 32], 0.0)
            pool_one[:, lanes_at((2 * k + n) * 256, 256)] = part.astype(bf16)

    for low, end, keep_pre in ((0, 5, False), (5, 9, True), (9, 14, False)):

        @pl.loop(low, end)
        def _(k, keep_pre=keep_pre):
            top(k, keep_pre)

    pre_zero.send()
    page_own.send()
    p_one[...] = pool_one[:, 9 * 256 : 19 * 256]
    p_one.send()
    stack_one[...] = stack_cols(pool_one[...], 256)
    halve_one = halving(256, 0.25)

    @pl.loop(0, 6)
    def _(k):
        pre = sum(
            mm(w_one[i], stack_one[:, lanes_at((4 * k + 1 + i) * 256, 1024)]) for i in range(3)
        )

        @pl.when((k >= 1) & (k < 5))
        def _():
            pre_one[:, lanes_at((k - 1) * 1024, 1024)] = pre.astype(bf16)

        enc = gelu_of(pre)
        pairs = jnp.concatenate(
            [enc[:, :256] + enc[:, 256:512], enc[:, 512:768] + enc[:, 768:]], axis=0
        )
        pooled = mm_fine(pairs, halve_one)
        first = tile * 4 - 4 + 2 * k
        for n in range(2):
            ok = (first + n >= 0) & (first + n < high // 4)
            part = jnp.where(ok, pooled[64 * n : 64 * n + 64], 0.0)
            pool_two[:, lanes_at((2 * k + n) * 128, 128)] = part.astype(bf16)

    pre_one.send()
    p_two[...] = pool_two[:, 3 * 128 : 9 * 128]
    p_two.send()
    stacked = stack_cols(pool_two[...], 128)
    pre = sum(mm(w_two[i], stacked[:, i * 128 : i * 128 + 1280]) for i in range(3))
    pre_two[...] = pre.astype(bf16)
    pre_two.send()
    enc = gelu_of(pre[:, 384:896])
    pairs = jnp.concatenate([enc[:, :128] + enc[:, 128:256], enc[:, 256:384] + enc[:, 384:]], axis=1)
    p_three[...] = mm_fine(pairs, pair_halving(0.25)).astype(bf16)


def run_down(ids, pages, w_zero, w_one, w_two):
    return call(
        10,
        down_body,
        [
            ((32, 16 * 512), bf16),
            ((64, 16 * 256), bf16),
            ((32, 10 * 256), bf16),
            ((128, 10 * 128), bf16),
            ((64, 6 * 128), bf16),
            ((128, 128), bf16),
            ((8, 18 * 512), bf16),
        ],
        [
            ((8, 80 * 512), f32),
            ((3, 8, 58 * 512), f32),
            ((32, 28 * 256), bf16),
            ((96, 28 * 256), bf16),
            ((64, 12 * 128), bf16),
        ],
        ids,
        (pages, w_zero, w_one, w_two),
        sent=(0, 1, 2, 3, 4, 6),
    )


def conv_taps(x, weight, width):
    total = None
    for i in range(3):
        lined = row_shift(x, i - 1, width)
        for j in range(3):
            term = mm(weight[i, j], col_shift(lined, j - 1, width))
            total = term if total is None else total + term
    return total


def conv_taps_back(x, weight, width):
    total = None
    for i in range(3):
        lined = row_shift(x, i - 1, width)
        for j in range(3):
            term = mm_tn(weight[2 - i, 2 - j], col_shift(lined, j - 1, width))
            total = term if total is None else total + term
    return total


def laid_out(blocks):
    return jnp.concatenate([blocks[n] for n in range(blocks.shape[0])], axis=1)


def bottom_body(cut, ids, p_three, w_three, w_four, w_up, pre_three, pre_four, p_four, e_four, pre_up, dec_three):
    lanes = 128 * p_three.shape[0]
    first, high = ids[3], ids[1]

    def kept(x, width, shrink):
        return keep_rows(x, first * (16 // shrink), width, high // shrink) if cut else x

    pre = conv_taps(laid_out(p_three), w_three, 64)
    pre_three[...] = pre.astype(bf16)
    pre_three.send()
    enc_three = kept(gelu_of(pre), 64, 8)
    spread = quad_map(lanes // 4, 32)
    high_part = enc_three.astype(bf16)
    low_part = (enc_three - high_part.astype(f32)).astype(bf16)
    pooled = ((mm_nt(high_part, spread) + mm_nt(low_part, spread)) * 0.25).astype(bf16)
    p_four[...] = pooled
    p_four.send()
    pre = conv_taps(pooled, w_four, 32)
    pre_four[...] = pre.astype(bf16)
    pre_four.send()
    low = kept(gelu_of(pre), 32, 16).astype(bf16)
    e_four[...] = low
    e_four.send()
    pre = conv_taps(mm(low, spread).astype(bf16), w_up, 64)
    pre_up[...] = pre.astype(bf16)
    pre_up.send()
    dec = kept(gelu_of(pre) + enc_three, 64, 8).astype(bf16)
    zero = jnp.zeros((256, 128), bf16)
    dec_three[:, 0:128] = zero
    dec_three[:, 128 : 128 + lanes] = dec
    dec_three[:, 128 + lanes :] = zero


def run_bottom(cut, ids, p_three, w_three, w_four, w_up):
    lanes = 128 * p_three.shape[0]
    return call(
        11,
        functools.partial(bottom_body, cut),
        [
            ((256, lanes), bf16),
            ((512, lanes // 4), bf16),
            ((256, lanes // 4), bf16),
            ((512, lanes // 4), bf16),
            ((256, lanes), bf16),
            ((256, lanes + 256), bf16),
        ],
        [],
        ids,
        (p_three, w_three, w_four, w_up),
        late=(2, 3),
        sent=(0, 1, 2, 3, 4),
    )


def widened(block):
    parts = []
    for n in range(block.shape[1] // 128):
        piece = block[:, 128 * n : 128 * n + 128]
        for side in range(2):
            line = mm(piece, side_doubling(side)).astype(bf16)
            parts += [line, line]
    return jnp.concatenate(parts, axis=1)


def spread_rows(source, target, width):
    spread = doubling(width)
    for n in range(source.shape[1] // width):
        line = mm(source[:, n * width : n * width + width], spread).astype(bf16)
        for m in range(2):
            target[:, (2 * n + m) * 2 * width : (2 * n + m + 1) * 2 * width] = line


def up_body(ids, dec_three, pre_two, pre_one, pre_zero, w_third, w_second, w_first, pre_up_two, pre_up_one, pre_up_zero, u_three, dec_two, dec_one, features, edge_end, edge_start, wide_two, stack_two, wide_one, stack_one):
    tile, high, place = ids[0], ids[1], ids[2]
    block = dec_three[:, lanes_at(place * 128, 384)]
    wide = widened(block)
    u_three[...] = wide[:, 384 : 384 + 768]
    u_three.send()
    total = None
    for j in range(3):
        moved = col_shift(wide, j - 1, 128)
        for i in range(3):
            term = mm(w_third[i, j], moved[:, i * 128 : i * 128 + 1280])
            total = term if total is None else total + term
    pre_up_two[...] = total.astype(bf16)
    pre_up_two.send()
    dec = gelu_of(total) + gelu_of(pre_two[...])
    dec = keep_rows(dec, tile * 4 - 3, 128, high // 4).astype(bf16)
    dec_two[...] = dec[:, 128 : 128 + 1024]
    dec_two.send()
    spread_rows(dec, wide_two, 128)
    stack_two[...] = stack_cols(wide_two[...], 256)
    for k in range(3):
        pre = sum(
            mm(w_second[i], stack_two[:, (6 * k + i) * 256 : (6 * k + i) * 256 + 1536])
            for i in range(3)
        )
        pre_up_one[:, 1536 * k : 1536 * k + 1536] = pre.astype(bf16)
    pre_up_one.send()
    dec = gelu_of(pre_up_one[:, 4 * 256 : 14 * 256]) + gelu_of(pre_one[:, 3 * 256 : 13 * 256])
    dec = keep_rows(dec, tile * 8 - 1, 256, high // 2).astype(bf16)
    dec_one[...] = dec
    dec_one.send()
    spread_rows(dec, wide_one, 256)
    stack_one[...] = stack_cols(wide_one[...], 512)
    pre_zero.ready()

    @pl.loop(0, 4)
    def _(k):
        pre = sum(
            mm(w_first[i], stack_one[:, lanes_at((4 * k + 1 + i) * 512, 2048)]) for i in range(3)
        )
        own = lanes_at(k * 2048, 2048)
        pre_up_zero[:, own] = pre.astype(bf16)
        found = (gelu_of(pre) + gelu_of(pre_zero[:, own])).astype(bf16)
        for n in range(4):
            features[pl.ds(pl.multiple_of((4 * k + n) * 32, 32), 32), :] = found[
                :, 512 * n : 512 * n + 512
            ]

    edge_end[...] = pre_up_zero[:, 5 * 512 : 16 * 512]
    edge_start[...] = pre_up_zero[:, 0 : 11 * 512]


def run_up(ids, dec_three, pre_two, pre_one, pre_zero, w_third, w_second, w_first):
    return call(
        9,
        up_body,
        [
            ((128, 10 * 128), bf16),
            ((64, 18 * 256), bf16),
            ((32, 16 * 512), bf16),
            ((256, 6 * 128), bf16),
            ((128, 8 * 128), bf16),
            ((64, 10 * 256), bf16),
            ((16 * 32, 512), bf16),
            ((32, 11 * 512), bf16),
            ((32, 11 * 512), bf16),
        ],
        [
            ((128, 20 * 256), bf16),
            ((384, 20 * 256), bf16),
            ((64, 20 * 512), bf16),
            ((192, 20 * 512), bf16),
        ],
        ids,
        (dec_three, pre_two, pre_one, pre_zero, w_third, w_second, w_first),
        late=(1, 2, 3),
        sent=(0, 1, 2, 3, 4, 5),
    )


def band_edges(boxes):
    left, top, right, bottom = (boxes[:, n : n + 1] for n in range(4))
    mid_col = (left + right) >> 1
    mid_row = (top + bottom) >> 1
    return ((left, mid_col, right), (top, mid_row, bottom))


def band_hits(edges, ids_wide, band):
    return (ids_wide >= edges[band]) & (ids_wide < edges[band + 1])


def area_inverse(cols, rows, a, b):
    return 1.0 / ((rows[a + 1] - rows[a]) * (cols[b + 1] - cols[b])).astype(f32)


def pool_body(step, ids, boxes, features, pooled):
    tile = ids[0]
    x_ids = lane_ids((1, 512))
    y_ids = (x_ids >> 5) + tile * 16
    group = lane_ids((1, 128)) >> 5

    @pl.loop(0, boxes.shape[0] // step)
    def _(k):
        own = pl.ds(pl.multiple_of(k * step, step), step)
        cols, rows = band_edges(boxes[own, :])
        result = jnp.zeros((step, 128), f32)
        inside = [jnp.where(band_hits(rows, y_ids, a), 1.0, 0.0) for a in range(2)]
        for b in range(2):
            hits = jnp.where(band_hits(cols, x_ids, b), 1.0, 0.0).astype(bf16)
            lines = mm_nt(hits, features[...])
            for a in range(2):
                part = lines * inside[a]
                part = part[:, :128] + part[:, 128:256] + (part[:, 256:384] + part[:, 384:])
                part = part + pltpu.roll(part, 64, 1)
                part = part + pltpu.roll(part, 32, 1)
                scaled = part * area_inverse(cols, rows, a, b)
                result = jnp.where(group == 2 * a + b, scaled, result)
        pooled[own, :] = result.astype(bf16)


def run_pool(ids, boxes, features, step):
    count = boxes.shape[0]
    return call(
        8, functools.partial(pool_body, step), [((count, 128), bf16)], [], ids, (boxes, features)
    )[0]


def unpool_body(step, ids, boxes, d_pooled, pre_before, pre_up, pre_behind, d_features, d_low, token, total):
    tile = ids[0]
    lines = 38
    x_ids = lane_ids((1, 512))
    y_ids = (lane_ids((1, lines * 32)) >> 5) + (tile * 16 - 11)
    group = lane_ids((1, 128)) >> 5
    source = row_ids_of((128, lines * 32))
    target = lane_ids((1, lines * 32)) & 31
    copies = [
        jnp.where(source == target + 32 * n, 1.0, 0.0).astype(bf16) for n in range(4)
    ]
    total[...] = jnp.zeros_like(total)

    @pl.loop(0, boxes.shape[0] // step)
    def _(k):
        own = pl.ds(pl.multiple_of(k * step, step), step)
        cols, rows = band_edges(boxes[own, :])
        scale = jnp.zeros((step, 128), f32)
        for a in range(2):
            for b in range(2):
                scale = jnp.where(group == 2 * a + b, area_inverse(cols, rows, a, b), scale)
        share = (d_pooled[own, :].astype(f32) * scale).astype(bf16)
        found = None
        inside = [jnp.where(band_hits(rows, y_ids, a), 1.0, 0.0) for a in range(2)]
        for b in range(2):
            placed = mm(share, copies[b]) * inside[0] + mm(share, copies[2 + b]) * inside[1]
            hits = jnp.where(band_hits(cols, x_ids, b), 1.0, 0.0).astype(bf16)
            term = mm_tn(placed.astype(bf16), hits)
            found = term if found is None else found + term
        total[...] += found

    for y in range(lines):
        line = total[32 * y : 32 * y + 32, :]
        if y < 11:
            pre = pre_before[:, 512 * y : 512 * y + 512]
        elif y < 27:
            own = slice(512 * (y - 11), 512 * (y - 10))
            d_features[:, own] = line
            pre = pre_up[:, own]
        else:
            pre = pre_behind[:, 512 * (y - 27) : 512 * (y - 26)]
        d_low[:, 512 * y : 512 * y + 512] = (line * gelu_slope(pre)).astype(bf16)


def run_unpool(ids, after, boxes, d_pooled, pre_before, pre_up, pre_behind, step):
    return call(
        14,
        functools.partial(unpool_body, step),
        [((32, 8192), f32), ((32, 38 * 512), bf16), TOKEN],
        [((38 * 32, 512), f32)],
        ids,
        (boxes, d_pooled, pre_before, pre_up, pre_behind),
        after,
        late=(2, 3, 4),
        sent=(0,),
    )


def up_back_body(ids, d_low, pre_up_one, pre_up_two, wd_first, wd_second, w_third, d_dec_one, d_dec_two, d_dec_three, low_one, low_two, token, stack_zero, wide_low):
    tile, high = ids[0], ids[1]
    stack_zero[...] = stack_cols(d_low[...], 512)
    halve = halving(512, 1.0)
    pre_up_one.ready()

    @pl.loop(0, 9)
    def _(k):
        back = sum(
            mm(wd_first[i], stack_zero[:, lanes_at((4 * k + i) * 512, 2048)]) for i in range(3)
        )
        pairs = jnp.concatenate(
            [back[:, :512] + back[:, 512:1024], back[:, 1024:1536] + back[:, 1536:]], axis=0
        )
        summed = mm_fine(pairs, halve)
        first = tile * 8 - 5 + 2 * k
        for n in range(2):
            ok = (first + n >= 0) & (first + n < high // 2)
            own = lanes_at((2 * k + n) * 256, 256)
            part = jnp.where(ok, summed[64 * n : 64 * n + 64], 0.0)
            d_dec_one[:, own] = part
            wide_low[:, own] = (part * gelu_slope(pre_up_one[:, own])).astype(bf16)

    d_dec_one.send()
    low_one[...] = wide_low[:, 5 * 256 : 13 * 256]
    low_one.send()
    stacked = stack_cols(wide_low[...], 256)
    halve_one = halving(256, 1.0)
    for k in range(4):
        back = sum(
            mm(wd_second[i], stacked[:, (4 * k + i) * 256 : (4 * k + i) * 256 + 1024])
            for i in range(3)
        )
        pairs = jnp.concatenate(
            [back[:, :256] + back[:, 256:512], back[:, 512:768] + back[:, 768:]], axis=0
        )
        summed = mm_fine(pairs, halve_one)
        for n in range(2):
            line = 2 * k + n
            row = tile * 4 - 2 + line
            ok = (row >= 0) & (row < high // 4)
            part = jnp.where(ok, summed[128 * n : 128 * n + 128], 0.0)
            d_dec_two[:, 128 * line : 128 * line + 128] = part
    low = d_dec_two[:, 128 : 7 * 128] * gelu_slope(pre_up_two[:, 2 * 128 : 8 * 128])
    low = low.astype(bf16)
    d_dec_two.send()
    low_two[...] = low[:, 128 : 5 * 128]
    low_two.send()
    total = None
    for j in range(3):
        moved = col_shift(low, j - 1, 128)
        for i in range(3):
            term = mm_tn(w_third[2 - i, 2 - j], moved[:, i * 128 : i * 128 + 512])
            total = term if total is None else total + term
    pairs = jnp.concatenate(
        [total[:, :128] + total[:, 128:256], total[:, 256:384] + total[:, 384:]], axis=1
    )
    d_dec_three[...] = mm_fine(pairs, pair_halving(1.0)).astype(bf16)


def run_up_back(ids, after, d_low, pre_up_one, pre_up_two, wd_first, wd_second, w_third):
    return call(
        9,
        up_back_body,
        [
            ((64, 18 * 256), f32),
            ((128, 8 * 128), f32),
            ((256, 128), bf16),
            ((64, 8 * 256), bf16),
            ((128, 4 * 128), bf16),
            TOKEN,
        ],
        [((96, 38 * 512), bf16), ((64, 18 * 256), bf16)],
        ids,
        (d_low, pre_up_one, pre_up_two, wd_first, wd_second, w_third),
        after,
        late=(1, 2),
        sent=(0, 1, 3, 4),
    )


def bottom_back_body(cut, ids, d_dec_three, pre_up, pre_four, pre_three, w_up, w_four, w_three, low_up, low_four, low_three, d_pool, token, padded):
    lanes = 128 * d_dec_three.shape[0]
    first, high, place = ids[3], ids[1], ids[2]

    def kept(x, width, shrink):
        return keep_rows(x, first * (16 // shrink), width, high // shrink) if cut else x

    d_dec = laid_out(d_dec_three).astype(f32)
    low = (d_dec * gelu_slope(pre_up[...])).astype(bf16)
    low_up[...] = low
    spread = quad_map(lanes // 4, 32)
    back = conv_taps_back(low, w_up, 64)
    high_part = back.astype(bf16)
    low_part = (back - high_part.astype(f32)).astype(bf16)
    d_enc = kept(mm_nt(high_part, spread) + mm_nt(low_part, spread), 32, 16)
    low = (d_enc * gelu_slope(pre_four[...])).astype(bf16)
    low_four[...] = low
    back = conv_taps_back(low, w_four, 32) * 0.25
    d_enc = kept(d_dec + mm_fine(back, spread), 64, 8)
    low = (d_enc * gelu_slope(pre_three[...])).astype(bf16)
    low_three[...] = low
    zero = jnp.zeros((256, 128), bf16)
    padded[:, 0:128] = zero
    padded[:, 128 : 128 + lanes] = low
    padded[:, 128 + lanes :] = zero
    window = padded[:, lanes_at(place * 128, 384)]
    d_pool[...] = conv_taps_back(window, w_three, 64)[:, 0:384]


def run_bottom_back(cut, ids, after, d_dec_three, pre_up, pre_four, pre_three, w_up, w_four, w_three):
    lanes = 128 * d_dec_three.shape[0]
    return call(
        10,
        functools.partial(bottom_back_body, cut),
        [
            ((256, lanes), bf16),
            ((512, lanes // 4), bf16),
            ((256, lanes), bf16),
            ((128, 384), f32),
            TOKEN,
        ],
        [((256, lanes + 256), bf16)],
        ids,
        (d_dec_three, pre_up, pre_four, pre_three, w_up, w_four, w_three),
        after,
        late=(1, 4, 2, 5, 3, 6),
        sent=(3,),
    )


def down_back_body(ids, d_pool_three, d_dec_two, pre_two, d_dec_one, pre_one, d_features, pre_zero, w_two, wd_one, low_two, low_one, low_zero, wide_one):
    tile, high = ids[0], ids[1]
    d_dec_one.ready()
    pre_one.ready()
    d_features.ready()
    pre_zero.ready()
    quarter = d_pool_three[...] * 0.25
    parts = []
    for n in range(3):
        piece = quarter[:, 128 * n : 128 * n + 128]
        for side in range(2):
            line = mm_fine(piece, side_doubling(side))
            parts += [line, line]
    spread = jnp.concatenate(parts[2:10], axis=1)
    d_enc = keep_rows(d_dec_two[...] + spread, tile * 4 - 2, 128, high // 4)
    low = (d_enc * gelu_slope(pre_two[:, 128 : 9 * 128])).astype(bf16)
    low_two[...] = low[:, 2 * 128 : 6 * 128]
    total = None
    for j in range(3):
        moved = col_shift(low, j - 1, 128)
        for i in range(3):
            term = mm_tn(w_two[2 - i, 2 - j], moved[:, i * 128 : i * 128 + 768])
            total = term if total is None else total + term
    total = total * 0.25
    wide = doubling(128)
    for n in range(6):
        line = mm_fine(total[:, 128 * n : 128 * n + 128], wide)
        for m in range(2):
            row = 2 * n + m
            value = d_dec_one[:, (3 + row) * 256 : (4 + row) * 256] + line
            ok = (tile * 8 - 2 + row >= 0) & (tile * 8 - 2 + row < high // 2)
            value = jnp.where(ok, value, 0.0)
            slope = gelu_slope(pre_one[:, (2 + row) * 256 : (3 + row) * 256])
            wide_one[:, row * 256 : row * 256 + 256] = (value * slope).astype(bf16)
    low_one[...] = wide_one[:, 2 * 256 : 10 * 256]
    stacked = stack_cols(wide_one[...], 256)
    back = sum(mm(wd_one[i], stacked[:, (1 + i) * 256 : (9 + i) * 256]) for i in range(3)) * 0.25
    wider = doubling(256)
    for n in range(8):
        line = mm_fine(back[:, 256 * n : 256 * n + 256], wider)
        for m in range(2):
            own = slice((2 * n + m) * 512, (2 * n + m + 1) * 512)
            value = (d_features[:, own] + line) * gelu_slope(pre_zero[:, own])
            low_zero[:, own] = value.astype(bf16)


def run_down_back(ids, after, *arrays):
    return call(
        4,
        down_back_body,
        [
            ((128, 4 * 128), bf16),
            ((64, 8 * 256), bf16),
            ((32, 16 * 512), bf16),
        ],
        [((64, 12 * 256), bf16)],
        ids,
        arrays,
        after,
        late=(0, 1, 2, 3, 4, 5, 6),
    )


def grad_up_first_body(ids, dec_one, d_low, grad, wide_one, stack_one):
    spread_rows(dec_one[...], wide_one, 256)
    stack_one[...] = stack_cols(wide_one[...], 512)
    for i in range(3):
        grad[i] = mm_nt(d_low[:, 11 * 512 : 27 * 512], stack_one[:, (1 + i) * 512 : (17 + i) * 512])


def run_grad_up_first(ids, after, dec_one, d_low):
    return call(
        4,
        grad_up_first_body,
        [((3, 32, 192), f32)],
        [((64, 20 * 512), bf16), ((192, 20 * 512), bf16)],
        ids,
        (dec_one, d_low),
        after,
        late=(0,),
    )[0]


def grad_up_body(ids, grad_first, dec_two, low_one, u_three, low_two, table, token, wide_two, stack_two):
    spread_rows(dec_two[...], wide_two, 128)
    stack_two[...] = stack_cols(wide_two[...], 256)
    for j in range(3):
        moved = col_shift(u_three[...], j - 1, 128)
        for i in range(3):
            first = (3 * i + j) * 128
            grad = mm_nt(low_two[...], moved[:, i * 128 : i * 128 + 512])
            table[first : first + 128, :] = grad.astype(bf16)
    rest = []
    for i in range(3):
        grad = mm_nt(low_one[...], stack_two[:, (3 + i) * 256 : (11 + i) * 256]).astype(bf16)
        table[1152 + 64 * i : 1216 + 64 * i, :] = grad[:, :256]
        rest.append(grad[:, 256:])
    rest = jnp.concatenate(rest, axis=0)
    table[1344:1440, :] = jnp.concatenate([rest[:96], rest[96:]], axis=1)
    table[1440:1536, :] = jnp.zeros((96, 256), bf16)
    for i in range(3):
        table[1440 + 32 * i : 1472 + 32 * i, 0:192] = grad_first[i].astype(bf16)


def run_grad_up(ids, after, *arrays):
    return call(
        4,
        grad_up_body,
        [((1536, 256), bf16), TOKEN],
        [((128, 16 * 256), bf16), ((384, 16 * 256), bf16)],
        ids,
        arrays,
        after,
        late=(1, 2, 3, 4),
    )


def halve_body(ids, kept, got, mine, other, token):
    half = mine.shape[0]
    for bit in range(2):

        @pl.when(ids[5] == bit)
        def _(bit=bit):
            for out, side in ((mine, bit), (other, 1 - bit)):
                own = slice(half * side, half * side + half)
                out[...] = (kept[own, :].astype(f32) + got[own, :].astype(f32)).astype(bf16)


def run_halve(ids, bit, kept, got, after):
    rows, width = kept.shape
    return call(
        max(1, rows // 1500),
        halve_body,
        [((rows // 2, width), bf16)] * 2 + [TOKEN],
        [],
        ids.at[5].set(bit),
        (kept, got),
        after,
    )


def finish_body(ids, kept, got, share):
    share[...] = (kept[...].astype(f32) + got[...].astype(f32)).astype(bf16)


def total_body(ids, parts, share, token):
    total = parts[0].astype(f32)
    for n in range(1, parts.shape[0]):
        total = total + parts[n].astype(f32)
    half = total.shape[0] // 2
    share[...] = jnp.concatenate([total[:half], total[half:]], axis=1).astype(bf16)


def run_total(ids, parts):
    rows, width = parts.shape[1:]
    outs = [((rows // 2, 2 * width), bf16), TOKEN]
    return call(1, total_body, outs, [], ids, (parts,))


def gather_body(ids, heavy, mixer, embed, early, share):
    rows, width = heavy.shape[1:]
    total = heavy[0].astype(f32)
    for n in range(1, heavy.shape[0]):
        total = total + heavy[n].astype(f32)
    share[0:rows, :] = total.astype(bf16)
    share[rows : rows + 144, :] = mixer[...]
    share[rows + 144 : rows + 208, :] = embed[...]
    pad = jnp.zeros((8, width), f32)
    share[rows + 208 :, :] = jnp.concatenate([early[...].astype(f32), pad], axis=0).astype(bf16)


def run_gather(ids, *arrays):
    rows, width = arrays[0].shape[1:]
    return call(1, gather_body, [((rows + 240, width), bf16)], [], ids, arrays)[0]


def run_finish(ids, kept, got, after):
    return call(1, finish_body, [(kept.shape, bf16)], [], ids, (kept, got), after)[0]


def taps_of(x, width):
    for i in range(3):
        lined = row_shift(x, i - 1, width)
        for j in range(3):
            yield 3 * i + j, col_shift(lined, j - 1, width)


def grad_bottom_body(split, ids, low_up, e_four, low_four, p_four, low_three, p_three, table, token, up_part, four_part, three_part):
    place = ids[2]
    lanes = low_up.shape[1]
    spread = quad_map(lanes // 4, 32)
    shares = table.shape[0]

    def own_part(low):
        rows = low.shape[0] // split
        return low[pl.ds(pl.multiple_of(place * rows, rows), rows), :]

    low = own_part(low_up)
    for tap, x in taps_of(mm(e_four[...], spread).astype(bf16), 64):
        up_part[tap] = mm_nt(low, x)
    low = own_part(low_four)
    for tap, x in taps_of(p_four[...], 32):
        four_part[tap] = mm_nt(low, x)
    low = own_part(low_three)
    for tap, x in taps_of(laid_out(p_three), 64):
        three_part[tap] = mm_nt(low, x)
    for n in range(shares):
        for tap in range(9):
            fifth = jnp.concatenate(
                [
                    four_part[tap, 16 * n : 16 * n + 8, :],
                    four_part[tap, 16 * n + 8 : 16 * n + 16, :],
                ],
                axis=1,
            )
            main = jnp.concatenate([up_part[tap, 8 * n : 8 * n + 8, :], fifth], axis=0)
            table[n, 16 * tap : 16 * tap + 16, :] = main.astype(bf16)
        zero = jnp.zeros((8, 128), f32)
        sides = [three_part[tap, 8 * n : 8 * n + 8, :] for tap in range(9)] + [zero] * 7
        sides = [jnp.concatenate(sides[4 * k : 4 * k + 4], axis=1) for k in range(4)]
        table[n, 144:176, :] = jnp.concatenate(sides, axis=0).astype(bf16)


def run_grad_bottom(split, shares, ids, after, *arrays):
    return call(
        6,
        functools.partial(grad_bottom_body, split),
        [((shares, 176, 512), bf16), TOKEN],
        [
            ((9, 256 // split, 512), f32),
            ((9, 512 // split, 256), f32),
            ((9, 256 // split, 128), f32),
        ],
        ids,
        arrays,
        after,
        late=(1, 3),
    )


def unpack_body(whole, *refs):
    stage, marks = refs[-2:]
    plain = list(refs[:-2])
    step = pl.program_id(0)
    last = pl.num_programs(0) - 1

    def fetch(n):
        return pltpu.make_async_copy(whole.at[n], stage.at[n % 4], marks.at[n % 4])

    @pl.when(step == 0)
    def _():
        for n in range(3):
            fetch(n).start()

    @pl.when(step + 3 <= last)
    def _():
        fetch(step + 3).start()

    fetch(step).wait()
    held = stage.at[step % 4]
    up, fifth, fourth, *plain, early = plain
    for tap in range(9):
        block = held[16 * tap : 16 * tap + 16, :].astype(f32)
        up[tap] = block[0:8, :]
        fifth[tap, 0:8, :] = block[8:16, 0:256]
        fifth[tap, 8:16, :] = block[8:16, 256:512]
    sides = held[144:176, :].astype(f32)
    for tap in range(9):
        rows = slice(8 * (tap // 4), 8 * (tap // 4) + 8)
        fourth[tap] = sides[rows, 128 * (tap % 4) : 128 * (tap % 4) + 128]
    first = 176
    for out in plain:
        rows = out.shape[0]
        out[...] = held[first : first + rows, :].astype(f32)
        first = first + rows
    block = held[first : first + 32, :].astype(f32)
    early[0:24, :] = block[0:24, 0:256]
    early[24:48, :] = block[0:24, 256:512]


def run_unpack(whole):
    tiles = whole.shape[0] // 4

    def by_page(n):
        return (0, n % tiles * 4 + n // tiles, 0)

    def by_chunk(n):
        tile, page = n % tiles, n // tiles
        return (page % 2 * 16 + page // 2 * 8 + tile % 2 * 4 + tile // 4 * 2 + tile // 2 % 2, 0)

    def plain(n):
        return (n, 0)

    def by_column(n):
        return (n % 8, n // 8)

    def out(shape, block, spot):
        return jax.ShapeDtypeStruct(shape, f32), pl.BlockSpec(block, spot)

    outs = [
        out((9, 256, 512), (9, 8, 512), by_page),
        out((9, 512, 256), (9, 16, 256), by_page),
        out((9, 256, 128), (9, 8, 128), by_page),
        out((2048, 512), (64, 512), plain),
        out((512, 2048), (64, 512), by_column),
        out((512, 512), (16, 512), plain),
        out((512, 512), (16, 512), by_chunk),
        out((512, 512), (16, 512), by_chunk),
        out((512, 512), (16, 512), by_chunk),
        out((512, 512), (16, 512), by_chunk),
        out((1536, 256), (48, 256), plain),
    ]
    return pl.pallas_call(
        unpack_body,
        cost_estimate=price(14),
        grid=(whole.shape[0],),
        out_shape=[shape for shape, _ in outs],
        in_specs=[pl.BlockSpec(memory_space=pltpu.HBM)],
        out_specs=[spec for _, spec in outs],
        scratch_shapes=[
            pltpu.VMEM((4, *whole.shape[1:]), bf16),
            pltpu.SemaphoreType.DMA((4,)),
        ],
        compiler_params=pltpu.CompilerParams(vmem_limit_bytes=VMEM_CAP),
    )(in_hbm(whole))


def grad_bottom_all_body(ids, low_up, e_four, low_four, p_four, low_three, p_three, grad_up, grad_four, grad_three):
    lanes = low_up.shape[1]
    spread = quad_map(lanes // 4, 32)

    def own_part(low):
        size = low.shape[1] // (lanes // 128)
        own = lane_ids(low.shape) // size == ids[2]
        return jnp.where(own, low[...], jnp.zeros((), bf16))

    low = own_part(low_up)
    for tap, x in taps_of(mm(e_four[...], spread).astype(bf16), 64):
        grad_up[tap] = mm_nt(low, x).astype(bf16)
    low = own_part(low_four)
    for tap, x in taps_of(p_four[...], 32):
        grad_four[tap] = mm_nt(low, x).astype(bf16)
    low = own_part(low_three)
    for tap, x in taps_of(laid_out(p_three), 64):
        grad_three[tap] = mm_nt(low, x).astype(bf16)


def run_grad_bottom_all(ids, *arrays):
    return call(
        6,
        grad_bottom_all_body,
        [((9, 256, 512), bf16), ((9, 512, 256), bf16), ((9, 256, 128), bf16)],
        [],
        ids,
        arrays,
    )


def grad_down_body(ids, p_two, low_two, p_one, low_one, page, low_zero, table, cols):
    stacked = stack_cols(p_two[...], 128)
    for i in range(3):
        grad = mm_nt(low_two[...], stacked[:, i * 128 : i * 128 + 512]).astype(bf16)
        table[128 * i : 128 * i + 128, 0:192] = grad
    table[0:384, 192:256] = jnp.zeros((384, 64), bf16)
    table[384:512, :] = jnp.zeros((128, 256), bf16)
    stacked = stack_cols(p_one[...], 256)
    parts = [
        mm_nt(low_one[...], stacked[:, i * 256 : i * 256 + 2048]).astype(bf16) for i in range(3)
    ]
    grad = jnp.concatenate(parts, axis=0)
    table[384:480, 0:96] = grad[:96]
    table[384:480, 128:224] = grad[96:]
    rows = page[...].astype(f32)
    for j in range(3):
        cols[j] = col_shift(rows, j - 1, 512)
    pieces = [cols[j, :, i * 512 : i * 512 + 8192] for i in range(3) for j in range(3)]
    grad = mm_nt(low_zero[...], jnp.concatenate(pieces, axis=0).astype(bf16))
    table[480:512, 0:72] = grad.astype(bf16)


def run_grad_down(ids, *arrays):
    return call(
        3,
        grad_down_body,
        [((512, 256), bf16)],
        [((3, 8, 18 * 512), f32)],
        ids,
        arrays,
        late=(0, 2, 4),
    )[0]


def bucket_of(signed_gap):
    distance = jnp.abs(signed_gap)
    far_steps = jnp.zeros_like(distance)
    for threshold in bounds:
        far_steps = far_steps + (distance >= threshold).astype(jnp.int32)
    nearness = jnp.where(distance < 8, distance, 8 + far_steps)
    return nearness + jnp.where(signed_gap > 0, 16, 0).astype(jnp.int32)


def rms_scale(value, gain):
    return value * lax.rsqrt(jnp.mean(value * value, axis=-1, keepdims=True) + eps) * gain


def gelu_back(pre_act, upstream):
    return jax.vjp(jax.nn.gelu, pre_act)[1](upstream)[0]


def block_scores(query_heads, key_heads, query_meta, key_meta, bias_table, score_scale):
    query_pos, query_cx, query_cy, query_seg = query_meta
    key_pos, key_cx, key_cy, key_seg = key_meta
    rel_bucket = bucket_of(key_pos[None, :] - query_pos[:, None])
    hor_bucket = bucket_of(key_cx[None, :] - query_cx[:, None]) + NB
    ver_bucket = bucket_of(key_cy[None, :] - query_cy[:, None]) + 2 * NB
    slot_ids = jnp.arange(3 * NB)
    one_hot = (
        (rel_bucket[..., None] == slot_ids)
        | (hor_bucket[..., None] == slot_ids)
        | (ver_bucket[..., None] == slot_ids)
    ).astype(jnp.bfloat16)
    scores = (
        jnp.einsum("hqd,hkd->hqk", query_heads, key_heads, preferred_element_type=jnp.float32)
        * score_scale
    )
    scores = scores + jnp.einsum(
        "qkn,hn->hqk", one_hot, bias_table, preferred_element_type=jnp.float32
    )
    allowed = query_seg[:, None] == key_seg[None, :]
    return (scores, allowed, one_hot)


def norm_parts(value):
    scale = lax.rsqrt(jnp.mean(value * value, axis=-1, keepdims=True) + eps)
    return scale


def norm_back(value, gain, upstream):
    scale = norm_parts(value)
    weighted = upstream * gain
    inner = jnp.mean(weighted * value, axis=-1, keepdims=True)
    d_value = weighted * scale - value * (inner * scale * scale * scale)
    d_gain = jnp.sum(upstream * value * scale, axis=0, keepdims=True)
    return d_value, d_gain


def embed_body(ids, pieces, emb, roi, gain, wq, wk, wv, residual, normed, pooled, shared):
    total = pieces[0].astype(f32)
    for n in range(1, pieces.shape[0]):
        total = total + pieces[n].astype(f32)
    low = total.astype(bf16)
    pooled[...] = low
    pooled.send()
    resid = emb[...].astype(f32) + mm(low, roi[...])
    residual[...] = resid
    residual.send()
    normal = (resid * norm_parts(resid) * gain[...].astype(f32)).astype(bf16)
    normed[...] = normal
    normed.send()
    for n, weight in enumerate((wq, wk, wv)):
        turned = mm(normal, weight[...]).T.astype(bf16)
        for h in range(HEADS):
            shared[h, HD * n : HD * n + HD, :] = turned[HD * h : HD * h + HD, :]


def run_embed(ids, pieces, emb, *arrays):
    rows, width = emb.shape
    return call(
        2,
        embed_body,
        [
            ((rows, width), f32),
            ((rows, width), bf16),
            ((rows, pieces.shape[2]), bf16),
            ((HEADS, 3 * HD, rows), bf16),
        ],
        [],
        ids,
        (pieces, emb, *arrays),
        sent=(0, 1, 2),
    )


def looked_up(bucket, table, head, first):
    value = jnp.zeros(bucket.shape, f32)
    for n in range(NB):
        value = jnp.where(bucket == n, table[head, first + n], value)
    return value


def toeplitz(span, table, head, first):
    lane = lane_ids((1, 2 * span))
    gap = jnp.where(lane < span, -lane, 2 * span - lane)
    line = looked_up(bucket_of(gap), table, head, first)
    square = jnp.broadcast_to(line, (span, 2 * span))
    return pltpu.roll(square, 0, 1, stride=1, stride_axis=0)[:, :span].astype(bf16)


def centers(meta):
    return ((meta[0:1, :] + meta[2:3, :]) >> 1, (meta[1:2, :] + meta[3:4, :]) >> 1)


def one_hot_rows(value, span, turned):
    row = row_ids_of((span, value.shape[1]))
    if turned:
        row = span - 1 - row
    return jnp.where(row == value, 1.0, 0.0).astype(bf16)


def attend_body(tall, ids, table, meta, meta_cols, shared, prob, out_low, out_full, hits, spread, near):
    head = ids[0]
    seq = meta.shape[1]
    count = shared.shape[0]
    spans = (512, tall)
    for n, (value, span) in enumerate(zip(centers(meta), spans)):
        chart = toeplitz(span, table, head, NB * (n + 1))
        low = sum(spans[:n])
        spread[low : low + span, :] = mm(chart, one_hot_rows(value, span, False)).astype(bf16)
    cols = meta_cols[...]
    for n, span in enumerate(spans):
        value = (cols[:, n : n + 1] + cols[:, n + 2 : n + 3]) >> 1
        low = sum(spans[:n])
        same = lane_ids((1, span)) == value
        hits[:, low : low + span] = jnp.where(same, 1.0, 0.0).astype(bf16)
    edge = seq - 128
    near[0 : edge - 128, :] = jnp.full((edge - 128, 128), table[head, NB // 2 - 1], f32)
    near[edge + 256 :, :] = jnp.full((seq - 256, 128), table[head, NB - 1], f32)
    gap = row_ids_of((384, 128)) - 128 - lane_ids((384, 128))
    near[edge - 128 : edge + 256, :] = looked_up(bucket_of(gap), table, head, 0)
    query = jnp.concatenate([shared[n, 0:HD, :] for n in range(count)], axis=1)
    key = jnp.concatenate([shared[n, HD : 2 * HD, :] for n in range(count)], axis=1)
    value = jnp.concatenate([shared[n, 2 * HD :, :] for n in range(count)], axis=1)
    key = (key.astype(f32) * (HD**-0.5)).astype(bf16)
    seg_key = cols[:, 4:5]
    for block in range(seq // 256):
        own = slice(256 * block, 256 * block + 256)
        first = edge - 256 * block
        scores = mm_tn(key, query[:, own]) + mm(hits[...], spread[:, own])
        scores = scores + jnp.concatenate(
            [near[first : first + seq, :], near[first - 128 : first - 128 + seq, :]], axis=1
        )
        scores = jnp.where(seg_key == meta[4:5, own], scores, neg_large)
        weight = jnp.exp(scores - jnp.max(scores, axis=0, keepdims=True))
        weight = weight * (1.0 / jnp.sum(weight, axis=0, keepdims=True))
        low = weight.astype(bf16)
        prob[block] = low
        found = mm(value, low)
        out_full[:, own] = found
        for n in range(2):
            out_low[2 * block + n] = found[:, 128 * n : 128 * n + 128].astype(bf16)


def run_attend(tall, ids, table, meta, meta_cols, shared):
    seq = meta.shape[1]
    count = shared.shape[0]
    return call(
        9,
        functools.partial(attend_body, tall),
        [
            ((seq // 256, seq, 256), bf16),
            ((count, HD, seq // count), bf16),
            ((HD, seq), f32),
        ],
        [
            ((seq, 512 + tall), bf16),
            ((512 + tall, seq), bf16),
            ((2 * seq - 128, 128), f32),
        ],
        ids,
        (meta, meta_cols, shared),
        sent=(0, 2),
        table=table,
    )


def bucket_sums(value, bucket):
    lines = [
        jnp.sum(jnp.where(bucket == n, value, 0.0), axis=0, keepdims=True) for n in range(NB)
    ]
    return jnp.sum(jnp.concatenate(lines, axis=0), axis=1, keepdims=True)


def attend_back_body(tall, ids, meta, shared, prob, out_full, d_out, d_shared, d_table, near, drift, key_sum, value_sum):
    seq = meta.shape[1]
    count = shared.shape[0]
    spans = (512, tall)
    query = jnp.concatenate([shared[n, 0:HD, :] for n in range(count)], axis=1)
    key = jnp.concatenate([shared[n, HD : 2 * HD, :] for n in range(count)], axis=1)
    value = jnp.concatenate([shared[n, 2 * HD :, :] for n in range(count)], axis=1)
    d_found = jnp.concatenate([d_out[n] for n in range(count)], axis=1)
    delta = jnp.sum(d_found.astype(f32) * out_full[...], axis=0, keepdims=True)
    near[...] = jnp.zeros_like(near)
    key_sum[...] = jnp.zeros_like(key_sum)
    value_sum[...] = jnp.zeros_like(value_sum)
    places = centers(meta)
    turned = jnp.concatenate(
        [one_hot_rows(place, span, True) for place, span in zip(places, spans)], axis=0
    )
    edge = seq - 128
    scale = HD**-0.5
    for block in range(seq // 256):
        own = slice(256 * block, 256 * block + 256)
        first = edge - 256 * block
        low = prob[block]
        d_prob = mm_tn(value, d_found[:, own])
        d_score = low.astype(f32) * (d_prob - delta[:, own])
        near[first : first + seq, :] += d_score[:, :128]
        near[first - 128 : first - 128 + seq, :] += d_score[:, 128:]
        d_low = d_score.astype(bf16)
        d_query = (mm(key, d_low) * scale).astype(bf16)
        for n in range(2):
            d_shared[2 * block + n, 0:HD, :] = d_query[:, 128 * n : 128 * n + 128]
        key_sum[...] += mm_nt(query[:, own], d_low)
        value_sum[...] += mm_nt(d_found[:, own], low)
        drift[:, own] = mm(turned, d_low).astype(bf16)
    d_key = (key_sum[...] * scale).astype(bf16)
    d_value = value_sum[...].astype(bf16)
    for n in range(count):
        d_shared[n, HD : 2 * HD, :] = d_key[:, 128 * n : 128 * n + 128]
        d_shared[n, 2 * HD :, :] = d_value[:, 128 * n : 128 * n + 128]
    sums = []
    slot = 3 * ids[0]
    gap = row_ids_of((384, 128)) - 128 - lane_ids((384, 128))
    sums.append(bucket_sums(near[edge - 128 : edge + 256, :], bucket_of(gap)))
    row = row_ids_of((NB, 128))
    lane = lane_ids((NB, 128))
    behind = jnp.sum(near[0 : edge - 128, :], axis=0, keepdims=True)
    ahead = jnp.sum(near[edge + 256 :, :], axis=0, keepdims=True)
    far = jnp.where(row == NB // 2 - 1, behind, jnp.where(row == NB - 1, ahead, 0.0))
    sums[0] = sums[0] + jnp.sum(far, axis=1, keepdims=True)
    for n, (place, span) in enumerate(zip(places, spans)):
        low = sum(spans[:n])
        square = mm_nt(drift[low : low + span, :], one_hot_rows(place, span, False))
        square = jnp.concatenate([square, jnp.zeros_like(square)], axis=1)
        lined = pltpu.roll(square, 0, 1, stride=1, stride_axis=0)
        line = jnp.sum(lined, axis=0, keepdims=True)
        bucket = bucket_of(span - 1 - lane_ids((1, 2 * span)))
        sums.append(bucket_sums(line, bucket))
    d_table[...] = jnp.where(
        lane == slot,
        sums[0],
        jnp.where(lane == slot + 1, sums[1], jnp.where(lane == slot + 2, sums[2], 0.0)),
    )


def run_attend_back(tall, ids, after, meta, *arrays):
    seq = meta.shape[1]
    shared = arrays[0]
    return call(
        6,
        functools.partial(attend_back_body, tall),
        [(shared.shape, bf16), ((NB, 128), f32)],
        [
            ((2 * seq - 128, 128), f32),
            ((512 + tall, seq), bf16),
            ((HD, seq), f32),
            ((HD, seq), f32),
        ],
        ids,
        (meta, *arrays),
        after,
        late=(3, 2),
    )


def mixer_body(ids, found, residual, upstream, w_out, gain, w_in, w_down, result, act, d_pre, ffn_low, d_mixed, d_low, d_found, d_gain):
    attn = jnp.concatenate([found[h] for h in range(HEADS)], axis=0)
    mixed = residual[...] + mm_tn(attn, w_out[...])
    wide_gain = gain[...].astype(f32)
    low = (mixed * norm_parts(mixed) * wide_gain).astype(bf16)
    ffn_low[...] = low
    ffn_low.send()
    pre = mm(low, w_in[...])
    hidden = gelu_of(pre).astype(bf16)
    act[...] = hidden
    act.send()
    result[...] = (mixed + mm(hidden, w_down[...])).astype(bf16)
    result.send()
    d_hidden = (mm_nt(upstream[...], w_down[...]) * gelu_slope(pre)).astype(bf16)
    d_pre[...] = d_hidden
    d_pre.send()
    d_norm, gain_sum = norm_back(mixed, wide_gain, mm_nt(d_hidden, w_in[...]))
    d_gain[...] = gain_sum
    d_sum = upstream[...].astype(f32) + d_norm
    d_mixed[...] = d_sum
    d_mixed.send()
    narrow = d_sum.astype(bf16)
    d_low[...] = narrow
    d_low.send()
    back = mm_nt(w_out[...], narrow).astype(bf16)
    for h in range(HEADS):
        d_found[h] = back[HD * h : HD * h + HD, :]


def run_mixer(ids, found, residual, upstream, w_out, gain, w_in, w_down):
    rows, width = residual.shape
    wide = w_in.shape[1]
    return call(
        5,
        mixer_body,
        [
            ((rows, width), bf16),
            ((rows, wide), bf16),
            ((rows, wide), bf16),
            ((rows, width), bf16),
            ((rows, width), f32),
            ((rows, width), bf16),
            ((HEADS, HD, rows), bf16),
            ((1, width), f32),
        ],
        [],
        ids,
        (found, residual, upstream, w_out, gain, w_in, w_down),
        late=(5, 6),
        sent=(0, 1, 2, 3, 4, 5),
    )


def put_halves(ids, first, second, mine, other):
    for bit in range(2):

        @pl.when(ids[5] == bit)
        def _(bit=bit):
            mine[...] = first[...] if bit == 0 else second[...]
            other[...] = second[...] if bit == 0 else first[...]


def mixer_grads_body(ids, found, act, d_pre, ffn_low, d_low, upstream, table, token):
    width = ffn_low.shape[1]
    grad_out = mm_tn(act[...], upstream[...]).astype(bf16)
    grad_in = mm_tn(ffn_low[...], d_pre[...]).astype(bf16)
    attn = jnp.concatenate([found[h] for h in range(HEADS)], axis=0)
    grad_attn = mm(attn, d_low[...]).astype(bf16)
    for c in range(32):
        spot, row = 144 * c, 64 * (c % 8)
        table[spot : spot + 64, :] = grad_out[64 * c : 64 * c + 64, :]
        column = width * (c // 8)
        table[spot + 64 : spot + 128, :] = grad_in[row : row + 64, column : column + width]
        table[spot + 128 : spot + 144, :] = grad_attn[16 * c : 16 * c + 16, :]


def run_mixer_grads(ids, *arrays):
    return call(
        4,
        mixer_grads_body,
        [((4608, 512), bf16), TOKEN],
        [],
        ids,
        arrays,
        late=(1, 5, 3, 2, 4),
        sent=(0,),
    )


def embed_back_body(ids, d_shared, residual, d_mixed, gain, wq, wk, wv, roi, d_resid, d_low, d_pooled, d_gain, d_rows, token):
    turned = None
    for n, weight in enumerate((wq, wk, wv)):
        lines = jnp.concatenate([d_shared[h, HD * n : HD * n + HD, :] for h in range(HEADS)], axis=0)
        d_rows[n] = lines
        term = mm(weight[...], lines)
        turned = term if turned is None else turned + term
    d_norm, gain_sum = norm_back(residual[...], gain[...].astype(f32), turned.T)
    d_gain[...] = gain_sum
    total = d_mixed[...] + d_norm
    d_resid[...] = total
    d_resid.send()
    low = total.astype(bf16)
    d_low[...] = low
    d_pooled[...] = mm_nt(low, roi[...]).astype(bf16)


def run_embed_back(ids, d_shared, residual, *arrays):
    rows, width = residual.shape
    roi = arrays[-1]
    return call(
        2,
        embed_back_body,
        [
            ((rows, width), f32),
            ((rows, width), bf16),
            ((rows, roi.shape[0]), bf16),
            ((1, width), f32),
            ((3, HEADS * HD, rows), bf16),
            TOKEN,
        ],
        [],
        ids,
        (d_shared, residual, *arrays),
        late=(1, 2),
        sent=(0,),
    )


def embed_grads_body(ids, normed, d_rows, pooled, d_low, gains_one, gains_two, d_table, mine, other, token, table):
    width = normed.shape[1]
    turned = normed[...].astype(f32).T.astype(bf16)
    grads = [mm_nt(turned, d_rows[n]).astype(bf16) for n in range(3)]
    roi = mm_tn(pooled[...], d_low[...])
    lane = lane_ids((1, width))
    buckets = jnp.concatenate([d_table[...]] * (width // 128), axis=1)
    buckets = jnp.where(lane < 128, buckets, 0.0)
    blank = jnp.zeros((1, width), f32)
    for c in range(32):
        spot = 64 * (c % 16)
        for n in range(3):
            table[c // 16, spot + 16 * n : spot + 16 * n + 16, :] = grads[n][16 * c : 16 * c + 16, :]
        gains = [gains_one[...], gains_two[...]] if c == 0 else [blank, blank]
        lines = [roi[4 * c : 4 * c + 4, :], buckets[c : c + 1, :], *gains, blank]
        lines = jnp.concatenate(lines + [jnp.zeros((8, width), f32)], axis=0)
        table[c // 16, spot + 48 : spot + 64, :] = lines.astype(bf16)
    put_halves(ids, table.at[0], table.at[1], mine, other)


def run_embed_grads(ids, bit, after, *arrays):
    return call(
        3,
        embed_grads_body,
        [((1024, 512), bf16)] * 2 + [TOKEN],
        [((2, 1024, 512), bf16)],
        ids.at[5].set(bit),
        arrays,
        after,
    )


def on_device(
    embeddings,
    page_images,
    token_boxes,
    segment_ids,
    down_first,
    down_second,
    down_third,
    down_fourth,
    down_fifth,
    up_fourth,
    up_third,
    up_second,
    up_first,
    roi_proj,
    gain_attn,
    w_query,
    w_key,
    w_value,
    w_output,
    bias_table,
    gain_ffn,
    ffn_in,
    ffn_out,
    cotangent,
):
    tok_rows = embeddings.shape[1]
    model_width = embeddings.shape[2]
    tile_rows = page_images.shape[2]
    my_tile = lax.axis_index("tile")
    tile_count = lax.axis_size("tile")
    score_scale = HD ** (-0.5)
    cut = tile_count > 12
    window = 12 if cut else tile_count
    place = 6 if cut else my_tile
    ids = jnp.stack(
        [
            my_tile,
            jnp.asarray(tile_rows * tile_count, my_tile.dtype),
            jnp.asarray(place, my_tile.dtype),
            my_tile - place,
            jnp.asarray(2 if cut else my_tile, my_tile.dtype),
            jnp.asarray(0, my_tile.dtype),
        ]
    ).astype(jnp.int32)

    def gathered(block):
        copies = jnp.broadcast_to(block[None], (tile_count, *block.shape))
        return lax.all_to_all(copies, "tile", 0, 0, tiled=True)

    def windowed(block):
        if not cut:
            return gathered(block)
        blocks = lax.all_gather(block, "tile", axis=0)
        blocks = jnp.pad(blocks, ((6, 6), (0, 0), (0, 0)))
        return lax.dynamic_slice_in_dim(blocks, my_tile, window, 0)

    def from_side(block, step):
        hops = [
            (source, source + step) for source in range(tile_count) if 0 <= source + step < tile_count
        ]
        return lax.ppermute(block, "tile", hops)

    def lined(weight):
        return weight.transpose(0, 2, 1, 3).reshape(3, weight.shape[2], -1)

    def lined_back(weight):
        flipped = weight[::-1, ::-1]
        return flipped.transpose(0, 3, 1, 2).reshape(3, weight.shape[3], -1)

    def beside(table, count):
        return jnp.concatenate(jnp.split(table, count, axis=0), axis=1)

    def below(table, count):
        return jnp.concatenate(jnp.split(table, count, axis=1), axis=0)

    def as_rows(member):
        return member.reshape(-1, member.shape[-1])

    def bit_of(axis, mask):
        return (lax.axis_index(axis) & mask) // mask

    def swapped(block, axis, mask):
        hops = [(source, source ^ mask) for source in range(lax.axis_size(axis))]
        return lax.ppermute(block, axis, hops)

    def halved(halves, step, *after):
        mine, other, _ = halves
        got = swapped(other, *HOPS[step])
        if step + 1 == len(HOPS):
            return run_finish(ids, mine, got, after)
        return run_halve(ids, bit_of(*HOPS[step + 1]), mine, got, after)

    line = page_images.shape[3]
    meta = jnp.concatenate([token_boxes[:, 0], segment_ids])
    digits = jnp.concatenate([meta // 256, meta % 256, jnp.zeros((2, tok_rows), jnp.int32)])
    digits = digits.astype(jnp.bfloat16).reshape(24, -1)
    sheet = jnp.concatenate([page_images[0].reshape(24, -1), digits], axis=1)
    sheets = gathered(sheet)
    digits_all = sheets[:, :, 2 * line :].reshape(tile_count, 12, tok_rows)
    digits_all = digits_all.transpose(1, 0, 2).reshape(12, -1).astype(jnp.int32)
    meta_all = jnp.pad(digits_all[:5] * 256 + digits_all[5:10], ((0, 3), (0, 0)))
    if cut:
        sheets = jnp.pad(sheets, ((2, 2), (0, 0), (0, 0)))
        sheets = lax.dynamic_slice_in_dim(sheets, my_tile, 5, 0)
    left_all, top_all, right_all, bottom_all, seg_all = (meta_all[n] for n in range(5))
    box_rows = meta_all.T
    seq_all = seg_all.shape[0]
    w_zero = jnp.pad(down_first.transpose(2, 0, 1, 3), ((0, 0), (0, 0), (0, 0), (0, 5)))
    w_zero = w_zero.reshape(w_zero.shape[0], -1)
    pre_zero, pre_one, p_one, pre_two, p_two, p_three, page_own = run_down(
        ids, sheets, w_zero, lined(down_second), lined(down_third)
    )
    p_three_all = windowed(p_three)
    pre_three, pre_four, p_four, e_four, pre_up_three, dec_three = run_bottom(
        cut, ids, p_three_all, down_fourth, down_fifth, up_fourth
    )
    (
        pre_up_two,
        pre_up_one,
        pre_up_zero,
        u_three,
        dec_two,
        dec_one,
        features,
        edge_end,
        edge_start,
    ) = run_up(
        ids, dec_three, pre_two, pre_one, pre_zero, up_third, lined(up_second), lined(up_first)
    )
    pre_up_edges = (from_side(edge_end, 1), from_side(edge_start, -1))
    pooled_own = run_pool(ids, box_rows, features, 256)
    pieces = lax.all_to_all(
        pooled_own.reshape(tile_count, tok_rows, -1), "tile", 0, 0, tiled=True
    )
    gain_row_one = gain_attn.reshape(1, -1)
    gain_row_two = gain_ffn.reshape(1, -1)
    heads_first = tile_count == HEADS
    if heads_first:
        tall = tile_rows * tile_count
        residual, normed_low, pooled_low, shared = run_embed(
            ids, pieces, embeddings[0], roi_proj, gain_row_one, w_query, w_key, w_value
        )
        shared = lax.all_to_all(shared, "tile", 0, 0, tiled=True)
        prob, found_low, found_full = run_attend(
            tall, ids, bias_table.astype(jnp.float32), meta_all, box_rows, shared
        )
        found = lax.all_to_all(found_low, "tile", 0, 0, tiled=True)
        result_low, act_low, d_pre, ffn_low, d_mixed, d_mixed_low, d_found, grad_gain_ffn = run_mixer(
            ids, found, residual, cotangent[0], w_output, gain_row_two, ffn_in, ffn_out
        )
        d_found = lax.all_to_all(d_found, "tile", 0, 0, tiled=True)
        mixer_table, mixer_token = run_mixer_grads(
            ids, found, act_low, d_pre, ffn_low, d_mixed_low, cotangent[0]
        )
        mixer_share = lax.psum_scatter(
            mixer_table, (*PAGES, "tile"), scatter_dimension=0, tiled=True
        )
        d_shared, d_table = run_attend_back(
            tall, ids, (mixer_token,), meta_all, shared, prob, found_full, d_found
        )
        d_shared = lax.all_to_all(d_shared, "tile", 0, 0, tiled=True)
        d_residual, d_resid_low, d_pooled, grad_gain_attn, d_rows, embed_token = run_embed_back(
            ids, d_shared, residual, d_mixed, gain_row_one, w_query, w_key, w_value, roi_proj
        )
        embed_halves = run_embed_grads(
            ids,
            bit_of(*HOPS[0]),
            (),
            normed_low,
            d_rows,
            pooled_low,
            d_resid_low,
            grad_gain_attn,
            grad_gain_ffn,
            d_table,
        )
        embed_halves = halved(embed_halves, 0)
        ordering = embed_halves[2:]
    else:
        ordering = ()
        pooled_low = jnp.sum(pieces.astype(jnp.float32), axis=0).astype(jnp.bfloat16)
        residual = embeddings[0].astype(jnp.float32) + jnp.dot(
            pooled_low, roi_proj, preferred_element_type=jnp.float32
        )
        gain_one = gain_attn.astype(jnp.float32)
        normed_low = rms_scale(residual, gain_one).astype(jnp.bfloat16)
        query_low = jnp.dot(normed_low, w_query, preferred_element_type=jnp.float32).astype(
            jnp.bfloat16
        )
        key_low = jnp.dot(normed_low, w_key, preferred_element_type=jnp.float32).astype(jnp.bfloat16)
        value_low = jnp.dot(normed_low, w_value, preferred_element_type=jnp.float32).astype(
            jnp.bfloat16
        )

        def to_heads(flat_rows):
            return flat_rows.reshape(tok_rows, HEADS, HD).transpose(1, 0, 2)

        def from_heads(head_rows):
            return head_rows.transpose(1, 0, 2).reshape(tok_rows, model_width)

        query_heads = to_heads(query_low)
        own_keys = to_heads(key_low)
        own_values = to_heads(value_low)
        key_all, value_all = (
            lax.all_gather(own_keys, "tile", axis=1, tiled=True),
            lax.all_gather(own_values, "tile", axis=1, tiled=True),
        )
        center_x = (left_all + right_all) // 2
        center_y = (top_all + bottom_all) // 2
        key_meta = (jnp.arange(seq_all), center_x, center_y, seg_all)
        first_tok = my_tile * tok_rows
        query_meta = tuple(
            (lax.dynamic_slice_in_dim(member, first_tok, tok_rows, 0) for member in key_meta)
        )
        key_block = math.gcd(seq_all, 1024)
        block_count = seq_all // key_block

        def key_slice(block_id):
            first_key = block_id * key_block
            keys_blk = lax.dynamic_slice_in_dim(key_all, first_key, key_block, 1)
            values_blk = lax.dynamic_slice_in_dim(value_all, first_key, key_block, 1)
            meta_blk = tuple(
                (lax.dynamic_slice_in_dim(member, first_key, key_block, 0) for member in key_meta)
            )
            return (keys_blk, values_blk, meta_blk)

        def stats_step(running, block_id):
            run_max, run_sum = running
            keys_blk, values_blk, meta_blk = key_slice(block_id)
            scores, allowed, one_hot = block_scores(
                query_heads, keys_blk, query_meta, meta_blk, bias_table, score_scale
            )
            scores = jnp.where(allowed[None], scores, neg_large)
            new_max = jnp.maximum(run_max, jnp.max(scores, axis=-1))
            run_sum = run_sum * jnp.exp(run_max - new_max) + jnp.sum(
                jnp.exp(scores - new_max[..., None]), axis=-1
            )
            return ((new_max, run_sum), None)

        start_stats = (
            jnp.full((HEADS, tok_rows), neg_large, jnp.float32),
            jnp.zeros((HEADS, tok_rows), jnp.float32),
        )
        (run_max, run_sum), _ = lax.scan(stats_step, start_stats, jnp.arange(block_count))
        log_total = run_max + jnp.log(run_sum)

        def out_step(attn_acc, block_id):
            keys_blk, values_blk, meta_blk = key_slice(block_id)
            scores, allowed, one_hot = block_scores(
                query_heads, keys_blk, query_meta, meta_blk, bias_table, score_scale
            )
            attn_prob = jnp.where(allowed[None], jnp.exp(scores - log_total[..., None]), 0.0)
            attn_acc = attn_acc + jnp.einsum(
                "hqk,hkd->hqd",
                attn_prob.astype(jnp.bfloat16),
                values_blk,
                preferred_element_type=jnp.float32,
            )
            return (attn_acc, None)

        attn_heads, _ = lax.scan(
            out_step, jnp.zeros((HEADS, tok_rows, HD), jnp.float32), jnp.arange(block_count)
        )
        attn_low = from_heads(attn_heads).astype(jnp.bfloat16)
        mixed_rows = residual + jnp.dot(attn_low, w_output, preferred_element_type=jnp.float32)
        gain_two = gain_ffn.astype(jnp.float32)
        ffn_low = rms_scale(mixed_rows, gain_two).astype(jnp.bfloat16)
        pre_ffn = jnp.dot(ffn_low, ffn_in, preferred_element_type=jnp.float32)
        act_low = jax.nn.gelu(pre_ffn).astype(jnp.bfloat16)
        result_rows = mixed_rows + jnp.dot(act_low, ffn_out, preferred_element_type=jnp.float32)
        upstream = cotangent[0]
        grad_ffn_out = jnp.einsum("tf,td->fd", act_low, upstream, preferred_element_type=jnp.float32)
        d_act = jnp.einsum("td,fd->tf", upstream, ffn_out, preferred_element_type=jnp.float32)
        d_pre = gelu_back(pre_ffn, d_act).astype(jnp.bfloat16)
        grad_ffn_in = jnp.einsum("td,tf->df", ffn_low, d_pre, preferred_element_type=jnp.float32)
        d_ffn_norm = jnp.einsum("tf,df->td", d_pre, ffn_in, preferred_element_type=jnp.float32)
        d_mixed_norm, grad_gain_ffn = jax.vjp(rms_scale, mixed_rows, gain_two)[1](d_ffn_norm)
        d_mixed = upstream.astype(jnp.float32) + d_mixed_norm
        d_mixed_low = d_mixed.astype(jnp.bfloat16)
        grad_output = jnp.einsum("tc,td->cd", attn_low, d_mixed_low, preferred_element_type=jnp.float32)
        d_attn = jnp.einsum(
            "td,cd->tc", d_mixed_low, w_output, preferred_element_type=jnp.float32
        ).astype(jnp.bfloat16)
        dout_heads = to_heads(d_attn)
        row_delta = jnp.sum(dout_heads.astype(jnp.float32) * attn_heads, axis=-1)

        def back_step(running, block_id):
            keys_blk, values_blk, meta_blk = key_slice(block_id)
            scores, allowed, one_hot = block_scores(
                query_heads, keys_blk, query_meta, meta_blk, bias_table, score_scale
            )
            attn_prob = jnp.where(allowed[None], jnp.exp(scores - log_total[..., None]), 0.0)
            d_prob = jnp.einsum(
                "hqd,hkd->hqk", dout_heads, values_blk, preferred_element_type=jnp.float32
            )
            d_score = (attn_prob * (d_prob - row_delta[..., None])).astype(jnp.bfloat16)
            query_acc = running[0] + jnp.einsum(
                "hqk,hkd->hqd", d_score, keys_blk, preferred_element_type=jnp.float32
            )
            table_acc = running[1] + jnp.einsum(
                "hqk,qkn->hn", d_score, one_hot, preferred_element_type=jnp.float32
            )
            first_key = block_id * key_block
            key_part = (
                jnp.einsum("hqk,hqd->hkd", d_score, query_heads, preferred_element_type=jnp.float32)
                * score_scale
            )
            value_part = jnp.einsum(
                "hqk,hqd->hkd",
                attn_prob.astype(jnp.bfloat16),
                dout_heads,
                preferred_element_type=jnp.float32,
            )
            key_acc = lax.dynamic_update_slice_in_dim(running[2], key_part, first_key, 1)
            value_acc = lax.dynamic_update_slice_in_dim(running[3], value_part, first_key, 1)
            return ((query_acc, table_acc, key_acc, value_acc), None)

        start_back = (
            jnp.zeros((HEADS, tok_rows, HD), jnp.float32),
            jnp.zeros((HEADS, 3 * NB), jnp.float32),
        )
        start_back = start_back + (
            jnp.zeros((HEADS, seq_all, HD), jnp.float32),
            jnp.zeros((HEADS, seq_all, HD), jnp.float32),
        )
        back_out, _ = lax.scan(back_step, start_back, jnp.arange(block_count))
        query_acc = back_out[0]
        grad_bias_table = back_out[1]
        key_grad, value_grad = (
            lax.psum_scatter(back_out[2], "tile", scatter_dimension=1, tiled=True),
            lax.psum_scatter(back_out[3], "tile", scatter_dimension=1, tiled=True),
        )
        dq_low = from_heads(query_acc * score_scale).astype(jnp.bfloat16)
        dk_low = from_heads(key_grad).astype(jnp.bfloat16)
        dv_low = from_heads(value_grad).astype(jnp.bfloat16)
        grad_query = jnp.einsum("td,te->de", normed_low, dq_low, preferred_element_type=jnp.float32)
        grad_key = jnp.einsum("td,te->de", normed_low, dk_low, preferred_element_type=jnp.float32)
        grad_value = jnp.einsum("td,te->de", normed_low, dv_low, preferred_element_type=jnp.float32)
        d_normed = (
            jnp.einsum("te,de->td", dq_low, w_query, preferred_element_type=jnp.float32)
            + jnp.einsum("te,de->td", dk_low, w_key, preferred_element_type=jnp.float32)
            + jnp.einsum("te,de->td", dv_low, w_value, preferred_element_type=jnp.float32)
        )
        d_resid_norm, grad_gain_attn = jax.vjp(rms_scale, residual, gain_one)[1](d_normed)
        d_residual = d_mixed + d_resid_norm
        d_resid_low = d_residual.astype(jnp.bfloat16)
        grad_roi_proj = jnp.einsum(
            "tp,td->pd", pooled_low, d_resid_low, preferred_element_type=jnp.float32
        )
        d_pooled = jnp.einsum("td,pd->tp", d_resid_low, roi_proj, preferred_element_type=jnp.float32)
        d_pooled = d_pooled.astype(jnp.bfloat16)
        result_low = result_rows.astype(jnp.bfloat16)
        mixer_table = jnp.concatenate([grad_ffn_out, below(grad_ffn_in, 4), grad_output], axis=0)
        mixer_table = mixer_table.astype(jnp.bfloat16)
        chart = grad_bias_table.reshape(HEADS, 3, NB).transpose(2, 0, 1).reshape(NB, 3 * HEADS)
        embed_table = jnp.concatenate(
            [
                grad_query,
                grad_key,
                grad_value,
                grad_roi_proj,
                jnp.pad(jnp.stack([grad_gain_attn, grad_gain_ffn]), ((0, 14), (0, 0))),
                jnp.pad(chart, ((0, 80), (0, model_width - 3 * HEADS))),
            ],
            axis=0,
        ).astype(jnp.bfloat16)
    d_pooled_all = gathered(d_pooled).reshape(seq_all, -1)
    d_features, low_zero_up, box_token = run_unpool(
        ids,
        ordering,
        box_rows,
        d_pooled_all,
        pre_up_edges[0],
        pre_up_zero,
        pre_up_edges[1],
        256,
    )
    if heads_first:
        embed_halves = halved(embed_halves, 1, box_token)
        ordering = ()
    d_dec_one, d_dec_two, d_dec_three, low_one_up, low_two_up, up_token = run_up_back(
        ids,
        ordering,
        low_zero_up,
        pre_up_one,
        pre_up_two,
        lined_back(up_first),
        lined_back(up_second),
        up_third,
    )
    d_dec_three_all = windowed(d_dec_three)
    grad_up_first = run_grad_up_first(ids, (up_token,), dec_one, low_zero_up)
    if heads_first:
        embed_halves = halved(embed_halves, 2, up_token)
        ordering = embed_halves[2:]
    light_early, early_token = run_grad_up(
        ids, ordering, grad_up_first, dec_two, low_one_up, u_three, low_two_up
    )
    low_three_up, low_four, low_three, d_pool_three, bottom_token = run_bottom_back(
        cut,
        ids,
        (early_token,),
        d_dec_three_all,
        pre_up_three,
        pre_four,
        pre_three,
        up_fourth,
        down_fifth,
        down_fourth,
    )
    dp_count = lax.axis_size(PAGES)
    if heads_first:
        embed_share = halved(halved(embed_halves, 3, bottom_token), 4)
        early_parts = lax.all_to_all(
            light_early.reshape(32, -1, 256), (*PAGES, "tile"), 0, 0, tiled=True
        )
        early_share, _ = run_total(ids, early_parts)
        ordering = ()
    bottom_parts = (low_three_up, e_four, low_four, p_four, low_three, p_three_all)
    if cut:
        heavy = run_grad_bottom_all(ids, *bottom_parts)
        heavy_token = ()
    else:
        heavy, *heavy_token = run_grad_bottom(tile_count, dp_count, ids, ordering, *bottom_parts)
    low_two, low_one, low_zero = run_down_back(
        ids,
        heavy_token,
        d_pool_three,
        d_dec_two,
        pre_two,
        d_dec_one,
        pre_one,
        d_features,
        pre_zero,
        down_third,
        lined_back(down_second),
    )
    light_late = run_grad_down(ids, p_two, low_two, p_one, low_one, page_own, low_zero)
    both_axes = (*PAGES, "tile")
    device_total = dp_count * tile_count

    def summed_share(table):
        parts = table.reshape(device_total, -1, table.shape[1])
        parts = lax.all_to_all(parts, both_axes, 0, 0, tiled=True)
        return jnp.sum(parts.astype(jnp.float32), axis=0).astype(jnp.bfloat16)

    def spread_out(share):
        copies = jnp.broadcast_to(share[None], (device_total, *share.shape))
        return lax.all_to_all(copies, both_axes, 0, 0, tiled=True)

    late = spread_out(summed_share(light_late)).reshape(light_late.shape).astype(jnp.float32)
    wide = ffn_in.shape[1]
    if heads_first:
        parts = lax.all_to_all(heavy, PAGES, 0, 0, tiled=True)
        share = run_gather(ids, parts, mixer_share, embed_share, early_share)
        whole = lax.all_gather(share, both_axes, axis=0)
        *heavy_sums, sum_ffn_out, sum_ffn_in, sum_output, sum_query, sum_key, sum_value, rest, early = (
            run_unpack(whole)
        )
        rest = rest.reshape(NB, 16, model_width)
        sum_roi = rest[:, :4].reshape(-1, model_width)
        sum_bias = rest[:, 4, : 3 * HEADS].reshape(NB, HEADS, 3)
        sum_gain_attn, sum_gain_ffn = rest[0, 5], rest[0, 6]
    else:
        early = spread_out(summed_share(light_early)).reshape(light_early.shape)
        early = early.astype(jnp.float32)
        heavy_sums = [lax.psum(member, both_axes).astype(jnp.float32) for member in heavy]
        mixer_all = lax.psum(mixer_table, both_axes).astype(jnp.float32)
        embed_all = lax.psum(embed_table, both_axes).astype(jnp.float32)
        sum_ffn_out = mixer_all[:wide]
        sum_ffn_in = beside(mixer_all[wide : 2 * wide], wide // model_width)
        sum_output = mixer_all[2 * wide :]
        sum_query, sum_key, sum_value = (
            embed_all[n * model_width : (n + 1) * model_width] for n in range(3)
        )
        last = 3 * model_width + roi_proj.shape[0]
        sum_roi = embed_all[3 * model_width : last]
        sum_bias = embed_all[last + 16 : last + 16 + NB, : 3 * HEADS].reshape(NB, HEADS, 3)
        sum_gain_attn, sum_gain_ffn = embed_all[last], embed_all[last + 1]
    sum_bias = sum_bias.transpose(1, 2, 0).reshape(bias_table.shape)

    def unlined(table, kind):
        return table.reshape(3, kind.shape[2], 3, kind.shape[3]).transpose(0, 2, 1, 3)

    second_rest = below(early[1344:1440], 2)
    sum_up_second = jnp.concatenate([early[1152:1344], second_rest], axis=1)
    sum_down_second = jnp.concatenate([late[384:480, :96], late[384:480, 128:224]], axis=0)
    sum_first = late[480:512, :72].reshape(32, 3, 3, 8)[..., :3].transpose(1, 2, 0, 3)
    summed = [
        sum_first,
        unlined(sum_down_second, down_second),
        unlined(late[:384, :192], down_third),
        heavy_sums[2].reshape(down_fourth.shape),
        heavy_sums[1].reshape(down_fifth.shape),
        heavy_sums[0].reshape(up_fourth.shape),
        early[:1152].reshape(up_third.shape),
        unlined(sum_up_second, up_second),
        unlined(early[1440:1536, :192], up_first),
        sum_roi,
        sum_gain_attn,
        sum_query,
        sum_key,
        sum_value,
        sum_output,
        sum_bias,
        sum_gain_ffn,
        sum_ffn_in,
        sum_ffn_out,
    ]
    return (
        result_low[None],
        d_residual[None],
        summed[0],
        summed[1],
        summed[2],
        summed[3],
        summed[4],
        summed[5],
        summed[6],
        summed[7],
        summed[8],
        summed[9],
        summed[10],
        summed[11],
        summed[12],
        summed[13],
        summed[14],
        summed[15],
        summed[16],
        summed[17],
        summed[18],
    )


def solution(mesh):
    tiles = mesh.shape["tile"]
    split = Mesh(mesh.devices.reshape(mesh.shape["dp"] // 2, 2, tiles), (*PAGES, "tile"))
    return jax.shard_map(
        on_device,
        mesh=split,
        in_specs=(
            P(PAGES, "tile", None),
            P(PAGES, None, "tile", None),
            P(None, PAGES, "tile"),
            P(PAGES, "tile"),
            P(),
            P(),
            P(),
            P(),
            P(),
            P(),
            P(),
            P(),
            P(),
            P(),
            P(),
            P(),
            P(),
            P(),
            P(),
            P(),
            P(),
            P(),
            P(),
            P(PAGES, "tile", None),
        ),
        out_specs=(
            P(PAGES, "tile", None),
            P(PAGES, "tile", None),
            P(),
            P(),
            P(),
            P(),
            P(),
            P(),
            P(),
            P(),
            P(),
            P(),
            P(),
            P(),
            P(),
            P(),
            P(),
            P(),
            P(),
            P(),
            P(),
        ),
        check_vma=False,
    )
```

```python
import functools
import math

import jax
import jax.numpy as jnp
from jax import lax
from jax.experimental import pallas as pl
from jax.experimental.pallas import tpu as pltpu
from jax.sharding import Mesh
from jax.sharding import PartitionSpec as P

HEADS = 8
HD = 64
NB = 32

eps = 1e-06
bounds = (12, 16, 23, 32, 46, 64, 91)
neg_large = -1000000000.0
HOPS = (("core", 1), ("x", 1), ("tile", 1), ("tile", 4), ("tile", 2))
PAGES = ("x", "core")
f32 = jnp.float32
bf16 = jnp.bfloat16
gelu_scale = math.sqrt(2.0 / math.pi)
VMEM_CAP = 40 * 1024 * 1024


def gelu_of(x):
    x = x.astype(f32)
    half = 0.5 * x
    inner = x * (gelu_scale + (gelu_scale * 0.044715) * (x * x))
    return half + half * jnp.tanh(inner)


def gelu_slope(x):
    x = x.astype(f32)
    sq = x * x
    bent = jnp.tanh(x * (gelu_scale + (gelu_scale * 0.044715) * sq))
    rise = gelu_scale + (3.0 * gelu_scale * 0.044715) * sq
    return 0.5 + 0.5 * bent + (0.5 * x) * (1.0 - bent * bent) * rise


def mm(a, b):
    return jnp.dot(a, b, preferred_element_type=f32)


def mm_tn(a, b):
    return lax.dot_general(a, b, (((0,), (0,)), ((), ())), preferred_element_type=f32)


def mm_nt(a, b):
    return lax.dot_general(a, b, (((1,), (1,)), ((), ())), preferred_element_type=f32)


def mm_fine(a, b):
    high = a.astype(bf16)
    low = (a - high.astype(f32)).astype(bf16)
    return mm(high, b) + mm(low, b)


def lane_ids(shape):
    return lax.broadcasted_iota(jnp.int32, shape, len(shape) - 1)


def row_ids_of(shape):
    return lax.broadcasted_iota(jnp.int32, shape, len(shape) - 2)


def halving(wide, value):
    hit = row_ids_of((wide, wide // 2)) >> 1 == lane_ids((wide, wide // 2))
    return jnp.where(hit, value, 0.0).astype(bf16)


def doubling(narrow):
    hit = row_ids_of((narrow, 2 * narrow)) == lane_ids((narrow, 2 * narrow)) >> 1
    return jnp.where(hit, 1.0, 0.0).astype(bf16)


def pair_halving(value):
    shape = (256, 128)
    source = row_ids_of(shape)
    target = lane_ids(shape)
    hit = source >> 1 == target
    return jnp.where(hit, value, 0.0).astype(bf16)


def side_doubling(side):
    shape = (128, 128)
    hit = row_ids_of(shape) == (lane_ids(shape) >> 1) + 64 * side
    return jnp.where(hit, 1.0, 0.0).astype(bf16)


def quad_map(coarse_lanes, coarse_width):
    shape = (coarse_lanes, 4 * coarse_lanes)
    fine = lane_ids((1, shape[1]))
    shift = coarse_width.bit_length() - 1
    home = (fine >> (shift + 2) << shift) + ((fine & (2 * coarse_width - 1)) >> 1)
    return jnp.where(row_ids_of(shape) == home, 1.0, 0.0).astype(bf16)


def masked(x, keep):
    return x * jnp.where(keep, 1.0, 0.0).astype(x.dtype)


def col_shift(x, step, width):
    if step == 0:
        return x
    lanes = x.shape[1]
    col = lane_ids((1, lanes)) & (width - 1)
    keep = col < width - 1 if step > 0 else col > 0
    return masked(pltpu.roll(x, -step % lanes, 1), keep)


def row_shift(x, step, width):
    if step == 0:
        return x
    lanes = x.shape[1]
    lane = lane_ids((1, lanes))
    keep = lane < lanes - width if step > 0 else lane >= width
    return masked(pltpu.roll(x, (-step * width) % lanes, 1), keep)


def stack_cols(x, width):
    return jnp.concatenate([col_shift(x, step, width) for step in (-1, 0, 1)], axis=0)


def row_ok(first_row, rows, width, low, high):
    row = (lane_ids((1, rows * width)) >> (width.bit_length() - 1)) + first_row
    return (row >= low) & (row < high)


def keep_rows(x, first_row, width, high):
    ok = row_ok(first_row, x.shape[1] // width, width, 0, high)
    return jnp.where(ok, x, 0.0)


def price(micros):
    return pl.CostEstimate(
        flops=int(micros * 5e8), transcendentals=0, bytes_accessed=int(micros * 2e6)
    )


class Fetched:
    def __init__(self, ref, copy):
        self.ref, self.copy, self.waited = ref, copy, False
        self.shape = ref.shape
        copy.start()

    def ready(self):
        if not self.waited:
            self.copy.wait()
            self.waited = True
        return self.ref

    def __getitem__(self, spot):
        return self.ready()[spot]


class Sent:
    def __init__(self, ref, copy):
        self.ref, self.copy, self.started = ref, copy, False
        self.shape = ref.shape

    def send(self):
        if not self.started:
            self.copy.start()
            self.started = True

    def __getitem__(self, spot):
        return self.ref[spot]

    def __setitem__(self, spot, value):
        self.ref[spot] = value


def in_hbm(array):
    return pltpu.with_memory_space_constraint(array, pltpu.HBM)


TOKEN = ((8, 128), f32)


def call(micros, body, outs, scratch, ids, arrays, after=(), late=(), sent=(), table=None):
    count = len(arrays)
    moved = [(arrays[n].shape, arrays[n].dtype) for n in late] + [outs[n] for n in sent]
    arrays = [in_hbm(array) if n in late else array for n, array in enumerate(arrays)]
    after = [in_hbm(token) for token in after]

    scalars = (ids,) if table is None else (ids, table)

    def ordered(*refs):
        refs, heads = refs[len(scalars) :], refs[: len(scalars)]
        ins = list(refs[:count])
        refs = refs[count + len(after) :]
        results = list(refs[: len(outs)])
        own = refs[len(outs) : len(outs) + len(scratch)]
        if moved:
            *stages, marks = refs[len(outs) + len(scratch) :]
        for k, n in enumerate(late):
            ins[n] = Fetched(stages[k], pltpu.make_async_copy(ins[n], stages[k], marks.at[k]))
        for k, n in enumerate(sent, len(late)):
            copy = pltpu.make_async_copy(stages[k], results[n], marks.at[k])
            results[n] = Sent(stages[k], copy)
        body(*heads, *ins, *results, *own)
        for n in late:
            ins[n].ready()
        for n in sent:
            results[n].send()
        for n in sent:
            results[n].copy.wait()

    def place(chosen, total):
        return [
            pl.BlockSpec(memory_space=pltpu.HBM if n in chosen else pltpu.VMEM) for n in range(total)
        ]

    return pl.pallas_call(
        ordered,
        cost_estimate=price(micros),
        out_shape=[
            pltpu.HBM(*out) if n in sent or out == TOKEN else jax.ShapeDtypeStruct(*out)
            for n, out in enumerate(outs)
        ],
        in_specs=[pl.BlockSpec(memory_space=pltpu.SMEM)] * len(scalars)
        + place(late, count)
        + [pl.BlockSpec(memory_space=pltpu.HBM) for _ in after],
        out_specs=place([n for n, out in enumerate(outs) if n in sent or out == TOKEN], len(outs)),
        scratch_shapes=[pltpu.VMEM(shape, kind) for shape, kind in scratch]
        + [pltpu.VMEM(shape, kind) for shape, kind in moved]
        + ([pltpu.SemaphoreType.DMA((len(moved),))] if moved else []),
        compiler_params=pltpu.CompilerParams(vmem_limit_bytes=VMEM_CAP),
    )(*scalars, *arrays, *after)


def lanes_at(start, size):
    return pl.ds(pl.multiple_of(start, 128), size)


def down_body(ids, pages, w_zero, w_one, w_two, pre_zero, pre_one, p_one, pre_two, p_two, p_three, page_own, page, cols, pool_one, stack_one, pool_two):
    tile, high, at = ids[0], ids[1], ids[4]
    page[...] = jnp.zeros_like(page)
    for side in range(-2, 3):
        block = at + side

        @pl.when((block >= 0) & (block < pages.shape[0]))
        def _(block=block, side=side):
            lines = pages[block, :, 0:1024].astype(f32)
            for g in range(8):
                first = (2 + side) * 8192 + 1024 * g
                for c in range(3):
                    page[c : c + 1, first : first + 1024] = lines[8 * c + g : 8 * c + g + 1, :]

    page_full = page[:, 11 * 512 : 69 * 512]
    page_own[...] = page_full[:, 20 * 512 : 38 * 512].astype(bf16)
    for j in range(3):
        cols[j] = col_shift(page_full, j - 1, 512)
    halve = halving(512, 0.25)

    def top(k, keep_pre):
        pieces = [
            cols[j, :, lanes_at((4 * k + i) * 512, 2048)] for i in range(3) for j in range(3)
        ]
        pre = mm(w_zero[...], jnp.concatenate(pieces, axis=0).astype(bf16))
        if keep_pre:
            pre_zero[:, lanes_at((k - 5) * 2048, 2048)] = pre.astype(bf16)
        enc = gelu_of(pre)
        pairs = jnp.concatenate(
            [enc[:, :512] + enc[:, 512:1024], enc[:, 1024:1536] + enc[:, 1536:]], axis=0
        )
        pooled = mm_fine(pairs, halve)
        first = tile * 8 - 10 + 2 * k
        for n in range(2):
            ok = (first + n >= 0) & (first + n < high // 2)
            part = jnp.where(ok, pooled[32 * n : 32 * n + 32], 0.0)
            pool_one[:, lanes_at((2 * k + n) * 256, 256)] = part.astype(bf16)

    for low, end, keep_pre in ((0, 5, False), (5, 9, True), (9, 14, False)):

        @pl.loop(low, end)
        def _(k, keep_pre=keep_pre):
            top(k, keep_pre)

    pre_zero.send()
    page_own.send()
    p_one[...] = pool_one[:, 9 * 256 : 19 * 256]
    p_one.send()
    stack_one[...] = stack_cols(pool_one[...], 256)
    halve_one = halving(256, 0.25)

    @pl.loop(0, 6)
    def _(k):
        pre = sum(
            mm(w_one[i], stack_one[:, lanes_at((4 * k + 1 + i) * 256, 1024)]) for i in range(3)
        )

        @pl.when((k >= 1) & (k < 5))
        def _():
            pre_one[:, lanes_at((k - 1) * 1024, 1024)] = pre.astype(bf16)

        enc = gelu_of(pre)
        pairs = jnp.concatenate(
            [enc[:, :256] + enc[:, 256:512], enc[:, 512:768] + enc[:, 768:]], axis=0
        )
        pooled = mm_fine(pairs, halve_one)
        first = tile * 4 - 4 + 2 * k
        for n in range(2):
            ok = (first + n >= 0) & (first + n < high // 4)
            part = jnp.where(ok, pooled[64 * n : 64 * n + 64], 0.0)
            pool_two[:, lanes_at((2 * k + n) * 128, 128)] = part.astype(bf16)

    pre_one.send()
    p_two[...] = pool_two[:, 3 * 128 : 9 * 128]
    p_two.send()
    stacked = stack_cols(pool_two[...], 128)
    pre = sum(mm(w_two[i], stacked[:, i * 128 : i * 128 + 1280]) for i in range(3))
    pre_two[...] = pre.astype(bf16)
    pre_two.send()
    enc = gelu_of(pre[:, 384:896])
    pairs = jnp.concatenate([enc[:, :128] + enc[:, 128:256], enc[:, 256:384] + enc[:, 384:]], axis=1)
    p_three[...] = mm_fine(pairs, pair_halving(0.25)).astype(bf16)


def run_down(ids, pages, w_zero, w_one, w_two):
    return call(
        10,
        down_body,
        [
            ((32, 16 * 512), bf16),
            ((64, 16 * 256), bf16),
            ((32, 10 * 256), bf16),
            ((128, 10 * 128), bf16),
            ((64, 6 * 128), bf16),
            ((128, 128), bf16),
            ((8, 18 * 512), bf16),
        ],
        [
            ((8, 80 * 512), f32),
            ((3, 8, 58 * 512), f32),
            ((32, 28 * 256), bf16),
            ((96, 28 * 256), bf16),
            ((64, 12 * 128), bf16),
        ],
        ids,
        (pages, w_zero, w_one, w_two),
        sent=(0, 1, 2, 3, 4, 6),
    )


def conv_taps(x, weight, width):
    lines = [row_shift(x, i - 1, width) for i in range(3)]
    taps = [col_shift(line, j - 1, width) for line in lines for j in range(3)]
    joined = jnp.concatenate([weight[i, j] for i in range(3) for j in range(3)], axis=1)
    return mm(joined, jnp.concatenate(taps, axis=0))


def conv_taps_back(x, weight, width):
    lines = [row_shift(x, 1 - i, width) for i in range(3)]
    taps = [col_shift(line, 1 - j, width) for line in lines for j in range(3)]
    joined = jnp.concatenate([weight[i, j] for i in range(3) for j in range(3)], axis=0)
    return mm_tn(joined, jnp.concatenate(taps, axis=0))


def conv_rows(x, weight, width, lanes):
    moved = [col_shift(x, j - 1, width) for j in range(3)]
    taps = [moved[j][:, i * width : i * width + lanes] for i in range(3) for j in range(3)]
    joined = jnp.concatenate([weight[i, j] for i in range(3) for j in range(3)], axis=1)
    return mm(joined, jnp.concatenate(taps, axis=0))


def conv_rows_back(x, weight, width, lanes):
    moved = [col_shift(x, j - 1, width) for j in range(3)]
    taps = [moved[2 - j][:, (2 - i) * width : (2 - i) * width + lanes] for i in range(3) for j in range(3)]
    joined = jnp.concatenate([weight[i, j] for i in range(3) for j in range(3)], axis=0)
    return mm_tn(joined, jnp.concatenate(taps, axis=0))


def laid_out(blocks):
    return jnp.concatenate([blocks[n] for n in range(blocks.shape[0])], axis=1)


def bottom_body(cut, ids, p_three, w_three, w_four, w_up, pre_three, pre_four, p_four, e_four, pre_up, dec_three):
    lanes = 128 * p_three.shape[0]
    first, high = ids[3], ids[1]

    def kept(x, width, shrink):
        return keep_rows(x, first * (16 // shrink), width, high // shrink) if cut else x

    pre = conv_taps(laid_out(p_three), w_three, 64)
    pre_three[...] = pre.astype(bf16)
    pre_three.send()
    enc_three = kept(gelu_of(pre), 64, 8)
    spread = quad_map(lanes // 4, 32)
    high_part = enc_three.astype(bf16)
    low_part = (enc_three - high_part.astype(f32)).astype(bf16)
    pooled = ((mm_nt(high_part, spread) + mm_nt(low_part, spread)) * 0.25).astype(bf16)
    p_four[...] = pooled
    p_four.send()
    pre = conv_taps(pooled, w_four, 32)
    pre_four[...] = pre.astype(bf16)
    pre_four.send()
    low = kept(gelu_of(pre), 32, 16).astype(bf16)
    e_four[...] = low
    e_four.send()
    pre = conv_taps(mm(low, spread).astype(bf16), w_up, 64)
    pre_up[...] = pre.astype(bf16)
    pre_up.send()
    dec = kept(gelu_of(pre) + enc_three, 64, 8).astype(bf16)
    zero = jnp.zeros((256, 128), bf16)
    dec_three[:, 0:128] = zero
    dec_three[:, 128 : 128 + lanes] = dec
    dec_three[:, 128 + lanes :] = zero


def run_bottom(cut, ids, p_three, w_three, w_four, w_up):
    lanes = 128 * p_three.shape[0]
    return call(
        11,
        functools.partial(bottom_body, cut),
        [
            ((256, lanes), bf16),
            ((512, lanes // 4), bf16),
            ((256, lanes // 4), bf16),
            ((512, lanes // 4), bf16),
            ((256, lanes), bf16),
            ((256, lanes + 256), bf16),
        ],
        [],
        ids,
        (p_three, w_three, w_four, w_up),
        late=(2, 3),
        sent=(0, 1, 2, 3, 4),
    )


def widened(block):
    parts = []
    for n in range(block.shape[1] // 128):
        piece = block[:, 128 * n : 128 * n + 128]
        for side in range(2):
            line = mm(piece, side_doubling(side)).astype(bf16)
            parts += [line, line]
    return jnp.concatenate(parts, axis=1)


def spread_rows(source, target, width):
    spread = doubling(width)
    for n in range(source.shape[1] // width):
        line = mm(source[:, n * width : n * width + width], spread).astype(bf16)
        for m in range(2):
            target[:, (2 * n + m) * 2 * width : (2 * n + m + 1) * 2 * width] = line


def up_body(ids, dec_three, pre_two, pre_one, pre_zero, w_third, w_second, w_first, pre_up_two, pre_up_one, pre_up_zero, u_three, dec_two, dec_one, features, edge_end, edge_start, wide_two, stack_two, wide_one, stack_one):
    tile, high, place = ids[0], ids[1], ids[2]
    block = dec_three[:, lanes_at(place * 128, 384)]
    wide = widened(block)
    u_three[...] = wide[:, 384 : 384 + 768]
    u_three.send()
    total = conv_rows(wide, w_third, 128, 1280)
    pre_up_two[...] = total.astype(bf16)
    pre_up_two.send()
    dec = gelu_of(total) + gelu_of(pre_two[...])
    dec = keep_rows(dec, tile * 4 - 3, 128, high // 4).astype(bf16)
    dec_two[...] = dec[:, 128 : 128 + 1024]
    dec_two.send()
    spread_rows(dec, wide_two, 128)
    stack_two[...] = stack_cols(wide_two[...], 256)
    for k in range(3):
        pre = sum(
            mm(w_second[i], stack_two[:, (6 * k + i) * 256 : (6 * k + i) * 256 + 1536])
            for i in range(3)
        )
        pre_up_one[:, 1536 * k : 1536 * k + 1536] = pre.astype(bf16)
    pre_up_one.send()
    dec = gelu_of(pre_up_one[:, 4 * 256 : 14 * 256]) + gelu_of(pre_one[:, 3 * 256 : 13 * 256])
    dec = keep_rows(dec, tile * 8 - 1, 256, high // 2).astype(bf16)
    dec_one[...] = dec
    dec_one.send()
    spread_rows(dec, wide_one, 256)
    stack_one[...] = stack_cols(wide_one[...], 512)
    pre_zero.ready()

    @pl.loop(0, 4)
    def _(k):
        pre = sum(
            mm(w_first[i], stack_one[:, lanes_at((4 * k + 1 + i) * 512, 2048)]) for i in range(3)
        )
        own = lanes_at(k * 2048, 2048)
        pre_up_zero[:, own] = pre.astype(bf16)
        found = (gelu_of(pre) + gelu_of(pre_zero[:, own])).astype(bf16)
        for n in range(4):
            features[pl.ds(pl.multiple_of((4 * k + n) * 32, 32), 32), :] = found[
                :, 512 * n : 512 * n + 512
            ]

    edge_end[...] = pre_up_zero[:, 5 * 512 : 16 * 512]
    edge_start[...] = pre_up_zero[:, 0 : 11 * 512]


def run_up(ids, dec_three, pre_two, pre_one, pre_zero, w_third, w_second, w_first):
    return call(
        9,
        up_body,
        [
            ((128, 10 * 128), bf16),
            ((64, 18 * 256), bf16),
            ((32, 16 * 512), bf16),
            ((256, 6 * 128), bf16),
            ((128, 8 * 128), bf16),
            ((64, 10 * 256), bf16),
            ((16 * 32, 512), bf16),
            ((32, 11 * 512), bf16),
            ((32, 11 * 512), bf16),
        ],
        [
            ((128, 20 * 256), bf16),
            ((384, 20 * 256), bf16),
            ((64, 20 * 512), bf16),
            ((192, 20 * 512), bf16),
        ],
        ids,
        (dec_three, pre_two, pre_one, pre_zero, w_third, w_second, w_first),
        late=(1, 2, 3),
        sent=(0, 1, 2, 3, 4, 5),
    )


def band_edges(boxes):
    left, top, right, bottom = (boxes[:, n : n + 1] for n in range(4))
    mid_col = (left + right) >> 1
    mid_row = (top + bottom) >> 1
    return ((left, mid_col, right), (top, mid_row, bottom))


def band_hits(edges, ids_wide, band):
    return (ids_wide >= edges[band]) & (ids_wide < edges[band + 1])


def area_inverse(cols, rows, a, b):
    return 1.0 / ((rows[a + 1] - rows[a]) * (cols[b + 1] - cols[b])).astype(f32)


def pool_body(step, ids, boxes, features, pooled):
    tile = ids[0]
    x_ids = lane_ids((1, 512))
    y_ids = (x_ids >> 5) + tile * 16
    group = lane_ids((1, 128)) >> 5

    @pl.loop(0, boxes.shape[0] // step)
    def _(k):
        own = pl.ds(pl.multiple_of(k * step, step), step)
        cols, rows = band_edges(boxes[own, :])
        result = jnp.zeros((step, 128), f32)
        inside = [jnp.where(band_hits(rows, y_ids, a), 1.0, 0.0) for a in range(2)]
        for b in range(2):
            hits = jnp.where(band_hits(cols, x_ids, b), 1.0, 0.0).astype(bf16)
            lines = mm_nt(hits, features[...])
            for a in range(2):
                part = lines * inside[a]
                part = part[:, :128] + part[:, 128:256] + (part[:, 256:384] + part[:, 384:])
                part = part + pltpu.roll(part, 64, 1)
                part = part + pltpu.roll(part, 32, 1)
                scaled = part * area_inverse(cols, rows, a, b)
                result = jnp.where(group == 2 * a + b, scaled, result)
        pooled[own, :] = result.astype(bf16)


def run_pool(ids, boxes, features, step):
    count = boxes.shape[0]
    return call(
        8, functools.partial(pool_body, step), [((count, 128), bf16)], [], ids, (boxes, features)
    )[0]


def unpool_body(step, ids, boxes, d_pooled, pre_before, pre_up, pre_behind, d_features, d_low, token, total):
    tile = ids[0]
    lines = 38
    x_ids = lane_ids((1, 512))
    y_ids = (lane_ids((1, lines * 32)) >> 5) + (tile * 16 - 11)
    group = lane_ids((1, 128)) >> 5
    source = row_ids_of((128, lines * 32))
    target = lane_ids((1, lines * 32)) & 31
    copies = [
        jnp.where(source == target + 32 * n, 1.0, 0.0).astype(bf16) for n in range(4)
    ]
    total[...] = jnp.zeros_like(total)

    @pl.loop(0, boxes.shape[0] // step)
    def _(k):
        own = pl.ds(pl.multiple_of(k * step, step), step)
        cols, rows = band_edges(boxes[own, :])
        scale = jnp.zeros((step, 128), f32)
        for a in range(2):
            for b in range(2):
                scale = jnp.where(group == 2 * a + b, area_inverse(cols, rows, a, b), scale)
        share = (d_pooled[own, :].astype(f32) * scale).astype(bf16)
        found = None
        inside = [jnp.where(band_hits(rows, y_ids, a), 1.0, 0.0) for a in range(2)]
        for b in range(2):
            placed = mm(share, copies[b]) * inside[0] + mm(share, copies[2 + b]) * inside[1]
            hits = jnp.where(band_hits(cols, x_ids, b), 1.0, 0.0).astype(bf16)
            term = mm_tn(placed.astype(bf16), hits)
            found = term if found is None else found + term
        total[...] += found

    for y in range(lines):
        line = total[32 * y : 32 * y + 32, :]
        if y < 11:
            pre = pre_before[:, 512 * y : 512 * y + 512]
        elif y < 27:
            own = slice(512 * (y - 11), 512 * (y - 10))
            d_features[:, own] = line
            pre = pre_up[:, own]
        else:
            pre = pre_behind[:, 512 * (y - 27) : 512 * (y - 26)]
        d_low[:, 512 * y : 512 * y + 512] = (line * gelu_slope(pre)).astype(bf16)


def run_unpool(ids, after, boxes, d_pooled, pre_before, pre_up, pre_behind, step):
    return call(
        14,
        functools.partial(unpool_body, step),
        [((32, 8192), f32), ((32, 38 * 512), bf16), TOKEN],
        [((38 * 32, 512), f32)],
        ids,
        (boxes, d_pooled, pre_before, pre_up, pre_behind),
        after,
        late=(2, 3, 4),
        sent=(0,),
    )


def up_back_body(ids, d_low, pre_up_one, pre_up_two, wd_first, wd_second, w_third, d_dec_one, d_dec_two, d_dec_three, low_one, low_two, token, stack_zero, wide_low):
    tile, high = ids[0], ids[1]
    stack_zero[...] = stack_cols(d_low[...], 512)
    halve = halving(512, 1.0)
    pre_up_one.ready()

    @pl.loop(0, 9)
    def _(k):
        back = sum(
            mm(wd_first[i], stack_zero[:, lanes_at((4 * k + i) * 512, 2048)]) for i in range(3)
        )
        pairs = jnp.concatenate(
            [back[:, :512] + back[:, 512:1024], back[:, 1024:1536] + back[:, 1536:]], axis=0
        )
        summed = mm_fine(pairs, halve)
        first = tile * 8 - 5 + 2 * k
        for n in range(2):
            ok = (first + n >= 0) & (first + n < high // 2)
            own = lanes_at((2 * k + n) * 256, 256)
            part = jnp.where(ok, summed[64 * n : 64 * n + 64], 0.0)
            d_dec_one[:, own] = part
            wide_low[:, own] = (part * gelu_slope(pre_up_one[:, own])).astype(bf16)

    d_dec_one.send()
    low_one[...] = wide_low[:, 5 * 256 : 13 * 256]
    low_one.send()
    stacked = stack_cols(wide_low[...], 256)
    halve_one = halving(256, 1.0)
    for k in range(4):
        back = sum(
            mm(wd_second[i], stacked[:, (4 * k + i) * 256 : (4 * k + i) * 256 + 1024])
            for i in range(3)
        )
        pairs = jnp.concatenate(
            [back[:, :256] + back[:, 256:512], back[:, 512:768] + back[:, 768:]], axis=0
        )
        summed = mm_fine(pairs, halve_one)
        for n in range(2):
            line = 2 * k + n
            row = tile * 4 - 2 + line
            ok = (row >= 0) & (row < high // 4)
            part = jnp.where(ok, summed[128 * n : 128 * n + 128], 0.0)
            d_dec_two[:, 128 * line : 128 * line + 128] = part
    low = d_dec_two[:, 128 : 7 * 128] * gelu_slope(pre_up_two[:, 2 * 128 : 8 * 128])
    low = low.astype(bf16)
    d_dec_two.send()
    low_two[...] = low[:, 128 : 5 * 128]
    low_two.send()
    total = conv_rows_back(low, w_third, 128, 512)
    pairs = jnp.concatenate(
        [total[:, :128] + total[:, 128:256], total[:, 256:384] + total[:, 384:]], axis=1
    )
    d_dec_three[...] = mm_fine(pairs, pair_halving(1.0)).astype(bf16)


def run_up_back(ids, after, d_low, pre_up_one, pre_up_two, wd_first, wd_second, w_third):
    return call(
        9,
        up_back_body,
        [
            ((64, 18 * 256), f32),
            ((128, 8 * 128), f32),
            ((256, 128), bf16),
            ((64, 8 * 256), bf16),
            ((128, 4 * 128), bf16),
            TOKEN,
        ],
        [((96, 38 * 512), bf16), ((64, 18 * 256), bf16)],
        ids,
        (d_low, pre_up_one, pre_up_two, wd_first, wd_second, w_third),
        after,
        late=(1, 2),
        sent=(0, 1, 3, 4),
    )


def bottom_back_body(cut, ids, d_dec_three, pre_up, pre_four, pre_three, w_up, w_four, w_three, low_up, low_four, low_three, d_pool, token, padded):
    lanes = 128 * d_dec_three.shape[0]
    first, high, place = ids[3], ids[1], ids[2]

    def kept(x, width, shrink):
        return keep_rows(x, first * (16 // shrink), width, high // shrink) if cut else x

    d_dec = laid_out(d_dec_three).astype(f32)
    low = (d_dec * gelu_slope(pre_up[...])).astype(bf16)
    low_up[...] = low
    spread = quad_map(lanes // 4, 32)
    back = conv_taps_back(low, w_up, 64)
    high_part = back.astype(bf16)
    low_part = (back - high_part.astype(f32)).astype(bf16)
    d_enc = kept(mm_nt(high_part, spread) + mm_nt(low_part, spread), 32, 16)
    low = (d_enc * gelu_slope(pre_four[...])).astype(bf16)
    low_four[...] = low
    back = conv_taps_back(low, w_four, 32) * 0.25
    d_enc = kept(d_dec + mm_fine(back, spread), 64, 8)
    low = (d_enc * gelu_slope(pre_three[...])).astype(bf16)
    low_three[...] = low
    zero = jnp.zeros((256, 128), bf16)
    padded[:, 0:128] = zero
    padded[:, 128 : 128 + lanes] = low
    padded[:, 128 + lanes :] = zero
    window = padded[:, lanes_at(place * 128, 384)]
    d_pool[...] = conv_taps_back(window, w_three, 64)[:, 0:384]


def run_bottom_back(cut, ids, after, d_dec_three, pre_up, pre_four, pre_three, w_up, w_four, w_three):
    lanes = 128 * d_dec_three.shape[0]
    return call(
        10,
        functools.partial(bottom_back_body, cut),
        [
            ((256, lanes), bf16),
            ((512, lanes // 4), bf16),
            ((256, lanes), bf16),
            ((128, 384), f32),
            TOKEN,
        ],
        [((256, lanes + 256), bf16)],
        ids,
        (d_dec_three, pre_up, pre_four, pre_three, w_up, w_four, w_three),
        after,
        late=(1, 4, 2, 5, 3, 6),
        sent=(3,),
    )


def down_back_body(ids, d_pool_three, d_dec_two, pre_two, d_dec_one, pre_one, d_features, pre_zero, w_two, wd_one, low_two, low_one, low_zero, wide_one):
    tile, high = ids[0], ids[1]
    d_dec_one.ready()
    pre_one.ready()
    d_features.ready()
    pre_zero.ready()
    quarter = d_pool_three[...] * 0.25
    parts = []
    for n in range(3):
        piece = quarter[:, 128 * n : 128 * n + 128]
        for side in range(2):
            line = mm_fine(piece, side_doubling(side))
            parts += [line, line]
    spread = jnp.concatenate(parts[2:10], axis=1)
    d_enc = keep_rows(d_dec_two[...] + spread, tile * 4 - 2, 128, high // 4)
    low = (d_enc * gelu_slope(pre_two[:, 128 : 9 * 128])).astype(bf16)
    low_two[...] = low[:, 2 * 128 : 6 * 128]
    total = None
    for j in range(3):
        moved = col_shift(low, j - 1, 128)
        for i in range(3):
            term = mm_tn(w_two[2 - i, 2 - j], moved[:, i * 128 : i * 128 + 768])
            total = term if total is None else total + term
    total = total * 0.25
    wide = doubling(128)
    for n in range(6):
        line = mm_fine(total[:, 128 * n : 128 * n + 128], wide)
        for m in range(2):
            row = 2 * n + m
            value = d_dec_one[:, (3 + row) * 256 : (4 + row) * 256] + line
            ok = (tile * 8 - 2 + row >= 0) & (tile * 8 - 2 + row < high // 2)
            value = jnp.where(ok, value, 0.0)
            slope = gelu_slope(pre_one[:, (2 + row) * 256 : (3 + row) * 256])
            wide_one[:, row * 256 : row * 256 + 256] = (value * slope).astype(bf16)
    low_one[...] = wide_one[:, 2 * 256 : 10 * 256]
    stacked = stack_cols(wide_one[...], 256)
    back = sum(mm(wd_one[i], stacked[:, (1 + i) * 256 : (9 + i) * 256]) for i in range(3)) * 0.25
    wider = doubling(256)
    for n in range(8):
        line = mm_fine(back[:, 256 * n : 256 * n + 256], wider)
        for m in range(2):
            own = slice((2 * n + m) * 512, (2 * n + m + 1) * 512)
            value = (d_features[:, own] + line) * gelu_slope(pre_zero[:, own])
            low_zero[:, own] = value.astype(bf16)


def run_down_back(ids, after, *arrays):
    return call(
        4,
        down_back_body,
        [
            ((128, 4 * 128), bf16),
            ((64, 8 * 256), bf16),
            ((32, 16 * 512), bf16),
        ],
        [((64, 12 * 256), bf16)],
        ids,
        arrays,
        after,
        late=(0, 1, 2, 3, 4, 5, 6),
    )


def grad_up_first_body(ids, dec_one, d_low, grad, wide_one, stack_one):
    spread_rows(dec_one[...], wide_one, 256)
    stack_one[...] = stack_cols(wide_one[...], 512)
    for i in range(3):
        grad[i] = mm_nt(d_low[:, 11 * 512 : 27 * 512], stack_one[:, (1 + i) * 512 : (17 + i) * 512])


def run_grad_up_first(ids, after, dec_one, d_low):
    return call(
        4,
        grad_up_first_body,
        [((3, 32, 192), f32)],
        [((64, 20 * 512), bf16), ((192, 20 * 512), bf16)],
        ids,
        (dec_one, d_low),
        after,
        late=(0,),
    )[0]


def grad_up_body(ids, grad_first, dec_two, low_one, u_three, low_two, table, token, wide_two, stack_two):
    spread_rows(dec_two[...], wide_two, 128)
    stack_two[...] = stack_cols(wide_two[...], 256)
    for j in range(3):
        moved = col_shift(u_three[...], j - 1, 128)
        for i in range(3):
            first = (3 * i + j) * 128
            grad = mm_nt(low_two[...], moved[:, i * 128 : i * 128 + 512])
            table[first : first + 128, :] = grad.astype(bf16)
    rest = []
    for i in range(3):
        grad = mm_nt(low_one[...], stack_two[:, (3 + i) * 256 : (11 + i) * 256]).astype(bf16)
        table[1152 + 64 * i : 1216 + 64 * i, :] = grad[:, :256]
        rest.append(grad[:, 256:])
    rest = jnp.concatenate(rest, axis=0)
    table[1344:1440, :] = jnp.concatenate([rest[:96], rest[96:]], axis=1)
    table[1440:1536, :] = jnp.zeros((96, 256), bf16)
    for i in range(3):
        table[1440 + 32 * i : 1472 + 32 * i, 0:192] = grad_first[i].astype(bf16)


def run_grad_up(ids, after, *arrays):
    return call(
        4,
        grad_up_body,
        [((1536, 256), bf16), TOKEN],
        [((128, 16 * 256), bf16), ((384, 16 * 256), bf16)],
        ids,
        arrays,
        after,
        late=(1, 2, 3, 4),
    )


def halve_body(ids, kept, got, mine, other, token):
    half = mine.shape[0]
    for bit in range(2):

        @pl.when(ids[5] == bit)
        def _(bit=bit):
            for out, side in ((mine, bit), (other, 1 - bit)):
                own = slice(half * side, half * side + half)
                out[...] = (kept[own, :].astype(f32) + got[own, :].astype(f32)).astype(bf16)


def run_halve(ids, bit, kept, got, after):
    rows, width = kept.shape
    return call(
        max(1, rows // 1500),
        halve_body,
        [((rows // 2, width), bf16)] * 2 + [TOKEN],
        [],
        ids.at[5].set(bit),
        (kept, got),
        after,
    )


def finish_body(ids, kept, got, share):
    share[...] = (kept[...].astype(f32) + got[...].astype(f32)).astype(bf16)


def total_body(ids, parts, share, token):
    total = parts[0].astype(f32)
    for n in range(1, parts.shape[0]):
        total = total + parts[n].astype(f32)
    half = total.shape[0] // 2
    share[...] = jnp.concatenate([total[:half], total[half:]], axis=1).astype(bf16)


def run_total(ids, parts):
    rows, width = parts.shape[1:]
    outs = [((rows // 2, 2 * width), bf16), TOKEN]
    return call(1, total_body, outs, [], ids, (parts,))


def gather_body(ids, heavy, mixer, embed, early, share):
    rows, width = heavy.shape[1:]
    total = heavy[0].astype(f32)
    for n in range(1, heavy.shape[0]):
        total = total + heavy[n].astype(f32)
    share[0:rows, :] = total.astype(bf16)
    share[rows : rows + 144, :] = mixer[...]
    share[rows + 144 : rows + 208, :] = embed[...]
    pad = jnp.zeros((8, width), f32)
    share[rows + 208 :, :] = jnp.concatenate([early[...].astype(f32), pad], axis=0).astype(bf16)


def run_gather(ids, *arrays):
    rows, width = arrays[0].shape[1:]
    return call(1, gather_body, [((rows + 240, width), bf16)], [], ids, arrays)[0]


def run_finish(ids, kept, got, after):
    return call(1, finish_body, [(kept.shape, bf16)], [], ids, (kept, got), after)[0]


def taps_of(x, width):
    for i in range(3):
        lined = row_shift(x, i - 1, width)
        for j in range(3):
            yield 3 * i + j, col_shift(lined, j - 1, width)


def grad_bottom_body(split, ids, low_up, e_four, low_four, p_four, low_three, p_three, table, token, up_part, four_part, three_part):
    place = ids[2]
    lanes = low_up.shape[1]
    spread = quad_map(lanes // 4, 32)
    shares = table.shape[0]

    def own_part(low):
        rows = low.shape[0] // split
        return low[pl.ds(pl.multiple_of(place * rows, rows), rows), :]

    low = own_part(low_up)
    for tap, x in taps_of(mm(e_four[...], spread).astype(bf16), 64):
        up_part[tap] = mm_nt(low, x)
    low = own_part(low_four)
    for tap, x in taps_of(p_four[...], 32):
        four_part[tap] = mm_nt(low, x)
    low = own_part(low_three)
    for tap, x in taps_of(laid_out(p_three), 64):
        three_part[tap] = mm_nt(low, x)
    for n in range(shares):
        for tap in range(9):
            fifth = jnp.concatenate(
                [
                    four_part[tap, 16 * n : 16 * n + 8, :],
                    four_part[tap, 16 * n + 8 : 16 * n + 16, :],
                ],
                axis=1,
            )
            main = jnp.concatenate([up_part[tap, 8 * n : 8 * n + 8, :], fifth], axis=0)
            table[n, 16 * tap : 16 * tap + 16, :] = main.astype(bf16)
        zero = jnp.zeros((8, 128), f32)
        sides = [three_part[tap, 8 * n : 8 * n + 8, :] for tap in range(9)] + [zero] * 7
        sides = [jnp.concatenate(sides[4 * k : 4 * k + 4], axis=1) for k in range(4)]
        table[n, 144:176, :] = jnp.concatenate(sides, axis=0).astype(bf16)


def run_grad_bottom(split, shares, ids, after, *arrays):
    return call(
        6,
        functools.partial(grad_bottom_body, split),
        [((shares, 176, 512), bf16), TOKEN],
        [
            ((9, 256 // split, 512), f32),
            ((9, 512 // split, 256), f32),
            ((9, 256 // split, 128), f32),
        ],
        ids,
        arrays,
        after,
        late=(1, 3),
    )


def unpack_body(whole, *refs):
    stage, marks = refs[-2:]
    plain = list(refs[:-2])
    step = pl.program_id(0)
    last = pl.num_programs(0) - 1

    def fetch(n):
        return pltpu.make_async_copy(whole.at[n], stage.at[n % 4], marks.at[n % 4])

    @pl.when(step == 0)
    def _():
        for n in range(3):
            fetch(n).start()

    @pl.when(step + 3 <= last)
    def _():
        fetch(step + 3).start()

    fetch(step).wait()
    held = stage.at[step % 4]
    up, fifth, fourth, *plain, early = plain
    for tap in range(9):
        block = held[16 * tap : 16 * tap + 16, :].astype(f32)
        up[tap] = block[0:8, :]
        fifth[tap, 0:8, :] = block[8:16, 0:256]
        fifth[tap, 8:16, :] = block[8:16, 256:512]
    sides = held[144:176, :].astype(f32)
    for tap in range(9):
        rows = slice(8 * (tap // 4), 8 * (tap // 4) + 8)
        fourth[tap] = sides[rows, 128 * (tap % 4) : 128 * (tap % 4) + 128]
    first = 176
    for out in plain:
        rows = out.shape[0]
        out[...] = held[first : first + rows, :].astype(f32)
        first = first + rows
    block = held[first : first + 32, :].astype(f32)
    early[0:24, :] = block[0:24, 0:256]
    early[24:48, :] = block[0:24, 256:512]


def run_unpack(whole):
    tiles = whole.shape[0] // 4

    def by_page(n):
        return (0, n % tiles * 4 + n // tiles, 0)

    def by_chunk(n):
        tile, page = n % tiles, n // tiles
        return (page % 2 * 16 + page // 2 * 8 + tile % 2 * 4 + tile // 4 * 2 + tile // 2 % 2, 0)

    def plain(n):
        return (n, 0)

    def by_column(n):
        return (n % 8, n // 8)

    def out(shape, block, spot):
        return jax.ShapeDtypeStruct(shape, f32), pl.BlockSpec(block, spot)

    outs = [
        out((9, 256, 512), (9, 8, 512), by_page),
        out((9, 512, 256), (9, 16, 256), by_page),
        out((9, 256, 128), (9, 8, 128), by_page),
        out((2048, 512), (64, 512), plain),
        out((512, 2048), (64, 512), by_column),
        out((512, 512), (16, 512), plain),
        out((512, 512), (16, 512), by_chunk),
        out((512, 512), (16, 512), by_chunk),
        out((512, 512), (16, 512), by_chunk),
        out((512, 512), (16, 512), by_chunk),
        out((1536, 256), (48, 256), plain),
    ]
    return pl.pallas_call(
        unpack_body,
        cost_estimate=price(14),
        grid=(whole.shape[0],),
        out_shape=[shape for shape, _ in outs],
        in_specs=[pl.BlockSpec(memory_space=pltpu.HBM)],
        out_specs=[spec for _, spec in outs],
        scratch_shapes=[
            pltpu.VMEM((4, *whole.shape[1:]), bf16),
            pltpu.SemaphoreType.DMA((4,)),
        ],
        compiler_params=pltpu.CompilerParams(vmem_limit_bytes=VMEM_CAP),
    )(in_hbm(whole))


def grad_bottom_all_body(ids, low_up, e_four, low_four, p_four, low_three, p_three, grad_up, grad_four, grad_three):
    lanes = low_up.shape[1]
    spread = quad_map(lanes // 4, 32)

    def own_part(low):
        size = low.shape[1] // (lanes // 128)
        own = lane_ids(low.shape) // size == ids[2]
        return jnp.where(own, low[...], jnp.zeros((), bf16))

    low = own_part(low_up)
    for tap, x in taps_of(mm(e_four[...], spread).astype(bf16), 64):
        grad_up[tap] = mm_nt(low, x).astype(bf16)
    low = own_part(low_four)
    for tap, x in taps_of(p_four[...], 32):
        grad_four[tap] = mm_nt(low, x).astype(bf16)
    low = own_part(low_three)
    for tap, x in taps_of(laid_out(p_three), 64):
        grad_three[tap] = mm_nt(low, x).astype(bf16)


def run_grad_bottom_all(ids, *arrays):
    return call(
        6,
        grad_bottom_all_body,
        [((9, 256, 512), bf16), ((9, 512, 256), bf16), ((9, 256, 128), bf16)],
        [],
        ids,
        arrays,
    )


def grad_down_body(ids, p_two, low_two, p_one, low_one, page, low_zero, table, cols):
    stacked = stack_cols(p_two[...], 128)
    for i in range(3):
        grad = mm_nt(low_two[...], stacked[:, i * 128 : i * 128 + 512]).astype(bf16)
        table[128 * i : 128 * i + 128, 0:192] = grad
    table[0:384, 192:256] = jnp.zeros((384, 64), bf16)
    table[384:512, :] = jnp.zeros((128, 256), bf16)
    stacked = stack_cols(p_one[...], 256)
    parts = [
        mm_nt(low_one[...], stacked[:, i * 256 : i * 256 + 2048]).astype(bf16) for i in range(3)
    ]
    grad = jnp.concatenate(parts, axis=0)
    table[384:480, 0:96] = grad[:96]
    table[384:480, 128:224] = grad[96:]
    rows = page[...].astype(f32)
    for j in range(3):
        cols[j] = col_shift(rows, j - 1, 512)
    pieces = [cols[j, :, i * 512 : i * 512 + 8192] for i in range(3) for j in range(3)]
    grad = mm_nt(low_zero[...], jnp.concatenate(pieces, axis=0).astype(bf16))
    table[480:512, 0:72] = grad.astype(bf16)


def run_grad_down(ids, *arrays):
    return call(
        3,
        grad_down_body,
        [((512, 256), bf16)],
        [((3, 8, 18 * 512), f32)],
        ids,
        arrays,
        late=(0, 2, 4),
    )[0]


def bucket_of(signed_gap):
    distance = jnp.abs(signed_gap)
    far_steps = jnp.zeros_like(distance)
    for threshold in bounds:
        far_steps = far_steps + (distance >= threshold).astype(jnp.int32)
    nearness = jnp.where(distance < 8, distance, 8 + far_steps)
    return nearness + jnp.where(signed_gap > 0, 16, 0).astype(jnp.int32)


def rms_scale(value, gain):
    return value * lax.rsqrt(jnp.mean(value * value, axis=-1, keepdims=True) + eps) * gain


def gelu_back(pre_act, upstream):
    return jax.vjp(jax.nn.gelu, pre_act)[1](upstream)[0]


def block_scores(query_heads, key_heads, query_meta, key_meta, bias_table, score_scale):
    query_pos, query_cx, query_cy, query_seg = query_meta
    key_pos, key_cx, key_cy, key_seg = key_meta
    rel_bucket = bucket_of(key_pos[None, :] - query_pos[:, None])
    hor_bucket = bucket_of(key_cx[None, :] - query_cx[:, None]) + NB
    ver_bucket = bucket_of(key_cy[None, :] - query_cy[:, None]) + 2 * NB
    slot_ids = jnp.arange(3 * NB)
    one_hot = (
        (rel_bucket[..., None] == slot_ids)
        | (hor_bucket[..., None] == slot_ids)
        | (ver_bucket[..., None] == slot_ids)
    ).astype(jnp.bfloat16)
    scores = (
        jnp.einsum("hqd,hkd->hqk", query_heads, key_heads, preferred_element_type=jnp.float32)
        * score_scale
    )
    scores = scores + jnp.einsum(
        "qkn,hn->hqk", one_hot, bias_table, preferred_element_type=jnp.float32
    )
    allowed = query_seg[:, None] == key_seg[None, :]
    return (scores, allowed, one_hot)


def norm_parts(value):
    scale = lax.rsqrt(jnp.mean(value * value, axis=-1, keepdims=True) + eps)
    return scale


def norm_back(value, gain, upstream):
    scale = norm_parts(value)
    weighted = upstream * gain
    inner = jnp.mean(weighted * value, axis=-1, keepdims=True)
    d_value = weighted * scale - value * (inner * scale * scale * scale)
    d_gain = jnp.sum(upstream * value * scale, axis=0, keepdims=True)
    return d_value, d_gain


def embed_body(ids, pieces, emb, roi, gain, wq, wk, wv, residual, normed, pooled, shared):
    total = pieces[0].astype(f32)
    for n in range(1, pieces.shape[0]):
        total = total + pieces[n].astype(f32)
    low = total.astype(bf16)
    pooled[...] = low
    pooled.send()
    resid = emb[...].astype(f32) + mm(low, roi[...])
    residual[...] = resid
    residual.send()
    normal = (resid * norm_parts(resid) * gain[...].astype(f32)).astype(bf16)
    normed[...] = normal
    normed.send()
    for n, weight in enumerate((wq, wk, wv)):
        turned = mm(normal, weight[...]).T.astype(bf16)
        for h in range(HEADS):
            shared[h, HD * n : HD * n + HD, :] = turned[HD * h : HD * h + HD, :]


def run_embed(ids, pieces, emb, *arrays):
    rows, width = emb.shape
    return call(
        2,
        embed_body,
        [
            ((rows, width), f32),
            ((rows, width), bf16),
            ((rows, pieces.shape[2]), bf16),
            ((HEADS, 3 * HD, rows), bf16),
        ],
        [],
        ids,
        (pieces, emb, *arrays),
        sent=(0, 1, 2),
    )


def looked_up(bucket, table, head, first):
    value = jnp.zeros(bucket.shape, f32)
    for n in range(NB):
        value = jnp.where(bucket == n, table[head, first + n], value)
    return value


def toeplitz(span, table, head, first):
    lane = lane_ids((1, 2 * span))
    gap = jnp.where(lane < span, -lane, 2 * span - lane)
    line = looked_up(bucket_of(gap), table, head, first)
    square = jnp.broadcast_to(line, (span, 2 * span))
    return pltpu.roll(square, 0, 1, stride=1, stride_axis=0)[:, :span].astype(bf16)


def centers(meta):
    return ((meta[0:1, :] + meta[2:3, :]) >> 1, (meta[1:2, :] + meta[3:4, :]) >> 1)


def one_hot_rows(value, span, turned):
    row = row_ids_of((span, value.shape[1]))
    if turned:
        row = span - 1 - row
    return jnp.where(row == value, 1.0, 0.0).astype(bf16)


def attend_body(tall, ids, table, meta, meta_cols, shared, prob, out_low, out_full, hits, spread, near):
    head = ids[0]
    seq = meta.shape[1]
    count = shared.shape[0]
    spans = (512, tall)
    for n, (value, span) in enumerate(zip(centers(meta), spans)):
        chart = toeplitz(span, table, head, NB * (n + 1))
        low = sum(spans[:n])
        spread[low : low + span, :] = mm(chart, one_hot_rows(value, span, False)).astype(bf16)
    cols = meta_cols[...]
    for n, span in enumerate(spans):
        value = (cols[:, n : n + 1] + cols[:, n + 2 : n + 3]) >> 1
        low = sum(spans[:n])
        same = lane_ids((1, span)) == value
        hits[:, low : low + span] = jnp.where(same, 1.0, 0.0).astype(bf16)
    edge = seq - 128
    near[0 : edge - 128, :] = jnp.full((edge - 128, 128), table[head, NB // 2 - 1], f32)
    near[edge + 256 :, :] = jnp.full((seq - 256, 128), table[head, NB - 1], f32)
    gap = row_ids_of((384, 128)) - 128 - lane_ids((384, 128))
    near[edge - 128 : edge + 256, :] = looked_up(bucket_of(gap), table, head, 0)
    query = jnp.concatenate([shared[n, 0:HD, :] for n in range(count)], axis=1)
    key = jnp.concatenate([shared[n, HD : 2 * HD, :] for n in range(count)], axis=1)
    value = jnp.concatenate([shared[n, 2 * HD :, :] for n in range(count)], axis=1)
    key = (key.astype(f32) * (HD**-0.5)).astype(bf16)
    seg_key = cols[:, 4:5]
    for block in range(seq // 256):
        own = slice(256 * block, 256 * block + 256)
        first = edge - 256 * block
        scores = mm_tn(key, query[:, own]) + mm(hits[...], spread[:, own])
        scores = scores + jnp.concatenate(
            [near[first : first + seq, :], near[first - 128 : first - 128 + seq, :]], axis=1
        )
        scores = jnp.where(seg_key == meta[4:5, own], scores, neg_large)
        weight = jnp.exp(scores - jnp.max(scores, axis=0, keepdims=True))
        weight = weight * (1.0 / jnp.sum(weight, axis=0, keepdims=True))
        low = weight.astype(bf16)
        prob[block] = low
        found = mm(value, low)
        out_full[:, own] = found
        for n in range(2):
            out_low[2 * block + n] = found[:, 128 * n : 128 * n + 128].astype(bf16)


def run_attend(tall, ids, after, table, meta, meta_cols, shared):
    seq = meta.shape[1]
    count = shared.shape[0]
    return call(
        9,
        functools.partial(attend_body, tall),
        [
            ((seq // 256, seq, 256), bf16),
            ((count, HD, seq // count), bf16),
            ((HD, seq), f32),
        ],
        [
            ((seq, 512 + tall), bf16),
            ((512 + tall, seq), bf16),
            ((2 * seq - 128, 128), f32),
        ],
        ids,
        (meta, meta_cols, shared),
        after,
        sent=(0, 2),
        table=table,
    )


def bucket_sums(value, bucket):
    lines = [
        jnp.sum(jnp.where(bucket == n, value, 0.0), axis=0, keepdims=True) for n in range(NB)
    ]
    return jnp.sum(jnp.concatenate(lines, axis=0), axis=1, keepdims=True)


def attend_back_body(tall, ids, meta, shared, prob, out_full, d_out, d_shared, d_table, near, drift, key_sum, value_sum):
    seq = meta.shape[1]
    count = shared.shape[0]
    spans = (512, tall)
    query = jnp.concatenate([shared[n, 0:HD, :] for n in range(count)], axis=1)
    key = jnp.concatenate([shared[n, HD : 2 * HD, :] for n in range(count)], axis=1)
    value = jnp.concatenate([shared[n, 2 * HD :, :] for n in range(count)], axis=1)
    d_found = jnp.concatenate([d_out[n] for n in range(count)], axis=1)
    delta = jnp.sum(d_found.astype(f32) * out_full[...], axis=0, keepdims=True)
    near[...] = jnp.zeros_like(near)
    key_sum[...] = jnp.zeros_like(key_sum)
    value_sum[...] = jnp.zeros_like(value_sum)
    places = centers(meta)
    turned = jnp.concatenate(
        [one_hot_rows(place, span, True) for place, span in zip(places, spans)], axis=0
    )
    edge = seq - 128
    scale = HD**-0.5
    for block in range(seq // 256):
        own = slice(256 * block, 256 * block + 256)
        first = edge - 256 * block
        low = prob[block]
        d_prob = mm_tn(value, d_found[:, own])
        d_score = low.astype(f32) * (d_prob - delta[:, own])
        near[first : first + seq, :] += d_score[:, :128]
        near[first - 128 : first - 128 + seq, :] += d_score[:, 128:]
        d_low = d_score.astype(bf16)
        d_query = (mm(key, d_low) * scale).astype(bf16)
        for n in range(2):
            d_shared[2 * block + n, 0:HD, :] = d_query[:, 128 * n : 128 * n + 128]
        key_sum[...] += mm_nt(query[:, own], d_low)
        value_sum[...] += mm_nt(d_found[:, own], low)
        drift[:, own] = mm(turned, d_low).astype(bf16)
    d_key = (key_sum[...] * scale).astype(bf16)
    d_value = value_sum[...].astype(bf16)
    for n in range(count):
        d_shared[n, HD : 2 * HD, :] = d_key[:, 128 * n : 128 * n + 128]
        d_shared[n, 2 * HD :, :] = d_value[:, 128 * n : 128 * n + 128]
    sums = []
    slot = 3 * ids[0]
    gap = row_ids_of((384, 128)) - 128 - lane_ids((384, 128))
    sums.append(bucket_sums(near[edge - 128 : edge + 256, :], bucket_of(gap)))
    row = row_ids_of((NB, 128))
    lane = lane_ids((NB, 128))
    behind = jnp.sum(near[0 : edge - 128, :], axis=0, keepdims=True)
    ahead = jnp.sum(near[edge + 256 :, :], axis=0, keepdims=True)
    far = jnp.where(row == NB // 2 - 1, behind, jnp.where(row == NB - 1, ahead, 0.0))
    sums[0] = sums[0] + jnp.sum(far, axis=1, keepdims=True)
    for n, (place, span) in enumerate(zip(places, spans)):
        low = sum(spans[:n])
        square = mm_nt(drift[low : low + span, :], one_hot_rows(place, span, False))
        square = jnp.concatenate([square, jnp.zeros_like(square)], axis=1)
        lined = pltpu.roll(square, 0, 1, stride=1, stride_axis=0)
        line = jnp.sum(lined, axis=0, keepdims=True)
        bucket = bucket_of(span - 1 - lane_ids((1, 2 * span)))
        sums.append(bucket_sums(line, bucket))
    d_table[...] = jnp.where(
        lane == slot,
        sums[0],
        jnp.where(lane == slot + 1, sums[1], jnp.where(lane == slot + 2, sums[2], 0.0)),
    )


def run_attend_back(tall, ids, after, meta, *arrays):
    seq = meta.shape[1]
    shared = arrays[0]
    return call(
        6,
        functools.partial(attend_back_body, tall),
        [(shared.shape, bf16), ((NB, 128), f32)],
        [
            ((2 * seq - 128, 128), f32),
            ((512 + tall, seq), bf16),
            ((HD, seq), f32),
            ((HD, seq), f32),
        ],
        ids,
        (meta, *arrays),
        after,
        late=(3, 2),
    )


def mixer_body(ids, found, residual, upstream, w_out, gain, w_in, w_down, result, act, d_pre, ffn_low, d_mixed, d_low, d_found, d_gain):
    attn = jnp.concatenate([found[h] for h in range(HEADS)], axis=0)
    mixed = residual[...] + mm_tn(attn, w_out[...])
    wide_gain = gain[...].astype(f32)
    low = (mixed * norm_parts(mixed) * wide_gain).astype(bf16)
    ffn_low[...] = low
    ffn_low.send()
    pre = mm(low, w_in[...])
    hidden = gelu_of(pre).astype(bf16)
    act[...] = hidden
    act.send()
    result[...] = (mixed + mm(hidden, w_down[...])).astype(bf16)
    result.send()
    d_hidden = (mm_nt(upstream[...], w_down[...]) * gelu_slope(pre)).astype(bf16)
    d_pre[...] = d_hidden
    d_pre.send()
    d_norm, gain_sum = norm_back(mixed, wide_gain, mm_nt(d_hidden, w_in[...]))
    d_gain[...] = gain_sum
    d_sum = upstream[...].astype(f32) + d_norm
    d_mixed[...] = d_sum
    d_mixed.send()
    narrow = d_sum.astype(bf16)
    d_low[...] = narrow
    d_low.send()
    back = mm_nt(w_out[...], narrow).astype(bf16)
    for h in range(HEADS):
        d_found[h] = back[HD * h : HD * h + HD, :]


def run_mixer(ids, found, residual, upstream, w_out, gain, w_in, w_down):
    rows, width = residual.shape
    wide = w_in.shape[1]
    return call(
        5,
        mixer_body,
        [
            ((rows, width), bf16),
            ((rows, wide), bf16),
            ((rows, wide), bf16),
            ((rows, width), bf16),
            ((rows, width), f32),
            ((rows, width), bf16),
            ((HEADS, HD, rows), bf16),
            ((1, width), f32),
        ],
        [],
        ids,
        (found, residual, upstream, w_out, gain, w_in, w_down),
        late=(5, 6),
        sent=(0, 1, 2, 3, 4, 5),
    )


def put_halves(ids, first, second, mine, other):
    for bit in range(2):

        @pl.when(ids[5] == bit)
        def _(bit=bit):
            mine[...] = first[...] if bit == 0 else second[...]
            other[...] = second[...] if bit == 0 else first[...]


def mixer_grads_body(ids, found, act, d_pre, ffn_low, d_low, upstream, table, token):
    width = ffn_low.shape[1]
    grad_out = mm_tn(act[...], upstream[...]).astype(bf16)
    grad_in = mm_tn(ffn_low[...], d_pre[...]).astype(bf16)
    attn = jnp.concatenate([found[h] for h in range(HEADS)], axis=0)
    grad_attn = mm(attn, d_low[...]).astype(bf16)
    for c in range(32):
        spot, row = 144 * c, 64 * (c % 8)
        table[spot : spot + 64, :] = grad_out[64 * c : 64 * c + 64, :]
        column = width * (c // 8)
        table[spot + 64 : spot + 128, :] = grad_in[row : row + 64, column : column + width]
        table[spot + 128 : spot + 144, :] = grad_attn[16 * c : 16 * c + 16, :]


def run_mixer_grads(ids, *arrays):
    return call(
        4,
        mixer_grads_body,
        [((4608, 512), bf16), TOKEN],
        [],
        ids,
        arrays,
        late=(1, 5, 3, 2, 4),
        sent=(0,),
    )


def embed_back_body(ids, d_shared, residual, d_mixed, gain, wq, wk, wv, roi, d_resid, d_low, d_pooled, d_gain, d_rows, token):
    turned = None
    for n, weight in enumerate((wq, wk, wv)):
        lines = jnp.concatenate([d_shared[h, HD * n : HD * n + HD, :] for h in range(HEADS)], axis=0)
        d_rows[n] = lines
        term = mm(weight[...], lines)
        turned = term if turned is None else turned + term
    d_norm, gain_sum = norm_back(residual[...], gain[...].astype(f32), turned.T)
    d_gain[...] = gain_sum
    total = d_mixed[...] + d_norm
    d_resid[...] = total
    d_resid.send()
    low = total.astype(bf16)
    d_low[...] = low
    d_pooled[...] = mm_nt(low, roi[...]).astype(bf16)


def run_embed_back(ids, d_shared, residual, *arrays):
    rows, width = residual.shape
    roi = arrays[-1]
    return call(
        2,
        embed_back_body,
        [
            ((rows, width), f32),
            ((rows, width), bf16),
            ((rows, roi.shape[0]), bf16),
            ((1, width), f32),
            ((3, HEADS * HD, rows), bf16),
            TOKEN,
        ],
        [],
        ids,
        (d_shared, residual, *arrays),
        late=(1, 2),
        sent=(0,),
    )


def embed_grads_body(ids, normed, d_rows, pooled, d_low, gains_one, gains_two, d_table, mine, other, token, table):
    width = normed.shape[1]
    turned = normed[...].astype(f32).T.astype(bf16)
    grads = [mm_nt(turned, d_rows[n]).astype(bf16) for n in range(3)]
    roi = mm_tn(pooled[...], d_low[...])
    lane = lane_ids((1, width))
    buckets = jnp.concatenate([d_table[...]] * (width // 128), axis=1)
    buckets = jnp.where(lane < 128, buckets, 0.0)
    blank = jnp.zeros((1, width), f32)
    for c in range(32):
        spot = 64 * (c % 16)
        for n in range(3):
            table[c // 16, spot + 16 * n : spot + 16 * n + 16, :] = grads[n][16 * c : 16 * c + 16, :]
        gains = [gains_one[...], gains_two[...]] if c == 0 else [blank, blank]
        lines = [roi[4 * c : 4 * c + 4, :], buckets[c : c + 1, :], *gains, blank]
        lines = jnp.concatenate(lines + [jnp.zeros((8, width), f32)], axis=0)
        table[c // 16, spot + 48 : spot + 64, :] = lines.astype(bf16)
    put_halves(ids, table.at[0], table.at[1], mine, other)


def run_embed_grads(ids, bit, after, *arrays):
    return call(
        3,
        embed_grads_body,
        [((1024, 512), bf16)] * 2 + [TOKEN],
        [((2, 1024, 512), bf16)],
        ids.at[5].set(bit),
        arrays,
        after,
    )


def on_device(
    embeddings,
    page_images,
    token_boxes,
    segment_ids,
    down_first,
    down_second,
    down_third,
    down_fourth,
    down_fifth,
    up_fourth,
    up_third,
    up_second,
    up_first,
    roi_proj,
    gain_attn,
    w_query,
    w_key,
    w_value,
    w_output,
    bias_table,
    gain_ffn,
    ffn_in,
    ffn_out,
    cotangent,
):
    tok_rows = embeddings.shape[1]
    model_width = embeddings.shape[2]
    tile_rows = page_images.shape[2]
    my_tile = lax.axis_index("tile")
    tile_count = lax.axis_size("tile")
    score_scale = HD ** (-0.5)
    cut = tile_count > 12
    window = 12 if cut else tile_count
    place = 6 if cut else my_tile
    ids = jnp.stack(
        [
            my_tile,
            jnp.asarray(tile_rows * tile_count, my_tile.dtype),
            jnp.asarray(place, my_tile.dtype),
            my_tile - place,
            jnp.asarray(2 if cut else my_tile, my_tile.dtype),
            jnp.asarray(0, my_tile.dtype),
        ]
    ).astype(jnp.int32)

    def gathered(block):
        copies = jnp.broadcast_to(block[None], (tile_count, *block.shape))
        return lax.all_to_all(copies, "tile", 0, 0, tiled=True)

    def windowed(block):
        if not cut:
            return gathered(block)
        blocks = lax.all_gather(block, "tile", axis=0)
        blocks = jnp.pad(blocks, ((6, 6), (0, 0), (0, 0)))
        return lax.dynamic_slice_in_dim(blocks, my_tile, window, 0)

    def from_side(block, step):
        hops = [
            (source, source + step) for source in range(tile_count) if 0 <= source + step < tile_count
        ]
        return lax.ppermute(block, "tile", hops)

    def lined(weight):
        return weight.transpose(0, 2, 1, 3).reshape(3, weight.shape[2], -1)

    def lined_back(weight):
        flipped = weight[::-1, ::-1]
        return flipped.transpose(0, 3, 1, 2).reshape(3, weight.shape[3], -1)

    def beside(table, count):
        return jnp.concatenate(jnp.split(table, count, axis=0), axis=1)

    def below(table, count):
        return jnp.concatenate(jnp.split(table, count, axis=1), axis=0)

    def as_rows(member):
        return member.reshape(-1, member.shape[-1])

    def bit_of(axis, mask):
        return (lax.axis_index(axis) & mask) // mask

    def swapped(block, axis, mask):
        hops = [(source, source ^ mask) for source in range(lax.axis_size(axis))]
        return lax.ppermute(block, axis, hops)

    def halved(halves, step, *after):
        mine, other, _ = halves
        got = swapped(other, *HOPS[step])
        if step + 1 == len(HOPS):
            return run_finish(ids, mine, got, after)
        return run_halve(ids, bit_of(*HOPS[step + 1]), mine, got, after)

    line = page_images.shape[3]
    meta = jnp.concatenate([token_boxes[:, 0], segment_ids])
    digits = jnp.concatenate([meta // 256, meta % 256, jnp.zeros((2, tok_rows), jnp.int32)])
    digits = digits.astype(jnp.bfloat16).reshape(24, -1)
    sheet = jnp.concatenate([page_images[0].reshape(24, -1), digits], axis=1)
    sheets = gathered(sheet)
    digits_all = sheets[:, :, 2 * line :].reshape(tile_count, 12, tok_rows)
    digits_all = digits_all.transpose(1, 0, 2).reshape(12, -1).astype(jnp.int32)
    meta_all = jnp.pad(digits_all[:5] * 256 + digits_all[5:10], ((0, 3), (0, 0)))
    if cut:
        sheets = jnp.pad(sheets, ((2, 2), (0, 0), (0, 0)))
        sheets = lax.dynamic_slice_in_dim(sheets, my_tile, 5, 0)
    left_all, top_all, right_all, bottom_all, seg_all = (meta_all[n] for n in range(5))
    box_rows = meta_all.T
    seq_all = seg_all.shape[0]
    w_zero = jnp.pad(down_first.transpose(2, 0, 1, 3), ((0, 0), (0, 0), (0, 0), (0, 5)))
    w_zero = w_zero.reshape(w_zero.shape[0], -1)
    pre_zero, pre_one, p_one, pre_two, p_two, p_three, page_own = run_down(
        ids, sheets, w_zero, lined(down_second), lined(down_third)
    )
    p_three_all = windowed(p_three)
    pre_three, pre_four, p_four, e_four, pre_up_three, dec_three = run_bottom(
        cut, ids, p_three_all, down_fourth, down_fifth, up_fourth
    )
    (
        pre_up_two,
        pre_up_one,
        pre_up_zero,
        u_three,
        dec_two,
        dec_one,
        features,
        edge_end,
        edge_start,
    ) = run_up(
        ids, dec_three, pre_two, pre_one, pre_zero, up_third, lined(up_second), lined(up_first)
    )
    pre_up_edges = (from_side(edge_end, 1), from_side(edge_start, -1))
    pooled_own = run_pool(ids, box_rows, features, 256)
    pieces = lax.all_to_all(
        pooled_own.reshape(tile_count, tok_rows, -1), "tile", 0, 0, tiled=True
    )
    gain_row_one = gain_attn.reshape(1, -1)
    gain_row_two = gain_ffn.reshape(1, -1)
    heads_first = tile_count == HEADS
    if heads_first:
        tall = tile_rows * tile_count
        residual, normed_low, pooled_low, shared = run_embed(
            ids, pieces, embeddings[0], roi_proj, gain_row_one, w_query, w_key, w_value
        )
        shared = lax.all_to_all(shared, "tile", 0, 0, tiled=True)
        prob, found_low, found_full = run_attend(
            tall, ids, pre_up_edges, bias_table.astype(jnp.float32), meta_all, box_rows, shared
        )
        found = lax.all_to_all(found_low, "tile", 0, 0, tiled=True)
        result_low, act_low, d_pre, ffn_low, d_mixed, d_mixed_low, d_found, grad_gain_ffn = run_mixer(
            ids, found, residual, cotangent[0], w_output, gain_row_two, ffn_in, ffn_out
        )
        d_found = lax.all_to_all(d_found, "tile", 0, 0, tiled=True)
        mixer_table, mixer_token = run_mixer_grads(
            ids, found, act_low, d_pre, ffn_low, d_mixed_low, cotangent[0]
        )
        mixer_share = lax.psum_scatter(
            mixer_table, (*PAGES, "tile"), scatter_dimension=0, tiled=True
        )
        d_shared, d_table = run_attend_back(
            tall, ids, (mixer_token,), meta_all, shared, prob, found_full, d_found
        )
        d_shared = lax.all_to_all(d_shared, "tile", 0, 0, tiled=True)
        d_residual, d_resid_low, d_pooled, grad_gain_attn, d_rows, embed_token = run_embed_back(
            ids, d_shared, residual, d_mixed, gain_row_one, w_query, w_key, w_value, roi_proj
        )
        embed_halves = run_embed_grads(
            ids,
            bit_of(*HOPS[0]),
            (),
            normed_low,
            d_rows,
            pooled_low,
            d_resid_low,
            grad_gain_attn,
            grad_gain_ffn,
            d_table,
        )
        embed_halves = halved(embed_halves, 0)
        ordering = embed_halves[2:]
    else:
        ordering = ()
        pooled_low = jnp.sum(pieces.astype(jnp.float32), axis=0).astype(jnp.bfloat16)
        residual = embeddings[0].astype(jnp.float32) + jnp.dot(
            pooled_low, roi_proj, preferred_element_type=jnp.float32
        )
        gain_one = gain_attn.astype(jnp.float32)
        normed_low = rms_scale(residual, gain_one).astype(jnp.bfloat16)
        query_low = jnp.dot(normed_low, w_query, preferred_element_type=jnp.float32).astype(
            jnp.bfloat16
        )
        key_low = jnp.dot(normed_low, w_key, preferred_element_type=jnp.float32).astype(jnp.bfloat16)
        value_low = jnp.dot(normed_low, w_value, preferred_element_type=jnp.float32).astype(
            jnp.bfloat16
        )

        def to_heads(flat_rows):
            return flat_rows.reshape(tok_rows, HEADS, HD).transpose(1, 0, 2)

        def from_heads(head_rows):
            return head_rows.transpose(1, 0, 2).reshape(tok_rows, model_width)

        query_heads = to_heads(query_low)
        own_keys = to_heads(key_low)
        own_values = to_heads(value_low)
        key_all, value_all = (
            lax.all_gather(own_keys, "tile", axis=1, tiled=True),
            lax.all_gather(own_values, "tile", axis=1, tiled=True),
        )
        center_x = (left_all + right_all) // 2
        center_y = (top_all + bottom_all) // 2
        key_meta = (jnp.arange(seq_all), center_x, center_y, seg_all)
        first_tok = my_tile * tok_rows
        query_meta = tuple(
            (lax.dynamic_slice_in_dim(member, first_tok, tok_rows, 0) for member in key_meta)
        )
        key_block = math.gcd(seq_all, 1024)
        block_count = seq_all // key_block

        def key_slice(block_id):
            first_key = block_id * key_block
            keys_blk = lax.dynamic_slice_in_dim(key_all, first_key, key_block, 1)
            values_blk = lax.dynamic_slice_in_dim(value_all, first_key, key_block, 1)
            meta_blk = tuple(
                (lax.dynamic_slice_in_dim(member, first_key, key_block, 0) for member in key_meta)
            )
            return (keys_blk, values_blk, meta_blk)

        def stats_step(running, block_id):
            run_max, run_sum = running
            keys_blk, values_blk, meta_blk = key_slice(block_id)
            scores, allowed, one_hot = block_scores(
                query_heads, keys_blk, query_meta, meta_blk, bias_table, score_scale
            )
            scores = jnp.where(allowed[None], scores, neg_large)
            new_max = jnp.maximum(run_max, jnp.max(scores, axis=-1))
            run_sum = run_sum * jnp.exp(run_max - new_max) + jnp.sum(
                jnp.exp(scores - new_max[..., None]), axis=-1
            )
            return ((new_max, run_sum), None)

        start_stats = (
            jnp.full((HEADS, tok_rows), neg_large, jnp.float32),
            jnp.zeros((HEADS, tok_rows), jnp.float32),
        )
        (run_max, run_sum), _ = lax.scan(stats_step, start_stats, jnp.arange(block_count))
        log_total = run_max + jnp.log(run_sum)

        def out_step(attn_acc, block_id):
            keys_blk, values_blk, meta_blk = key_slice(block_id)
            scores, allowed, one_hot = block_scores(
                query_heads, keys_blk, query_meta, meta_blk, bias_table, score_scale
            )
            attn_prob = jnp.where(allowed[None], jnp.exp(scores - log_total[..., None]), 0.0)
            attn_acc = attn_acc + jnp.einsum(
                "hqk,hkd->hqd",
                attn_prob.astype(jnp.bfloat16),
                values_blk,
                preferred_element_type=jnp.float32,
            )
            return (attn_acc, None)

        attn_heads, _ = lax.scan(
            out_step, jnp.zeros((HEADS, tok_rows, HD), jnp.float32), jnp.arange(block_count)
        )
        attn_low = from_heads(attn_heads).astype(jnp.bfloat16)
        mixed_rows = residual + jnp.dot(attn_low, w_output, preferred_element_type=jnp.float32)
        gain_two = gain_ffn.astype(jnp.float32)
        ffn_low = rms_scale(mixed_rows, gain_two).astype(jnp.bfloat16)
        pre_ffn = jnp.dot(ffn_low, ffn_in, preferred_element_type=jnp.float32)
        act_low = jax.nn.gelu(pre_ffn).astype(jnp.bfloat16)
        result_rows = mixed_rows + jnp.dot(act_low, ffn_out, preferred_element_type=jnp.float32)
        upstream = cotangent[0]
        grad_ffn_out = jnp.einsum("tf,td->fd", act_low, upstream, preferred_element_type=jnp.float32)
        d_act = jnp.einsum("td,fd->tf", upstream, ffn_out, preferred_element_type=jnp.float32)
        d_pre = gelu_back(pre_ffn, d_act).astype(jnp.bfloat16)
        grad_ffn_in = jnp.einsum("td,tf->df", ffn_low, d_pre, preferred_element_type=jnp.float32)
        d_ffn_norm = jnp.einsum("tf,df->td", d_pre, ffn_in, preferred_element_type=jnp.float32)
        d_mixed_norm, grad_gain_ffn = jax.vjp(rms_scale, mixed_rows, gain_two)[1](d_ffn_norm)
        d_mixed = upstream.astype(jnp.float32) + d_mixed_norm
        d_mixed_low = d_mixed.astype(jnp.bfloat16)
        grad_output = jnp.einsum("tc,td->cd", attn_low, d_mixed_low, preferred_element_type=jnp.float32)
        d_attn = jnp.einsum(
            "td,cd->tc", d_mixed_low, w_output, preferred_element_type=jnp.float32
        ).astype(jnp.bfloat16)
        dout_heads = to_heads(d_attn)
        row_delta = jnp.sum(dout_heads.astype(jnp.float32) * attn_heads, axis=-1)

        def back_step(running, block_id):
            keys_blk, values_blk, meta_blk = key_slice(block_id)
            scores, allowed, one_hot = block_scores(
                query_heads, keys_blk, query_meta, meta_blk, bias_table, score_scale
            )
            attn_prob = jnp.where(allowed[None], jnp.exp(scores - log_total[..., None]), 0.0)
            d_prob = jnp.einsum(
                "hqd,hkd->hqk", dout_heads, values_blk, preferred_element_type=jnp.float32
            )
            d_score = (attn_prob * (d_prob - row_delta[..., None])).astype(jnp.bfloat16)
            query_acc = running[0] + jnp.einsum(
                "hqk,hkd->hqd", d_score, keys_blk, preferred_element_type=jnp.float32
            )
            table_acc = running[1] + jnp.einsum(
                "hqk,qkn->hn", d_score, one_hot, preferred_element_type=jnp.float32
            )
            first_key = block_id * key_block
            key_part = (
                jnp.einsum("hqk,hqd->hkd", d_score, query_heads, preferred_element_type=jnp.float32)
                * score_scale
            )
            value_part = jnp.einsum(
                "hqk,hqd->hkd",
                attn_prob.astype(jnp.bfloat16),
                dout_heads,
                preferred_element_type=jnp.float32,
            )
            key_acc = lax.dynamic_update_slice_in_dim(running[2], key_part, first_key, 1)
            value_acc = lax.dynamic_update_slice_in_dim(running[3], value_part, first_key, 1)
            return ((query_acc, table_acc, key_acc, value_acc), None)

        start_back = (
            jnp.zeros((HEADS, tok_rows, HD), jnp.float32),
            jnp.zeros((HEADS, 3 * NB), jnp.float32),
        )
        start_back = start_back + (
            jnp.zeros((HEADS, seq_all, HD), jnp.float32),
            jnp.zeros((HEADS, seq_all, HD), jnp.float32),
        )
        back_out, _ = lax.scan(back_step, start_back, jnp.arange(block_count))
        query_acc = back_out[0]
        grad_bias_table = back_out[1]
        key_grad, value_grad = (
            lax.psum_scatter(back_out[2], "tile", scatter_dimension=1, tiled=True),
            lax.psum_scatter(back_out[3], "tile", scatter_dimension=1, tiled=True),
        )
        dq_low = from_heads(query_acc * score_scale).astype(jnp.bfloat16)
        dk_low = from_heads(key_grad).astype(jnp.bfloat16)
        dv_low = from_heads(value_grad).astype(jnp.bfloat16)
        grad_query = jnp.einsum("td,te->de", normed_low, dq_low, preferred_element_type=jnp.float32)
        grad_key = jnp.einsum("td,te->de", normed_low, dk_low, preferred_element_type=jnp.float32)
        grad_value = jnp.einsum("td,te->de", normed_low, dv_low, preferred_element_type=jnp.float32)
        d_normed = (
            jnp.einsum("te,de->td", dq_low, w_query, preferred_element_type=jnp.float32)
            + jnp.einsum("te,de->td", dk_low, w_key, preferred_element_type=jnp.float32)
            + jnp.einsum("te,de->td", dv_low, w_value, preferred_element_type=jnp.float32)
        )
        d_resid_norm, grad_gain_attn = jax.vjp(rms_scale, residual, gain_one)[1](d_normed)
        d_residual = d_mixed + d_resid_norm
        d_resid_low = d_residual.astype(jnp.bfloat16)
        grad_roi_proj = jnp.einsum(
            "tp,td->pd", pooled_low, d_resid_low, preferred_element_type=jnp.float32
        )
        d_pooled = jnp.einsum("td,pd->tp", d_resid_low, roi_proj, preferred_element_type=jnp.float32)
        d_pooled = d_pooled.astype(jnp.bfloat16)
        result_low = result_rows.astype(jnp.bfloat16)
        mixer_table = jnp.concatenate([grad_ffn_out, below(grad_ffn_in, 4), grad_output], axis=0)
        mixer_table = mixer_table.astype(jnp.bfloat16)
        chart = grad_bias_table.reshape(HEADS, 3, NB).transpose(2, 0, 1).reshape(NB, 3 * HEADS)
        embed_table = jnp.concatenate(
            [
                grad_query,
                grad_key,
                grad_value,
                grad_roi_proj,
                jnp.pad(jnp.stack([grad_gain_attn, grad_gain_ffn]), ((0, 14), (0, 0))),
                jnp.pad(chart, ((0, 80), (0, model_width - 3 * HEADS))),
            ],
            axis=0,
        ).astype(jnp.bfloat16)
    d_pooled_all = gathered(d_pooled).reshape(seq_all, -1)
    d_features, low_zero_up, box_token = run_unpool(
        ids,
        ordering,
        box_rows,
        d_pooled_all,
        pre_up_edges[0],
        pre_up_zero,
        pre_up_edges[1],
        256,
    )
    if heads_first:
        embed_halves = halved(embed_halves, 1, box_token)
        ordering = embed_halves[2:]
    d_dec_one, d_dec_two, d_dec_three, low_one_up, low_two_up, up_token = run_up_back(
        ids,
        ordering,
        low_zero_up,
        pre_up_one,
        pre_up_two,
        lined_back(up_first),
        lined_back(up_second),
        up_third,
    )
    d_dec_three_all = windowed(d_dec_three)
    if heads_first:
        embed_halves = halved(embed_halves, 2, up_token)
        ordering = embed_halves[2:]
    grad_up_first = run_grad_up_first(ids, (up_token, *ordering), dec_one, low_zero_up)
    if heads_first:
        embed_halves = halved(embed_halves, 3)
        ordering = embed_halves[2:]
    light_early, early_token = run_grad_up(
        ids, ordering, grad_up_first, dec_two, low_one_up, u_three, low_two_up
    )
    low_three_up, low_four, low_three, d_pool_three, bottom_token = run_bottom_back(
        cut,
        ids,
        (early_token,),
        d_dec_three_all,
        pre_up_three,
        pre_four,
        pre_three,
        up_fourth,
        down_fifth,
        down_fourth,
    )
    dp_count = lax.axis_size(PAGES)
    if heads_first:
        embed_share = halved(embed_halves, 4, bottom_token)
        early_parts = lax.all_to_all(
            light_early.reshape(32, -1, 256), (*PAGES, "tile"), 0, 0, tiled=True
        )
        early_share, _ = run_total(ids, early_parts)
        ordering = ()
    bottom_parts = (low_three_up, e_four, low_four, p_four, low_three, p_three_all)
    if cut:
        heavy = run_grad_bottom_all(ids, *bottom_parts)
        heavy_token = ()
    else:
        heavy, *heavy_token = run_grad_bottom(tile_count, dp_count, ids, ordering, *bottom_parts)
    low_two, low_one, low_zero = run_down_back(
        ids,
        heavy_token,
        d_pool_three,
        d_dec_two,
        pre_two,
        d_dec_one,
        pre_one,
        d_features,
        pre_zero,
        down_third,
        lined_back(down_second),
    )
    light_late = run_grad_down(ids, p_two, low_two, p_one, low_one, page_own, low_zero)
    both_axes = (*PAGES, "tile")
    device_total = dp_count * tile_count

    def summed_share(table):
        parts = table.reshape(device_total, -1, table.shape[1])
        parts = lax.all_to_all(parts, both_axes, 0, 0, tiled=True)
        return jnp.sum(parts.astype(jnp.float32), axis=0).astype(jnp.bfloat16)

    def spread_out(share):
        copies = jnp.broadcast_to(share[None], (device_total, *share.shape))
        return lax.all_to_all(copies, both_axes, 0, 0, tiled=True)

    late = spread_out(summed_share(light_late)).reshape(light_late.shape).astype(jnp.float32)
    wide = ffn_in.shape[1]
    if heads_first:
        parts = lax.all_to_all(heavy, PAGES, 0, 0, tiled=True)
        share = run_gather(ids, parts, mixer_share, embed_share, early_share)
        whole = lax.all_gather(share, both_axes, axis=0)
        *heavy_sums, sum_ffn_out, sum_ffn_in, sum_output, sum_query, sum_key, sum_value, rest, early = (
            run_unpack(whole)
        )
        rest = rest.reshape(NB, 16, model_width)
        sum_roi = rest[:, :4].reshape(-1, model_width)
        sum_bias = rest[:, 4, : 3 * HEADS].reshape(NB, HEADS, 3)
        sum_gain_attn, sum_gain_ffn = rest[0, 5], rest[0, 6]
    else:
        early = spread_out(summed_share(light_early)).reshape(light_early.shape)
        early = early.astype(jnp.float32)
        heavy_sums = [lax.psum(member, both_axes).astype(jnp.float32) for member in heavy]
        mixer_all = lax.psum(mixer_table, both_axes).astype(jnp.float32)
        embed_all = lax.psum(embed_table, both_axes).astype(jnp.float32)
        sum_ffn_out = mixer_all[:wide]
        sum_ffn_in = beside(mixer_all[wide : 2 * wide], wide // model_width)
        sum_output = mixer_all[2 * wide :]
        sum_query, sum_key, sum_value = (
            embed_all[n * model_width : (n + 1) * model_width] for n in range(3)
        )
        last = 3 * model_width + roi_proj.shape[0]
        sum_roi = embed_all[3 * model_width : last]
        sum_bias = embed_all[last + 16 : last + 16 + NB, : 3 * HEADS].reshape(NB, HEADS, 3)
        sum_gain_attn, sum_gain_ffn = embed_all[last], embed_all[last + 1]
    sum_bias = sum_bias.transpose(1, 2, 0).reshape(bias_table.shape)

    def unlined(table, kind):
        return table.reshape(3, kind.shape[2], 3, kind.shape[3]).transpose(0, 2, 1, 3)

    second_rest = below(early[1344:1440], 2)
    sum_up_second = jnp.concatenate([early[1152:1344], second_rest], axis=1)
    sum_down_second = jnp.concatenate([late[384:480, :96], late[384:480, 128:224]], axis=0)
    sum_first = late[480:512, :72].reshape(32, 3, 3, 8)[..., :3].transpose(1, 2, 0, 3)
    summed = [
        sum_first,
        unlined(sum_down_second, down_second),
        unlined(late[:384, :192], down_third),
        heavy_sums[2].reshape(down_fourth.shape),
        heavy_sums[1].reshape(down_fifth.shape),
        heavy_sums[0].reshape(up_fourth.shape),
        early[:1152].reshape(up_third.shape),
        unlined(sum_up_second, up_second),
        unlined(early[1440:1536, :192], up_first),
        sum_roi,
        sum_gain_attn,
        sum_query,
        sum_key,
        sum_value,
        sum_output,
        sum_bias,
        sum_gain_ffn,
        sum_ffn_in,
        sum_ffn_out,
    ]
    return (
        result_low[None],
        d_residual[None],
        summed[0],
        summed[1],
        summed[2],
        summed[3],
        summed[4],
        summed[5],
        summed[6],
        summed[7],
        summed[8],
        summed[9],
        summed[10],
        summed[11],
        summed[12],
        summed[13],
        summed[14],
        summed[15],
        summed[16],
        summed[17],
        summed[18],
    )


def solution(mesh):
    tiles = mesh.shape["tile"]
    split = Mesh(mesh.devices.reshape(mesh.shape["dp"] // 2, 2, tiles), (*PAGES, "tile"))
    return jax.shard_map(
        on_device,
        mesh=split,
        in_specs=(
            P(PAGES, "tile", None),
            P(PAGES, None, "tile", None),
            P(None, PAGES, "tile"),
            P(PAGES, "tile"),
            P(),
            P(),
            P(),
            P(),
            P(),
            P(),
            P(),
            P(),
            P(),
            P(),
            P(),
            P(),
            P(),
            P(),
            P(),
            P(),
            P(),
            P(),
            P(),
            P(PAGES, "tile", None),
        ),
        out_specs=(
            P(PAGES, "tile", None),
            P(PAGES, "tile", None),
            P(),
            P(),
            P(),
            P(),
            P(),
            P(),
            P(),
            P(),
            P(),
            P(),
            P(),
            P(),
            P(),
            P(),
            P(),
            P(),
            P(),
            P(),
            P(),
        ),
        check_vma=False,
    )
```

```python
import functools
import math

import jax
import jax.numpy as jnp
from jax import lax
from jax.experimental import pallas as pl
from jax.experimental.pallas import tpu as pltpu
from jax.sharding import Mesh
from jax.sharding import PartitionSpec as P

HEADS = 8
HD = 64
NB = 32

eps = 1e-06
bounds = (12, 16, 23, 32, 46, 64, 91)
neg_large = -1000000000.0
HOPS = (("core", 1), ("x", 1), ("tile", 1), ("tile", 4), ("tile", 2))
PAGES = ("x", "core")
f32 = jnp.float32
bf16 = jnp.bfloat16
gelu_scale = math.sqrt(2.0 / math.pi)
VMEM_CAP = 40 * 1024 * 1024


def gelu_of(x):
    x = x.astype(f32)
    half = 0.5 * x
    inner = x * (gelu_scale + (gelu_scale * 0.044715) * (x * x))
    return half + half * jnp.tanh(inner)


def gelu_slope(x):
    x = x.astype(f32)
    sq = x * x
    bent = jnp.tanh(x * (gelu_scale + (gelu_scale * 0.044715) * sq))
    rise = gelu_scale + (3.0 * gelu_scale * 0.044715) * sq
    return 0.5 + 0.5 * bent + (0.5 * x) * (1.0 - bent * bent) * rise


def mm(a, b):
    return jnp.dot(a, b, preferred_element_type=f32)


def mm_tn(a, b):
    return lax.dot_general(a, b, (((0,), (0,)), ((), ())), preferred_element_type=f32)


def mm_nt(a, b):
    return lax.dot_general(a, b, (((1,), (1,)), ((), ())), preferred_element_type=f32)


def mm_fine(a, b):
    high = a.astype(bf16)
    low = (a - high.astype(f32)).astype(bf16)
    return mm(high, b) + mm(low, b)


def lane_ids(shape):
    return lax.broadcasted_iota(jnp.int32, shape, len(shape) - 1)


def row_ids_of(shape):
    return lax.broadcasted_iota(jnp.int32, shape, len(shape) - 2)


def halving(wide, value):
    hit = row_ids_of((wide, wide // 2)) >> 1 == lane_ids((wide, wide // 2))
    return jnp.where(hit, value, 0.0).astype(bf16)


def doubling(narrow):
    hit = row_ids_of((narrow, 2 * narrow)) == lane_ids((narrow, 2 * narrow)) >> 1
    return jnp.where(hit, 1.0, 0.0).astype(bf16)


def pair_halving(value):
    shape = (256, 128)
    source = row_ids_of(shape)
    target = lane_ids(shape)
    hit = source >> 1 == target
    return jnp.where(hit, value, 0.0).astype(bf16)


def side_doubling(side):
    shape = (128, 128)
    hit = row_ids_of(shape) == (lane_ids(shape) >> 1) + 64 * side
    return jnp.where(hit, 1.0, 0.0).astype(bf16)


def quad_map(coarse_lanes, coarse_width):
    shape = (coarse_lanes, 4 * coarse_lanes)
    fine = lane_ids((1, shape[1]))
    shift = coarse_width.bit_length() - 1
    home = (fine >> (shift + 2) << shift) + ((fine & (2 * coarse_width - 1)) >> 1)
    return jnp.where(row_ids_of(shape) == home, 1.0, 0.0).astype(bf16)


def masked(x, keep):
    return x * jnp.where(keep, 1.0, 0.0).astype(x.dtype)


def col_shift(x, step, width):
    if step == 0:
        return x
    lanes = x.shape[1]
    col = lane_ids((1, lanes)) & (width - 1)
    keep = col < width - 1 if step > 0 else col > 0
    return masked(pltpu.roll(x, -step % lanes, 1), keep)


def row_shift(x, step, width):
    if step == 0:
        return x
    lanes = x.shape[1]
    lane = lane_ids((1, lanes))
    keep = lane < lanes - width if step > 0 else lane >= width
    return masked(pltpu.roll(x, (-step * width) % lanes, 1), keep)


def stack_cols(x, width):
    return jnp.concatenate([col_shift(x, step, width) for step in (-1, 0, 1)], axis=0)


def row_ok(first_row, rows, width, low, high):
    row = (lane_ids((1, rows * width)) >> (width.bit_length() - 1)) + first_row
    return (row >= low) & (row < high)


def keep_rows(x, first_row, width, high):
    ok = row_ok(first_row, x.shape[1] // width, width, 0, high)
    return jnp.where(ok, x, 0.0)


def price(micros):
    return pl.CostEstimate(
        flops=int(micros * 5e8), transcendentals=0, bytes_accessed=int(micros * 2e6)
    )


class Fetched:
    def __init__(self, ref, copy):
        self.ref, self.copy, self.waited = ref, copy, False
        self.shape = ref.shape
        copy.start()

    def ready(self):
        if not self.waited:
            self.copy.wait()
            self.waited = True
        return self.ref

    def __getitem__(self, spot):
        return self.ready()[spot]


class Sent:
    def __init__(self, ref, copy):
        self.ref, self.copy, self.started = ref, copy, False
        self.shape = ref.shape

    def send(self):
        if not self.started:
            self.copy.start()
            self.started = True

    def __getitem__(self, spot):
        return self.ref[spot]

    def __setitem__(self, spot, value):
        self.ref[spot] = value


def in_hbm(array):
    return pltpu.with_memory_space_constraint(array, pltpu.HBM)


TOKEN = ((8, 128), f32)


def call(micros, body, outs, scratch, ids, arrays, after=(), late=(), sent=(), table=None):
    count = len(arrays)
    moved = [(arrays[n].shape, arrays[n].dtype) for n in late] + [outs[n] for n in sent]
    arrays = [in_hbm(array) if n in late else array for n, array in enumerate(arrays)]
    after = [in_hbm(token) for token in after]

    scalars = (ids,) if table is None else (ids, table)

    def ordered(*refs):
        refs, heads = refs[len(scalars) :], refs[: len(scalars)]
        ins = list(refs[:count])
        refs = refs[count + len(after) :]
        results = list(refs[: len(outs)])
        own = refs[len(outs) : len(outs) + len(scratch)]
        if moved:
            *stages, marks = refs[len(outs) + len(scratch) :]
        for k, n in enumerate(late):
            ins[n] = Fetched(stages[k], pltpu.make_async_copy(ins[n], stages[k], marks.at[k]))
        for k, n in enumerate(sent, len(late)):
            copy = pltpu.make_async_copy(stages[k], results[n], marks.at[k])
            results[n] = Sent(stages[k], copy)
        body(*heads, *ins, *results, *own)
        for n in late:
            ins[n].ready()
        for n in sent:
            results[n].send()
        for n in sent:
            results[n].copy.wait()

    def place(chosen, total):
        return [
            pl.BlockSpec(memory_space=pltpu.HBM if n in chosen else pltpu.VMEM) for n in range(total)
        ]

    return pl.pallas_call(
        ordered,
        cost_estimate=price(micros),
        out_shape=[
            pltpu.HBM(*out) if n in sent or out == TOKEN else jax.ShapeDtypeStruct(*out)
            for n, out in enumerate(outs)
        ],
        in_specs=[pl.BlockSpec(memory_space=pltpu.SMEM)] * len(scalars)
        + place(late, count)
        + [pl.BlockSpec(memory_space=pltpu.HBM) for _ in after],
        out_specs=place([n for n, out in enumerate(outs) if n in sent or out == TOKEN], len(outs)),
        scratch_shapes=[pltpu.VMEM(shape, kind) for shape, kind in scratch]
        + [pltpu.VMEM(shape, kind) for shape, kind in moved]
        + ([pltpu.SemaphoreType.DMA((len(moved),))] if moved else []),
        compiler_params=pltpu.CompilerParams(vmem_limit_bytes=VMEM_CAP),
    )(*scalars, *arrays, *after)


def lanes_at(start, size):
    return pl.ds(pl.multiple_of(start, 128), size)


def down_body(ids, pages, w_zero, w_one, w_two, pre_zero, pre_one, p_one, pre_two, p_two, p_three, page_own, page, cols, pool_one, stack_one, pool_two):
    tile, high, at = ids[0], ids[1], ids[4]
    page[...] = jnp.zeros_like(page)
    for side in range(-2, 3):
        block = at + side

        @pl.when((block >= 0) & (block < pages.shape[0]))
        def _(block=block, side=side):
            lines = pages[block, :, 0:1024].astype(f32)
            for g in range(8):
                first = (2 + side) * 8192 + 1024 * g
                for c in range(3):
                    page[c : c + 1, first : first + 1024] = lines[8 * c + g : 8 * c + g + 1, :]

    page_full = page[:, 11 * 512 : 69 * 512]
    page_own[...] = page_full[:, 20 * 512 : 38 * 512].astype(bf16)
    for j in range(3):
        cols[j] = col_shift(page_full, j - 1, 512)
    halve = halving(512, 0.25)

    def top(k, keep_pre):
        pieces = [
            cols[j, :, lanes_at((4 * k + i) * 512, 2048)] for i in range(3) for j in range(3)
        ]
        pre = mm(w_zero[...], jnp.concatenate(pieces, axis=0).astype(bf16))
        if keep_pre:
            pre_zero[:, lanes_at((k - 5) * 2048, 2048)] = pre.astype(bf16)
        enc = gelu_of(pre)
        pairs = jnp.concatenate(
            [enc[:, :512] + enc[:, 512:1024], enc[:, 1024:1536] + enc[:, 1536:]], axis=0
        )
        pooled = mm_fine(pairs, halve)
        first = tile * 8 - 10 + 2 * k
        for n in range(2):
            ok = (first + n >= 0) & (first + n < high // 2)
            part = jnp.where(ok, pooled[32 * n : 32 * n + 32], 0.0)
            pool_one[:, lanes_at((2 * k + n) * 256, 256)] = part.astype(bf16)

    for low, end, keep_pre in ((0, 5, False), (5, 9, True), (9, 14, False)):

        @pl.loop(low, end)
        def _(k, keep_pre=keep_pre):
            top(k, keep_pre)

    pre_zero.send()
    page_own.send()
    p_one[...] = pool_one[:, 9 * 256 : 19 * 256]
    p_one.send()
    stack_one[...] = stack_cols(pool_one[...], 256)
    halve_one = halving(256, 0.25)

    @pl.loop(0, 6)
    def _(k):
        pre = sum(
            mm(w_one[i], stack_one[:, lanes_at((4 * k + 1 + i) * 256, 1024)]) for i in range(3)
        )

        @pl.when((k >= 1) & (k < 5))
        def _():
            pre_one[:, lanes_at((k - 1) * 1024, 1024)] = pre.astype(bf16)

        enc = gelu_of(pre)
        pairs = jnp.concatenate(
            [enc[:, :256] + enc[:, 256:512], enc[:, 512:768] + enc[:, 768:]], axis=0
        )
        pooled = mm_fine(pairs, halve_one)
        first = tile * 4 - 4 + 2 * k
        for n in range(2):
            ok = (first + n >= 0) & (first + n < high // 4)
            part = jnp.where(ok, pooled[64 * n : 64 * n + 64], 0.0)
            pool_two[:, lanes_at((2 * k + n) * 128, 128)] = part.astype(bf16)

    pre_one.send()
    p_two[...] = pool_two[:, 3 * 128 : 9 * 128]
    p_two.send()
    stacked = stack_cols(pool_two[...], 128)
    pre = sum(mm(w_two[i], stacked[:, i * 128 : i * 128 + 1280]) for i in range(3))
    pre_two[...] = pre.astype(bf16)
    pre_two.send()
    enc = gelu_of(pre[:, 384:896])
    pairs = jnp.concatenate([enc[:, :128] + enc[:, 128:256], enc[:, 256:384] + enc[:, 384:]], axis=1)
    p_three[...] = mm_fine(pairs, pair_halving(0.25)).astype(bf16)


def run_down(ids, pages, w_zero, w_one, w_two):
    return call(
        10,
        down_body,
        [
            ((32, 16 * 512), bf16),
            ((64, 16 * 256), bf16),
            ((32, 10 * 256), bf16),
            ((128, 10 * 128), bf16),
            ((64, 6 * 128), bf16),
            ((128, 128), bf16),
            ((8, 18 * 512), bf16),
        ],
        [
            ((8, 80 * 512), f32),
            ((3, 8, 58 * 512), f32),
            ((32, 28 * 256), bf16),
            ((96, 28 * 256), bf16),
            ((64, 12 * 128), bf16),
        ],
        ids,
        (pages, w_zero, w_one, w_two),
        sent=(0, 1, 2, 3, 4, 6),
    )


def conv_taps(x, weight, width):
    lines = [row_shift(x, i - 1, width) for i in range(3)]
    taps = [col_shift(line, j - 1, width) for line in lines for j in range(3)]
    joined = jnp.concatenate([weight[i, j] for i in range(3) for j in range(3)], axis=1)
    return mm(joined, jnp.concatenate(taps, axis=0))


def conv_taps_back(x, weight, width):
    total = None
    for i in range(3):
        lined = row_shift(x, i - 1, width)
        for j in range(3):
            term = mm_tn(weight[2 - i, 2 - j], col_shift(lined, j - 1, width))
            total = term if total is None else total + term
    return total


def conv_rows(x, weight, width, lanes):
    moved = [col_shift(x, j - 1, width) for j in range(3)]
    taps = [moved[j][:, i * width : i * width + lanes] for i in range(3) for j in range(3)]
    joined = jnp.concatenate([weight[i, j] for i in range(3) for j in range(3)], axis=1)
    return mm(joined, jnp.concatenate(taps, axis=0))


def conv_rows_back(x, weight, width, lanes):
    moved = [col_shift(x, j - 1, width) for j in range(3)]
    taps = [moved[2 - j][:, (2 - i) * width : (2 - i) * width + lanes] for i in range(3) for j in range(3)]
    joined = jnp.concatenate([weight[i, j] for i in range(3) for j in range(3)], axis=0)
    return mm_tn(joined, jnp.concatenate(taps, axis=0))


def laid_out(blocks):
    return jnp.concatenate([blocks[n] for n in range(blocks.shape[0])], axis=1)


def bottom_body(cut, ids, p_three, w_three, w_four, w_up, pre_three, pre_four, p_four, e_four, pre_up, dec_three):
    lanes = 128 * p_three.shape[0]
    first, high = ids[3], ids[1]

    def kept(x, width, shrink):
        return keep_rows(x, first * (16 // shrink), width, high // shrink) if cut else x

    pre = conv_taps(laid_out(p_three), w_three, 64)
    pre_three[...] = pre.astype(bf16)
    pre_three.send()
    enc_three = kept(gelu_of(pre), 64, 8)
    spread = quad_map(lanes // 4, 32)
    high_part = enc_three.astype(bf16)
    low_part = (enc_three - high_part.astype(f32)).astype(bf16)
    pooled = ((mm_nt(high_part, spread) + mm_nt(low_part, spread)) * 0.25).astype(bf16)
    p_four[...] = pooled
    p_four.send()
    pre = conv_taps(pooled, w_four, 32)
    pre_four[...] = pre.astype(bf16)
    pre_four.send()
    low = kept(gelu_of(pre), 32, 16).astype(bf16)
    e_four[...] = low
    e_four.send()
    pre = conv_taps(mm(low, spread).astype(bf16), w_up, 64)
    pre_up[...] = pre.astype(bf16)
    pre_up.send()
    dec = kept(gelu_of(pre) + enc_three, 64, 8).astype(bf16)
    zero = jnp.zeros((256, 128), bf16)
    dec_three[:, 0:128] = zero
    dec_three[:, 128 : 128 + lanes] = dec
    dec_three[:, 128 + lanes :] = zero


def run_bottom(cut, ids, p_three, w_three, w_four, w_up):
    lanes = 128 * p_three.shape[0]
    return call(
        11,
        functools.partial(bottom_body, cut),
        [
            ((256, lanes), bf16),
            ((512, lanes // 4), bf16),
            ((256, lanes // 4), bf16),
            ((512, lanes // 4), bf16),
            ((256, lanes), bf16),
            ((256, lanes + 256), bf16),
        ],
        [],
        ids,
        (p_three, w_three, w_four, w_up),
        late=(2, 3),
        sent=(0, 1, 2, 3, 4),
    )


def widened(block):
    parts = []
    for n in range(block.shape[1] // 128):
        piece = block[:, 128 * n : 128 * n + 128]
        for side in range(2):
            line = mm(piece, side_doubling(side)).astype(bf16)
            parts += [line, line]
    return jnp.concatenate(parts, axis=1)


def spread_rows(source, target, width):
    spread = doubling(width)
    for n in range(source.shape[1] // width):
        line = mm(source[:, n * width : n * width + width], spread).astype(bf16)
        for m in range(2):
            target[:, (2 * n + m) * 2 * width : (2 * n + m + 1) * 2 * width] = line


def up_body(ids, dec_three, pre_two, pre_one, pre_zero, w_third, w_second, w_first, pre_up_two, pre_up_one, pre_up_zero, u_three, dec_two, dec_one, features, edge_end, edge_start, wide_two, stack_two, wide_one, stack_one):
    tile, high, place = ids[0], ids[1], ids[2]
    block = dec_three[:, lanes_at(place * 128, 384)]
    wide = widened(block)
    u_three[...] = wide[:, 384 : 384 + 768]
    u_three.send()
    total = conv_rows(wide, w_third, 128, 1280)
    pre_up_two[...] = total.astype(bf16)
    pre_up_two.send()
    dec = gelu_of(total) + gelu_of(pre_two[...])
    dec = keep_rows(dec, tile * 4 - 3, 128, high // 4).astype(bf16)
    dec_two[...] = dec[:, 128 : 128 + 1024]
    dec_two.send()
    spread_rows(dec, wide_two, 128)
    stack_two[...] = stack_cols(wide_two[...], 256)
    for k in range(3):
        pre = sum(
            mm(w_second[i], stack_two[:, (6 * k + i) * 256 : (6 * k + i) * 256 + 1536])
            for i in range(3)
        )
        pre_up_one[:, 1536 * k : 1536 * k + 1536] = pre.astype(bf16)
    pre_up_one.send()
    dec = gelu_of(pre_up_one[:, 4 * 256 : 14 * 256]) + gelu_of(pre_one[:, 3 * 256 : 13 * 256])
    dec = keep_rows(dec, tile * 8 - 1, 256, high // 2).astype(bf16)
    dec_one[...] = dec
    dec_one.send()
    spread_rows(dec, wide_one, 256)
    stack_one[...] = stack_cols(wide_one[...], 512)
    pre_zero.ready()

    @pl.loop(0, 4)
    def _(k):
        pre = sum(
            mm(w_first[i], stack_one[:, lanes_at((4 * k + 1 + i) * 512, 2048)]) for i in range(3)
        )
        own = lanes_at(k * 2048, 2048)
        pre_up_zero[:, own] = pre.astype(bf16)
        found = (gelu_of(pre) + gelu_of(pre_zero[:, own])).astype(bf16)
        for n in range(4):
            features[pl.ds(pl.multiple_of((4 * k + n) * 32, 32), 32), :] = found[
                :, 512 * n : 512 * n + 512
            ]

    edge_end[...] = pre_up_zero[:, 5 * 512 : 16 * 512]
    edge_start[...] = pre_up_zero[:, 0 : 11 * 512]


def run_up(ids, dec_three, pre_two, pre_one, pre_zero, w_third, w_second, w_first):
    return call(
        9,
        up_body,
        [
            ((128, 10 * 128), bf16),
            ((64, 18 * 256), bf16),
            ((32, 16 * 512), bf16),
            ((256, 6 * 128), bf16),
            ((128, 8 * 128), bf16),
            ((64, 10 * 256), bf16),
            ((16 * 32, 512), bf16),
            ((32, 11 * 512), bf16),
            ((32, 11 * 512), bf16),
        ],
        [
            ((128, 20 * 256), bf16),
            ((384, 20 * 256), bf16),
            ((64, 20 * 512), bf16),
            ((192, 20 * 512), bf16),
        ],
        ids,
        (dec_three, pre_two, pre_one, pre_zero, w_third, w_second, w_first),
        late=(1, 2, 3),
        sent=(0, 1, 2, 3, 4, 5),
    )


def band_edges(boxes):
    left, top, right, bottom = (boxes[:, n : n + 1] for n in range(4))
    mid_col = (left + right) >> 1
    mid_row = (top + bottom) >> 1
    return ((left, mid_col, right), (top, mid_row, bottom))


def band_hits(edges, ids_wide, band):
    return (ids_wide >= edges[band]) & (ids_wide < edges[band + 1])


def area_inverse(cols, rows, a, b):
    return 1.0 / ((rows[a + 1] - rows[a]) * (cols[b + 1] - cols[b])).astype(f32)


def pool_body(step, ids, boxes, features, pooled):
    tile = ids[0]
    x_ids = lane_ids((1, 512))
    y_ids = (x_ids >> 5) + tile * 16
    group = lane_ids((1, 128)) >> 5

    @pl.loop(0, boxes.shape[0] // step)
    def _(k):
        own = pl.ds(pl.multiple_of(k * step, step), step)
        cols, rows = band_edges(boxes[own, :])
        result = jnp.zeros((step, 128), f32)
        inside = [jnp.where(band_hits(rows, y_ids, a), 1.0, 0.0) for a in range(2)]
        for b in range(2):
            hits = jnp.where(band_hits(cols, x_ids, b), 1.0, 0.0).astype(bf16)
            lines = mm_nt(hits, features[...])
            for a in range(2):
                part = lines * inside[a]
                part = part[:, :128] + part[:, 128:256] + (part[:, 256:384] + part[:, 384:])
                part = part + pltpu.roll(part, 64, 1)
                part = part + pltpu.roll(part, 32, 1)
                scaled = part * area_inverse(cols, rows, a, b)
                result = jnp.where(group == 2 * a + b, scaled, result)
        pooled[own, :] = result.astype(bf16)


def run_pool(ids, boxes, features, step):
    count = boxes.shape[0]
    return call(
        8, functools.partial(pool_body, step), [((count, 128), bf16)], [], ids, (boxes, features)
    )[0]


def unpool_body(step, ids, boxes, d_pooled, pre_up, d_features, d_low, d_before, d_behind, token, total):
    tile = ids[0]
    lines = 38
    x_ids = lane_ids((1, 512))
    y_ids = (lane_ids((1, lines * 32)) >> 5) + (tile * 16 - 11)
    group = lane_ids((1, 128)) >> 5
    source = row_ids_of((128, lines * 32))
    target = lane_ids((1, lines * 32)) & 31
    copies = [
        jnp.where(source == target + 32 * n, 1.0, 0.0).astype(bf16) for n in range(4)
    ]
    total[...] = jnp.zeros_like(total)

    @pl.loop(0, boxes.shape[0] // step)
    def _(k):
        own = pl.ds(pl.multiple_of(k * step, step), step)
        cols, rows = band_edges(boxes[own, :])
        scale = jnp.zeros((step, 128), f32)
        for a in range(2):
            for b in range(2):
                scale = jnp.where(group == 2 * a + b, area_inverse(cols, rows, a, b), scale)
        share = (d_pooled[own, :].astype(f32) * scale).astype(bf16)
        found = None
        inside = [jnp.where(band_hits(rows, y_ids, a), 1.0, 0.0) for a in range(2)]
        for b in range(2):
            placed = mm(share, copies[b]) * inside[0] + mm(share, copies[2 + b]) * inside[1]
            hits = jnp.where(band_hits(cols, x_ids, b), 1.0, 0.0).astype(bf16)
            term = mm_tn(placed.astype(bf16), hits)
            found = term if found is None else found + term
        total[...] += found

    for y in range(lines):
        line = total[32 * y : 32 * y + 32, :]
        if y < 11:
            d_before[:, 512 * y : 512 * y + 512] = line.astype(bf16)
        elif y < 27:
            own = slice(512 * (y - 11), 512 * (y - 10))
            d_features[:, own] = line
            d_low[:, own] = (line * gelu_slope(pre_up[:, own])).astype(bf16)
        else:
            d_behind[:, 512 * (y - 27) : 512 * (y - 26)] = line.astype(bf16)


def run_unpool(ids, after, boxes, d_pooled, pre_up, step):
    return call(
        14,
        functools.partial(unpool_body, step),
        [
            ((32, 8192), f32),
            ((32, 8192), bf16),
            ((32, 11 * 512), bf16),
            ((32, 11 * 512), bf16),
            TOKEN,
        ],
        [((38 * 32, 512), f32)],
        ids,
        (boxes, d_pooled, pre_up),
        after,
        late=(2,),
        sent=(0,),
    )


def up_back_body(ids, d_before, d_low, d_behind, pre_before, pre_behind, pre_up_one, pre_up_two, wd_first, wd_second, w_third, d_dec_one, d_dec_two, d_dec_three, low_one, low_two, token, stack_zero, wide_low):
    tile, high = ids[0], ids[1]
    reach = 11 * 512
    stack_zero[:, reach : reach + 8192] = stack_cols(d_low[...], 512)
    for first, grad, pre in ((0, d_before, pre_before), (reach + 8192, d_behind, pre_behind)):
        low = (grad[...].astype(f32) * gelu_slope(pre[...])).astype(bf16)
        stack_zero[:, first : first + reach] = stack_cols(low, 512)
    halve = halving(512, 1.0)
    pre_up_one.ready()

    @pl.loop(0, 9)
    def _(k):
        back = sum(
            mm(wd_first[i], stack_zero[:, lanes_at((4 * k + i) * 512, 2048)]) for i in range(3)
        )
        pairs = jnp.concatenate(
            [back[:, :512] + back[:, 512:1024], back[:, 1024:1536] + back[:, 1536:]], axis=0
        )
        summed = mm_fine(pairs, halve)
        first = tile * 8 - 5 + 2 * k
        for n in range(2):
            ok = (first + n >= 0) & (first + n < high // 2)
            own = lanes_at((2 * k + n) * 256, 256)
            part = jnp.where(ok, summed[64 * n : 64 * n + 64], 0.0)
            d_dec_one[:, own] = part
            wide_low[:, own] = (part * gelu_slope(pre_up_one[:, own])).astype(bf16)

    d_dec_one.send()
    low_one[...] = wide_low[:, 5 * 256 : 13 * 256]
    low_one.send()
    stacked = stack_cols(wide_low[...], 256)
    halve_one = halving(256, 1.0)
    for k in range(4):
        back = sum(
            mm(wd_second[i], stacked[:, (4 * k + i) * 256 : (4 * k + i) * 256 + 1024])
            for i in range(3)
        )
        pairs = jnp.concatenate(
            [back[:, :256] + back[:, 256:512], back[:, 512:768] + back[:, 768:]], axis=0
        )
        summed = mm_fine(pairs, halve_one)
        for n in range(2):
            line = 2 * k + n
            row = tile * 4 - 2 + line
            ok = (row >= 0) & (row < high // 4)
            part = jnp.where(ok, summed[128 * n : 128 * n + 128], 0.0)
            d_dec_two[:, 128 * line : 128 * line + 128] = part
    low = d_dec_two[:, 128 : 7 * 128] * gelu_slope(pre_up_two[:, 2 * 128 : 8 * 128])
    low = low.astype(bf16)
    d_dec_two.send()
    low_two[...] = low[:, 128 : 5 * 128]
    low_two.send()
    total = conv_rows_back(low, w_third, 128, 512)
    pairs = jnp.concatenate(
        [total[:, :128] + total[:, 128:256], total[:, 256:384] + total[:, 384:]], axis=1
    )
    d_dec_three[...] = mm_fine(pairs, pair_halving(1.0)).astype(bf16)


def run_up_back(ids, after, d_before, d_low, d_behind, pre_before, pre_behind, pre_up_one, pre_up_two, wd_first, wd_second, w_third):
    return call(
        9,
        up_back_body,
        [
            ((64, 18 * 256), f32),
            ((128, 8 * 128), f32),
            ((256, 128), bf16),
            ((64, 8 * 256), bf16),
            ((128, 4 * 128), bf16),
            TOKEN,
        ],
        [((96, 38 * 512), bf16), ((64, 18 * 256), bf16)],
        ids,
        (
            d_before,
            d_low,
            d_behind,
            pre_before,
            pre_behind,
            pre_up_one,
            pre_up_two,
            wd_first,
            wd_second,
            w_third,
        ),
        after,
        late=(3, 4, 5, 6),
        sent=(0, 1, 3, 4),
    )


def bottom_back_body(cut, ids, d_dec_three, pre_up, pre_four, pre_three, w_up, w_four, w_three, low_up, low_four, low_three, d_pool, token, padded):
    lanes = 128 * d_dec_three.shape[0]
    first, high, place = ids[3], ids[1], ids[2]

    def kept(x, width, shrink):
        return keep_rows(x, first * (16 // shrink), width, high // shrink) if cut else x

    d_dec = laid_out(d_dec_three).astype(f32)
    low = (d_dec * gelu_slope(pre_up[...])).astype(bf16)
    low_up[...] = low
    spread = quad_map(lanes // 4, 32)
    back = conv_taps_back(low, w_up, 64)
    high_part = back.astype(bf16)
    low_part = (back - high_part.astype(f32)).astype(bf16)
    d_enc = kept(mm_nt(high_part, spread) + mm_nt(low_part, spread), 32, 16)
    low = (d_enc * gelu_slope(pre_four[...])).astype(bf16)
    low_four[...] = low
    back = conv_taps_back(low, w_four, 32) * 0.25
    d_enc = kept(d_dec + mm_fine(back, spread), 64, 8)
    low = (d_enc * gelu_slope(pre_three[...])).astype(bf16)
    low_three[...] = low
    zero = jnp.zeros((256, 128), bf16)
    padded[:, 0:128] = zero
    padded[:, 128 : 128 + lanes] = low
    padded[:, 128 + lanes :] = zero
    window = padded[:, lanes_at(place * 128, 384)]
    d_pool[...] = conv_taps_back(window, w_three, 64)[:, 0:384]


def run_bottom_back(cut, ids, after, d_dec_three, pre_up, pre_four, pre_three, w_up, w_four, w_three):
    lanes = 128 * d_dec_three.shape[0]
    return call(
        10,
        functools.partial(bottom_back_body, cut),
        [
            ((256, lanes), bf16),
            ((512, lanes // 4), bf16),
            ((256, lanes), bf16),
            ((128, 384), f32),
            TOKEN,
        ],
        [((256, lanes + 256), bf16)],
        ids,
        (d_dec_three, pre_up, pre_four, pre_three, w_up, w_four, w_three),
        after,
        late=(1, 4, 2, 5, 3, 6),
        sent=(3,),
    )


def down_back_body(ids, d_pool_three, d_dec_two, pre_two, d_dec_one, pre_one, d_features, pre_zero, w_two, wd_one, low_two, low_one, low_zero, wide_one):
    tile, high = ids[0], ids[1]
    d_dec_one.ready()
    pre_one.ready()
    d_features.ready()
    pre_zero.ready()
    quarter = d_pool_three[...] * 0.25
    parts = []
    for n in range(3):
        piece = quarter[:, 128 * n : 128 * n + 128]
        for side in range(2):
            line = mm_fine(piece, side_doubling(side))
            parts += [line, line]
    spread = jnp.concatenate(parts[2:10], axis=1)
    d_enc = keep_rows(d_dec_two[...] + spread, tile * 4 - 2, 128, high // 4)
    low = (d_enc * gelu_slope(pre_two[:, 128 : 9 * 128])).astype(bf16)
    low_two[...] = low[:, 2 * 128 : 6 * 128]
    total = None
    for j in range(3):
        moved = col_shift(low, j - 1, 128)
        for i in range(3):
            term = mm_tn(w_two[2 - i, 2 - j], moved[:, i * 128 : i * 128 + 768])
            total = term if total is None else total + term
    total = total * 0.25
    wide = doubling(128)
    for n in range(6):
        line = mm_fine(total[:, 128 * n : 128 * n + 128], wide)
        for m in range(2):
            row = 2 * n + m
            value = d_dec_one[:, (3 + row) * 256 : (4 + row) * 256] + line
            ok = (tile * 8 - 2 + row >= 0) & (tile * 8 - 2 + row < high // 2)
            value = jnp.where(ok, value, 0.0)
            slope = gelu_slope(pre_one[:, (2 + row) * 256 : (3 + row) * 256])
            wide_one[:, row * 256 : row * 256 + 256] = (value * slope).astype(bf16)
    low_one[...] = wide_one[:, 2 * 256 : 10 * 256]
    stacked = stack_cols(wide_one[...], 256)
    back = sum(mm(wd_one[i], stacked[:, (1 + i) * 256 : (9 + i) * 256]) for i in range(3)) * 0.25
    wider = doubling(256)
    for n in range(8):
        line = mm_fine(back[:, 256 * n : 256 * n + 256], wider)
        for m in range(2):
            own = slice((2 * n + m) * 512, (2 * n + m + 1) * 512)
            value = (d_features[:, own] + line) * gelu_slope(pre_zero[:, own])
            low_zero[:, own] = value.astype(bf16)


def run_down_back(ids, after, *arrays):
    return call(
        4,
        down_back_body,
        [
            ((128, 4 * 128), bf16),
            ((64, 8 * 256), bf16),
            ((32, 16 * 512), bf16),
        ],
        [((64, 12 * 256), bf16)],
        ids,
        arrays,
        after,
        late=(0, 1, 2, 3, 4, 5, 6),
    )


def grad_up_first_body(ids, dec_one, d_low, grad, wide_one, stack_one):
    spread_rows(dec_one[...], wide_one, 256)
    stack_one[...] = stack_cols(wide_one[...], 512)
    for i in range(3):
        grad[i] = mm_nt(d_low[...], stack_one[:, (1 + i) * 512 : (17 + i) * 512])


def run_grad_up_first(ids, after, dec_one, d_low):
    return call(
        4,
        grad_up_first_body,
        [((3, 32, 192), f32)],
        [((64, 20 * 512), bf16), ((192, 20 * 512), bf16)],
        ids,
        (dec_one, d_low),
        after,
        late=(0,),
    )[0]


def grad_up_body(ids, grad_first, dec_two, low_one, u_three, low_two, table, token, wide_two, stack_two):
    spread_rows(dec_two[...], wide_two, 128)
    stack_two[...] = stack_cols(wide_two[...], 256)
    for j in range(3):
        moved = col_shift(u_three[...], j - 1, 128)
        for i in range(3):
            first = (3 * i + j) * 128
            grad = mm_nt(low_two[...], moved[:, i * 128 : i * 128 + 512])
            table[first : first + 128, :] = grad.astype(bf16)
    rest = []
    for i in range(3):
        grad = mm_nt(low_one[...], stack_two[:, (3 + i) * 256 : (11 + i) * 256]).astype(bf16)
        table[1152 + 64 * i : 1216 + 64 * i, :] = grad[:, :256]
        rest.append(grad[:, 256:])
    rest = jnp.concatenate(rest, axis=0)
    table[1344:1440, :] = jnp.concatenate([rest[:96], rest[96:]], axis=1)
    table[1440:1536, :] = jnp.zeros((96, 256), bf16)
    for i in range(3):
        table[1440 + 32 * i : 1472 + 32 * i, 0:192] = grad_first[i].astype(bf16)


def run_grad_up(ids, after, *arrays):
    return call(
        4,
        grad_up_body,
        [((1536, 256), bf16), TOKEN],
        [((128, 16 * 256), bf16), ((384, 16 * 256), bf16)],
        ids,
        arrays,
        after,
        late=(1, 2, 3, 4),
    )


def halve_body(ids, kept, got, mine, other, token):
    half = mine.shape[0]
    for bit in range(2):

        @pl.when(ids[5] == bit)
        def _(bit=bit):
            for out, side in ((mine, bit), (other, 1 - bit)):
                own = slice(half * side, half * side + half)
                out[...] = (kept[own, :].astype(f32) + got[own, :].astype(f32)).astype(bf16)


def run_halve(ids, bit, kept, got, after):
    rows, width = kept.shape
    return call(
        max(1, rows // 1500),
        halve_body,
        [((rows // 2, width), bf16)] * 2 + [TOKEN],
        [],
        ids.at[5].set(bit),
        (kept, got),
        after,
    )


def finish_body(ids, kept, got, share):
    share[...] = (kept[...].astype(f32) + got[...].astype(f32)).astype(bf16)


def total_body(ids, parts, share, token):
    total = parts[0].astype(f32)
    for n in range(1, parts.shape[0]):
        total = total + parts[n].astype(f32)
    half = total.shape[0] // 2
    share[...] = jnp.concatenate([total[:half], total[half:]], axis=1).astype(bf16)


def run_total(ids, parts):
    rows, width = parts.shape[1:]
    outs = [((rows // 2, 2 * width), bf16), TOKEN]
    return call(1, total_body, outs, [], ids, (parts,))


def gather_body(ids, heavy, mixer, embed, early, share):
    rows, width = heavy.shape[1:]
    total = heavy[0].astype(f32)
    for n in range(1, heavy.shape[0]):
        total = total + heavy[n].astype(f32)
    share[0:rows, :] = total.astype(bf16)
    share[rows : rows + 144, :] = mixer[...]
    share[rows + 144 : rows + 208, :] = embed[...]
    pad = jnp.zeros((8, width), f32)
    share[rows + 208 :, :] = jnp.concatenate([early[...].astype(f32), pad], axis=0).astype(bf16)


def run_gather(ids, *arrays):
    rows, width = arrays[0].shape[1:]
    return call(1, gather_body, [((rows + 240, width), bf16)], [], ids, arrays)[0]


def run_finish(ids, kept, got, after):
    return call(1, finish_body, [(kept.shape, bf16)], [], ids, (kept, got), after)[0]


def taps_of(x, width):
    for i in range(3):
        lined = row_shift(x, i - 1, width)
        for j in range(3):
            yield 3 * i + j, col_shift(lined, j - 1, width)


def grad_bottom_body(split, ids, low_up, e_four, low_four, p_four, low_three, p_three, table, token, up_part, four_part, three_part):
    place = ids[2]
    lanes = low_up.shape[1]
    spread = quad_map(lanes // 4, 32)
    shares = table.shape[0]

    def own_part(low):
        rows = low.shape[0] // split
        return low[pl.ds(pl.multiple_of(place * rows, rows), rows), :]

    low = own_part(low_up)
    for tap, x in taps_of(mm(e_four[...], spread).astype(bf16), 64):
        up_part[tap] = mm_nt(low, x)
    low = own_part(low_four)
    for tap, x in taps_of(p_four[...], 32):
        four_part[tap] = mm_nt(low, x)
    low = own_part(low_three)
    for tap, x in taps_of(laid_out(p_three), 64):
        three_part[tap] = mm_nt(low, x)
    for n in range(shares):
        for tap in range(9):
            fifth = jnp.concatenate(
                [
                    four_part[tap, 16 * n : 16 * n + 8, :],
                    four_part[tap, 16 * n + 8 : 16 * n + 16, :],
                ],
                axis=1,
            )
            main = jnp.concatenate([up_part[tap, 8 * n : 8 * n + 8, :], fifth], axis=0)
            table[n, 16 * tap : 16 * tap + 16, :] = main.astype(bf16)
        zero = jnp.zeros((8, 128), f32)
        sides = [three_part[tap, 8 * n : 8 * n + 8, :] for tap in range(9)] + [zero] * 7
        sides = [jnp.concatenate(sides[4 * k : 4 * k + 4], axis=1) for k in range(4)]
        table[n, 144:176, :] = jnp.concatenate(sides, axis=0).astype(bf16)


def run_grad_bottom(split, shares, ids, after, *arrays):
    return call(
        6,
        functools.partial(grad_bottom_body, split),
        [((shares, 176, 512), bf16), TOKEN],
        [
            ((9, 256 // split, 512), f32),
            ((9, 512 // split, 256), f32),
            ((9, 256 // split, 128), f32),
        ],
        ids,
        arrays,
        after,
        late=(1, 3),
    )


def unpack_body(whole, *refs):
    stage, marks = refs[-2:]
    plain = list(refs[:-2])
    step = pl.program_id(0)
    last = pl.num_programs(0) - 1

    def fetch(n):
        return pltpu.make_async_copy(whole.at[n], stage.at[n % 4], marks.at[n % 4])

    @pl.when(step == 0)
    def _():
        for n in range(3):
            fetch(n).start()

    @pl.when(step + 3 <= last)
    def _():
        fetch(step + 3).start()

    fetch(step).wait()
    held = stage.at[step % 4]
    up, fifth, fourth, *plain, early = plain
    for tap in range(9):
        block = held[16 * tap : 16 * tap + 16, :].astype(f32)
        up[tap] = block[0:8, :]
        fifth[tap, 0:8, :] = block[8:16, 0:256]
        fifth[tap, 8:16, :] = block[8:16, 256:512]
    sides = held[144:176, :].astype(f32)
    for tap in range(9):
        rows = slice(8 * (tap // 4), 8 * (tap // 4) + 8)
        fourth[tap] = sides[rows, 128 * (tap % 4) : 128 * (tap % 4) + 128]
    first = 176
    for out in plain:
        rows = out.shape[0]
        out[...] = held[first : first + rows, :].astype(f32)
        first = first + rows
    block = held[first : first + 32, :].astype(f32)
    early[0:24, :] = block[0:24, 0:256]
    early[24:48, :] = block[0:24, 256:512]


def run_unpack(whole):
    tiles = whole.shape[0] // 4

    def by_page(n):
        return (0, n % tiles * 4 + n // tiles, 0)

    def by_chunk(n):
        tile, page = n % tiles, n // tiles
        return (page % 2 * 16 + page // 2 * 8 + tile % 2 * 4 + tile // 4 * 2 + tile // 2 % 2, 0)

    def plain(n):
        return (n, 0)

    def by_column(n):
        return (n % 8, n // 8)

    def out(shape, block, spot):
        return jax.ShapeDtypeStruct(shape, f32), pl.BlockSpec(block, spot)

    outs = [
        out((9, 256, 512), (9, 8, 512), by_page),
        out((9, 512, 256), (9, 16, 256), by_page),
        out((9, 256, 128), (9, 8, 128), by_page),
        out((2048, 512), (64, 512), plain),
        out((512, 2048), (64, 512), by_column),
        out((512, 512), (16, 512), plain),
        out((512, 512), (16, 512), by_chunk),
        out((512, 512), (16, 512), by_chunk),
        out((512, 512), (16, 512), by_chunk),
        out((512, 512), (16, 512), by_chunk),
        out((1536, 256), (48, 256), plain),
    ]
    return pl.pallas_call(
        unpack_body,
        cost_estimate=price(14),
        grid=(whole.shape[0],),
        out_shape=[shape for shape, _ in outs],
        in_specs=[pl.BlockSpec(memory_space=pltpu.HBM)],
        out_specs=[spec for _, spec in outs],
        scratch_shapes=[
            pltpu.VMEM((4, *whole.shape[1:]), bf16),
            pltpu.SemaphoreType.DMA((4,)),
        ],
        compiler_params=pltpu.CompilerParams(vmem_limit_bytes=VMEM_CAP),
    )(in_hbm(whole))


def grad_bottom_all_body(ids, low_up, e_four, low_four, p_four, low_three, p_three, grad_up, grad_four, grad_three):
    lanes = low_up.shape[1]
    spread = quad_map(lanes // 4, 32)

    def own_part(low):
        size = low.shape[1] // (lanes // 128)
        own = lane_ids(low.shape) // size == ids[2]
        return jnp.where(own, low[...], jnp.zeros((), bf16))

    low = own_part(low_up)
    for tap, x in taps_of(mm(e_four[...], spread).astype(bf16), 64):
        grad_up[tap] = mm_nt(low, x).astype(bf16)
    low = own_part(low_four)
    for tap, x in taps_of(p_four[...], 32):
        grad_four[tap] = mm_nt(low, x).astype(bf16)
    low = own_part(low_three)
    for tap, x in taps_of(laid_out(p_three), 64):
        grad_three[tap] = mm_nt(low, x).astype(bf16)


def run_grad_bottom_all(ids, *arrays):
    return call(
        6,
        grad_bottom_all_body,
        [((9, 256, 512), bf16), ((9, 512, 256), bf16), ((9, 256, 128), bf16)],
        [],
        ids,
        arrays,
    )


def grad_down_body(ids, p_two, low_two, p_one, low_one, page, low_zero, table, cols):
    stacked = stack_cols(p_two[...], 128)
    for i in range(3):
        grad = mm_nt(low_two[...], stacked[:, i * 128 : i * 128 + 512]).astype(bf16)
        table[128 * i : 128 * i + 128, 0:192] = grad
    table[0:384, 192:256] = jnp.zeros((384, 64), bf16)
    table[384:512, :] = jnp.zeros((128, 256), bf16)
    stacked = stack_cols(p_one[...], 256)
    parts = [
        mm_nt(low_one[...], stacked[:, i * 256 : i * 256 + 2048]).astype(bf16) for i in range(3)
    ]
    grad = jnp.concatenate(parts, axis=0)
    table[384:480, 0:96] = grad[:96]
    table[384:480, 128:224] = grad[96:]
    rows = page[...].astype(f32)
    for j in range(3):
        cols[j] = col_shift(rows, j - 1, 512)
    pieces = [cols[j, :, i * 512 : i * 512 + 8192] for i in range(3) for j in range(3)]
    grad = mm_nt(low_zero[...], jnp.concatenate(pieces, axis=0).astype(bf16))
    table[480:512, 0:72] = grad.astype(bf16)


def run_grad_down(ids, *arrays):
    return call(
        3,
        grad_down_body,
        [((512, 256), bf16)],
        [((3, 8, 18 * 512), f32)],
        ids,
        arrays,
        late=(0, 2, 4),
    )[0]


def bucket_of(signed_gap):
    distance = jnp.abs(signed_gap)
    far_steps = jnp.zeros_like(distance)
    for threshold in bounds:
        far_steps = far_steps + (distance >= threshold).astype(jnp.int32)
    nearness = jnp.where(distance < 8, distance, 8 + far_steps)
    return nearness + jnp.where(signed_gap > 0, 16, 0).astype(jnp.int32)


def rms_scale(value, gain):
    return value * lax.rsqrt(jnp.mean(value * value, axis=-1, keepdims=True) + eps) * gain


def gelu_back(pre_act, upstream):
    return jax.vjp(jax.nn.gelu, pre_act)[1](upstream)[0]


def block_scores(query_heads, key_heads, query_meta, key_meta, bias_table, score_scale):
    query_pos, query_cx, query_cy, query_seg = query_meta
    key_pos, key_cx, key_cy, key_seg = key_meta
    rel_bucket = bucket_of(key_pos[None, :] - query_pos[:, None])
    hor_bucket = bucket_of(key_cx[None, :] - query_cx[:, None]) + NB
    ver_bucket = bucket_of(key_cy[None, :] - query_cy[:, None]) + 2 * NB
    slot_ids = jnp.arange(3 * NB)
    one_hot = (
        (rel_bucket[..., None] == slot_ids)
        | (hor_bucket[..., None] == slot_ids)
        | (ver_bucket[..., None] == slot_ids)
    ).astype(jnp.bfloat16)
    scores = (
        jnp.einsum("hqd,hkd->hqk", query_heads, key_heads, preferred_element_type=jnp.float32)
        * score_scale
    )
    scores = scores + jnp.einsum(
        "qkn,hn->hqk", one_hot, bias_table, preferred_element_type=jnp.float32
    )
    allowed = query_seg[:, None] == key_seg[None, :]
    return (scores, allowed, one_hot)


def norm_parts(value):
    scale = lax.rsqrt(jnp.mean(value * value, axis=-1, keepdims=True) + eps)
    return scale


def norm_back(value, gain, upstream):
    scale = norm_parts(value)
    weighted = upstream * gain
    inner = jnp.mean(weighted * value, axis=-1, keepdims=True)
    d_value = weighted * scale - value * (inner * scale * scale * scale)
    d_gain = jnp.sum(upstream * value * scale, axis=0, keepdims=True)
    return d_value, d_gain


def embed_body(ids, pieces, emb, roi, gain, wq, wk, wv, residual, normed, pooled, shared):
    total = pieces[0].astype(f32)
    for n in range(1, pieces.shape[0]):
        total = total + pieces[n].astype(f32)
    low = total.astype(bf16)
    pooled[...] = low
    pooled.send()
    resid = emb[...].astype(f32) + mm(low, roi[...])
    residual[...] = resid
    residual.send()
    normal = (resid * norm_parts(resid) * gain[...].astype(f32)).astype(bf16)
    normed[...] = normal
    normed.send()
    for n, weight in enumerate((wq, wk, wv)):
        turned = mm(normal, weight[...]).T.astype(bf16)
        for h in range(HEADS):
            shared[h, HD * n : HD * n + HD, :] = turned[HD * h : HD * h + HD, :]


def run_embed(ids, pieces, emb, *arrays):
    rows, width = emb.shape
    return call(
        2,
        embed_body,
        [
            ((rows, width), f32),
            ((rows, width), bf16),
            ((rows, pieces.shape[2]), bf16),
            ((HEADS, 3 * HD, rows), bf16),
        ],
        [],
        ids,
        (pieces, emb, *arrays),
        sent=(0, 1, 2),
    )


def looked_up(bucket, table, head, first):
    value = jnp.zeros(bucket.shape, f32)
    for n in range(NB):
        value = jnp.where(bucket == n, table[head, first + n], value)
    return value


def toeplitz(span, table, head, first):
    lane = lane_ids((1, 2 * span))
    gap = jnp.where(lane < span, -lane, 2 * span - lane)
    line = looked_up(bucket_of(gap), table, head, first)
    square = jnp.broadcast_to(line, (span, 2 * span))
    return pltpu.roll(square, 0, 1, stride=1, stride_axis=0)[:, :span].astype(bf16)


def centers(meta):
    return ((meta[0:1, :] + meta[2:3, :]) >> 1, (meta[1:2, :] + meta[3:4, :]) >> 1)


def one_hot_rows(value, span, turned):
    row = row_ids_of((span, value.shape[1]))
    if turned:
        row = span - 1 - row
    return jnp.where(row == value, 1.0, 0.0).astype(bf16)


def attend_body(tall, ids, table, meta, meta_cols, shared, prob, out_low, out_full, hits, spread, near):
    head = ids[0]
    seq = meta.shape[1]
    count = shared.shape[0]
    spans = (512, tall)
    for n, (value, span) in enumerate(zip(centers(meta), spans)):
        chart = toeplitz(span, table, head, NB * (n + 1))
        low = sum(spans[:n])
        spread[low : low + span, :] = mm(chart, one_hot_rows(value, span, False)).astype(bf16)
    cols = meta_cols[...]
    for n, span in enumerate(spans):
        value = (cols[:, n : n + 1] + cols[:, n + 2 : n + 3]) >> 1
        low = sum(spans[:n])
        same = lane_ids((1, span)) == value
        hits[:, low : low + span] = jnp.where(same, 1.0, 0.0).astype(bf16)
    edge = seq - 128
    near[0 : edge - 128, :] = jnp.full((edge - 128, 128), table[head, NB // 2 - 1], f32)
    near[edge + 256 :, :] = jnp.full((seq - 256, 128), table[head, NB - 1], f32)
    gap = row_ids_of((384, 128)) - 128 - lane_ids((384, 128))
    near[edge - 128 : edge + 256, :] = looked_up(bucket_of(gap), table, head, 0)
    query = jnp.concatenate([shared[n, 0:HD, :] for n in range(count)], axis=1)
    key = jnp.concatenate([shared[n, HD : 2 * HD, :] for n in range(count)], axis=1)
    value = jnp.concatenate([shared[n, 2 * HD :, :] for n in range(count)], axis=1)
    key = (key.astype(f32) * (HD**-0.5)).astype(bf16)
    seg_key = cols[:, 4:5]
    for block in range(seq // 256):
        own = slice(256 * block, 256 * block + 256)
        first = edge - 256 * block
        scores = mm_tn(key, query[:, own]) + mm(hits[...], spread[:, own])
        scores = scores + jnp.concatenate(
            [near[first : first + seq, :], near[first - 128 : first - 128 + seq, :]], axis=1
        )
        scores = jnp.where(seg_key == meta[4:5, own], scores, neg_large)
        weight = jnp.exp(scores - jnp.max(scores, axis=0, keepdims=True))
        weight = weight * (1.0 / jnp.sum(weight, axis=0, keepdims=True))
        low = weight.astype(bf16)
        prob[block] = low
        found = mm(value, low)
        out_full[:, own] = found
        for n in range(2):
            out_low[2 * block + n] = found[:, 128 * n : 128 * n + 128].astype(bf16)


def run_attend(tall, ids, after, table, meta, meta_cols, shared):
    seq = meta.shape[1]
    count = shared.shape[0]
    return call(
        9,
        functools.partial(attend_body, tall),
        [
            ((seq // 256, seq, 256), bf16),
            ((count, HD, seq // count), bf16),
            ((HD, seq), f32),
        ],
        [
            ((seq, 512 + tall), bf16),
            ((512 + tall, seq), bf16),
            ((2 * seq - 128, 128), f32),
        ],
        ids,
        (meta, meta_cols, shared),
        after,
        sent=(0, 2),
        table=table,
    )


def bucket_sums(value, bucket):
    lines = [
        jnp.sum(jnp.where(bucket == n, value, 0.0), axis=0, keepdims=True) for n in range(NB)
    ]
    return jnp.sum(jnp.concatenate(lines, axis=0), axis=1, keepdims=True)


def attend_back_body(tall, ids, meta, shared, prob, out_full, d_out, d_shared, d_table, near, drift, key_sum, value_sum):
    seq = meta.shape[1]
    count = shared.shape[0]
    spans = (512, tall)
    query = jnp.concatenate([shared[n, 0:HD, :] for n in range(count)], axis=1)
    key = jnp.concatenate([shared[n, HD : 2 * HD, :] for n in range(count)], axis=1)
    value = jnp.concatenate([shared[n, 2 * HD :, :] for n in range(count)], axis=1)
    d_found = jnp.concatenate([d_out[n] for n in range(count)], axis=1)
    delta = jnp.sum(d_found.astype(f32) * out_full[...], axis=0, keepdims=True)
    near[...] = jnp.zeros_like(near)
    key_sum[...] = jnp.zeros_like(key_sum)
    value_sum[...] = jnp.zeros_like(value_sum)
    places = centers(meta)
    turned = jnp.concatenate(
        [one_hot_rows(place, span, True) for place, span in zip(places, spans)], axis=0
    )
    edge = seq - 128
    scale = HD**-0.5
    for block in range(seq // 256):
        own = slice(256 * block, 256 * block + 256)
        first = edge - 256 * block
        low = prob[block]
        d_prob = mm_tn(value, d_found[:, own])
        d_score = low.astype(f32) * (d_prob - delta[:, own])
        near[first : first + seq, :] += d_score[:, :128]
        near[first - 128 : first - 128 + seq, :] += d_score[:, 128:]
        d_low = d_score.astype(bf16)
        d_query = (mm(key, d_low) * scale).astype(bf16)
        for n in range(2):
            d_shared[2 * block + n, 0:HD, :] = d_query[:, 128 * n : 128 * n + 128]
        key_sum[...] += mm_nt(query[:, own], d_low)
        value_sum[...] += mm_nt(d_found[:, own], low)
        drift[:, own] = mm(turned, d_low).astype(bf16)
    d_key = (key_sum[...] * scale).astype(bf16)
    d_value = value_sum[...].astype(bf16)
    for n in range(count):
        d_shared[n, HD : 2 * HD, :] = d_key[:, 128 * n : 128 * n + 128]
        d_shared[n, 2 * HD :, :] = d_value[:, 128 * n : 128 * n + 128]
    sums = []
    slot = 3 * ids[0]
    gap = row_ids_of((384, 128)) - 128 - lane_ids((384, 128))
    sums.append(bucket_sums(near[edge - 128 : edge + 256, :], bucket_of(gap)))
    row = row_ids_of((NB, 128))
    lane = lane_ids((NB, 128))
    behind = jnp.sum(near[0 : edge - 128, :], axis=0, keepdims=True)
    ahead = jnp.sum(near[edge + 256 :, :], axis=0, keepdims=True)
    far = jnp.where(row == NB // 2 - 1, behind, jnp.where(row == NB - 1, ahead, 0.0))
    sums[0] = sums[0] + jnp.sum(far, axis=1, keepdims=True)
    for n, (place, span) in enumerate(zip(places, spans)):
        low = sum(spans[:n])
        square = mm_nt(drift[low : low + span, :], one_hot_rows(place, span, False))
        square = jnp.concatenate([square, jnp.zeros_like(square)], axis=1)
        lined = pltpu.roll(square, 0, 1, stride=1, stride_axis=0)
        line = jnp.sum(lined, axis=0, keepdims=True)
        bucket = bucket_of(span - 1 - lane_ids((1, 2 * span)))
        sums.append(bucket_sums(line, bucket))
    d_table[...] = jnp.where(
        lane == slot,
        sums[0],
        jnp.where(lane == slot + 1, sums[1], jnp.where(lane == slot + 2, sums[2], 0.0)),
    )


def run_attend_back(tall, ids, after, meta, *arrays):
    seq = meta.shape[1]
    shared = arrays[0]
    return call(
        6,
        functools.partial(attend_back_body, tall),
        [(shared.shape, bf16), ((NB, 128), f32)],
        [
            ((2 * seq - 128, 128), f32),
            ((512 + tall, seq), bf16),
            ((HD, seq), f32),
            ((HD, seq), f32),
        ],
        ids,
        (meta, *arrays),
        after,
        late=(3, 2),
    )


def mixer_body(ids, found, residual, upstream, w_out, gain, w_in, w_down, result, act, d_pre, ffn_low, d_mixed, d_low, d_found, d_gain):
    attn = jnp.concatenate([found[h] for h in range(HEADS)], axis=0)
    mixed = residual[...] + mm_tn(attn, w_out[...])
    wide_gain = gain[...].astype(f32)
    low = (mixed * norm_parts(mixed) * wide_gain).astype(bf16)
    ffn_low[...] = low
    ffn_low.send()
    pre = mm(low, w_in[...])
    hidden = gelu_of(pre).astype(bf16)
    act[...] = hidden
    act.send()
    result[...] = (mixed + mm(hidden, w_down[...])).astype(bf16)
    result.send()
    d_hidden = (mm_nt(upstream[...], w_down[...]) * gelu_slope(pre)).astype(bf16)
    d_pre[...] = d_hidden
    d_pre.send()
    d_norm, gain_sum = norm_back(mixed, wide_gain, mm_nt(d_hidden, w_in[...]))
    d_gain[...] = gain_sum
    d_sum = upstream[...].astype(f32) + d_norm
    d_mixed[...] = d_sum
    d_mixed.send()
    narrow = d_sum.astype(bf16)
    d_low[...] = narrow
    d_low.send()
    back = mm_nt(w_out[...], narrow).astype(bf16)
    for h in range(HEADS):
        d_found[h] = back[HD * h : HD * h + HD, :]


def run_mixer(ids, found, residual, upstream, w_out, gain, w_in, w_down):
    rows, width = residual.shape
    wide = w_in.shape[1]
    return call(
        5,
        mixer_body,
        [
            ((rows, width), bf16),
            ((rows, wide), bf16),
            ((rows, wide), bf16),
            ((rows, width), bf16),
            ((rows, width), f32),
            ((rows, width), bf16),
            ((HEADS, HD, rows), bf16),
            ((1, width), f32),
        ],
        [],
        ids,
        (found, residual, upstream, w_out, gain, w_in, w_down),
        late=(5, 6),
        sent=(0, 1, 2, 3, 4, 5),
    )


def put_halves(ids, first, second, mine, other):
    for bit in range(2):

        @pl.when(ids[5] == bit)
        def _(bit=bit):
            mine[...] = first[...] if bit == 0 else second[...]
            other[...] = second[...] if bit == 0 else first[...]


def mixer_grads_body(ids, found, act, d_pre, ffn_low, d_low, upstream, table, token):
    width = ffn_low.shape[1]
    grad_out = mm_tn(act[...], upstream[...]).astype(bf16)
    grad_in = mm_tn(ffn_low[...], d_pre[...]).astype(bf16)
    attn = jnp.concatenate([found[h] for h in range(HEADS)], axis=0)
    grad_attn = mm(attn, d_low[...]).astype(bf16)
    for c in range(32):
        spot, row = 144 * c, 64 * (c % 8)
        table[spot : spot + 64, :] = grad_out[64 * c : 64 * c + 64, :]
        column = width * (c // 8)
        table[spot + 64 : spot + 128, :] = grad_in[row : row + 64, column : column + width]
        table[spot + 128 : spot + 144, :] = grad_attn[16 * c : 16 * c + 16, :]


def run_mixer_grads(ids, *arrays):
    return call(
        4,
        mixer_grads_body,
        [((4608, 512), bf16), TOKEN],
        [],
        ids,
        arrays,
        late=(1, 5, 3, 2, 4),
        sent=(0,),
    )


def embed_back_body(ids, d_shared, residual, d_mixed, gain, wq, wk, wv, roi, d_resid, d_low, d_pooled, d_gain, d_rows, token):
    turned = None
    for n, weight in enumerate((wq, wk, wv)):
        lines = jnp.concatenate([d_shared[h, HD * n : HD * n + HD, :] for h in range(HEADS)], axis=0)
        d_rows[n] = lines
        term = mm(weight[...], lines)
        turned = term if turned is None else turned + term
    d_norm, gain_sum = norm_back(residual[...], gain[...].astype(f32), turned.T)
    d_gain[...] = gain_sum
    total = d_mixed[...] + d_norm
    d_resid[...] = total
    d_resid.send()
    low = total.astype(bf16)
    d_low[...] = low
    d_pooled[...] = mm_nt(low, roi[...]).astype(bf16)


def run_embed_back(ids, d_shared, residual, *arrays):
    rows, width = residual.shape
    roi = arrays[-1]
    return call(
        2,
        embed_back_body,
        [
            ((rows, width), f32),
            ((rows, width), bf16),
            ((rows, roi.shape[0]), bf16),
            ((1, width), f32),
            ((3, HEADS * HD, rows), bf16),
            TOKEN,
        ],
        [],
        ids,
        (d_shared, residual, *arrays),
        late=(1, 2),
        sent=(0,),
    )


def embed_grads_body(ids, normed, d_rows, pooled, d_low, gains_one, gains_two, d_table, mine, other, token, table):
    width = normed.shape[1]
    turned = normed[...].astype(f32).T.astype(bf16)
    grads = [mm_nt(turned, d_rows[n]).astype(bf16) for n in range(3)]
    roi = mm_tn(pooled[...], d_low[...])
    lane = lane_ids((1, width))
    buckets = jnp.concatenate([d_table[...]] * (width // 128), axis=1)
    buckets = jnp.where(lane < 128, buckets, 0.0)
    blank = jnp.zeros((1, width), f32)
    for c in range(32):
        spot = 64 * (c % 16)
        for n in range(3):
            table[c // 16, spot + 16 * n : spot + 16 * n + 16, :] = grads[n][16 * c : 16 * c + 16, :]
        gains = [gains_one[...], gains_two[...]] if c == 0 else [blank, blank]
        lines = [roi[4 * c : 4 * c + 4, :], buckets[c : c + 1, :], *gains, blank]
        lines = jnp.concatenate(lines + [jnp.zeros((8, width), f32)], axis=0)
        table[c // 16, spot + 48 : spot + 64, :] = lines.astype(bf16)
    put_halves(ids, table.at[0], table.at[1], mine, other)


def run_embed_grads(ids, bit, after, *arrays):
    return call(
        3,
        embed_grads_body,
        [((1024, 512), bf16)] * 2 + [TOKEN],
        [((2, 1024, 512), bf16)],
        ids.at[5].set(bit),
        arrays,
        after,
    )


def on_device(
    embeddings,
    page_images,
    token_boxes,
    segment_ids,
    down_first,
    down_second,
    down_third,
    down_fourth,
    down_fifth,
    up_fourth,
    up_third,
    up_second,
    up_first,
    roi_proj,
    gain_attn,
    w_query,
    w_key,
    w_value,
    w_output,
    bias_table,
    gain_ffn,
    ffn_in,
    ffn_out,
    cotangent,
):
    tok_rows = embeddings.shape[1]
    model_width = embeddings.shape[2]
    tile_rows = page_images.shape[2]
    my_tile = lax.axis_index("tile")
    tile_count = lax.axis_size("tile")
    score_scale = HD ** (-0.5)
    cut = tile_count > 12
    window = 12 if cut else tile_count
    place = 6 if cut else my_tile
    ids = jnp.stack(
        [
            my_tile,
            jnp.asarray(tile_rows * tile_count, my_tile.dtype),
            jnp.asarray(place, my_tile.dtype),
            my_tile - place,
            jnp.asarray(2 if cut else my_tile, my_tile.dtype),
            jnp.asarray(0, my_tile.dtype),
        ]
    ).astype(jnp.int32)

    def gathered(block):
        copies = jnp.broadcast_to(block[None], (tile_count, *block.shape))
        return lax.all_to_all(copies, "tile", 0, 0, tiled=True)

    def windowed(block):
        if not cut:
            return gathered(block)
        blocks = lax.all_gather(block, "tile", axis=0)
        blocks = jnp.pad(blocks, ((6, 6), (0, 0), (0, 0)))
        return lax.dynamic_slice_in_dim(blocks, my_tile, window, 0)

    def from_side(block, step):
        hops = [
            (source, source + step) for source in range(tile_count) if 0 <= source + step < tile_count
        ]
        return lax.ppermute(block, "tile", hops)

    def lined(weight):
        return weight.transpose(0, 2, 1, 3).reshape(3, weight.shape[2], -1)

    def lined_back(weight):
        flipped = weight[::-1, ::-1]
        return flipped.transpose(0, 3, 1, 2).reshape(3, weight.shape[3], -1)

    def beside(table, count):
        return jnp.concatenate(jnp.split(table, count, axis=0), axis=1)

    def below(table, count):
        return jnp.concatenate(jnp.split(table, count, axis=1), axis=0)

    def as_rows(member):
        return member.reshape(-1, member.shape[-1])

    def bit_of(axis, mask):
        return (lax.axis_index(axis) & mask) // mask

    def swapped(block, axis, mask):
        hops = [(source, source ^ mask) for source in range(lax.axis_size(axis))]
        return lax.ppermute(block, axis, hops)

    def halved(halves, step, *after):
        mine, other, _ = halves
        got = swapped(other, *HOPS[step])
        if step + 1 == len(HOPS):
            return run_finish(ids, mine, got, after)
        return run_halve(ids, bit_of(*HOPS[step + 1]), mine, got, after)

    line = page_images.shape[3]
    meta = jnp.concatenate([token_boxes[:, 0], segment_ids])
    digits = jnp.concatenate([meta // 256, meta % 256, jnp.zeros((2, tok_rows), jnp.int32)])
    digits = digits.astype(jnp.bfloat16).reshape(24, -1)
    sheet = jnp.concatenate([page_images[0].reshape(24, -1), digits], axis=1)
    sheets = gathered(sheet)
    digits_all = sheets[:, :, 2 * line :].reshape(tile_count, 12, tok_rows)
    digits_all = digits_all.transpose(1, 0, 2).reshape(12, -1).astype(jnp.int32)
    meta_all = jnp.pad(digits_all[:5] * 256 + digits_all[5:10], ((0, 3), (0, 0)))
    if cut:
        sheets = jnp.pad(sheets, ((2, 2), (0, 0), (0, 0)))
        sheets = lax.dynamic_slice_in_dim(sheets, my_tile, 5, 0)
    left_all, top_all, right_all, bottom_all, seg_all = (meta_all[n] for n in range(5))
    box_rows = meta_all.T
    seq_all = seg_all.shape[0]
    w_zero = jnp.pad(down_first.transpose(2, 0, 1, 3), ((0, 0), (0, 0), (0, 0), (0, 5)))
    w_zero = w_zero.reshape(w_zero.shape[0], -1)
    pre_zero, pre_one, p_one, pre_two, p_two, p_three, page_own = run_down(
        ids, sheets, w_zero, lined(down_second), lined(down_third)
    )
    p_three_all = windowed(p_three)
    pre_three, pre_four, p_four, e_four, pre_up_three, dec_three = run_bottom(
        cut, ids, p_three_all, down_fourth, down_fifth, up_fourth
    )
    (
        pre_up_two,
        pre_up_one,
        pre_up_zero,
        u_three,
        dec_two,
        dec_one,
        features,
        edge_end,
        edge_start,
    ) = run_up(
        ids, dec_three, pre_two, pre_one, pre_zero, up_third, lined(up_second), lined(up_first)
    )
    pre_up_edges = (from_side(edge_end, 1), from_side(edge_start, -1))
    pooled_own = run_pool(ids, box_rows, features, 256)
    pieces = lax.all_to_all(
        pooled_own.reshape(tile_count, tok_rows, -1), "tile", 0, 0, tiled=True
    )
    gain_row_one = gain_attn.reshape(1, -1)
    gain_row_two = gain_ffn.reshape(1, -1)
    heads_first = tile_count == HEADS
    if heads_first:
        tall = tile_rows * tile_count
        residual, normed_low, pooled_low, shared = run_embed(
            ids, pieces, embeddings[0], roi_proj, gain_row_one, w_query, w_key, w_value
        )
        shared = lax.all_to_all(shared, "tile", 0, 0, tiled=True)
        prob, found_low, found_full = run_attend(
            tall, ids, (), bias_table.astype(jnp.float32), meta_all, box_rows, shared
        )
        found = lax.all_to_all(found_low, "tile", 0, 0, tiled=True)
        result_low, act_low, d_pre, ffn_low, d_mixed, d_mixed_low, d_found, grad_gain_ffn = run_mixer(
            ids, found, residual, cotangent[0], w_output, gain_row_two, ffn_in, ffn_out
        )
        d_found = lax.all_to_all(d_found, "tile", 0, 0, tiled=True)
        mixer_table, mixer_token = run_mixer_grads(
            ids, found, act_low, d_pre, ffn_low, d_mixed_low, cotangent[0]
        )
        mixer_share = lax.psum_scatter(
            mixer_table, (*PAGES, "tile"), scatter_dimension=0, tiled=True
        )
        d_shared, d_table = run_attend_back(
            tall, ids, (mixer_token,), meta_all, shared, prob, found_full, d_found
        )
        d_shared = lax.all_to_all(d_shared, "tile", 0, 0, tiled=True)
        d_residual, d_resid_low, d_pooled, grad_gain_attn, d_rows, embed_token = run_embed_back(
            ids, d_shared, residual, d_mixed, gain_row_one, w_query, w_key, w_value, roi_proj
        )
        embed_halves = run_embed_grads(
            ids,
            bit_of(*HOPS[0]),
            (),
            normed_low,
            d_rows,
            pooled_low,
            d_resid_low,
            grad_gain_attn,
            grad_gain_ffn,
            d_table,
        )
        embed_halves = halved(embed_halves, 0)
        ordering = embed_halves[2:]
    else:
        ordering = ()
        pooled_low = jnp.sum(pieces.astype(jnp.float32), axis=0).astype(jnp.bfloat16)
        residual = embeddings[0].astype(jnp.float32) + jnp.dot(
            pooled_low, roi_proj, preferred_element_type=jnp.float32
        )
        gain_one = gain_attn.astype(jnp.float32)
        normed_low = rms_scale(residual, gain_one).astype(jnp.bfloat16)
        query_low = jnp.dot(normed_low, w_query, preferred_element_type=jnp.float32).astype(
            jnp.bfloat16
        )
        key_low = jnp.dot(normed_low, w_key, preferred_element_type=jnp.float32).astype(jnp.bfloat16)
        value_low = jnp.dot(normed_low, w_value, preferred_element_type=jnp.float32).astype(
            jnp.bfloat16
        )

        def to_heads(flat_rows):
            return flat_rows.reshape(tok_rows, HEADS, HD).transpose(1, 0, 2)

        def from_heads(head_rows):
            return head_rows.transpose(1, 0, 2).reshape(tok_rows, model_width)

        query_heads = to_heads(query_low)
        own_keys = to_heads(key_low)
        own_values = to_heads(value_low)
        key_all, value_all = (
            lax.all_gather(own_keys, "tile", axis=1, tiled=True),
            lax.all_gather(own_values, "tile", axis=1, tiled=True),
        )
        center_x = (left_all + right_all) // 2
        center_y = (top_all + bottom_all) // 2
        key_meta = (jnp.arange(seq_all), center_x, center_y, seg_all)
        first_tok = my_tile * tok_rows
        query_meta = tuple(
            (lax.dynamic_slice_in_dim(member, first_tok, tok_rows, 0) for member in key_meta)
        )
        key_block = math.gcd(seq_all, 1024)
        block_count = seq_all // key_block

        def key_slice(block_id):
            first_key = block_id * key_block
            keys_blk = lax.dynamic_slice_in_dim(key_all, first_key, key_block, 1)
            values_blk = lax.dynamic_slice_in_dim(value_all, first_key, key_block, 1)
            meta_blk = tuple(
                (lax.dynamic_slice_in_dim(member, first_key, key_block, 0) for member in key_meta)
            )
            return (keys_blk, values_blk, meta_blk)

        def stats_step(running, block_id):
            run_max, run_sum = running
            keys_blk, values_blk, meta_blk = key_slice(block_id)
            scores, allowed, one_hot = block_scores(
                query_heads, keys_blk, query_meta, meta_blk, bias_table, score_scale
            )
            scores = jnp.where(allowed[None], scores, neg_large)
            new_max = jnp.maximum(run_max, jnp.max(scores, axis=-1))
            run_sum = run_sum * jnp.exp(run_max - new_max) + jnp.sum(
                jnp.exp(scores - new_max[..., None]), axis=-1
            )
            return ((new_max, run_sum), None)

        start_stats = (
            jnp.full((HEADS, tok_rows), neg_large, jnp.float32),
            jnp.zeros((HEADS, tok_rows), jnp.float32),
        )
        (run_max, run_sum), _ = lax.scan(stats_step, start_stats, jnp.arange(block_count))
        log_total = run_max + jnp.log(run_sum)

        def out_step(attn_acc, block_id):
            keys_blk, values_blk, meta_blk = key_slice(block_id)
            scores, allowed, one_hot = block_scores(
                query_heads, keys_blk, query_meta, meta_blk, bias_table, score_scale
            )
            attn_prob = jnp.where(allowed[None], jnp.exp(scores - log_total[..., None]), 0.0)
            attn_acc = attn_acc + jnp.einsum(
                "hqk,hkd->hqd",
                attn_prob.astype(jnp.bfloat16),
                values_blk,
                preferred_element_type=jnp.float32,
            )
            return (attn_acc, None)

        attn_heads, _ = lax.scan(
            out_step, jnp.zeros((HEADS, tok_rows, HD), jnp.float32), jnp.arange(block_count)
        )
        attn_low = from_heads(attn_heads).astype(jnp.bfloat16)
        mixed_rows = residual + jnp.dot(attn_low, w_output, preferred_element_type=jnp.float32)
        gain_two = gain_ffn.astype(jnp.float32)
        ffn_low = rms_scale(mixed_rows, gain_two).astype(jnp.bfloat16)
        pre_ffn = jnp.dot(ffn_low, ffn_in, preferred_element_type=jnp.float32)
        act_low = jax.nn.gelu(pre_ffn).astype(jnp.bfloat16)
        result_rows = mixed_rows + jnp.dot(act_low, ffn_out, preferred_element_type=jnp.float32)
        upstream = cotangent[0]
        grad_ffn_out = jnp.einsum("tf,td->fd", act_low, upstream, preferred_element_type=jnp.float32)
        d_act = jnp.einsum("td,fd->tf", upstream, ffn_out, preferred_element_type=jnp.float32)
        d_pre = gelu_back(pre_ffn, d_act).astype(jnp.bfloat16)
        grad_ffn_in = jnp.einsum("td,tf->df", ffn_low, d_pre, preferred_element_type=jnp.float32)
        d_ffn_norm = jnp.einsum("tf,df->td", d_pre, ffn_in, preferred_element_type=jnp.float32)
        d_mixed_norm, grad_gain_ffn = jax.vjp(rms_scale, mixed_rows, gain_two)[1](d_ffn_norm)
        d_mixed = upstream.astype(jnp.float32) + d_mixed_norm
        d_mixed_low = d_mixed.astype(jnp.bfloat16)
        grad_output = jnp.einsum("tc,td->cd", attn_low, d_mixed_low, preferred_element_type=jnp.float32)
        d_attn = jnp.einsum(
            "td,cd->tc", d_mixed_low, w_output, preferred_element_type=jnp.float32
        ).astype(jnp.bfloat16)
        dout_heads = to_heads(d_attn)
        row_delta = jnp.sum(dout_heads.astype(jnp.float32) * attn_heads, axis=-1)

        def back_step(running, block_id):
            keys_blk, values_blk, meta_blk = key_slice(block_id)
            scores, allowed, one_hot = block_scores(
                query_heads, keys_blk, query_meta, meta_blk, bias_table, score_scale
            )
            attn_prob = jnp.where(allowed[None], jnp.exp(scores - log_total[..., None]), 0.0)
            d_prob = jnp.einsum(
                "hqd,hkd->hqk", dout_heads, values_blk, preferred_element_type=jnp.float32
            )
            d_score = (attn_prob * (d_prob - row_delta[..., None])).astype(jnp.bfloat16)
            query_acc = running[0] + jnp.einsum(
                "hqk,hkd->hqd", d_score, keys_blk, preferred_element_type=jnp.float32
            )
            table_acc = running[1] + jnp.einsum(
                "hqk,qkn->hn", d_score, one_hot, preferred_element_type=jnp.float32
            )
            first_key = block_id * key_block
            key_part = (
                jnp.einsum("hqk,hqd->hkd", d_score, query_heads, preferred_element_type=jnp.float32)
                * score_scale
            )
            value_part = jnp.einsum(
                "hqk,hqd->hkd",
                attn_prob.astype(jnp.bfloat16),
                dout_heads,
                preferred_element_type=jnp.float32,
            )
            key_acc = lax.dynamic_update_slice_in_dim(running[2], key_part, first_key, 1)
            value_acc = lax.dynamic_update_slice_in_dim(running[3], value_part, first_key, 1)
            return ((query_acc, table_acc, key_acc, value_acc), None)

        start_back = (
            jnp.zeros((HEADS, tok_rows, HD), jnp.float32),
            jnp.zeros((HEADS, 3 * NB), jnp.float32),
        )
        start_back = start_back + (
            jnp.zeros((HEADS, seq_all, HD), jnp.float32),
            jnp.zeros((HEADS, seq_all, HD), jnp.float32),
        )
        back_out, _ = lax.scan(back_step, start_back, jnp.arange(block_count))
        query_acc = back_out[0]
        grad_bias_table = back_out[1]
        key_grad, value_grad = (
            lax.psum_scatter(back_out[2], "tile", scatter_dimension=1, tiled=True),
            lax.psum_scatter(back_out[3], "tile", scatter_dimension=1, tiled=True),
        )
        dq_low = from_heads(query_acc * score_scale).astype(jnp.bfloat16)
        dk_low = from_heads(key_grad).astype(jnp.bfloat16)
        dv_low = from_heads(value_grad).astype(jnp.bfloat16)
        grad_query = jnp.einsum("td,te->de", normed_low, dq_low, preferred_element_type=jnp.float32)
        grad_key = jnp.einsum("td,te->de", normed_low, dk_low, preferred_element_type=jnp.float32)
        grad_value = jnp.einsum("td,te->de", normed_low, dv_low, preferred_element_type=jnp.float32)
        d_normed = (
            jnp.einsum("te,de->td", dq_low, w_query, preferred_element_type=jnp.float32)
            + jnp.einsum("te,de->td", dk_low, w_key, preferred_element_type=jnp.float32)
            + jnp.einsum("te,de->td", dv_low, w_value, preferred_element_type=jnp.float32)
        )
        d_resid_norm, grad_gain_attn = jax.vjp(rms_scale, residual, gain_one)[1](d_normed)
        d_residual = d_mixed + d_resid_norm
        d_resid_low = d_residual.astype(jnp.bfloat16)
        grad_roi_proj = jnp.einsum(
            "tp,td->pd", pooled_low, d_resid_low, preferred_element_type=jnp.float32
        )
        d_pooled = jnp.einsum("td,pd->tp", d_resid_low, roi_proj, preferred_element_type=jnp.float32)
        d_pooled = d_pooled.astype(jnp.bfloat16)
        result_low = result_rows.astype(jnp.bfloat16)
        mixer_table = jnp.concatenate([grad_ffn_out, below(grad_ffn_in, 4), grad_output], axis=0)
        mixer_table = mixer_table.astype(jnp.bfloat16)
        chart = grad_bias_table.reshape(HEADS, 3, NB).transpose(2, 0, 1).reshape(NB, 3 * HEADS)
        embed_table = jnp.concatenate(
            [
                grad_query,
                grad_key,
                grad_value,
                grad_roi_proj,
                jnp.pad(jnp.stack([grad_gain_attn, grad_gain_ffn]), ((0, 14), (0, 0))),
                jnp.pad(chart, ((0, 80), (0, model_width - 3 * HEADS))),
            ],
            axis=0,
        ).astype(jnp.bfloat16)
    d_pooled_all = gathered(d_pooled).reshape(seq_all, -1)
    d_features, low_zero_up, d_before, d_behind, box_token = run_unpool(
        ids, ordering, box_rows, d_pooled_all, pre_up_zero, 256
    )
    if heads_first:
        embed_halves = halved(embed_halves, 1, box_token)
        ordering = ()
    d_dec_one, d_dec_two, d_dec_three, low_one_up, low_two_up, up_token = run_up_back(
        ids,
        ordering,
        d_before,
        low_zero_up,
        d_behind,
        *pre_up_edges,
        pre_up_one,
        pre_up_two,
        lined_back(up_first),
        lined_back(up_second),
        up_third,
    )
    d_dec_three_all = windowed(d_dec_three)
    grad_up_first = run_grad_up_first(ids, (up_token,), dec_one, low_zero_up)
    if heads_first:
        embed_halves = halved(embed_halves, 2, up_token)
        ordering = embed_halves[2:]
    light_early, early_token = run_grad_up(
        ids, ordering, grad_up_first, dec_two, low_one_up, u_three, low_two_up
    )
    low_three_up, low_four, low_three, d_pool_three, bottom_token = run_bottom_back(
        cut,
        ids,
        (early_token,),
        d_dec_three_all,
        pre_up_three,
        pre_four,
        pre_three,
        up_fourth,
        down_fifth,
        down_fourth,
    )
    dp_count = lax.axis_size(PAGES)
    if heads_first:
        embed_share = halved(halved(embed_halves, 3, bottom_token), 4)
        early_parts = lax.all_to_all(
            light_early.reshape(32, -1, 256), (*PAGES, "tile"), 0, 0, tiled=True
        )
        early_share, _ = run_total(ids, early_parts)
        ordering = ()
    bottom_parts = (low_three_up, e_four, low_four, p_four, low_three, p_three_all)
    if cut:
        heavy = run_grad_bottom_all(ids, *bottom_parts)
        heavy_token = ()
    else:
        heavy, *heavy_token = run_grad_bottom(tile_count, dp_count, ids, ordering, *bottom_parts)
    low_two, low_one, low_zero = run_down_back(
        ids,
        heavy_token,
        d_pool_three,
        d_dec_two,
        pre_two,
        d_dec_one,
        pre_one,
        d_features,
        pre_zero,
        down_third,
        lined_back(down_second),
    )
    light_late = run_grad_down(ids, p_two, low_two, p_one, low_one, page_own, low_zero)
    both_axes = (*PAGES, "tile")
    device_total = dp_count * tile_count

    def summed_share(table):
        parts = table.reshape(device_total, -1, table.shape[1])
        parts = lax.all_to_all(parts, both_axes, 0, 0, tiled=True)
        return jnp.sum(parts.astype(jnp.float32), axis=0).astype(jnp.bfloat16)

    def spread_out(share):
        copies = jnp.broadcast_to(share[None], (device_total, *share.shape))
        return lax.all_to_all(copies, both_axes, 0, 0, tiled=True)

    late = spread_out(summed_share(light_late)).reshape(light_late.shape).astype(jnp.float32)
    wide = ffn_in.shape[1]
    if heads_first:
        parts = lax.all_to_all(heavy, PAGES, 0, 0, tiled=True)
        share = run_gather(ids, parts, mixer_share, embed_share, early_share)
        whole = lax.all_gather(share, both_axes, axis=0)
        *heavy_sums, sum_ffn_out, sum_ffn_in, sum_output, sum_query, sum_key, sum_value, rest, early = (
            run_unpack(whole)
        )
        rest = rest.reshape(NB, 16, model_width)
        sum_roi = rest[:, :4].reshape(-1, model_width)
        sum_bias = rest[:, 4, : 3 * HEADS].reshape(NB, HEADS, 3)
        sum_gain_attn, sum_gain_ffn = rest[0, 5], rest[0, 6]
    else:
        early = spread_out(summed_share(light_early)).reshape(light_early.shape)
        early = early.astype(jnp.float32)
        heavy_sums = [lax.psum(member, both_axes).astype(jnp.float32) for member in heavy]
        mixer_all = lax.psum(mixer_table, both_axes).astype(jnp.float32)
        embed_all = lax.psum(embed_table, both_axes).astype(jnp.float32)
        sum_ffn_out = mixer_all[:wide]
        sum_ffn_in = beside(mixer_all[wide : 2 * wide], wide // model_width)
        sum_output = mixer_all[2 * wide :]
        sum_query, sum_key, sum_value = (
            embed_all[n * model_width : (n + 1) * model_width] for n in range(3)
        )
        last = 3 * model_width + roi_proj.shape[0]
        sum_roi = embed_all[3 * model_width : last]
        sum_bias = embed_all[last + 16 : last + 16 + NB, : 3 * HEADS].reshape(NB, HEADS, 3)
        sum_gain_attn, sum_gain_ffn = embed_all[last], embed_all[last + 1]
    sum_bias = sum_bias.transpose(1, 2, 0).reshape(bias_table.shape)

    def unlined(table, kind):
        return table.reshape(3, kind.shape[2], 3, kind.shape[3]).transpose(0, 2, 1, 3)

    second_rest = below(early[1344:1440], 2)
    sum_up_second = jnp.concatenate([early[1152:1344], second_rest], axis=1)
    sum_down_second = jnp.concatenate([late[384:480, :96], late[384:480, 128:224]], axis=0)
    sum_first = late[480:512, :72].reshape(32, 3, 3, 8)[..., :3].transpose(1, 2, 0, 3)
    summed = [
        sum_first,
        unlined(sum_down_second, down_second),
        unlined(late[:384, :192], down_third),
        heavy_sums[2].reshape(down_fourth.shape),
        heavy_sums[1].reshape(down_fifth.shape),
        heavy_sums[0].reshape(up_fourth.shape),
        early[:1152].reshape(up_third.shape),
        unlined(sum_up_second, up_second),
        unlined(early[1440:1536, :192], up_first),
        sum_roi,
        sum_gain_attn,
        sum_query,
        sum_key,
        sum_value,
        sum_output,
        sum_bias,
        sum_gain_ffn,
        sum_ffn_in,
        sum_ffn_out,
    ]
    return (
        result_low[None],
        d_residual[None],
        summed[0],
        summed[1],
        summed[2],
        summed[3],
        summed[4],
        summed[5],
        summed[6],
        summed[7],
        summed[8],
        summed[9],
        summed[10],
        summed[11],
        summed[12],
        summed[13],
        summed[14],
        summed[15],
        summed[16],
        summed[17],
        summed[18],
    )


def solution(mesh):
    tiles = mesh.shape["tile"]
    split = Mesh(mesh.devices.reshape(mesh.shape["dp"] // 2, 2, tiles), (*PAGES, "tile"))
    return jax.shard_map(
        on_device,
        mesh=split,
        in_specs=(
            P(PAGES, "tile", None),
            P(PAGES, None, "tile", None),
            P(None, PAGES, "tile"),
            P(PAGES, "tile"),
            P(),
            P(),
            P(),
            P(),
            P(),
            P(),
            P(),
            P(),
            P(),
            P(),
            P(),
            P(),
            P(),
            P(),
            P(),
            P(),
            P(),
            P(),
            P(),
            P(PAGES, "tile", None),
        ),
        out_specs=(
            P(PAGES, "tile", None),
            P(PAGES, "tile", None),
            P(),
            P(),
            P(),
            P(),
            P(),
            P(),
            P(),
            P(),
            P(),
            P(),
            P(),
            P(),
            P(),
            P(),
            P(),
            P(),
            P(),
            P(),
            P(),
        ),
        check_vma=False,
    )
```
